32 devices in a mesh: dp: 8 (over y, x, core), tensor: 4 (over z).
Axes of the slice: x: 2, y: 2, z: 4, core: 2. Of those that a mesh axis runs over, the one named last changes fastest.
Arguments:
- tokens: bfloat16 [10240, 2048], P(('dp', 'tensor')), may hold values from -6 to 6
- cotangent: bfloat16 [10240, 2048], P(('dp', 'tensor')), may hold values from -6 to 6
- attention_gain: bfloat16 [2048], replicated, may hold values from 0.5 to 1.5
- feed_gain: bfloat16 [2048], replicated, may hold values from 0.5 to 1.5
- query_weight: bfloat16 [2048, 2048], P('dp', 'tensor'), may hold values from -0.125 to 0.125
- key_weight: bfloat16 [2048, 2048], P('dp', 'tensor'), may hold values from -0.125 to 0.125
- value_weight: bfloat16 [2048, 2048], P('dp', 'tensor'), may hold values from -0.125 to 0.125
- output_weight: bfloat16 [2048, 2048], P('dp', 'tensor'), may hold values from -0.75 to 0.75
- gate_weight: bfloat16 [2048, 8192], P('dp', 'tensor'), may hold values from -0.125 to 0.125
- up_weight: bfloat16 [2048, 8192], P('dp', 'tensor'), may hold values from -0.125 to 0.125
- down_weight: bfloat16 [2048, 8192], P('dp', 'tensor'), may hold values from -0.0625 to 0.0625
- entry_maps: bfloat16 [5, 8, 2048, 16], replicated, may hold values from -0.125 to 0.125
- head_exits: bfloat16 [3, 8, 16, 2048], P(None, None, None, 'tensor'), may hold values from -1.5 to 1.5
- unit_exits: bfloat16 [2, 8, 16, 8192], P(None, None, None, 'tensor'), may hold values from -1.5 to 1.5
- output_entry: bfloat16 [8, 2048, 16], P(None, 'tensor'), may hold values from -0.75 to 0.75
- down_entry: bfloat16 [8, 8192, 16], P(None, 'tensor'), may hold values from -0.0625 to 0.0625
- final_exits: bfloat16 [2, 8, 16, 2048], replicated, may hold values from -1.5 to 1.5
- parents: int32 [8, 20], P('dp'), may hold values from -1 to 11, as said below
- adapter_pick: int32 [8], P('dp'), may hold values from 0 to 7
Outputs:
- result: bfloat16 [10240, 2048], P(('dp', 'tensor'))
- grad_tokens: bfloat16 [10240, 2048], P(('dp', 'tensor'))
- grad_entries: float32 [5, 8, 2048, 16], replicated
- grad_heads: float32 [3, 8, 16, 2048], P(None, None, None, 'tensor')
- grad_units: float32 [2, 8, 16, 8192], P(None, None, None, 'tensor')
- grad_output: float32 [8, 2048, 16], P(None, 'tensor')
- grad_down: float32 [8, 8192, 16], P(None, 'tensor')
- grad_finals: float32 [2, 8, 16, 2048], replicated
The draws below stay inside these ranges and needn't reach their ends.
Inputs may be any that keep to these rules, and one draw needn't show every extreme that they name: `parents`: in every tree, blocks 0 to 7 form the trunk, each the child of the block before it (block 0 has -1); blocks 8 to 11 are branches whose parent is block 7; blocks 12 to 19 are leaves whose parent is a branch block, each branch the parent of two leaves.
All inputs are finite; a program needn't handle non-finite values.
Results may differ from the reference program's by a relative error of at most 0.024.
Values may be sent and summed in bfloat16 or wider, within the bound.
A program may use at most 320 MiB of HBM per device.

```python
import jax
import jax.numpy as jnp
from jax import lax

D = 2048
HEAD_DIM = 64
FF = 8192
RANK = 16
ADAPTERS = 8
SEG = 64
TREE_TOK = 1280
TREES = 8
TOKENS = 10240


def draw_parents(key, part):
    key = jax.random.fold_in(key, 7)
    keys = jax.random.split(key, TREES)

    def one_tree(tree_key):
        order = jax.random.permutation(tree_key, 8)
        trunk = jnp.arange(8, dtype=jnp.int32) - 1
        branch = jnp.full((4,), 7, dtype=jnp.int32)
        leaves = (8 + order // 2).astype(jnp.int32)
        return jnp.concatenate([trunk, branch, leaves])
    return jax.vmap(one_tree)(keys)


def place_ends(array, key, smallest, largest):
    dims = array.shape
    spot = [jax.random.randint(jax.random.fold_in(key, axis), (), 0, dims[axis]) for axis in range(len(dims))]
    array = array.at[tuple(spot)].set(smallest)
    longest = dims.index(max(dims))
    spot[longest] = (spot[longest] + 1) % dims[longest]
    return array.at[tuple(spot)].set(largest)


def block_levels(own_key, shape, shards, low, top_value):
    def one(dim, parts):
        steps = jax.random.uniform(jax.random.fold_in(jax.random.fold_in(own_key, 6), dim), (parts,), jnp.float32, low / len(shards), top_value / len(shards))
        return jnp.repeat(jnp.exp(steps), shape[dim] // parts).reshape((-1,) + (1,) * (len(shape) - dim - 1))

    factor_of = one(*shards[0])
    for cut in shards[1:]:
        factor_of = factor_of * one(*cut)
    return factor_of


def noise(rng, dims, width, limit, cuts=(), kind=jnp.bfloat16):
    result = jax.random.normal(rng, dims, jnp.float32) * width
    if len(cuts) > 0:
        result = block_levels(rng, dims, cuts, -0.22, 0.18) * result
    return jnp.clip(result, min=-limit, max=limit).astype(kind)


def setup_inputs(seed: int = 0) -> dict:
    streams_of = jax.random.split(jax.random.key(seed), 20)
    return {
        "tokens": noise(streams_of[0], (TOKENS, D), 1.0, 6.0, ((0, 32),)),
        "cotangent": noise(streams_of[1], (TOKENS, D), 1.0, 6.0, ((0, 32),)),
        "attention_gain": jnp.clip(1.0 + 0.1 * jax.random.normal(streams_of[2], (D,), jnp.float32), 0.5, 1.5).astype(jnp.bfloat16),
        "feed_gain": jnp.clip(1.0 + 0.1 * jax.random.normal(streams_of[3], (D,), jnp.float32), 0.5, 1.5).astype(jnp.bfloat16),
        "query_weight": noise(streams_of[4], (D, D), D ** -0.5, 0.125, ((0, 8), (1, 4))),
        "key_weight": noise(streams_of[5], (D, D), D ** -0.5, 0.125, ((0, 8), (1, 4))),
        "value_weight": noise(streams_of[6], (D, D), D ** -0.5, 0.125, ((0, 8), (1, 4))),
        "output_weight": noise(streams_of[7], (D, D), (D // 32) ** -0.5, 0.75, ((0, 8), (1, 4))),
        "gate_weight": noise(streams_of[8], (D, FF), D ** -0.5, 0.125, ((0, 8), (1, 4))),
        "up_weight": noise(streams_of[9], (D, FF), D ** -0.5, 0.125, ((0, 8), (1, 4))),
        "down_weight": noise(streams_of[10], (D, FF), FF ** -0.5, 0.0625, ((0, 8), (1, 4))),
        "entry_maps": noise(streams_of[11], (5, ADAPTERS, D, RANK), D ** -0.5, 0.125),
        "head_exits": noise(streams_of[12], (3, ADAPTERS, RANK, D), RANK ** -0.5, 1.5, ((3, 4),)),
        "unit_exits": noise(streams_of[13], (2, ADAPTERS, RANK, FF), RANK ** -0.5, 1.5, ((3, 4),)),
        "output_entry": noise(streams_of[14], (ADAPTERS, D, RANK), (D // 32) ** -0.5, 0.75, ((1, 4),)),
        "down_entry": noise(streams_of[15], (ADAPTERS, FF, RANK), FF ** -0.5, 0.0625, ((1, 4),)),
        "final_exits": noise(streams_of[16], (2, ADAPTERS, RANK, D), RANK ** -0.5, 1.5),
        "parents": draw_parents(jax.random.fold_in(streams_of[19], 71), 0),
        "adapter_pick": place_ends(jax.random.randint(streams_of[18], (TREES,), 0, ADAPTERS), jax.random.fold_in(streams_of[18], 1), 0, ADAPTERS - 1).astype(jnp.int32),
    }


@jax.custom_vjp
def low(v):
    return lax.optimization_barrier(v.astype(jnp.bfloat16)).astype(jnp.float32)

@jax.custom_vjp
def low_back(v):
    return v

def low_keep(v):
    return (low(v), None)

def low_pass(kept, grad):
    return (grad,)

def back_keep(v):
    return (v, None)

def back_low(kept, grad):
    return (low(grad),)
low.defvjp(low_keep, low_pass)
low_back.defvjp(back_keep, back_low)
eps = 1e-05
theta = 130000.0
highest = lax.Precision.HIGHEST

def product(left, right):
    return jnp.dot(left, right, precision=highest, preferred_element_type=jnp.float32)

def ancestry(parent_row):
    count = parent_row.shape[0]
    ids = jnp.arange(count, dtype=jnp.int32)
    step = (parent_row[:, None] == ids[None, :]).astype(jnp.float32)
    identity = jnp.eye(count, dtype=jnp.float32)

    def grow(index, reach):
        return jnp.minimum(identity + product(step, reach), 1.0)
    return lax.fori_loop(0, count, grow, identity)

def tree_layout(parent_row, seg):
    reach = ancestry(parent_row)
    depth = lax.optimization_barrier(jnp.sum(reach, axis=1)) - 1.0
    total = reach.shape[0] * seg
    place = jnp.arange(total, dtype=jnp.int32)
    offset = (place % seg).astype(jnp.float32)
    position = jnp.repeat(depth, seg) * seg + offset
    allowed = jnp.repeat(jnp.repeat(reach, seg, axis=0), seg, axis=1) > 0.5
    allowed = allowed & (place[None, :] <= place[:, None])
    return (position, allowed)

def rotate(values, position, sign):
    half = values.shape[-1] // 2
    freq = theta ** (-jnp.arange(half, dtype=jnp.float32) / half)
    angle = position[:, None] * freq[None, :]
    cosine = jnp.cos(angle)[:, None, :]
    sine = sign * jnp.sin(angle)[:, None, :]
    first = values[..., :half]
    second = values[..., half:]
    return jnp.concatenate([first * cosine - second * sine, second * cosine + first * sine], axis=-1)

def head_attention(q_head, k_head, v_head, allowed, scale):
    scores = low_back(product(q_head, k_head.T) * scale)
    scores = jnp.where(allowed, scores, -1e+30)
    top = lax.optimization_barrier(jnp.max(scores, axis=1, keepdims=True))
    weights = jnp.exp(scores - top)
    probs = weights / lax.optimization_barrier(jnp.sum(weights, axis=1, keepdims=True))
    return low_back(low(product(low(probs), v_head)))

def layer(inputs, gains, weights, adapters, pick, position, allowed):
    attention_gain, feed_gain = gains
    w_query, w_key, w_value, w_output, w_gate, w_rise, w_fall = weights
    entry_maps, head_exits, unit_exits, output_entry, down_entry, final_exits = adapters
    entries = entry_maps[:, pick]
    heads_exit = head_exits[:, pick]
    units_exit = unit_exits[:, pick]
    out_entry = output_entry[pick]
    fall_entry = down_entry[pick]
    finals = final_exits[:, pick]
    count = inputs.shape[0]
    scale = HEAD_DIM ** (-0.5)

    def project(source, weight, entry, leave):
        return product(source, weight) + product(product(source, entry), leave)
    normed_one = low(inputs * lax.rsqrt(lax.optimization_barrier(jnp.mean(inputs * inputs, axis=1, keepdims=True)) + eps) * attention_gain)
    query_pre = low_back(project(normed_one, w_query, entries[0], heads_exit[0]))
    key_pre = low_back(project(normed_one, w_key, entries[1], heads_exit[1]))
    values = low(low_back(project(normed_one, w_value, entries[2], heads_exit[2])))
    query = low(rotate(query_pre.reshape(count, -1, HEAD_DIM), position, 1.0))
    keys = low(rotate(key_pre.reshape(count, -1, HEAD_DIM), position, 1.0))
    values = values.reshape(count, -1, HEAD_DIM)

    def attend_one(trio):
        return head_attention(trio[0], trio[1], trio[2], allowed, scale)
    per_head = lax.map(jax.checkpoint(attend_one), (query.transpose(1, 0, 2), keys.transpose(1, 0, 2), values.transpose(1, 0, 2)))
    attended = per_head.transpose(1, 0, 2).reshape(count, -1)
    adapt_o = low_back(product(attended, out_entry))
    branch = low_back(product(attended, w_output.T) + product(adapt_o, finals[0]))
    middle = inputs + branch
    normed_two = low(middle * lax.rsqrt(lax.optimization_barrier(jnp.mean(middle * middle, axis=1, keepdims=True)) + eps) * feed_gain)
    gate = low_back(project(normed_two, w_gate, entries[3], units_exit[0]))
    rise = low_back(project(normed_two, w_rise, entries[4], units_exit[1]))
    hidden = low(jax.nn.silu(gate) * rise)
    adapt_d = low_back(product(hidden, fall_entry))
    return middle + product(hidden, w_fall.T) + product(adapt_d, finals[1])

def reference(tokens, cotangent, attention_gain, feed_gain, query_weight, key_weight, value_weight, output_weight, gate_weight, up_weight, down_weight, entry_maps, head_exits, unit_exits, output_entry, down_entry, final_exits, parents, adapter_pick):
    gains = (attention_gain.astype(jnp.float32), feed_gain.astype(jnp.float32))
    weights = tuple((w.astype(jnp.float32) for w in (query_weight, key_weight, value_weight, output_weight, gate_weight, up_weight, down_weight)))
    adapters = tuple((a.astype(jnp.float32) for a in (entry_maps, head_exits, unit_exits, output_entry, down_entry, final_exits)))
    inputs_all = tokens.astype(jnp.float32).reshape(TREES, TREE_TOK, D)
    backs_all = cotangent.astype(jnp.float32).reshape(TREES, TREE_TOK, D)

    def per_tree(totals, item):
        inputs, back, parent_row, pick = item
        position, allowed = tree_layout(parent_row, SEG)

        def forward(source, adapt):
            return layer(source, gains, weights, adapt, pick, position, allowed)
        output, pullback = jax.vjp(forward, inputs, adapters)
        grad_inputs, grad_adapt = pullback(back)
        totals = jax.tree.map(jnp.add, totals, grad_adapt)
        return (totals, (output.astype(jnp.bfloat16), grad_inputs.astype(jnp.bfloat16)))
    zeros = jax.tree.map(jnp.zeros_like, adapters)
    totals, (outputs, grads) = lax.scan(per_tree, zeros, (inputs_all, backs_all, parents, adapter_pick))
    return (outputs.reshape(TOKENS, D), grads.reshape(TOKENS, D), totals[0], totals[1], totals[2], totals[3], totals[4], totals[5])
```

```python
import functools

import jax
import jax.numpy as jnp
import numpy as np
from jax import lax
from jax.experimental import pallas as pl
from jax.experimental.pallas import tpu as pltpu
from jax.sharding import PartitionSpec as P

HEAD_DIM = 64
TRUNK, BRANCHES = 8, 4
QT = 256
RANK_PAD = 128
VMEM_LIMIT = 60 * 1024 * 1024

eps = 1e-05
theta = 130000.0
bf16, f32 = jnp.bfloat16, jnp.float32


def nn(left, right):
    return jnp.dot(left, right, preferred_element_type=f32)


def nt(left, right):
    return lax.dot_general(left, right, (((1,), (1,)), ((), ())), preferred_element_type=f32)


def tn(left, right):
    return lax.dot_general(left, right, (((0,), (0,)), ((), ())), preferred_element_type=f32)


def permute(value, pairs):
    return lax.ppermute(value, "tensor", pairs)


def line_gather(value, edge):
    one = permute(value, [(0, 1), (1, 0), (2, 3), (3, 2)])
    mid = permute(value, [(1, 2), (2, 1)])
    two_edge = permute(mid, [(1, 0), (2, 3)])
    two_mid = permute(one, [(1, 2), (2, 1)])
    three_edge = permute(two_mid, [(1, 0), (2, 3)])
    two = jnp.where(edge, two_edge, two_mid)
    three = jnp.where(edge, three_edge, mid)
    return [value, one, two, three]


def add_rows(left, right):
    return (left.astype(f32) + right.astype(f32)).astype(bf16)


def line_scatter(parts, place):
    right = [(0, 1), (1, 2), (2, 3)]
    left = [(3, 2), (2, 1), (1, 0)]
    first = permute(parts[3], [(0, 1), (3, 2)])
    held = add_rows(parts[2], first)
    second_right = permute(held, right[:2])
    second_left = permute(held, left[:2])
    base_right = jnp.where(place == 1, parts[3], parts[1])
    base_left = jnp.where(place == 2, parts[3], parts[1])
    third_right = permute(add_rows(base_right, second_right), right)
    third_left = permute(add_rows(base_left, second_left), left)
    return parts[0].astype(f32) + third_right.astype(f32) + third_left.astype(f32)


def rope_tables(blocks, seg):
    depth = np.minimum(np.arange(blocks), TRUNK)
    depth[TRUNK + BRANCHES :] = TRUNK + 1
    position = (np.repeat(depth, seg) * seg + np.arange(blocks * seg) % seg).astype(np.float32)
    half = HEAD_DIM // 2
    freq = (np.float32(theta) ** (-np.arange(half, dtype=np.float32) / half)).astype(np.float32)
    angle = (position[:, None] * freq[None, :]).astype(np.float32)
    cosine = np.tile(np.cos(angle), (1, 4)).astype(np.float32)
    sine = np.sin(angle).astype(np.float32)
    sine = np.concatenate([-sine, sine, -sine, sine], axis=1)
    return jnp.asarray(cosine), jnp.asarray(sine)


def turn(values, cosine, sine):
    width = values.shape[1]
    reps = width // cosine.shape[1]
    if reps > 1:
        cosine = jnp.concatenate([cosine] * reps, axis=1)
        sine = jnp.concatenate([sine] * reps, axis=1)
    lane = lax.broadcasted_iota(jnp.int32, values.shape, 1)
    half = HEAD_DIM // 2
    other = jnp.where(
        lane % HEAD_DIM < half, pltpu.roll(values, width - half, 1), pltpu.roll(values, half, 1)
    )
    return values * cosine + other * sine


def project_body(rope, groups, *refs):
    if rope:
        slot_ref, x_ref, w_ref, e_ref, a_ref, cos_ref, sin_ref = refs[:7]
    else:
        slot_ref, x_ref, w_ref, e_ref, a_ref = refs[:5]
    y_ref, l_ref = refs[-2:]
    group = pl.program_id(0)

    @pl.when(group == 0)
    def _():
        l_ref[...] = nt(x_ref[...], e_ref[...]).astype(bf16)

    total = nn(x_ref[...], w_ref[...]) + nn(l_ref[...], a_ref[...])
    if rope:

        @pl.when(group < groups - 1)
        def _():
            y_ref[0] = turn(total, cos_ref[...], sin_ref[...]).astype(bf16)

        @pl.when(group == groups - 1)
        def _():
            y_ref[0] = total.astype(bf16)
    else:
        y_ref[0] = total.astype(bf16)


def project(slot, x, weight, entry, exits, groups, rows_total, tables, before):
    rows, features = x.shape
    width = weight.shape[1] // groups
    in_specs = [
        pl.BlockSpec((rows, features), lambda g, s: (0, 0)),
        pl.BlockSpec((features, width), lambda g, s: (0, g)),
        pl.BlockSpec((RANK_PAD, features), lambda g, s: (0, 0)),
        pl.BlockSpec((RANK_PAD, width), lambda g, s: (0, g)),
    ]
    operands = [x, weight, entry, exits]
    if tables is not None:
        in_specs += [pl.BlockSpec((rows, tables[0].shape[1]), lambda g, s: (s[0], 0))] * 2
        operands += list(tables)
    aliases = {}
    if before is not None:
        aliases = {len(operands) + 1: 0, len(operands) + 2: 1}
        in_specs += [pl.BlockSpec(memory_space=pl.ANY)] * 2
        operands += list(before)
    return pl.pallas_call(
        functools.partial(project_body, tables is not None, groups),
        grid_spec=pltpu.PrefetchScalarGridSpec(
            num_scalar_prefetch=1,
            grid=(groups,),
            in_specs=in_specs,
            out_specs=[
                pl.BlockSpec((1, rows, width), lambda g, s: (g, s[0], 0)),
                pl.BlockSpec((rows, RANK_PAD), lambda g, s: (s[0], 0)),
            ],
        ),
        out_shape=[
            jax.ShapeDtypeStruct((groups, rows_total, width), bf16),
            jax.ShapeDtypeStruct((rows_total, RANK_PAD), bf16),
        ],
        input_output_aliases=aliases,
        compiler_params=pltpu.CompilerParams(vmem_limit_bytes=VMEM_LIMIT),
        cost_estimate=pl.CostEstimate(
            flops=2 * rows * features * weight.shape[1],
            bytes_accessed=2 * weight.size + 4 * x.size,
            transcendentals=0,
        ),
    )(slot, *operands)


def collect_body(groups, slot_ref, d_ref, w_ref, a_ref, e_ref, y_ref, b_ref):
    tile = pl.program_id(0)
    width = d_ref.shape[2]

    @pl.when(tile == 0)
    def _():
        low = nt(d_ref[0], a_ref[:, :width])
        for g in range(1, groups):
            low += nt(d_ref[g], a_ref[:, g * width : (g + 1) * width])
        b_ref[...] = low.astype(bf16)

    total = nn(b_ref[...], e_ref[...])
    for g in range(groups):
        total += nt(d_ref[g], w_ref[:, g * width : (g + 1) * width])
    y_ref[...] = total.astype(bf16)


def collect(slot, d, weight, exits, entry, rows, tile=1024):
    groups, _, width = d.shape
    features = weight.shape[0]
    return pl.pallas_call(
        functools.partial(collect_body, groups),
        grid_spec=pltpu.PrefetchScalarGridSpec(
            num_scalar_prefetch=1,
            grid=(features // tile,),
            in_specs=[
                pl.BlockSpec((groups, rows, width), lambda i, s: (0, s[0], 0)),
                pl.BlockSpec((tile, groups * width), lambda i, s: (i, 0)),
                pl.BlockSpec((RANK_PAD, groups * width), lambda i, s: (0, 0)),
                pl.BlockSpec((RANK_PAD, tile), lambda i, s: (0, i)),
            ],
            out_specs=[
                pl.BlockSpec((rows, tile), lambda i, s: (0, i)),
                pl.BlockSpec((rows, RANK_PAD), lambda i, s: (0, 0)),
            ],
        ),
        out_shape=[
            jax.ShapeDtypeStruct((rows, features), bf16),
            jax.ShapeDtypeStruct((rows, RANK_PAD), bf16),
        ],
        compiler_params=pltpu.CompilerParams(vmem_limit_bytes=VMEM_LIMIT),
        cost_estimate=pl.CostEstimate(
            flops=2 * rows * weight.size, bytes_accessed=2 * weight.size + 4 * rows * features, transcendentals=0
        ),
    )(slot, d, weight, exits, entry)


def tree_tiles(seg, rows, parent_row):
    trunk = TRUNK * seg
    leaves = trunk + BRANCHES * seg
    key = lax.broadcasted_iota(jnp.int32, (QT, QT), 0)
    query = lax.broadcasted_iota(jnp.int32, (QT, QT), 1)
    causal = key <= query
    own = causal & (key // seg == query // seg)
    tiles = []
    for start in range(0, trunk, QT):
        pieces = [(0, start, None)] if start else []
        tiles.append((start, pieces + [(start, QT, causal)]))
    tiles.append((trunk, [(0, trunk, None), (trunk, QT, own)]))
    branch = lax.broadcasted_iota(jnp.int32, (BRANCHES * seg, QT), 0) // seg
    for start in range(leaves, rows, QT):
        mine = branch == parent_row[:, start - leaves : start - leaves + QT]
        tiles.append(
            (start, [(0, trunk, None), (trunk, BRANCHES * seg, mine), (start, QT, own)])
        )
    return tiles


def attend_body(seg, q_ref, k_ref, v_ref, p_ref, o_ref, lse_ref):
    rows = q_ref.shape[1]
    value_t = v_ref[0].T
    lane = lax.broadcasted_iota(jnp.int32, (QT, 2 * HEAD_DIM), 1)
    for start, pieces in tree_tiles(seg, rows, p_ref[...]):
        query = q_ref[0, start : start + QT] * bf16(HEAD_DIM**-0.5)
        outs = []
        for h in range(2):
            own_query = jnp.where(lane // HEAD_DIM == h, query, bf16(0))
            scores = []
            for k0, count, mask in pieces:
                s = nt(k_ref[0, k0 : k0 + count], own_query)
                scores.append(s if mask is None else jnp.where(mask, s, -1e30))
            top = functools.reduce(
                jnp.maximum, [jnp.max(s, axis=0, keepdims=True) for s in scores]
            )
            summed, out = 0.0, 0.0
            for (k0, count, _), s in zip(pieces, scores):
                weights = jnp.exp(s - top)
                summed += jnp.sum(weights, axis=0, keepdims=True)
                out += nn(
                    value_t[h * HEAD_DIM : (h + 1) * HEAD_DIM, k0 : k0 + count],
                    weights.astype(bf16),
                )
            outs.append(out / summed)
            lse_ref[0, h : h + 1, start : start + QT] = top + jnp.log(summed)
        o_ref[0, start : start + QT] = jnp.concatenate(outs, axis=0).T.astype(bf16)


def attend(qkv, leaf_parent, seg):
    _, rows, width = qkv.shape
    pairs = width // (2 * HEAD_DIM)
    return pl.pallas_call(
        functools.partial(attend_body, seg),
        grid=(pairs,),
        in_specs=[
            pl.BlockSpec((1, rows, 2 * HEAD_DIM), lambda j, g=g: (g, 0, j)) for g in range(3)
        ]
        + [pl.BlockSpec(leaf_parent.shape, lambda j: (0, 0))],
        out_specs=[
            pl.BlockSpec((1, rows, 2 * HEAD_DIM), lambda j: (0, 0, j)),
            pl.BlockSpec((1, 2, rows), lambda j: (j, 0, 0)),
        ],
        out_shape=[
            jax.ShapeDtypeStruct((1, rows, width), bf16),
            jax.ShapeDtypeStruct((pairs, 2, rows), f32),
        ],
        compiler_params=pltpu.CompilerParams(vmem_limit_bytes=VMEM_LIMIT),
        cost_estimate=pl.CostEstimate(
            flops=8 * rows * rows * width, bytes_accessed=8 * rows * width, transcendentals=0
        ),
    )(qkv, qkv, qkv, leaf_parent)


def attend_back_body(
    seg, q_ref, k_ref, v_ref, o_ref, g_ref, lse_ref, p_ref, cos_ref, sin_ref, d_ref, dq_t, dk, dv
):
    rows = q_ref.shape[1]
    scale = bf16(HEAD_DIM**-0.5)
    key_t = k_ref[0].T
    weighed_t = (g_ref[0].astype(f32) * o_ref[0].astype(f32)).T
    lane = lax.broadcasted_iota(jnp.int32, (QT, 2 * HEAD_DIM), 1)
    dk[...] = jnp.zeros_like(dk)
    dv[...] = jnp.zeros_like(dv)
    for start, pieces in tree_tiles(seg, rows, p_ref[...]):
        query = q_ref[0, start : start + QT] * scale
        grad = g_ref[0, start : start + QT]
        for h in range(2):
            mine = lane // HEAD_DIM == h
            own_query = jnp.where(mine, query, bf16(0))
            own_grad = jnp.where(mine, grad, bf16(0))
            band = slice(h * HEAD_DIM, (h + 1) * HEAD_DIM)
            delta = jnp.sum(weighed_t[band, start : start + QT], axis=0, keepdims=True)
            lse = lse_ref[0, h : h + 1, start : start + QT]
            grad_q = 0.0
            for k0, count, mask in pieces:
                probs = jnp.exp(nt(k_ref[0, k0 : k0 + count], own_query) - lse)
                if mask is not None:
                    probs = jnp.where(mask, probs, 0.0)
                grad_probs = nt(v_ref[0, k0 : k0 + count], own_grad)
                grad_scores = (probs * (grad_probs - delta)).astype(bf16)
                dk[k0 : k0 + count] += nn(grad_scores, own_query)
                dv[k0 : k0 + count] += nn(probs.astype(bf16), own_grad)
                grad_q += nn(key_t[band, k0 : k0 + count], grad_scores)
            dq_t[band, start : start + QT] = grad_q
    cosine, sine = cos_ref[...], -sin_ref[...]
    d_ref[0] = turn(dq_t[...].T * HEAD_DIM**-0.5, cosine, sine).astype(bf16)
    d_ref[1] = turn(dk[...], cosine, sine).astype(bf16)
    d_ref[2] = dv[...].astype(bf16)


def attend_back(qkv, attended, grad, lse, leaf_parent, tables, seg):
    _, rows, width = qkv.shape
    pairs = width // (2 * HEAD_DIM)
    pair = 2 * HEAD_DIM
    return pl.pallas_call(
        functools.partial(attend_back_body, seg),
        grid=(pairs,),
        in_specs=[pl.BlockSpec((1, rows, pair), lambda j, g=g: (g, 0, j)) for g in range(3)]
        + [
            pl.BlockSpec((1, rows, pair), lambda j: (0, 0, j)),
            pl.BlockSpec((1, rows, pair), lambda j: (0, 0, j)),
            pl.BlockSpec((1, 2, rows), lambda j: (j, 0, 0)),
            pl.BlockSpec(leaf_parent.shape, lambda j: (0, 0)),
            pl.BlockSpec((rows, pair), lambda j: (0, 0)),
            pl.BlockSpec((rows, pair), lambda j: (0, 0)),
        ],
        out_specs=pl.BlockSpec((3, rows, pair), lambda j: (0, 0, j)),
        out_shape=jax.ShapeDtypeStruct((3, rows, width), bf16),
        scratch_shapes=[
            pltpu.VMEM((pair, rows), f32),
            pltpu.VMEM((rows, pair), f32),
            pltpu.VMEM((rows, pair), f32),
        ],
        compiler_params=pltpu.CompilerParams(vmem_limit_bytes=VMEM_LIMIT),
        cost_estimate=pl.CostEstimate(
            flops=20 * rows * rows * width, bytes_accessed=16 * rows * width, transcendentals=0
        ),
    )(qkv, qkv, qkv, attended, grad, lse, leaf_parent, *tables)


def feed_body(
    rank, n_ref, c_ref, wg_ref, wu_ref, wd_ref, xg_ref, xu_ref, xd_ref, e_ref, f_ref,
    res_ref, back_ref, unit_ref, model_ref, low, low_t, acc_res, acc_back, acc_low,
):
    tile = pl.program_id(0)

    @pl.when(tile == 0)
    def _():
        first = nt(n_ref[...], e_ref[...]) + nt(c_ref[...], f_ref[...])
        low[...] = first.astype(bf16)
        low_t[...] = first.T.astype(bf16)
        acc_res[...] = jnp.zeros_like(acc_res)
        acc_back[...] = jnp.zeros_like(acc_back)
        acc_low[...] = jnp.zeros_like(acc_low)

    gate = nn(n_ref[...], wg_ref[...]) + nn(low[...], xg_ref[...])
    rise = nn(n_ref[...], wu_ref[...]) + nn(low[...], xu_ref[...])
    grad_hidden = nn(c_ref[...], wd_ref[...]) + nn(low[...], xd_ref[...])
    sigmoid = jax.nn.sigmoid(gate)
    silu = gate * sigmoid
    hidden = (silu * rise).astype(bf16)
    grad_gate = (grad_hidden * rise * sigmoid * (1.0 + gate * (1.0 - sigmoid))).astype(bf16)
    grad_rise = (grad_hidden * silu).astype(bf16)
    acc_back[...] += nt(grad_gate, wg_ref[...]) + nt(grad_rise, wu_ref[...])
    acc_res[...] += nt(hidden, wd_ref[...])
    acc_low[...] += (
        nt(grad_gate, xg_ref[...]) + nt(grad_rise, xu_ref[...]) + nt(hidden, xd_ref[...])
    )
    unit_ref[:rank] = nn(low_t[:rank], grad_gate)
    unit_ref[rank : 2 * rank] = nn(low_t[rank : 2 * rank], grad_rise)
    unit_ref[2 * rank :] = nn(low_t[2 * rank : 3 * rank], hidden)

    @pl.when(tile == pl.num_programs(0) - 1)
    def _():
        joined = acc_low[...].astype(bf16)
        joined_t = acc_low[...].T.astype(bf16)
        back_ref[...] = (acc_back[...] + nn(joined, e_ref[...])).astype(bf16)
        res_ref[...] = (acc_res[...] + nn(joined, f_ref[...])).astype(bf16)
        model_ref[: 2 * rank] = nn(joined_t[: 2 * rank], n_ref[...])
        model_ref[2 * rank :] = nn(joined_t[2 * rank : 3 * rank], c_ref[...])


def feed(normed, cot, w_gate, w_rise, w_fall, x_gate, x_rise, x_fall, entry, final, rank, tile=512):
    rows, features = normed.shape
    units = w_gate.shape[1]
    whole = pl.BlockSpec((rows, features), lambda i: (0, 0))
    weight = pl.BlockSpec((features, tile), lambda i: (0, i))
    exits = pl.BlockSpec((RANK_PAD, tile), lambda i: (0, i))
    entries = pl.BlockSpec((RANK_PAD, features), lambda i: (0, 0))
    return pl.pallas_call(
        functools.partial(feed_body, rank),
        grid=(units // tile,),
        in_specs=[whole, whole, weight, weight, weight, exits, exits, exits, entries, entries],
        out_specs=[
            whole,
            whole,
            pl.BlockSpec((3 * rank, tile), lambda i: (0, i)),
            pl.BlockSpec((3 * rank, features), lambda i: (0, 0)),
        ],
        out_shape=[
            jax.ShapeDtypeStruct((rows, features), bf16),
            jax.ShapeDtypeStruct((rows, features), bf16),
            jax.ShapeDtypeStruct((3 * rank, units), f32),
            jax.ShapeDtypeStruct((3 * rank, features), f32),
        ],
        scratch_shapes=[
            pltpu.VMEM((rows, RANK_PAD), bf16),
            pltpu.VMEM((RANK_PAD, rows), bf16),
            pltpu.VMEM((rows, features), f32),
            pltpu.VMEM((rows, features), f32),
            pltpu.VMEM((rows, RANK_PAD), f32),
        ],
        compiler_params=pltpu.CompilerParams(vmem_limit_bytes=VMEM_LIMIT),
        cost_estimate=pl.CostEstimate(
            flops=12 * rows * w_gate.size, bytes_accessed=6 * w_gate.size, transcendentals=0
        ),
    )(normed, cot, w_gate, w_rise, w_fall, x_gate, x_rise, x_fall, entry, final)


def norm_forward(rows, gain):
    rms = lax.rsqrt(jnp.mean(rows * rows, axis=1, keepdims=True) + eps)
    return (rows * rms * gain).astype(bf16), rms


def norm_backward(rows, rms, gain, grad):
    scaled = grad * gain
    return rms * (scaled - rows * (rms * rms) * jnp.mean(scaled * rows, axis=1, keepdims=True))


def stack_rows(blocks, rows=RANK_PAD):
    joined = jnp.concatenate(blocks, axis=0)
    return jnp.pad(joined, ((0, rows - joined.shape[0]), (0, 0)))


def place_rows(block, start):
    return jnp.pad(block, ((start, RANK_PAD - start - block.shape[0]), (0, 0)))


def per_tree(block):
    return lax.all_gather(block.astype(bf16), "dp", axis=0, tiled=False)


def by_adapter(gathered, picks, adapters):
    out = []
    for a in range(adapters):
        total = 0.0
        for tree in range(gathered.shape[0]):
            total += jnp.where(picks[tree] == a, gathered[tree].astype(f32), 0.0)
        out.append(total)
    return jnp.stack(out)


def local(
    tokens,
    cotangent,
    attention_gain,
    feed_gain,
    query_weight,
    key_weight,
    value_weight,
    output_weight,
    gate_weight,
    up_weight,
    down_weight,
    entry_maps,
    head_exits,
    unit_exits,
    output_entry,
    down_entry,
    final_exits,
    parents,
    adapter_pick,
):
    pick = adapter_pick[0]
    picks = lax.all_gather(adapter_pick, "dp", axis=0, tiled=True)
    adapters, rank = entry_maps.shape[1], entry_maps.shape[3]
    place = lax.axis_index("tensor")
    edge = (place == 0) | (place == 3)
    slots = [(place ^ s).reshape(1).astype(jnp.int32) for s in range(4)]
    rows_here = tokens.astype(f32)
    local_rows = rows_here.shape[0]
    total = local_rows * lax.axis_size("tensor")
    blocks = parents.shape[1]
    seg = total // blocks
    tables = rope_tables(blocks, seg)
    leaf_parent = (jnp.repeat(parents[0, TRUNK + BRANCHES :], seg) - TRUNK)[None, :]
    gain_one = attention_gain.astype(f32)
    gain_two = feed_gain.astype(f32)

    w_qkv = lax.all_gather(
        jnp.concatenate([query_weight, key_weight, value_weight], axis=1), "dp", axis=0, tiled=True
    )
    w_output = lax.all_gather(output_weight, "dp", axis=0, tiled=True)
    w_gate = lax.all_gather(gate_weight, "dp", axis=0, tiled=True)
    w_rise = lax.all_gather(up_weight, "dp", axis=0, tiled=True)
    w_fall = lax.all_gather(down_weight, "dp", axis=0, tiled=True)

    entries = jnp.swapaxes(entry_maps, 2, 3)[:, pick]
    heads_exit = head_exits[:, pick]
    units_exit = unit_exits[:, pick]
    out_entry = jnp.swapaxes(output_entry, 1, 2)[pick]
    fall_entry = jnp.swapaxes(down_entry, 1, 2)[pick]
    finals = final_exits[:, pick]
    width = heads_exit.shape[2]
    entry_one = stack_rows([entries[0], entries[1], entries[2]])
    exit_one = stack_rows(
        [
            jnp.pad(heads_exit[k], ((0, 0), (k * width, (2 - k) * width)))
            for k in range(3)
        ]
    )
    final_one = place_rows(finals[0], 0)
    exit_out = place_rows(out_entry, 0)
    entry_two = stack_rows([entries[3], entries[4]])
    final_two = place_rows(finals[1], 2 * rank)
    x_gate = place_rows(units_exit[0], 0)
    x_rise = place_rows(units_exit[1], rank)
    x_fall = place_rows(fall_entry, 2 * rank)

    normed_one, rms_one = norm_forward(rows_here, gain_one)
    full_one = line_gather(normed_one, edge)
    state = None
    for s in range(4):
        state = project(slots[s], full_one[s], w_qkv, entry_one, exit_one, 3, total, tables, state)
    qkv, low_one = state
    cot_start, _ = lax.optimization_barrier((cotangent, full_one[3]))
    full_cot = line_gather(cot_start, edge)
    attended, lse = attend(qkv, leaf_parent, seg)
    partial_one = [
        collect(slots[s], attended, w_output, exit_out, final_one, local_rows) for s in (3, 2, 1, 0)
    ][::-1]
    middle = rows_here + line_scatter([p[0] for p in partial_one], place)

    normed_two, rms_two = norm_forward(middle, gain_two)
    full_two = line_gather(normed_two, edge)
    fed = [
        feed(
            full_two[s], full_cot[s], w_gate, w_rise, w_fall, x_gate, x_rise, x_fall,
            entry_two, final_two, rank,
        )
        for s in range(4)
    ]
    grad_middle = cotangent.astype(f32) + norm_backward(
        middle, rms_two, gain_two, line_scatter([f[1] for f in fed], place)
    )
    result = (middle + line_scatter([f[0] for f in fed], place)).astype(bf16)
    unit_grads = functools.reduce(jnp.add, [f[2] for f in fed])
    model_grads = functools.reduce(jnp.add, [f[3] for f in fed])

    full_branch = line_gather(grad_middle.astype(bf16), edge)
    state = None
    for s in range(4):
        state = project(slots[s], full_branch[s], w_output, final_one, exit_out, 1, total, None, state)
    grad_attended, back_o = state
    head_grads = attend_back(qkv, attended, grad_attended, lse, leaf_parent, tables, seg)
    partial_four = [
        collect(slots[s], head_grads, w_qkv, exit_one, entry_one, local_rows) for s in (3, 2, 1, 0)
    ][::-1]
    grad_tokens = (
        grad_middle
        + norm_backward(rows_here, rms_one, gain_one, line_scatter([p[0] for p in partial_four], place))
    ).astype(bf16)

    out_grads = tn(back_o, attended[0])[:rank]
    final_one_grads = functools.reduce(
        jnp.add, [tn(partial_one[s][1], full_branch[s])[:rank] for s in range(4)]
    )
    entry_one_grads = functools.reduce(
        jnp.add, [tn(partial_four[s][1], full_one[s])[: 3 * rank] for s in range(4)]
    )
    head_parts = [
        tn(low_one[:, k * rank : (k + 1) * rank], head_grads[k]) for k in range(3)
    ]
    early = per_tree(
        lax.psum(jnp.concatenate([model_grads, final_one_grads]).astype(bf16), "tensor")
    )
    late = per_tree(lax.psum(entry_one_grads.astype(bf16), "tensor"))
    unit_all = per_tree(unit_grads)
    head_all = per_tree(jnp.concatenate(head_parts + [out_grads]))

    early = by_adapter(early, picks, adapters)
    late = by_adapter(late, picks, adapters)
    unit_all = by_adapter(unit_all, picks, adapters)
    head_all = by_adapter(head_all, picks, adapters)

    def cut(block, index):
        return block[:, index * rank : (index + 1) * rank]

    grad_entries = jnp.stack(
        [cut(late, 0), cut(late, 1), cut(late, 2), cut(early, 0), cut(early, 1)]
    ).swapaxes(2, 3)
    grad_finals = jnp.stack([cut(early, 3), cut(early, 2)])
    grad_heads = jnp.stack([cut(head_all, k) for k in range(3)])
    grad_output = cut(head_all, 3).swapaxes(1, 2)
    grad_units = jnp.stack([cut(unit_all, 0), cut(unit_all, 1)])
    grad_down = cut(unit_all, 2).swapaxes(1, 2)
    return (
        result,
        grad_tokens,
        grad_entries,
        grad_heads,
        grad_units,
        grad_output,
        grad_down,
        grad_finals,
    )


def solution(mesh):
    in_specs = (
        P(("dp", "tensor"), None),
        P(("dp", "tensor"), None),
        P(),
        P(),
        P("dp", "tensor"),
        P("dp", "tensor"),
        P("dp", "tensor"),
        P("dp", "tensor"),
        P("dp", "tensor"),
        P("dp", "tensor"),
        P("dp", "tensor"),
        P(),
        P(None, None, None, "tensor"),
        P(None, None, None, "tensor"),
        P(None, "tensor", None),
        P(None, "tensor", None),
        P(),
        P("dp", None),
        P("dp"),
    )
    out_specs = (
        P(("dp", "tensor"), None),
        P(("dp", "tensor"), None),
        P(),
        P(None, None, None, "tensor"),
        P(None, None, None, "tensor"),
        P(None, "tensor", None),
        P(None, "tensor", None),
        P(),
    )
    return jax.shard_map(local, mesh=mesh, in_specs=in_specs, out_specs=out_specs, check_vma=False)
```

```python
import functools

import jax
import jax.numpy as jnp
import numpy as np
from jax import lax
from jax.experimental import pallas as pl
from jax.experimental.pallas import tpu as pltpu
from jax.sharding import PartitionSpec as P

HEAD_DIM = 64
TRUNK, BRANCHES = 8, 4
QT = 256
RANK_PAD = 128
VMEM_LIMIT = 60 * 1024 * 1024
LINE = 4
MESH = pl.DeviceIdType.MESH

eps = 1e-05
theta = 130000.0
bf16, f32 = jnp.bfloat16, jnp.float32


def nn(left, right):
    return jnp.dot(left, right, preferred_element_type=f32)


def nt(left, right):
    return lax.dot_general(left, right, (((1,), (1,)), ((), ())), preferred_element_type=f32)


def tn(left, right):
    return lax.dot_general(left, right, (((0,), (0,)), ((), ())), preferred_element_type=f32)


def permute(value, pairs):
    return lax.ppermute(value, "tensor", pairs)


def line_gather_start(value):
    one = permute(value, [(0, 1), (1, 0), (2, 3), (3, 2)])
    mid = permute(value, [(1, 2), (2, 1)])
    return one, mid


def line_gather_finish(value, one, mid, edge):
    two_edge = permute(mid, [(1, 0), (2, 3)])
    two_mid = permute(one, [(1, 2), (2, 1)])
    three_edge = permute(one, [(2, 0), (1, 3)])
    two = jnp.where(edge, two_edge, two_mid)
    three = jnp.where(edge, three_edge, mid)
    return [value, one, two, three]


def add_rows(left, right):
    return (left.astype(f32) + right.astype(f32)).astype(bf16)


def line_scatter(parts, place):
    right = [(0, 1), (1, 2), (2, 3)]
    left = [(3, 2), (2, 1), (1, 0)]
    first = permute(parts[3], [(0, 1), (3, 2)])
    held = add_rows(parts[2], first)
    second_right = permute(held, right[:2])
    second_left = permute(held, left[:2])
    base_right = jnp.where(place == 1, parts[3], parts[1])
    base_left = jnp.where(place == 2, parts[3], parts[1])
    third_right = permute(add_rows(base_right, second_right), right)
    third_left = permute(add_rows(base_left, second_left), left)
    return parts[0].astype(f32) + third_right.astype(f32) + third_left.astype(f32)


def rope_tables(blocks, seg):
    depth = np.minimum(np.arange(blocks), TRUNK)
    depth[TRUNK + BRANCHES :] = TRUNK + 1
    position = (np.repeat(depth, seg) * seg + np.arange(blocks * seg) % seg).astype(np.float32)
    half = HEAD_DIM // 2
    freq = (np.float32(theta) ** (-np.arange(half, dtype=np.float32) / half)).astype(np.float32)
    angle = (position[:, None] * freq[None, :]).astype(np.float32)
    cosine = np.tile(np.cos(angle), (1, 4)).astype(np.float32)
    sine = np.sin(angle).astype(np.float32)
    sine = np.concatenate([-sine, sine, -sine, sine], axis=1)
    return jnp.asarray(cosine), jnp.asarray(sine)


def turn(values, cosine, sine):
    width = values.shape[1]
    reps = width // cosine.shape[1]
    if reps > 1:
        cosine = jnp.concatenate([cosine] * reps, axis=1)
        sine = jnp.concatenate([sine] * reps, axis=1)
    lane = lax.broadcasted_iota(jnp.int32, values.shape, 1)
    half = HEAD_DIM // 2
    other = jnp.where(
        lane % HEAD_DIM < half, pltpu.roll(values, width - half, 1), pltpu.roll(values, half, 1)
    )
    return values * cosine + other * sine


SIDES = (1, -1)


def far_of(place, side):
    return place if side == 1 else LINE - 1 - place


def greet(place):
    barrier = pltpu.get_barrier_semaphore()
    for side in SIDES:

        @pl.when(far_of(place, side) < LINE - 1)
        def _():
            pl.semaphore_signal(
                barrier, inc=1, device_id={"tensor": place + side}, device_id_type=MESH
            )

    edge = (place == 0) | (place == LINE - 1)

    @pl.when(edge)
    def _():
        pl.semaphore_wait(barrier, 1)

    @pl.when(jnp.logical_not(edge))
    def _():
        pl.semaphore_wait(barrier, 2)


def chunk_rows(chunk, rows):
    return pl.ds(chunk * rows, rows)


class Gather:
    def __init__(self, place, buf, send, recv, chunks):
        self.place, self.buf, self.sems, self.chunks = place, buf, (send, recv), chunks
        self.rows = buf.shape[1] // chunks

    def copy(self, side, step, chunk, shard, target):
        where = self.buf.at[shard, chunk_rows(chunk, self.rows)]
        spot = (0 if side == 1 else 1, step - 1, chunk)
        return pltpu.make_async_remote_copy(
            src_ref=where,
            dst_ref=where,
            send_sem=self.sems[0].at[spot],
            recv_sem=self.sems[1].at[spot],
            device_id={"tensor": target},
            device_id_type=MESH,
        )

    def each_send(self, step, chunk, act):
        for side in SIDES:
            far = far_of(self.place, side)

            @pl.when((far < LINE - 1) & (far >= step - 1))
            def _():
                shard = self.place - side * (step - 1)
                act(self.copy(side, step, chunk, shard, self.place + side))

    def send(self, step, chunk):
        self.each_send(step, chunk, lambda copy: copy.start())

    def arrive(self, step, chunk):
        for side in SIDES:

            @pl.when(far_of(self.place, side) >= step)
            def _():
                shard = self.place - side * step
                self.copy(side, step, chunk, shard, self.place - side).wait_recv()

    def drain(self):
        for step in range(1, LINE):
            for chunk in range(self.chunks):
                self.each_send(step, chunk, lambda copy: copy.wait_send())


class Sum:
    def __init__(self, place, part, held, send, recv, chunks):
        self.place, self.part, self.held = place, part, held
        self.sems, self.chunks = (send, recv), chunks
        self.rows = part.shape[1] // chunks

    def copy(self, side, step, chunk, shard, target):
        rows = chunk_rows(chunk, self.rows)
        index = 0 if side == 1 else 1
        spot = (index, step - 1, chunk)
        return pltpu.make_async_remote_copy(
            src_ref=self.part.at[shard, rows],
            dst_ref=self.held.at[index, step - 1, rows],
            send_sem=self.sems[0].at[spot],
            recv_sem=self.sems[1].at[spot],
            device_id={"tensor": target},
            device_id_type=MESH,
        )

    def send(self, step, chunk):
        rows = chunk_rows(chunk, self.rows)
        for index, side in enumerate(SIDES):
            far = far_of(self.place, side)
            shard = self.place + side * (LINE - step)
            if step > 1:

                @pl.when((far >= 1) & (far <= step - 1))
                def _():
                    self.copy(side, step - 1, chunk, self.place, self.place - side).wait_recv()
                    self.part[shard, rows] = (
                        self.part[shard, rows].astype(f32)
                        + self.held[index, step - 2, rows].astype(f32)
                    ).astype(bf16)

            @pl.when(far <= step - 1)
            def _():
                self.copy(side, step, chunk, shard, self.place + side).start()

    def total(self, chunk, out):
        rows = chunk_rows(chunk, self.rows)
        out[rows] = self.part[self.place, rows].astype(f32)
        for index, side in enumerate(SIDES):

            @pl.when(far_of(self.place, side) >= 1)
            def _():
                self.copy(side, LINE - 1, chunk, self.place, self.place - side).wait_recv()
                out[rows] += self.held[index, LINE - 2, rows].astype(f32)

    def drain(self):
        for step in range(1, LINE):
            for chunk in range(self.chunks):
                for side in SIDES:
                    far = far_of(self.place, side)
                    shard = self.place + side * (LINE - step)

                    @pl.when(far <= step - 1)
                    def _():
                        self.copy(side, step, chunk, shard, self.place + side).wait_send()


def line_sems(chunks):
    return [pltpu.SemaphoreType.DMA((2, LINE - 1, chunks))] * 2


def fetch(pairs, sems):
    copies = [pltpu.make_async_copy(src, dst, sems.at[i]) for i, (src, dst) in enumerate(pairs)]
    for copy in copies:
        copy.start()
    return copies


IN_VMEM = pl.BlockSpec(memory_space=pltpu.VMEM)
IN_HBM = pl.BlockSpec(memory_space=pl.ANY)


def comm_params(number):
    return pltpu.CompilerParams(
        vmem_limit_bytes=VMEM_LIMIT, collective_id=number, has_side_effects=True
    )


def gather_norm_body(x_ref, gain_ref, buf, send, recv):
    place = lax.axis_index("tensor")
    greet(place)
    rows = x_ref[...].astype(f32)
    rms = lax.rsqrt(jnp.mean(rows * rows, axis=1, keepdims=True) + eps)
    buf[place] = (rows * rms * gain_ref[...]).astype(bf16)
    gather = Gather(place, buf, send, recv, 1)
    gather.send(1, 0)
    for step in range(1, LINE):
        gather.arrive(step, 0)
        if step < LINE - 1:
            gather.send(step + 1, 0)
    gather.drain()


def gather_norm(x, gain):
    rows, features = x.shape
    return pl.pallas_call(
        gather_norm_body,
        in_specs=[IN_VMEM, IN_VMEM],
        out_specs=IN_VMEM,
        out_shape=jax.ShapeDtypeStruct((LINE, rows, features), bf16),
        scratch_shapes=line_sems(1),
        compiler_params=comm_params(0),
    )(x, gain[None, :])


def project_body(groups, x_ref, w_ref, e_ref, a_ref, cos_ref, sin_ref, y_ref, l_ref):
    tile = pl.program_id(0)

    @pl.when(tile == 0)
    def _():
        l_ref[...] = nt(x_ref[...], e_ref[...]).astype(bf16)

    total = nn(x_ref[...], w_ref[...]) + nn(l_ref[...], a_ref[...])

    @pl.when(tile < pl.num_programs(0) // groups * (groups - 1))
    def _():
        y_ref[0] = turn(total, cos_ref[...], sin_ref[...]).astype(bf16)

    @pl.when(tile >= pl.num_programs(0) // groups * (groups - 1))
    def _():
        y_ref[0] = total.astype(bf16)


def project(x, weight, entry, exits, groups, tables, tile=256):
    rows, features = x.shape
    width = exits.shape[1] // groups
    per = width // tile
    return pl.pallas_call(
        functools.partial(project_body, groups),
        grid=(groups * per,),
        in_specs=[
            pl.BlockSpec((rows, features), lambda i: (0, 0)),
            pl.BlockSpec((features, tile), lambda i: (0, i)),
            pl.BlockSpec((RANK_PAD, features), lambda i: (0, 0)),
            pl.BlockSpec((RANK_PAD, tile), lambda i: (0, i)),
            pl.BlockSpec((rows, tables[0].shape[1]), lambda i: (0, 0)),
            pl.BlockSpec((rows, tables[0].shape[1]), lambda i: (0, 0)),
        ],
        out_specs=[
            pl.BlockSpec((1, rows, tile), lambda i: (i // per, 0, i % per)),
            pl.BlockSpec((rows, RANK_PAD), lambda i: (0, 0)),
        ],
        out_shape=[
            jax.ShapeDtypeStruct((groups, rows, width), bf16),
            jax.ShapeDtypeStruct((rows, RANK_PAD), bf16),
        ],
        compiler_params=pltpu.CompilerParams(vmem_limit_bytes=VMEM_LIMIT),
        cost_estimate=pl.CostEstimate(
            flops=2 * rows * features * exits.shape[1], bytes_accessed=2 * rows * features, transcendentals=0
        ),
    )(x, weight, entry, exits, *tables)


def middle_body(
    chunks, d_ref, w_ref, a_ref, e_ref, x_ref, gain_ref, mid_ref, buf, low_ref,
    part, held, wv, wsem, s_send, s_recv, g_send, g_recv,
):
    place = lax.axis_index("tensor")
    width = d_ref.shape[1]
    (load,) = fetch([(w_ref.at[:, 3 * width :], wv)], wsem)
    greet(place)
    load.wait()
    rows = part.shape[1]
    summed = Sum(place, part, held, s_send, s_recv, chunks)
    gather = Gather(place, buf, g_send, g_recv, chunks)
    for slot in (3, 2, 1, 0):
        shard = place ^ slot
        mine = pl.ds(pl.multiple_of(shard * rows, rows), rows)
        d = d_ref[mine]
        low = nt(d, a_ref[...]).astype(bf16)
        low_ref[mine] = low
        part[shard] = (nt(d, wv[...]) + nn(low, e_ref[...])).astype(bf16)
        if slot == 3:
            for chunk in range(chunks):
                summed.send(1, chunk)
    size = rows // chunks
    for turn_ in range(chunks + 2):
        if turn_ < chunks:
            summed.send(2, turn_)
            summed.send(3, turn_)
            summed.total(turn_, mid_ref)
            here = chunk_rows(turn_, size)
            value = mid_ref[here] + x_ref[here].astype(f32)
            mid_ref[here] = value
            rms = lax.rsqrt(jnp.mean(value * value, axis=1, keepdims=True) + eps)
            buf[place, here] = (value * rms * gain_ref[...]).astype(bf16)
            gather.send(1, turn_)
        for step in (1, 2):
            chunk = turn_ - step
            if 0 <= chunk < chunks:
                gather.arrive(step, chunk)
                gather.send(step + 1, chunk)
    for chunk in range(chunks):
        gather.arrive(3, chunk)
    summed.drain()
    gather.drain()


def middle_rows(attended, weight, exits, entry, x, gain, chunks=4):
    rows, features = x.shape
    width = attended.shape[1]
    return pl.pallas_call(
        functools.partial(middle_body, chunks),
        in_specs=[IN_VMEM, IN_HBM, IN_VMEM, IN_VMEM, IN_VMEM, IN_VMEM],
        out_specs=[IN_VMEM] * 3,
        out_shape=[
            jax.ShapeDtypeStruct((rows, features), f32),
            jax.ShapeDtypeStruct((LINE, rows, features), bf16),
            jax.ShapeDtypeStruct((LINE * rows, RANK_PAD), bf16),
        ],
        scratch_shapes=[
            pltpu.VMEM((LINE, rows, features), bf16),
            pltpu.VMEM((2, LINE - 1, rows, features), bf16),
            pltpu.VMEM((features, width), bf16),
            pltpu.SemaphoreType.DMA((1,)),
        ]
        + line_sems(chunks)
        + line_sems(chunks),
        compiler_params=comm_params(1),
    )(attended, weight, exits, entry, x, gain[None, :])


def branch_body(b_ref, w_ref, e_ref, a_ref, buf, y_ref, l_ref, wv, wsem, send, recv):
    place = lax.axis_index("tensor")
    rows = b_ref.shape[0]
    width = y_ref.shape[2]
    (load,) = fetch([(w_ref.at[:, 3 * width :], wv)], wsem)
    greet(place)
    buf[place] = b_ref[...]
    gather = Gather(place, buf, send, recv, 1)
    gather.send(1, 0)
    load.wait()
    for slot in range(LINE):
        if slot:
            gather.arrive(slot, 0)
            if slot < LINE - 1:
                gather.send(slot + 1, 0)
        shard = place ^ slot
        mine = pl.ds(pl.multiple_of(shard * rows, rows), rows)
        low = nt(buf[shard], e_ref[...]).astype(bf16)
        l_ref[mine] = low
        y_ref[0, mine] = (nn(buf[shard], wv[...]) + nn(low, a_ref[...])).astype(bf16)
    gather.drain()


def branch_back(branch, weight, entry, exits):
    rows, features = branch.shape
    width = exits.shape[1]
    return pl.pallas_call(
        branch_body,
        in_specs=[IN_VMEM, IN_HBM, IN_VMEM, IN_VMEM],
        out_specs=[IN_VMEM] * 3,
        out_shape=[
            jax.ShapeDtypeStruct((LINE, rows, features), bf16),
            jax.ShapeDtypeStruct((1, LINE * rows, width), bf16),
            jax.ShapeDtypeStruct((LINE * rows, RANK_PAD), bf16),
        ],
        scratch_shapes=[pltpu.VMEM((features, width), bf16), pltpu.SemaphoreType.DMA((1,))]
        + line_sems(1),
        compiler_params=comm_params(2),
    )(branch, weight, entry, exits)


def tokens_body(
    chunks, d_ref, w_ref, a_ref, e_ref, x_ref, gain_ref, mid_ref, out_ref, low_ref,
    part, held, acc, dv, wv, wsem, send, recv,
):
    place = lax.axis_index("tensor")
    groups, _, width = d_ref.shape
    loads = fetch([(d_ref, dv), (w_ref.at[:, : groups * width], wv)], wsem)
    greet(place)
    for load in loads:
        load.wait()
    rows = part.shape[1]
    summed = Sum(place, part, held, send, recv, chunks)
    for slot in (3, 2, 1, 0):
        shard = place ^ slot
        mine = pl.ds(pl.multiple_of(shard * rows, rows), rows)
        d = jnp.concatenate([dv[g, mine] for g in range(groups)], axis=1)
        low = nt(d, a_ref[...]).astype(bf16)
        low_ref[mine] = low
        part[shard] = (nt(d, wv[...]) + nn(low, e_ref[...])).astype(bf16)
        if slot == 3:
            for chunk in range(chunks):
                summed.send(1, chunk)
    size = rows // chunks
    for chunk in range(chunks):
        summed.send(2, chunk)
        summed.send(3, chunk)
        if chunk:
            finish_tokens(summed, chunk - 1, size, acc, x_ref, gain_ref, mid_ref, out_ref)
    finish_tokens(summed, chunks - 1, size, acc, x_ref, gain_ref, mid_ref, out_ref)
    summed.drain()


def finish_tokens(summed, chunk, size, acc, x_ref, gain_ref, mid_ref, out_ref):
    summed.total(chunk, acc)
    here = chunk_rows(chunk, size)
    rows = x_ref[here].astype(f32)
    rms = lax.rsqrt(jnp.mean(rows * rows, axis=1, keepdims=True) + eps)
    scaled = acc[here] * gain_ref[...]
    mean = jnp.mean(scaled * rows, axis=1, keepdims=True)
    out_ref[here] = (mid_ref[here] + rms * (scaled - rows * (rms * rms) * mean)).astype(bf16)


def tokens_back(head_grads, weight, exits, entry, x, gain, grad_middle, chunks=4):
    rows, features = x.shape
    groups, total, width = head_grads.shape
    return pl.pallas_call(
        functools.partial(tokens_body, chunks),
        in_specs=[IN_HBM, IN_HBM] + [IN_VMEM] * 5,
        out_specs=[IN_VMEM] * 2,
        out_shape=[
            jax.ShapeDtypeStruct((rows, features), bf16),
            jax.ShapeDtypeStruct((total, RANK_PAD), bf16),
        ],
        scratch_shapes=[
            pltpu.VMEM((LINE, rows, features), bf16),
            pltpu.VMEM((2, LINE - 1, rows, features), bf16),
            pltpu.VMEM((rows, features), f32),
            pltpu.VMEM((groups, total, width), bf16),
            pltpu.VMEM((features, groups * width), bf16),
            pltpu.SemaphoreType.DMA((2,)),
        ]
        + line_sems(chunks),
        compiler_params=comm_params(3),
    )(head_grads, weight, exits, entry, x, gain[None, :], grad_middle)


def tree_tiles(seg, rows, parent_row):
    trunk = TRUNK * seg
    leaves = trunk + BRANCHES * seg
    key = lax.broadcasted_iota(jnp.int32, (QT, QT), 0)
    query = lax.broadcasted_iota(jnp.int32, (QT, QT), 1)
    causal = key <= query
    own = causal & (key // seg == query // seg)
    tiles = []
    for start in range(0, trunk, QT):
        pieces = [(0, start, None)] if start else []
        tiles.append((start, pieces + [(start, QT, causal)]))
    tiles.append((trunk, [(0, trunk, None), (trunk, QT, own)]))
    branch = lax.broadcasted_iota(jnp.int32, (BRANCHES * seg, QT), 0) // seg
    for start in range(leaves, rows, QT):
        mine = branch == parent_row[:, start - leaves : start - leaves + QT]
        tiles.append(
            (start, [(0, trunk, None), (trunk, BRANCHES * seg, mine), (start, QT, own)])
        )
    return tiles


def attend_body(seg, q_ref, k_ref, v_ref, p_ref, o_ref, lse_ref):
    rows = q_ref.shape[1]
    value_t = v_ref[0].T
    lane = lax.broadcasted_iota(jnp.int32, (QT, 2 * HEAD_DIM), 1)
    for start, pieces in tree_tiles(seg, rows, p_ref[...]):
        query = q_ref[0, start : start + QT] * bf16(HEAD_DIM**-0.5)
        outs = []
        for h in range(2):
            own_query = jnp.where(lane // HEAD_DIM == h, query, bf16(0))
            scores = []
            for k0, count, mask in pieces:
                s = nt(k_ref[0, k0 : k0 + count], own_query)
                scores.append(s if mask is None else jnp.where(mask, s, -1e30))
            top = functools.reduce(
                jnp.maximum, [jnp.max(s, axis=0, keepdims=True) for s in scores]
            )
            summed, out = 0.0, 0.0
            for (k0, count, _), s in zip(pieces, scores):
                weights = jnp.exp(s - top)
                summed += jnp.sum(weights, axis=0, keepdims=True)
                out += nn(
                    value_t[h * HEAD_DIM : (h + 1) * HEAD_DIM, k0 : k0 + count],
                    weights.astype(bf16),
                )
            outs.append(out / summed)
            lse_ref[0, h : h + 1, start : start + QT] = top + jnp.log(summed)
        o_ref[0, start : start + QT] = jnp.concatenate(outs, axis=0).T.astype(bf16)


def attend(qkv, leaf_parent, seg):
    _, rows, width = qkv.shape
    pairs = width // (2 * HEAD_DIM)
    return pl.pallas_call(
        functools.partial(attend_body, seg),
        grid=(pairs,),
        in_specs=[
            pl.BlockSpec((1, rows, 2 * HEAD_DIM), lambda j, g=g: (g, 0, j)) for g in range(3)
        ]
        + [pl.BlockSpec(leaf_parent.shape, lambda j: (0, 0))],
        out_specs=[
            pl.BlockSpec((1, rows, 2 * HEAD_DIM), lambda j: (0, 0, j)),
            pl.BlockSpec((1, 2, rows), lambda j: (j, 0, 0)),
        ],
        out_shape=[
            jax.ShapeDtypeStruct((1, rows, width), bf16),
            jax.ShapeDtypeStruct((pairs, 2, rows), f32),
        ],
        compiler_params=pltpu.CompilerParams(vmem_limit_bytes=VMEM_LIMIT),
        cost_estimate=pl.CostEstimate(
            flops=8 * rows * rows * width, bytes_accessed=8 * rows * width, transcendentals=0
        ),
    )(qkv, qkv, qkv, leaf_parent)


def attend_back_body(
    seg, q_ref, k_ref, v_ref, o_ref, g_ref, lse_ref, p_ref, cos_ref, sin_ref, d_ref, dq_t, dk, dv
):
    rows = q_ref.shape[1]
    scale = bf16(HEAD_DIM**-0.5)
    key_t = k_ref[0].T
    weighed_t = (g_ref[0].astype(f32) * o_ref[0].astype(f32)).T
    lane = lax.broadcasted_iota(jnp.int32, (QT, 2 * HEAD_DIM), 1)
    dk[...] = jnp.zeros_like(dk)
    dv[...] = jnp.zeros_like(dv)
    for start, pieces in tree_tiles(seg, rows, p_ref[...]):
        query = q_ref[0, start : start + QT] * scale
        grad = g_ref[0, start : start + QT]
        for h in range(2):
            mine = lane // HEAD_DIM == h
            own_query = jnp.where(mine, query, bf16(0))
            own_grad = jnp.where(mine, grad, bf16(0))
            band = slice(h * HEAD_DIM, (h + 1) * HEAD_DIM)
            delta = jnp.sum(weighed_t[band, start : start + QT], axis=0, keepdims=True)
            lse = lse_ref[0, h : h + 1, start : start + QT]
            grad_q = 0.0
            for k0, count, mask in pieces:
                probs = jnp.exp(nt(k_ref[0, k0 : k0 + count], own_query) - lse)
                if mask is not None:
                    probs = jnp.where(mask, probs, 0.0)
                grad_probs = nt(v_ref[0, k0 : k0 + count], own_grad)
                grad_scores = (probs * (grad_probs - delta)).astype(bf16)
                dk[k0 : k0 + count] += nn(grad_scores, own_query)
                dv[k0 : k0 + count] += nn(probs.astype(bf16), own_grad)
                grad_q += nn(key_t[band, k0 : k0 + count], grad_scores)
            dq_t[band, start : start + QT] = grad_q
    cosine, sine = cos_ref[...], -sin_ref[...]
    d_ref[0] = turn(dq_t[...].T * HEAD_DIM**-0.5, cosine, sine).astype(bf16)
    d_ref[1] = turn(dk[...], cosine, sine).astype(bf16)
    d_ref[2] = dv[...].astype(bf16)


def attend_back(qkv, attended, grad, lse, leaf_parent, tables, seg):
    _, rows, width = qkv.shape
    pairs = width // (2 * HEAD_DIM)
    pair = 2 * HEAD_DIM
    return pl.pallas_call(
        functools.partial(attend_back_body, seg),
        grid=(pairs,),
        in_specs=[pl.BlockSpec((1, rows, pair), lambda j, g=g: (g, 0, j)) for g in range(3)]
        + [
            pl.BlockSpec((1, rows, pair), lambda j: (0, 0, j)),
            pl.BlockSpec((1, rows, pair), lambda j: (0, 0, j)),
            pl.BlockSpec((1, 2, rows), lambda j: (j, 0, 0)),
            pl.BlockSpec(leaf_parent.shape, lambda j: (0, 0)),
            pl.BlockSpec((rows, pair), lambda j: (0, 0)),
            pl.BlockSpec((rows, pair), lambda j: (0, 0)),
        ],
        out_specs=pl.BlockSpec((3, rows, pair), lambda j: (0, 0, j)),
        out_shape=jax.ShapeDtypeStruct((3, rows, width), bf16),
        scratch_shapes=[
            pltpu.VMEM((pair, rows), f32),
            pltpu.VMEM((rows, pair), f32),
            pltpu.VMEM((rows, pair), f32),
        ],
        compiler_params=pltpu.CompilerParams(vmem_limit_bytes=VMEM_LIMIT),
        cost_estimate=pl.CostEstimate(
            flops=20 * rows * rows * width, bytes_accessed=16 * rows * width, transcendentals=0
        ),
    )(qkv, qkv, qkv, attended, grad, lse, leaf_parent, *tables)


def feed_body(
    rank, slot_ref, n_ref, c_ref, wg_ref, wu_ref, wd_ref, xg_ref, xu_ref, xd_ref, e_ref, f_ref,
    res_ref, back_ref, unit_ref, model_ref, low, low_t, acc_res, acc_back, acc_low,
):
    tile = pl.program_id(0)

    @pl.when(tile == 0)
    def _():
        first = nt(n_ref[0], e_ref[...]) + nt(c_ref[...], f_ref[...])
        low[...] = first.astype(bf16)
        low_t[...] = first.T.astype(bf16)
        acc_res[...] = jnp.zeros_like(acc_res)
        acc_back[...] = jnp.zeros_like(acc_back)
        acc_low[...] = jnp.zeros_like(acc_low)

    gate = nn(n_ref[0], wg_ref[...]) + nn(low[...], xg_ref[...])
    rise = nn(n_ref[0], wu_ref[...]) + nn(low[...], xu_ref[...])
    grad_hidden = nn(c_ref[...], wd_ref[...]) + nn(low[...], xd_ref[...])
    sigmoid = jax.nn.sigmoid(gate)
    silu = gate * sigmoid
    hidden = (silu * rise).astype(bf16)
    grad_gate = (grad_hidden * rise * sigmoid * (1.0 + gate * (1.0 - sigmoid))).astype(bf16)
    grad_rise = (grad_hidden * silu).astype(bf16)
    acc_back[...] += nt(grad_gate, wg_ref[...]) + nt(grad_rise, wu_ref[...])
    acc_res[...] += nt(hidden, wd_ref[...])
    acc_low[...] += (
        nt(grad_gate, xg_ref[...]) + nt(grad_rise, xu_ref[...]) + nt(hidden, xd_ref[...])
    )
    unit_ref[:rank] = nn(low_t[:rank], grad_gate)
    unit_ref[rank : 2 * rank] = nn(low_t[rank : 2 * rank], grad_rise)
    unit_ref[2 * rank :] = nn(low_t[2 * rank : 3 * rank], hidden)

    @pl.when(tile == pl.num_programs(0) - 1)
    def _():
        joined = acc_low[...].astype(bf16)
        joined_t = acc_low[...].T.astype(bf16)
        back_ref[...] = (acc_back[...] + nn(joined, e_ref[...])).astype(bf16)
        res_ref[...] = (acc_res[...] + nn(joined, f_ref[...])).astype(bf16)
        model_ref[: 2 * rank] = nn(joined_t[: 2 * rank], n_ref[0])
        model_ref[2 * rank :] = nn(joined_t[2 * rank : 3 * rank], c_ref[...])


def feed(slot, normed, cot, weight, x_gate, x_rise, x_fall, entry, final, rank, tile=512):
    _, rows, features = normed.shape
    units = weight.shape[1] // 3
    tiles = units // tile
    whole = pl.BlockSpec((rows, features), lambda i, s: (0, 0))
    exits = pl.BlockSpec((RANK_PAD, tile), lambda i, s: (0, i))
    entries = pl.BlockSpec((RANK_PAD, features), lambda i, s: (0, 0))
    return pl.pallas_call(
        functools.partial(feed_body, rank),
        grid_spec=pltpu.PrefetchScalarGridSpec(
            num_scalar_prefetch=1,
            grid=(tiles,),
            in_specs=[pl.BlockSpec((1, rows, features), lambda i, s: (s[0], 0, 0)), whole]
            + [pl.BlockSpec((features, tile), lambda i, s, k=k: (0, k * tiles + i)) for k in range(3)]
            + [exits, exits, exits, entries, entries],
            out_specs=[
                whole,
                whole,
                pl.BlockSpec((3 * rank, tile), lambda i, s: (0, i)),
                pl.BlockSpec((3 * rank, features), lambda i, s: (0, 0)),
            ],
            scratch_shapes=[
                pltpu.VMEM((rows, RANK_PAD), bf16),
                pltpu.VMEM((RANK_PAD, rows), bf16),
                pltpu.VMEM((rows, features), f32),
                pltpu.VMEM((rows, features), f32),
                pltpu.VMEM((rows, RANK_PAD), f32),
            ],
        ),
        out_shape=[
            jax.ShapeDtypeStruct((rows, features), bf16),
            jax.ShapeDtypeStruct((rows, features), bf16),
            jax.ShapeDtypeStruct((3 * rank, units), f32),
            jax.ShapeDtypeStruct((3 * rank, features), f32),
        ],
        compiler_params=pltpu.CompilerParams(vmem_limit_bytes=VMEM_LIMIT),
        cost_estimate=pl.CostEstimate(
            flops=12 * rows * features * units, bytes_accessed=6 * features * units, transcendentals=0
        ),
    )(slot, normed, cot, weight, weight, weight, x_gate, x_rise, x_fall, entry, final)


def norm_backward(rows, rms, gain, grad):
    scaled = grad * gain
    return rms * (scaled - rows * (rms * rms) * jnp.mean(scaled * rows, axis=1, keepdims=True))


def stack_rows(blocks, rows=RANK_PAD):
    joined = jnp.concatenate(blocks, axis=0)
    return jnp.pad(joined, ((0, rows - joined.shape[0]), (0, 0)))


def place_rows(block, start):
    return jnp.pad(block, ((start, RANK_PAD - start - block.shape[0]), (0, 0)))


def per_tree(block):
    return lax.all_gather(block.astype(bf16), "dp", axis=0, tiled=False)


def by_adapter(gathered, picks, adapters):
    out = []
    for a in range(adapters):
        total = 0.0
        for tree in range(gathered.shape[0]):
            total += jnp.where(picks[tree] == a, gathered[tree].astype(f32), 0.0)
        out.append(total)
    return jnp.stack(out)


def local(
    tokens,
    cotangent,
    attention_gain,
    feed_gain,
    query_weight,
    key_weight,
    value_weight,
    output_weight,
    gate_weight,
    up_weight,
    down_weight,
    entry_maps,
    head_exits,
    unit_exits,
    output_entry,
    down_entry,
    final_exits,
    parents,
    adapter_pick,
):
    pick = adapter_pick[0]
    picks = lax.all_gather(adapter_pick, "dp", axis=0, tiled=True)
    adapters, rank = entry_maps.shape[1], entry_maps.shape[3]
    place = lax.axis_index("tensor")
    edge = (place == 0) | (place == 3)
    slots = [(place ^ s).reshape(1).astype(jnp.int32) for s in range(4)]
    local_rows = tokens.shape[0]
    total = local_rows * lax.axis_size("tensor")
    blocks = parents.shape[1]
    seg = total // blocks
    tables = rope_tables(blocks, seg)
    leaf_parent = (jnp.repeat(parents[0, TRUNK + BRANCHES :], seg) - TRUNK)[None, :]
    gain_one = attention_gain.astype(f32)
    gain_two = feed_gain.astype(f32)

    w_heads = lax.all_gather(
        jnp.concatenate([query_weight, key_weight, value_weight, output_weight], axis=1),
        "dp",
        axis=0,
        tiled=True,
    )
    w_units = lax.all_gather(
        jnp.concatenate([gate_weight, up_weight, down_weight], axis=1), "dp", axis=0, tiled=True
    )

    entries = jnp.swapaxes(entry_maps, 2, 3)[:, pick]
    heads_exit = head_exits[:, pick]
    units_exit = unit_exits[:, pick]
    out_entry = jnp.swapaxes(output_entry, 1, 2)[pick]
    fall_entry = jnp.swapaxes(down_entry, 1, 2)[pick]
    finals = final_exits[:, pick]
    width = heads_exit.shape[2]
    entry_one = stack_rows([entries[0], entries[1], entries[2]])
    exit_one = stack_rows(
        [
            jnp.pad(heads_exit[k], ((0, 0), (k * width, (2 - k) * width)))
            for k in range(3)
        ]
    )
    final_one = place_rows(finals[0], 0)
    exit_out = place_rows(out_entry, 0)
    entry_two = stack_rows([entries[3], entries[4]])
    final_two = place_rows(finals[1], 2 * rank)
    x_gate = place_rows(units_exit[0], 0)
    x_rise = place_rows(units_exit[1], rank)
    x_fall = place_rows(fall_entry, 2 * rank)

    full_one = gather_norm(tokens, gain_one)
    cot_tied, _ = lax.optimization_barrier((cotangent, full_one))
    one, mid = line_gather_start(cot_tied)
    flat_one = full_one.reshape(total, -1)
    qkv, low_one = project(flat_one, w_heads, entry_one, exit_one, 3, tables)
    attended, lse = attend(qkv, leaf_parent, seg)
    one, mid, attended = lax.optimization_barrier((one, mid, attended))
    full_cot = line_gather_finish(cot_tied, one, mid, edge)
    middle, full_two, adapt_o = middle_rows(
        attended[0], w_heads, exit_out, final_one, tokens, gain_two
    )

    fed = [None] * 4
    tie = middle
    for s in (3, 2, 1, 0):
        slot, _ = lax.optimization_barrier((slots[s], tie))
        fed[s] = feed(
            slot, full_two, full_cot[s], w_units, x_gate, x_rise, x_fall, entry_two, final_two, rank
        )
        tie = fed[s][3]
    rms_two = lax.rsqrt(jnp.mean(middle * middle, axis=1, keepdims=True) + eps)
    grad_middle = cotangent.astype(f32) + norm_backward(
        middle, rms_two, gain_two, line_scatter([f[1] for f in fed], place)
    )
    unit_grads = functools.reduce(jnp.add, [f[2] for f in fed])
    model_grads = functools.reduce(jnp.add, [f[3] for f in fed])

    full_branch, grad_attended, back_o = branch_back(
        grad_middle.astype(bf16), w_heads, final_one, exit_out
    )
    res_parts, _ = lax.optimization_barrier(([f[0] for f in fed], back_o))
    result = (middle + line_scatter(res_parts, place)).astype(bf16)
    head_grads = attend_back(qkv, attended, grad_attended, lse, leaf_parent, tables, seg)
    grad_tokens, back_one = tokens_back(
        head_grads, w_heads, exit_one, entry_one, tokens, gain_one, grad_middle
    )

    out_grads = tn(back_o, attended[0])[:rank]
    final_one_grads = tn(adapt_o, full_branch.reshape(total, -1))[:rank]
    entry_one_grads = tn(back_one, flat_one)[: 3 * rank]
    head_parts = [
        tn(low_one[:, k * rank : (k + 1) * rank], head_grads[k]) for k in range(3)
    ]
    early = per_tree(
        lax.psum(jnp.concatenate([model_grads, final_one_grads]).astype(bf16), "tensor")
    )
    late = per_tree(lax.psum(entry_one_grads.astype(bf16), "tensor"))
    unit_all = per_tree(unit_grads)
    head_all = per_tree(jnp.concatenate(head_parts + [out_grads]))

    early = by_adapter(early, picks, adapters)
    late = by_adapter(late, picks, adapters)
    unit_all = by_adapter(unit_all, picks, adapters)
    head_all = by_adapter(head_all, picks, adapters)

    def cut(block, index):
        return block[:, index * rank : (index + 1) * rank]

    grad_entries = jnp.stack(
        [cut(late, 0), cut(late, 1), cut(late, 2), cut(early, 0), cut(early, 1)]
    ).swapaxes(2, 3)
    grad_finals = jnp.stack([cut(early, 3), cut(early, 2)])
    grad_heads = jnp.stack([cut(head_all, k) for k in range(3)])
    grad_output = cut(head_all, 3).swapaxes(1, 2)
    grad_units = jnp.stack([cut(unit_all, 0), cut(unit_all, 1)])
    grad_down = cut(unit_all, 2).swapaxes(1, 2)
    return (
        result,
        grad_tokens,
        grad_entries,
        grad_heads,
        grad_units,
        grad_output,
        grad_down,
        grad_finals,
    )


def solution(mesh):
    in_specs = (
        P(("dp", "tensor"), None),
        P(("dp", "tensor"), None),
        P(),
        P(),
        P("dp", "tensor"),
        P("dp", "tensor"),
        P("dp", "tensor"),
        P("dp", "tensor"),
        P("dp", "tensor"),
        P("dp", "tensor"),
        P("dp", "tensor"),
        P(),
        P(None, None, None, "tensor"),
        P(None, None, None, "tensor"),
        P(None, "tensor", None),
        P(None, "tensor", None),
        P(),
        P("dp", None),
        P("dp"),
    )
    out_specs = (
        P(("dp", "tensor"), None),
        P(("dp", "tensor"), None),
        P(),
        P(None, None, None, "tensor"),
        P(None, None, None, "tensor"),
        P(None, "tensor", None),
        P(None, "tensor", None),
        P(),
    )
    return jax.shard_map(local, mesh=mesh, in_specs=in_specs, out_specs=out_specs, check_vma=False)
```

```python
import functools

import jax
import jax.numpy as jnp
import numpy as np
from jax import lax
from jax.experimental import pallas as pl
from jax.experimental.pallas import tpu as pltpu
from jax.sharding import PartitionSpec as P

HEAD_DIM = 64
TRUNK, BRANCHES = 8, 4
QT = 256
VMEM_LIMIT = 60 * 1024 * 1024
LINE = 4
MESH = pl.DeviceIdType.MESH

eps = 1e-05
theta = 130000.0
bf16, f32 = jnp.bfloat16, jnp.float32


def nn(left, right):
    return jnp.dot(left, right, preferred_element_type=f32)


def nt(left, right):
    return lax.dot_general(left, right, (((1,), (1,)), ((), ())), preferred_element_type=f32)


def tn(left, right):
    return lax.dot_general(left, right, (((0,), (0,)), ((), ())), preferred_element_type=f32)


def permute(value, pairs):
    return lax.ppermute(value, "tensor", pairs)


def line_gather_start(value):
    one = permute(value, [(0, 1), (1, 0), (2, 3), (3, 2)])
    mid = permute(value, [(1, 2), (2, 1)])
    return one, mid


def line_gather_finish(one, mid):
    two_edge = permute(mid, [(1, 0), (2, 3)])
    two_mid = permute(one, [(1, 2), (2, 1)])
    three_edge = permute(one, [(2, 0), (1, 3)])
    return two_edge, two_mid, three_edge, mid


def rope_tables(blocks, seg):
    depth = np.minimum(np.arange(blocks), TRUNK)
    depth[TRUNK + BRANCHES :] = TRUNK + 1
    position = (np.repeat(depth, seg) * seg + np.arange(blocks * seg) % seg).astype(np.float32)
    half = HEAD_DIM // 2
    freq = (np.float32(theta) ** (-np.arange(half, dtype=np.float32) / half)).astype(np.float32)
    angle = (position[:, None] * freq[None, :]).astype(np.float32)
    cosine = np.tile(np.cos(angle), (1, 4)).astype(np.float32)
    sine = np.sin(angle).astype(np.float32)
    sine = np.concatenate([-sine, sine, -sine, sine], axis=1)
    return jnp.asarray(cosine), jnp.asarray(sine)


def turn(values, cosine, sine):
    width = values.shape[1]
    reps = width // cosine.shape[1]
    if reps > 1:
        cosine = jnp.concatenate([cosine] * reps, axis=1)
        sine = jnp.concatenate([sine] * reps, axis=1)
    lane = lax.broadcasted_iota(jnp.int32, values.shape, 1)
    half = HEAD_DIM // 2
    other = jnp.where(
        lane % HEAD_DIM < half, pltpu.roll(values, width - half, 1), pltpu.roll(values, half, 1)
    )
    return values * cosine + other * sine


SIDES = (1, -1)


def far_of(place, side):
    return place if side == 1 else LINE - 1 - place


def greet(place):
    barrier = pltpu.get_barrier_semaphore()
    for side in SIDES:

        @pl.when(far_of(place, side) < LINE - 1)
        def _():
            pl.semaphore_signal(
                barrier, inc=1, device_id={"tensor": place + side}, device_id_type=MESH
            )

    edge = (place == 0) | (place == LINE - 1)

    @pl.when(edge)
    def _():
        pl.semaphore_wait(barrier, 1)

    @pl.when(jnp.logical_not(edge))
    def _():
        pl.semaphore_wait(barrier, 2)


def chunk_rows(chunk, rows):
    return pl.ds(chunk * rows, rows)


class Gather:
    def __init__(self, place, buf, send, recv, chunks):
        self.place, self.buf, self.sems, self.chunks = place, buf, (send, recv), chunks
        self.rows = buf.shape[1] // chunks

    def copy(self, side, step, chunk, shard, target):
        where = self.buf.at[shard, chunk_rows(chunk, self.rows)]
        spot = (0 if side == 1 else 1, step - 1, chunk)
        return pltpu.make_async_remote_copy(
            src_ref=where,
            dst_ref=where,
            send_sem=self.sems[0].at[spot],
            recv_sem=self.sems[1].at[spot],
            device_id={"tensor": target},
            device_id_type=MESH,
        )

    def each_send(self, step, chunk, act):
        for side in SIDES:
            far = far_of(self.place, side)

            @pl.when((far < LINE - 1) & (far >= step - 1))
            def _():
                shard = self.place - side * (step - 1)
                act(self.copy(side, step, chunk, shard, self.place + side))

    def send(self, step, chunk):
        self.each_send(step, chunk, lambda copy: copy.start())

    def arrive(self, step, chunk):
        for side in SIDES:

            @pl.when(far_of(self.place, side) >= step)
            def _():
                shard = self.place - side * step
                self.copy(side, step, chunk, shard, self.place - side).wait_recv()

    def drain(self, stop=LINE, start=1):
        for step in range(start, stop):
            for chunk in range(self.chunks):
                self.each_send(step, chunk, lambda copy: copy.wait_send())


class Sum:
    def __init__(self, place, part, held, send, recv, chunks):
        self.place, self.part, self.held = place, part, held
        self.sems, self.chunks = (send, recv), chunks
        self.rows = part.shape[1] // chunks

    def copy(self, side, step, chunk, shard, target):
        rows = chunk_rows(chunk, self.rows)
        index = 0 if side == 1 else 1
        spot = (index, step - 1, chunk)
        return pltpu.make_async_remote_copy(
            src_ref=self.part.at[shard, rows],
            dst_ref=self.held.at[index, step - 1, rows],
            send_sem=self.sems[0].at[spot],
            recv_sem=self.sems[1].at[spot],
            device_id={"tensor": target},
            device_id_type=MESH,
        )

    def add(self, step, chunk):
        rows = chunk_rows(chunk, self.rows)
        for index, side in enumerate(SIDES):
            far = far_of(self.place, side)
            shard = self.place + side * (LINE - step)

            @pl.when((far >= 1) & (far <= step - 1))
            def _():
                self.copy(side, step - 1, chunk, self.place, self.place - side).wait_recv()
                self.part[shard, rows] = (
                    self.part[shard, rows].astype(f32)
                    + self.held[index, step - 2, rows].astype(f32)
                ).astype(bf16)

    def send(self, step, chunk):
        if step > 1:
            self.add(step, chunk)
        for side in SIDES:
            far = far_of(self.place, side)
            shard = self.place + side * (LINE - step)

            @pl.when(far <= step - 1)
            def _():
                self.copy(side, step, chunk, shard, self.place + side).start()

    def total(self, chunk, out):
        rows = chunk_rows(chunk, self.rows)
        out[rows] = self.part[self.place, rows].astype(f32)
        for index, side in enumerate(SIDES):

            @pl.when(far_of(self.place, side) >= 1)
            def _():
                self.copy(side, LINE - 1, chunk, self.place, self.place - side).wait_recv()
                out[rows] += self.held[index, LINE - 2, rows].astype(f32)

    def drain(self, stop=LINE):
        for step in range(1, stop):
            for chunk in range(self.chunks):
                for side in SIDES:
                    far = far_of(self.place, side)
                    shard = self.place + side * (LINE - step)

                    @pl.when(far <= step - 1)
                    def _():
                        self.copy(side, step, chunk, shard, self.place + side).wait_send()


def line_sems(chunks):
    return [pltpu.SemaphoreType.DMA((2, LINE - 1, chunks))] * 2


def fetch(pairs, sems):
    copies = [pltpu.make_async_copy(src, dst, sems.at[i]) for i, (src, dst) in enumerate(pairs)]
    for copy in copies:
        copy.start()
    return copies


IN_VMEM = pl.BlockSpec(memory_space=pltpu.VMEM)
IN_HBM = pl.BlockSpec(memory_space=pl.ANY)


def comm_params(number):
    return pltpu.CompilerParams(
        vmem_limit_bytes=VMEM_LIMIT, collective_id=number, has_side_effects=True
    )


def gather_norm_body(x_ref, gain_ref, wg_ref, wu_ref, wd_ref, buf, w_ref, wsem, send, recv):
    place = lax.axis_index("tensor")
    width = wg_ref.shape[1]
    loads = fetch(
        [(w, w_ref.at[:, k * width : (k + 1) * width]) for k, w in enumerate((wg_ref, wu_ref, wd_ref))],
        wsem,
    )
    greet(place)
    rows = x_ref[...].astype(f32)
    rms = lax.rsqrt(jnp.mean(rows * rows, axis=1, keepdims=True) + eps)
    buf[place] = (rows * rms * gain_ref[...]).astype(bf16)
    gather = Gather(place, buf, send, recv, 1)
    for step in range(1, LINE - 1):
        gather.send(step, 0)
        gather.arrive(step, 0)
    gather.drain(stop=LINE - 1)
    for load in loads:
        load.wait()


def gather_norm(x, gain, weights):
    rows, features = x.shape
    deep, width = weights[0].shape
    return pl.pallas_call(
        gather_norm_body,
        in_specs=[IN_VMEM, IN_VMEM] + [IN_HBM] * 3,
        out_specs=[IN_VMEM, IN_HBM],
        out_shape=[
            jax.ShapeDtypeStruct((LINE, rows, features), bf16),
            jax.ShapeDtypeStruct((deep, 3 * width), bf16),
        ],
        scratch_shapes=[pltpu.SemaphoreType.DMA((3,))] + line_sems(1),
        compiler_params=comm_params(0),
    )(x, gain[None, :], *weights)


def project_body(
    x_ref, w_ref, e_ref, a_ref, cos_ref, sin_ref, buf, y_ref, l_ref, wv, xsem, wsem, send, recv
):
    place = lax.axis_index("tensor")
    groups, _, width = y_ref.shape
    rows, rank = x_ref.shape[1], a_ref.shape[1]
    edge = (place == 0) | (place == LINE - 1)
    copies = []
    for slot in range(LINE):
        copy = pltpu.make_async_copy(x_ref.at[place ^ slot], buf.at[place ^ slot], xsem.at[slot])
        if slot < LINE - 1:
            copy.start()
        else:
            pl.when(jnp.logical_not(edge))(copy.start)
        copies.append(copy)
    (load,) = fetch([(w_ref.at[:, : groups * width], wv)], wsem)
    greet(place)
    for copy in copies[:-1]:
        copy.wait()
    gather = Gather(place, buf, send, recv, 1)
    gather.send(LINE - 1, 0)
    load.wait()
    for slot in range(LINE):
        if slot == LINE - 1:
            pl.when(jnp.logical_not(edge))(copies[slot].wait)
            gather.arrive(slot, 0)
        shard = place ^ slot
        mine = pl.ds(pl.multiple_of(shard * rows, rows), rows)
        low = nt(buf[shard], e_ref[:groups].reshape(groups * rank, -1)).astype(bf16)
        l_ref[mine] = low
        for g in range(groups):
            band = slice(g * width, (g + 1) * width)
            value = nn(buf[shard], wv[:, band]) + nn(low[:, g * rank : (g + 1) * rank], a_ref[g])
            if g < groups - 1:
                value = turn(value, cos_ref[mine], sin_ref[mine])
            y_ref[g, mine] = value.astype(bf16)
    gather.drain(start=LINE - 1)


def project(x, weight, entries, exits, tables):
    _, rows, features = x.shape
    groups, rank, width = exits.shape
    return pl.pallas_call(
        project_body,
        in_specs=[IN_HBM, IN_HBM] + [IN_VMEM] * 4,
        out_specs=[IN_VMEM] * 3,
        out_shape=[
            jax.ShapeDtypeStruct((LINE, rows, features), bf16),
            jax.ShapeDtypeStruct((groups, LINE * rows, width), bf16),
            jax.ShapeDtypeStruct((LINE * rows, groups * rank), bf16),
        ],
        scratch_shapes=[
            pltpu.VMEM((features, groups * width), bf16),
            pltpu.SemaphoreType.DMA((LINE,)),
            pltpu.SemaphoreType.DMA((1,)),
        ]
        + line_sems(1),
        compiler_params=comm_params(4),
    )(x, weight, entries, exits, *tables)


def middle_body(
    chunks, d_ref, w_ref, a_ref, e_ref, x_ref, gain_ref, mid_ref, buf, low_ref,
    part, held, wv, wsem, s_send, s_recv, g_send, g_recv,
):
    place = lax.axis_index("tensor")
    width = d_ref.shape[1]
    (load,) = fetch([(w_ref.at[:, 3 * width :], wv)], wsem)
    greet(place)
    load.wait()
    rows = part.shape[1]
    summed = Sum(place, part, held, s_send, s_recv, chunks)
    gather = Gather(place, buf, g_send, g_recv, chunks)
    for slot in (3, 2, 1, 0):
        shard = place ^ slot
        mine = pl.ds(pl.multiple_of(shard * rows, rows), rows)
        d = d_ref[mine]
        low = nt(d, a_ref[...]).astype(bf16)
        low_ref[mine] = low
        part[shard] = (nt(d, wv[...]) + nn(low, e_ref[0])).astype(bf16)
        if slot == 3:
            for chunk in range(chunks):
                summed.send(1, chunk)
    size = rows // chunks
    for turn_ in range(chunks + 2):
        if turn_ < chunks:
            summed.send(2, turn_)
            summed.send(3, turn_)
            summed.total(turn_, mid_ref)
            here = chunk_rows(turn_, size)
            value = mid_ref[here] + x_ref[here].astype(f32)
            mid_ref[here] = value
            rms = lax.rsqrt(jnp.mean(value * value, axis=1, keepdims=True) + eps)
            buf[place, here] = (value * rms * gain_ref[...]).astype(bf16)
            gather.send(1, turn_)
        for step in (1, 2):
            chunk = turn_ - step
            if 0 <= chunk < chunks:
                gather.arrive(step, chunk)
                gather.send(step + 1, chunk)
    for chunk in range(chunks):
        gather.arrive(3, chunk)
    summed.drain()
    gather.drain()


def middle_rows(attended, weight, exits, finals, x, gain, chunks=4):
    rows, features = x.shape
    width = attended.shape[1]
    return pl.pallas_call(
        functools.partial(middle_body, chunks),
        in_specs=[IN_VMEM, IN_HBM, IN_VMEM, IN_VMEM, IN_VMEM, IN_VMEM],
        out_specs=[IN_VMEM] * 3,
        out_shape=[
            jax.ShapeDtypeStruct((rows, features), f32),
            jax.ShapeDtypeStruct((LINE, rows, features), bf16),
            jax.ShapeDtypeStruct((LINE * rows, exits.shape[0]), bf16),
        ],
        scratch_shapes=[
            pltpu.VMEM((LINE, rows, features), bf16),
            pltpu.VMEM((2, LINE - 1, rows, features), bf16),
            pltpu.VMEM((features, width), bf16),
            pltpu.SemaphoreType.DMA((1,)),
        ]
        + line_sems(chunks)
        + line_sems(chunks),
        compiler_params=comm_params(1),
    )(attended, weight, exits, finals, x, gain[None, :])


def branch_body(
    b_ref, w_ref, e_ref, a_ref, p_ref, buf, y_ref, l_ref, out_ref,
    part, held, wv, wsem, send, recv, s_send, s_recv,
):
    place = lax.axis_index("tensor")
    rows = b_ref.shape[0]
    load, parts = fetch([(w_ref.at[:, 3 * y_ref.shape[2] :], wv), (p_ref, part)], wsem)
    greet(place)
    buf[place] = b_ref[...]
    gather = Gather(place, buf, send, recv, 1)
    summed = Sum(place, part, held, s_send, s_recv, 1)
    gather.send(1, 0)
    parts.wait()
    summed.send(1, 0)
    load.wait()
    for slot in range(LINE):
        if slot:
            gather.arrive(slot, 0)
        if 0 < slot < LINE - 1:
            gather.send(slot + 1, 0)
        if slot == 1:
            summed.send(2, 0)
        if slot == 2:
            summed.add(3, 0)
            out_ref[0] = part[place]
            for index, side in enumerate(SIDES):

                @pl.when(far_of(place, side) < LINE - 1)
                def _():
                    out_ref[index + 1] = part[place + side]

                @pl.when(far_of(place, side) == LINE - 1)
                def _():
                    out_ref[index + 1] = jnp.zeros_like(part[place])

        shard = place ^ slot
        mine = pl.ds(pl.multiple_of(shard * rows, rows), rows)
        low = nt(buf[shard], e_ref[0]).astype(bf16)
        l_ref[mine] = low
        y_ref[0, mine] = (nn(buf[shard], wv[...]) + nn(low, a_ref[...])).astype(bf16)
    gather.drain()
    summed.drain(LINE - 1)


def branch_back(branch, weight, finals, exits, parts):
    rows, features = branch.shape
    rank, width = exits.shape
    return pl.pallas_call(
        branch_body,
        in_specs=[IN_VMEM, IN_HBM, IN_VMEM, IN_VMEM, IN_HBM],
        out_specs=[IN_VMEM] * 4,
        out_shape=[
            jax.ShapeDtypeStruct((LINE, rows, features), bf16),
            jax.ShapeDtypeStruct((1, LINE * rows, width), bf16),
            jax.ShapeDtypeStruct((LINE * rows, rank), bf16),
            jax.ShapeDtypeStruct((3, rows, features), bf16),
        ],
        scratch_shapes=[
            pltpu.VMEM((LINE, rows, features), bf16),
            pltpu.VMEM((2, LINE - 1, rows, features), bf16),
            pltpu.VMEM((features, width), bf16),
            pltpu.SemaphoreType.DMA((2,)),
        ]
        + line_sems(1)
        + line_sems(1),
        compiler_params=comm_params(2),
    )(branch, weight, finals, exits, parts)


def tokens_body(
    chunks, d_ref, w_ref, a_ref, e_ref, x_ref, gain_ref, mid_ref, n_ref, b_ref, lone_ref, lo_ref, bo_ref, o_ref,
    out_ref, model_ref, head_ref,
    part, held, acc, dv, wv, midv, nv, bv, low, block, extra, wsem, send, recv, x_send, x_recv,
):
    place = lax.axis_index("tensor")
    groups, total, width = d_ref.shape
    rank = a_ref.shape[1]
    loads = fetch(
        [(d_ref, dv), (w_ref.at[:, : groups * width], wv), (n_ref, nv), (b_ref, bv), (mid_ref, midv)],
        wsem,
    )
    block[...] = jnp.zeros_like(block)
    for g in range(groups):
        block[g * rank : (g + 1) * rank, g * width : (g + 1) * width] = a_ref[g]
    greet(place)
    for load in loads[:2]:
        load.wait()
    rows = part.shape[1]
    summed = Sum(place, part, held, send, recv, chunks)
    entry = e_ref[:groups].reshape(groups * rank, -1)
    for slot in (3, 2, 1, 0):
        shard = place ^ slot
        mine = pl.ds(pl.multiple_of(shard * rows, rows), rows)
        d = jnp.concatenate([dv[g, mine] for g in range(groups)], axis=1)
        mine_low = nt(d, block[...]).astype(bf16)
        low[mine] = mine_low
        part[shard] = (nt(d, wv[...]) + nn(mine_low, entry)).astype(bf16)
        if slot == 3:
            for chunk in range(chunks):
                summed.send(1, chunk)
    summed.send(2, 0)
    for load in loads[2:]:
        load.wait()

    def turned(value):
        return value.astype(f32).T.astype(bf16)

    joined = nn(turned(low[...]), nv[...].reshape(total, -1))
    final = nn(turned(lo_ref[...]), bv[...].reshape(total, -1))
    extra[place] = jnp.concatenate([joined, final], axis=0).astype(bf16)
    gather = Gather(place, extra, x_send, x_recv, 1)
    gather.send(1, 0)
    summed.send(3, 0)
    low_one = turned(lone_ref[...])
    for g in range(groups):
        band = slice(g * rank, (g + 1) * rank)
        head_ref[band] = nn(low_one[band], dv[g]).astype(bf16)
    head_ref[groups * rank :] = nn(turned(bo_ref[...]), o_ref[...]).astype(bf16)
    size = rows // chunks
    for chunk in range(1, chunks):
        summed.send(2, chunk)
        summed.send(3, chunk)
        gather.arrive(chunk, 0)
        if chunk < LINE - 1:
            gather.send(chunk + 1, 0)
        finish_tokens(summed, chunk - 1, size, acc, x_ref, gain_ref, midv, out_ref)
    model_ref[...] = functools.reduce(
        jnp.add, [extra[shard].astype(f32) for shard in range(LINE)]
    ).astype(bf16)
    finish_tokens(summed, chunks - 1, size, acc, x_ref, gain_ref, midv, out_ref)
    summed.drain()
    gather.drain()


def finish_tokens(summed, chunk, size, acc, x_ref, gain_ref, mid_ref, out_ref):
    summed.total(chunk, acc)
    here = chunk_rows(chunk, size)
    rows = x_ref[here].astype(f32)
    rms = lax.rsqrt(jnp.mean(rows * rows, axis=1, keepdims=True) + eps)
    scaled = acc[here] * gain_ref[...]
    mean = jnp.mean(scaled * rows, axis=1, keepdims=True)
    out_ref[here] = (mid_ref[here] + rms * (scaled - rows * (rms * rms) * mean)).astype(bf16)


def tokens_back(
    head_grads, weight, exits, entries, x, gain, grad_middle, normed, branch, low_one, low_out, back_out, attended
):
    chunks = LINE
    rows, features = x.shape
    groups, total, width = head_grads.shape
    rank = exits.shape[1]
    deep = (groups + 1) * rank
    return pl.pallas_call(
        functools.partial(tokens_body, chunks),
        in_specs=[IN_HBM, IN_HBM] + [IN_VMEM] * 4 + [IN_HBM] * 3 + [IN_VMEM] * 4,
        out_specs=[IN_VMEM] * 3,
        out_shape=[
            jax.ShapeDtypeStruct((rows, features), bf16),
            jax.ShapeDtypeStruct((deep, features), bf16),
            jax.ShapeDtypeStruct((deep, width), bf16),
        ],
        scratch_shapes=[
            pltpu.VMEM((LINE, rows, features), bf16),
            pltpu.VMEM((2, LINE - 1, rows, features), bf16),
            pltpu.VMEM((rows, features), f32),
            pltpu.VMEM((groups, total, width), bf16),
            pltpu.VMEM((features, groups * width), bf16),
            pltpu.VMEM((rows, features), f32),
            pltpu.VMEM((LINE, rows, features), bf16),
            pltpu.VMEM((LINE, rows, features), bf16),
            pltpu.VMEM((total, groups * rank), bf16),
            pltpu.VMEM((groups * rank, groups * width), bf16),
            pltpu.VMEM((LINE, deep, features), bf16),
            pltpu.SemaphoreType.DMA((5,)),
        ]
        + line_sems(chunks)
        + line_sems(1),
        compiler_params=comm_params(3),
    )(
        head_grads, weight, exits, entries, x, gain[None, :], grad_middle, normed, branch,
        low_one, low_out, back_out, attended,
    )


def tree_tiles(seg, rows, parent_row):
    trunk = TRUNK * seg
    leaves = trunk + BRANCHES * seg
    key = lax.broadcasted_iota(jnp.int32, (QT, QT), 0)
    query = lax.broadcasted_iota(jnp.int32, (QT, QT), 1)
    causal = key <= query
    own = causal & (key // seg == query // seg)
    tiles = []
    for start in range(0, trunk, QT):
        pieces = [(0, start, None)] if start else []
        tiles.append((start, pieces + [(start, QT, causal)]))
    tiles.append((trunk, [(0, trunk, None), (trunk, QT, own)]))
    branch = lax.broadcasted_iota(jnp.int32, (BRANCHES * seg, QT), 0) // seg
    for start in range(leaves, rows, QT):
        mine = branch == parent_row[:, start - leaves : start - leaves + QT]
        tiles.append(
            (start, [(0, trunk, None), (trunk, BRANCHES * seg, mine), (start, QT, own)])
        )
    return tiles


def attend_body(seg, q_ref, k_ref, v_ref, p_ref, o_ref, lse_ref):
    rows = q_ref.shape[1]
    value_t = v_ref[0].T
    lane = lax.broadcasted_iota(jnp.int32, (QT, 2 * HEAD_DIM), 1)
    for start, pieces in tree_tiles(seg, rows, p_ref[...]):
        query = q_ref[0, start : start + QT] * bf16(HEAD_DIM**-0.5)
        outs = []
        for h in range(2):
            own_query = jnp.where(lane // HEAD_DIM == h, query, bf16(0))
            scores = []
            for k0, count, mask in pieces:
                s = nt(k_ref[0, k0 : k0 + count], own_query)
                scores.append(s if mask is None else jnp.where(mask, s, -1e30))
            top = functools.reduce(
                jnp.maximum, [jnp.max(s, axis=0, keepdims=True) for s in scores]
            )
            summed, out = 0.0, 0.0
            for (k0, count, _), s in zip(pieces, scores):
                weights = jnp.exp(s - top)
                summed += jnp.sum(weights, axis=0, keepdims=True)
                out += nn(
                    value_t[h * HEAD_DIM : (h + 1) * HEAD_DIM, k0 : k0 + count],
                    weights.astype(bf16),
                )
            outs.append(out / summed)
            lse_ref[0, h : h + 1, start : start + QT] = top + jnp.log(summed)
        o_ref[0, start : start + QT] = jnp.concatenate(outs, axis=0).T.astype(bf16)


def attend(qkv, leaf_parent, seg):
    _, rows, width = qkv.shape
    pairs = width // (2 * HEAD_DIM)
    return pl.pallas_call(
        functools.partial(attend_body, seg),
        grid=(pairs,),
        in_specs=[
            pl.BlockSpec((1, rows, 2 * HEAD_DIM), lambda j, g=g: (g, 0, j)) for g in range(3)
        ]
        + [pl.BlockSpec(leaf_parent.shape, lambda j: (0, 0))],
        out_specs=[
            pl.BlockSpec((1, rows, 2 * HEAD_DIM), lambda j: (0, 0, j)),
            pl.BlockSpec((1, 2, rows), lambda j: (j, 0, 0)),
        ],
        out_shape=[
            jax.ShapeDtypeStruct((1, rows, width), bf16),
            jax.ShapeDtypeStruct((pairs, 2, rows), f32),
        ],
        compiler_params=pltpu.CompilerParams(vmem_limit_bytes=VMEM_LIMIT),
        cost_estimate=pl.CostEstimate(
            flops=8 * rows * rows * width, bytes_accessed=8 * rows * width, transcendentals=0
        ),
    )(qkv, qkv, qkv, leaf_parent)


def attend_back_body(
    seg, q_ref, k_ref, v_ref, o_ref, g_ref, lse_ref, p_ref, cos_ref, sin_ref, d_ref, dq_t, dk, dv
):
    rows = q_ref.shape[1]
    scale = bf16(HEAD_DIM**-0.5)
    key_t = k_ref[0].T
    weighed_t = (g_ref[0].astype(f32) * o_ref[0].astype(f32)).T
    lane = lax.broadcasted_iota(jnp.int32, (QT, 2 * HEAD_DIM), 1)
    dk[...] = jnp.zeros_like(dk)
    dv[...] = jnp.zeros_like(dv)
    for start, pieces in tree_tiles(seg, rows, p_ref[...]):
        query = q_ref[0, start : start + QT] * scale
        grad = g_ref[0, start : start + QT]
        for h in range(2):
            mine = lane // HEAD_DIM == h
            own_query = jnp.where(mine, query, bf16(0))
            own_grad = jnp.where(mine, grad, bf16(0))
            band = slice(h * HEAD_DIM, (h + 1) * HEAD_DIM)
            delta = jnp.sum(weighed_t[band, start : start + QT], axis=0, keepdims=True)
            lse = lse_ref[0, h : h + 1, start : start + QT]
            grad_q = 0.0
            for k0, count, mask in pieces:
                probs = jnp.exp(nt(k_ref[0, k0 : k0 + count], own_query) - lse)
                if mask is not None:
                    probs = jnp.where(mask, probs, 0.0)
                grad_probs = nt(v_ref[0, k0 : k0 + count], own_grad)
                grad_scores = (probs * (grad_probs - delta)).astype(bf16)
                dk[k0 : k0 + count] += nn(grad_scores, own_query)
                dv[k0 : k0 + count] += nn(probs.astype(bf16), own_grad)
                grad_q += nn(key_t[band, k0 : k0 + count], grad_scores)
            dq_t[band, start : start + QT] = grad_q
    cosine, sine = cos_ref[...], -sin_ref[...]
    d_ref[0] = turn(dq_t[...].T * HEAD_DIM**-0.5, cosine, sine).astype(bf16)
    d_ref[1] = turn(dk[...], cosine, sine).astype(bf16)
    d_ref[2] = dv[...].astype(bf16)


def attend_back(qkv, attended, grad, lse, leaf_parent, tables, seg):
    _, rows, width = qkv.shape
    pairs = width // (2 * HEAD_DIM)
    pair = 2 * HEAD_DIM
    return pl.pallas_call(
        functools.partial(attend_back_body, seg),
        grid=(pairs,),
        in_specs=[pl.BlockSpec((1, rows, pair), lambda j, g=g: (g, 0, j)) for g in range(3)]
        + [
            pl.BlockSpec((1, rows, pair), lambda j: (0, 0, j)),
            pl.BlockSpec((1, rows, pair), lambda j: (0, 0, j)),
            pl.BlockSpec((1, 2, rows), lambda j: (j, 0, 0)),
            pl.BlockSpec(leaf_parent.shape, lambda j: (0, 0)),
            pl.BlockSpec((rows, pair), lambda j: (0, 0)),
            pl.BlockSpec((rows, pair), lambda j: (0, 0)),
        ],
        out_specs=pl.BlockSpec((3, rows, pair), lambda j: (0, 0, j)),
        out_shape=jax.ShapeDtypeStruct((3, rows, width), bf16),
        scratch_shapes=[
            pltpu.VMEM((pair, rows), f32),
            pltpu.VMEM((rows, pair), f32),
            pltpu.VMEM((rows, pair), f32),
        ],
        compiler_params=pltpu.CompilerParams(vmem_limit_bytes=VMEM_LIMIT),
        cost_estimate=pl.CostEstimate(
            flops=20 * rows * rows * width, bytes_accessed=16 * rows * width, transcendentals=0
        ),
    )(qkv, qkv, qkv, attended, grad, lse, leaf_parent, *tables)


def feed_body(
    rank, tile, chunks,
    n_ref, c0_ref, c1_ref, c2e_ref, c2m_ref, c3e_ref, c3m_ref, w_ref, mid_ref,
    xu_in, xd_in, e_in, f_in, gain_ref,
    grad_ref, low_grad_ref, res_ref, unit_ref, model_ref,
    x_ref, e_ref, f_ref, midv, nbuf, cbuf, wbuf, low, low_t, acc_res, acc_back, acc_low, part, held, resv,
    nsem, csem, wsem, rsem, msem, send, recv,
):
    place = lax.axis_index("tensor")
    edge = (place == 0) | (place == LINE - 1)
    units = unit_ref.shape[1]
    tiles = units // tile
    summed = Sum(place, part, held, send, recv, chunks)

    def load_rows(order, act):
        into = order % 2
        slot = LINE - 1 - order
        act(pltpu.make_async_copy(n_ref.at[place ^ slot], nbuf.at[into], nsem.at[into]))
        for number, at_edge, inside in (
            (3, c3e_ref, c3m_ref),
            (2, c2e_ref, c2m_ref),
            (1, c1_ref, c1_ref),
            (0, c0_ref, c0_ref),
        ):
            if at_edge is inside:

                @pl.when(slot == number)
                def _():
                    act(pltpu.make_async_copy(inside, cbuf.at[into], csem.at[into]))
            else:

                @pl.when((slot == number) & edge)
                def _():
                    act(pltpu.make_async_copy(at_edge, cbuf.at[into], csem.at[into]))

                @pl.when((slot == number) & jnp.logical_not(edge))
                def _():
                    act(pltpu.make_async_copy(inside, cbuf.at[into], csem.at[into]))

    def load_weights(index, into, act):
        for k in range(3):
            columns = pl.ds(pl.multiple_of(k * units + index * tile, tile), tile)
            act(pltpu.make_async_copy(w_ref.at[:, columns], wbuf.at[into, k], wsem.at[into, k]))

    def start(copy):
        copy.start()

    def wait(copy):
        copy.wait()

    load_rows(jnp.int32(0), start)
    load_weights(0, 0, start)
    (load_middle,) = fetch([(mid_ref, midv)], msem)
    for padded in (x_ref, e_ref, f_ref):
        padded[...] = jnp.zeros_like(padded)
    x_ref[0, :rank] = xu_in[0]
    x_ref[1, rank : 2 * rank] = xu_in[1]
    x_ref[2, 2 * rank :] = xd_in[...]
    e_ref[: 2 * rank] = e_in[3:].reshape(2 * rank, -1)
    f_ref[2 * rank :] = f_in[1]
    unit_ref[...] = jnp.zeros_like(unit_ref)
    model_ref[...] = jnp.zeros_like(model_ref)
    greet(place)

    def one_shard(order, carry):
        into = order % 2
        shard = place ^ (LINE - 1 - order)
        load_rows(order, wait)

        @pl.when(order < LINE - 1)
        def _():
            load_rows(order + 1, start)

        first = nt(nbuf[into], e_ref[...]) + nt(cbuf[into], f_ref[...])
        low[...] = first.astype(bf16)
        low_t[...] = first.T.astype(bf16)
        acc_res[...] = jnp.zeros_like(acc_res)
        acc_back[...] = jnp.zeros_like(acc_back)
        acc_low[...] = jnp.zeros_like(acc_low)

        def one_tile(index, carry):
            stage = order * tiles + index
            at = stage % 2
            load_weights(index, at, wait)

            @pl.when(stage < LINE * tiles - 1)
            def _():
                load_weights((index + 1) % tiles, 1 - at, start)

            columns = pl.ds(pl.multiple_of(index * tile, tile), tile)
            x_gate, x_rise, x_fall = x_ref[0, :, columns], x_ref[1, :, columns], x_ref[2, :, columns]
            gate = nn(nbuf[into], wbuf[at, 0]) + nn(low[...], x_gate)
            rise = nn(nbuf[into], wbuf[at, 1]) + nn(low[...], x_rise)
            grad_hidden = nn(cbuf[into], wbuf[at, 2]) + nn(low[...], x_fall)
            sigmoid = jax.nn.sigmoid(gate)
            silu = gate * sigmoid
            hidden = (silu * rise).astype(bf16)
            grad_gate = (grad_hidden * rise * sigmoid * (1.0 + gate * (1.0 - sigmoid))).astype(bf16)
            grad_rise = (grad_hidden * silu).astype(bf16)
            acc_back[...] += nt(grad_gate, wbuf[at, 0]) + nt(grad_rise, wbuf[at, 1])
            acc_res[...] += nt(hidden, wbuf[at, 2])
            acc_low[...] += nt(grad_gate, x_gate) + nt(grad_rise, x_rise) + nt(hidden, x_fall)
            unit_ref[:rank, columns] += nn(low_t[:rank], grad_gate)
            unit_ref[rank : 2 * rank, columns] += nn(low_t[rank : 2 * rank], grad_rise)
            unit_ref[2 * rank :, columns] += nn(low_t[2 * rank : 3 * rank], hidden)
            return carry

        lax.fori_loop(0, tiles, one_tile, 0)
        joined = acc_low[...].astype(bf16)
        joined_t = acc_low[...].T.astype(bf16)
        part[shard] = (acc_back[...] + nn(joined, e_ref[...])).astype(bf16)

        @pl.when(order > 0)
        def _():
            pltpu.make_async_copy(resv, res_ref.at[shard], rsem.at[0]).wait()

        resv[...] = (acc_res[...] + nn(joined, f_ref[...])).astype(bf16)
        pltpu.make_async_copy(resv, res_ref.at[shard], rsem.at[0]).start()
        for step in (1, 2, 3):

            @pl.when(order == step - 1)
            def _():
                for chunk in range(chunks):
                    summed.send(step, chunk)

        model_ref[: 2 * rank] += nn(joined_t[: 2 * rank], nbuf[into])
        model_ref[2 * rank :] += nn(joined_t[2 * rank : 3 * rank], cbuf[into])
        return carry

    lax.fori_loop(0, LINE, one_shard, 0)
    size = part.shape[1] // chunks
    last = (LINE - 1) % 2
    load_middle.wait()
    for chunk in range(chunks):
        summed.total(chunk, acc_back)
        here = chunk_rows(chunk, size)
        middle = midv[here]
        rms = lax.rsqrt(jnp.mean(middle * middle, axis=1, keepdims=True) + eps)
        scaled = acc_back[here] * gain_ref[...]
        mean = jnp.mean(scaled * middle, axis=1, keepdims=True)
        grad = cbuf[last, here].astype(f32) + rms * (scaled - middle * (rms * rms) * mean)
        grad_ref[here] = grad
        low_grad_ref[here] = grad.astype(bf16)
    pltpu.make_async_copy(resv, res_ref.at[place], rsem.at[0]).wait()
    summed.drain()


def feed(normed, cots, weight, middle, units_exit, fall_entry, entries, finals, gain, tile=512, chunks=4):
    _, rows, features = normed.shape
    units = weight.shape[1] // 3
    rank = fall_entry.shape[0]
    return pl.pallas_call(
        functools.partial(feed_body, rank, tile, chunks),
        in_specs=[IN_HBM] * 9 + [IN_VMEM] * 5,
        out_specs=[IN_VMEM, IN_VMEM, IN_HBM, IN_VMEM, IN_VMEM],
        out_shape=[
            jax.ShapeDtypeStruct((rows, features), f32),
            jax.ShapeDtypeStruct((rows, features), bf16),
            jax.ShapeDtypeStruct((LINE, rows, features), bf16),
            jax.ShapeDtypeStruct((3 * rank, units), f32),
            jax.ShapeDtypeStruct((3 * rank, features), f32),
        ],
        scratch_shapes=[
            pltpu.VMEM((3, 3 * rank, units), bf16),
            pltpu.VMEM((3 * rank, features), bf16),
            pltpu.VMEM((3 * rank, features), bf16),
            pltpu.VMEM((rows, features), f32),
            pltpu.VMEM((2, rows, features), bf16),
            pltpu.VMEM((2, rows, features), bf16),
            pltpu.VMEM((2, 3, features, tile), bf16),
            pltpu.VMEM((rows, 3 * rank), bf16),
            pltpu.VMEM((3 * rank, rows), bf16),
            pltpu.VMEM((rows, features), f32),
            pltpu.VMEM((rows, features), f32),
            pltpu.VMEM((rows, 3 * rank), f32),
            pltpu.VMEM((LINE, rows, features), bf16),
            pltpu.VMEM((2, LINE - 1, rows, features), bf16),
            pltpu.VMEM((rows, features), bf16),
            pltpu.SemaphoreType.DMA((2,)),
            pltpu.SemaphoreType.DMA((2,)),
            pltpu.SemaphoreType.DMA((2, 3)),
            pltpu.SemaphoreType.DMA((1,)),
            pltpu.SemaphoreType.DMA((1,)),
        ]
        + line_sems(chunks),
        compiler_params=comm_params(5),
    )(normed, *cots, weight, middle, units_exit, fall_entry, entries, finals, gain[None, :])


def per_tree(block):
    return lax.all_gather(block, "dp", axis=0, tiled=False)


def by_adapter(gathered, picks, adapters):
    out = []
    for a in range(adapters):
        total = 0.0
        for tree in range(gathered.shape[0]):
            total += jnp.where(picks[tree] == a, gathered[tree].astype(f32), 0.0)
        out.append(total)
    return jnp.stack(out)


def local(
    tokens,
    cotangent,
    attention_gain,
    feed_gain,
    query_weight,
    key_weight,
    value_weight,
    output_weight,
    gate_weight,
    up_weight,
    down_weight,
    entry_maps,
    head_exits,
    unit_exits,
    output_entry,
    down_entry,
    final_exits,
    parents,
    adapter_pick,
):
    pick = adapter_pick[0]
    adapters, rank = entry_maps.shape[1], entry_maps.shape[3]
    local_rows = tokens.shape[0]
    total = local_rows * lax.axis_size("tensor")
    blocks = parents.shape[1]
    seg = total // blocks
    tables = rope_tables(blocks, seg)
    leaf_parent = (jnp.repeat(parents[0, TRUNK + BRANCHES :], seg) - TRUNK)[None, :]
    gain_one = attention_gain.astype(f32)
    gain_two = feed_gain.astype(f32)

    w_heads = lax.all_gather(
        jnp.concatenate([query_weight, key_weight, value_weight, output_weight], axis=1),
        "dp",
        axis=0,
        tiled=True,
    )

    entries = jnp.swapaxes(entry_maps, 2, 3)[:, pick]
    heads_exit = head_exits[:, pick]
    units_exit = unit_exits[:, pick]
    out_entry = jnp.swapaxes(output_entry, 1, 2)[pick]
    fall_entry = jnp.swapaxes(down_entry, 1, 2)[pick]
    finals = final_exits[:, pick]

    most_one, units_here = gather_norm(tokens, gain_one, (gate_weight, up_weight, down_weight))
    w_units = lax.all_gather(units_here, "dp", axis=0, tiled=True)
    cot_tied, _ = lax.optimization_barrier((cotangent, most_one))
    one, mid = line_gather_start(cot_tied)
    full_one, qkv, low_one = project(most_one, w_heads, entries, heads_exit, tables)
    one, mid, qkv = lax.optimization_barrier((one, mid, qkv))
    cots = (cotangent, one) + line_gather_finish(one, mid)
    attended, lse = attend(qkv, leaf_parent, seg)
    middle, full_two, adapt_o = middle_rows(
        attended[0], w_heads, out_entry, finals, tokens, gain_two
    )

    grad_middle, branch, res_parts, unit_grads, model_grads = feed(
        full_two, cots, w_units, middle, units_exit, fall_entry, entries, finals, gain_two
    )
    early = jnp.concatenate(
        [unit_grads.astype(bf16), jnp.full((rank, unit_grads.shape[1]), pick).astype(bf16)]
    )
    model_low = model_grads.astype(bf16)
    branch, early, model_low = lax.optimization_barrier((branch, early, model_low))
    early = per_tree(early)
    model_sum = lax.psum(model_low, "tensor")

    full_branch, grad_attended, back_o, res_rows = branch_back(
        branch, w_heads, finals, out_entry, res_parts
    )
    from_left = permute(res_rows[1], [(0, 1), (1, 2), (2, 3)])
    from_right = permute(res_rows[2], [(3, 2), (2, 1), (1, 0)])
    head_grads = attend_back(qkv, attended, grad_attended, lse, leaf_parent, tables, seg)
    head_grads, model_sum = lax.optimization_barrier((head_grads, model_sum))
    model_all = per_tree(model_sum)
    grad_tokens, late_model, late_head = tokens_back(
        head_grads, w_heads, heads_exit, entries, tokens, gain_one, grad_middle,
        full_one, full_branch, low_one, adapt_o, back_o, attended[0],
    )
    late = per_tree(
        jnp.concatenate([late_model, late_head.reshape(rank, -1)], axis=0)
    )
    result = (
        middle
        + res_rows[0].astype(f32)
        + from_left.astype(f32)
        + from_right.astype(f32)
    ).astype(bf16)

    picks = early[:, 3 * rank, 0].astype(f32)
    unit_all = by_adapter(early[:, : 3 * rank], picks, adapters)
    model_all = by_adapter(model_all, picks, adapters)
    late_model = by_adapter(late[:, : 4 * rank], picks, adapters)
    head_all = by_adapter(late[:, 4 * rank :].reshape((late.shape[0],) + late_head.shape), picks, adapters)

    def cut(block, index):
        return block[:, index * rank : (index + 1) * rank]

    grad_entries = jnp.stack(
        [cut(late_model, 0), cut(late_model, 1), cut(late_model, 2), cut(model_all, 0), cut(model_all, 1)]
    ).swapaxes(2, 3)
    grad_finals = jnp.stack([cut(late_model, 3), cut(model_all, 2)])
    grad_heads = jnp.stack([cut(head_all, k) for k in range(3)])
    grad_output = cut(head_all, 3).swapaxes(1, 2)
    grad_units = jnp.stack([cut(unit_all, 0), cut(unit_all, 1)])
    grad_down = cut(unit_all, 2).swapaxes(1, 2)
    return (
        result,
        grad_tokens,
        grad_entries,
        grad_heads,
        grad_units,
        grad_output,
        grad_down,
        grad_finals,
    )


def solution(mesh):
    in_specs = (
        P(("dp", "tensor"), None),
        P(("dp", "tensor"), None),
        P(),
        P(),
        P("dp", "tensor"),
        P("dp", "tensor"),
        P("dp", "tensor"),
        P("dp", "tensor"),
        P("dp", "tensor"),
        P("dp", "tensor"),
        P("dp", "tensor"),
        P(),
        P(None, None, None, "tensor"),
        P(None, None, None, "tensor"),
        P(None, "tensor", None),
        P(None, "tensor", None),
        P(),
        P("dp", None),
        P("dp"),
    )
    out_specs = (
        P(("dp", "tensor"), None),
        P(("dp", "tensor"), None),
        P(),
        P(None, None, None, "tensor"),
        P(None, None, None, "tensor"),
        P(None, "tensor", None),
        P(None, "tensor", None),
        P(),
    )
    return jax.shard_map(local, mesh=mesh, in_specs=in_specs, out_specs=out_specs, check_vma=False)
```

```python
import functools

import jax
import jax.numpy as jnp
import numpy as np
from jax import lax
from jax.experimental import pallas as pl
from jax.experimental.pallas import tpu as pltpu
from jax.sharding import PartitionSpec as P

HEAD_DIM = 64
TRUNK, BRANCHES = 8, 4
QT = 256
VMEM_LIMIT = 60 * 1024 * 1024
LINE = 4
MESH = pl.DeviceIdType.MESH

eps = 1e-05
theta = 130000.0
bf16, f32 = jnp.bfloat16, jnp.float32


def nn(left, right):
    return jnp.dot(left, right, preferred_element_type=f32)


def nt(left, right):
    return lax.dot_general(left, right, (((1,), (1,)), ((), ())), preferred_element_type=f32)


def tn(left, right):
    return lax.dot_general(left, right, (((0,), (0,)), ((), ())), preferred_element_type=f32)


def permute(value, pairs):
    return lax.ppermute(value, "tensor", pairs)


def rope_tables(blocks, seg):
    depth = np.minimum(np.arange(blocks), TRUNK)
    depth[TRUNK + BRANCHES :] = TRUNK + 1
    position = (np.repeat(depth, seg) * seg + np.arange(blocks * seg) % seg).astype(np.float32)
    half = HEAD_DIM // 2
    freq = (np.float32(theta) ** (-np.arange(half, dtype=np.float32) / half)).astype(np.float32)
    angle = (position[:, None] * freq[None, :]).astype(np.float32)
    cosine = np.tile(np.cos(angle), (1, 4)).astype(np.float32)
    sine = np.sin(angle).astype(np.float32)
    sine = np.concatenate([-sine, sine, -sine, sine], axis=1)
    return jnp.asarray(cosine), jnp.asarray(sine)


def turn(values, cosine, sine):
    width = values.shape[1]
    reps = width // cosine.shape[1]
    if reps > 1:
        cosine = jnp.concatenate([cosine] * reps, axis=1)
        sine = jnp.concatenate([sine] * reps, axis=1)
    lane = lax.broadcasted_iota(jnp.int32, values.shape, 1)
    half = HEAD_DIM // 2
    other = jnp.where(
        lane % HEAD_DIM < half, pltpu.roll(values, width - half, 1), pltpu.roll(values, half, 1)
    )
    return values * cosine + other * sine


SIDES = (1, -1)


def far_of(place, side):
    return place if side == 1 else LINE - 1 - place


def greet(place, partners=()):
    barrier = pltpu.get_barrier_semaphore()
    for partner in partners:
        pl.semaphore_signal(barrier, inc=1, device_id={"dp": partner}, device_id_type=MESH)
    for side in SIDES:

        @pl.when(far_of(place, side) < LINE - 1)
        def _():
            pl.semaphore_signal(
                barrier, inc=1, device_id={"tensor": place + side}, device_id_type=MESH
            )

    edge = (place == 0) | (place == LINE - 1)

    @pl.when(edge)
    def _():
        pl.semaphore_wait(barrier, 1 + len(partners))

    @pl.when(jnp.logical_not(edge))
    def _():
        pl.semaphore_wait(barrier, 2 + len(partners))


def chunk_rows(chunk, rows):
    return pl.ds(chunk * rows, rows)


class Gather:
    def __init__(self, place, buf, send, recv, chunks):
        self.place, self.buf, self.sems, self.chunks = place, buf, (send, recv), chunks
        self.rows = buf.shape[1] // chunks

    def copy(self, side, step, chunk, shard, target):
        where = self.buf.at[shard, chunk_rows(chunk, self.rows)]
        spot = (0 if side == 1 else 1, step - 1, chunk)
        return pltpu.make_async_remote_copy(
            src_ref=where,
            dst_ref=where,
            send_sem=self.sems[0].at[spot],
            recv_sem=self.sems[1].at[spot],
            device_id={"tensor": target},
            device_id_type=MESH,
        )

    def each_send(self, step, chunk, act):
        for side in SIDES:
            far = far_of(self.place, side)

            @pl.when((far < LINE - 1) & (far >= step - 1))
            def _():
                shard = self.place - side * (step - 1)
                act(self.copy(side, step, chunk, shard, self.place + side))

    def send(self, step, chunk):
        self.each_send(step, chunk, lambda copy: copy.start())

    def arrive(self, step, chunk):
        for side in SIDES:

            @pl.when(far_of(self.place, side) >= step)
            def _():
                shard = self.place - side * step
                self.copy(side, step, chunk, shard, self.place - side).wait_recv()

    def drain(self, stop=LINE, start=1):
        for step in range(start, stop):
            for chunk in range(self.chunks):
                self.each_send(step, chunk, lambda copy: copy.wait_send())


class Sum:
    def __init__(self, place, part, held, send, recv, chunks):
        self.place, self.part, self.held = place, part, held
        self.sems, self.chunks = (send, recv), chunks
        self.rows = part.shape[1] // chunks

    def copy(self, side, step, chunk, shard, target):
        rows = chunk_rows(chunk, self.rows)
        index = 0 if side == 1 else 1
        spot = (index, step - 1, chunk)
        return pltpu.make_async_remote_copy(
            src_ref=self.part.at[shard, rows],
            dst_ref=self.held.at[index, step - 1, rows],
            send_sem=self.sems[0].at[spot],
            recv_sem=self.sems[1].at[spot],
            device_id={"tensor": target},
            device_id_type=MESH,
        )

    def add(self, step, chunk):
        rows = chunk_rows(chunk, self.rows)
        for index, side in enumerate(SIDES):
            far = far_of(self.place, side)
            shard = self.place + side * (LINE - step)

            @pl.when((far >= 1) & (far <= step - 1))
            def _():
                self.copy(side, step - 1, chunk, self.place, self.place - side).wait_recv()
                self.part[shard, rows] = (
                    self.part[shard, rows].astype(f32)
                    + self.held[index, step - 2, rows].astype(f32)
                ).astype(bf16)

    def send(self, step, chunk):
        if step > 1:
            self.add(step, chunk)
        for side in SIDES:
            far = far_of(self.place, side)
            shard = self.place + side * (LINE - step)

            @pl.when(far <= step - 1)
            def _():
                self.copy(side, step, chunk, shard, self.place + side).start()

    def total(self, chunk, out):
        rows = chunk_rows(chunk, self.rows)
        out[rows] = self.part[self.place, rows].astype(f32)
        for index, side in enumerate(SIDES):

            @pl.when(far_of(self.place, side) >= 1)
            def _():
                self.copy(side, LINE - 1, chunk, self.place, self.place - side).wait_recv()
                out[rows] += self.held[index, LINE - 2, rows].astype(f32)

    def drain(self, stop=LINE):
        for step in range(1, stop):
            for chunk in range(self.chunks):
                for side in SIDES:
                    far = far_of(self.place, side)
                    shard = self.place + side * (LINE - step)

                    @pl.when(far <= step - 1)
                    def _():
                        self.copy(side, step, chunk, shard, self.place + side).wait_send()


def line_sems(chunks):
    return [pltpu.SemaphoreType.DMA((2, LINE - 1, chunks))] * 2


def fetch(pairs, sems):
    copies = [pltpu.make_async_copy(src, dst, sems.at[i]) for i, (src, dst) in enumerate(pairs)]
    for copy in copies:
        copy.start()
    return copies


IN_VMEM = pl.BlockSpec(memory_space=pltpu.VMEM)
IN_HBM = pl.BlockSpec(memory_space=pl.ANY)


def comm_params(number):
    return pltpu.CompilerParams(
        vmem_limit_bytes=VMEM_LIMIT, collective_id=number, has_side_effects=True
    )


def gather_norm_body(x_ref, gain_ref, buf, send, recv):
    place = lax.axis_index("tensor")
    greet(place)
    rows = x_ref[...].astype(f32)
    rms = lax.rsqrt(jnp.mean(rows * rows, axis=1, keepdims=True) + eps)
    buf[place] = (rows * rms * gain_ref[...]).astype(bf16)
    gather = Gather(place, buf, send, recv, 1)
    for step in range(1, LINE - 1):
        gather.send(step, 0)
        gather.arrive(step, 0)
    gather.drain(stop=LINE - 1)


def gather_norm(x, gain):
    rows, features = x.shape
    return pl.pallas_call(
        gather_norm_body,
        in_specs=[IN_VMEM, IN_VMEM],
        out_specs=IN_VMEM,
        out_shape=jax.ShapeDtypeStruct((LINE, rows, features), bf16),
        scratch_shapes=line_sems(1),
        compiler_params=comm_params(0),
    )(x, gain[None, :])


def project_body(
    x_ref, w_ref, e_ref, a_ref, cos_ref, sin_ref, buf, y_ref, l_ref, wv, xsem, wsem, send, recv
):
    place = lax.axis_index("tensor")
    groups, _, width = y_ref.shape
    rows, rank = x_ref.shape[1], a_ref.shape[1]
    edge = (place == 0) | (place == LINE - 1)
    copies = []
    for slot in range(LINE):
        copy = pltpu.make_async_copy(x_ref.at[place ^ slot], buf.at[place ^ slot], xsem.at[slot])
        if slot < LINE - 1:
            copy.start()
        else:
            pl.when(jnp.logical_not(edge))(copy.start)
        copies.append(copy)
    (load,) = fetch([(w_ref.at[:, : groups * width], wv)], wsem)
    greet(place)
    for copy in copies[:-1]:
        copy.wait()
    gather = Gather(place, buf, send, recv, 1)
    gather.send(LINE - 1, 0)
    load.wait()
    for slot in range(LINE):
        if slot == LINE - 1:
            pl.when(jnp.logical_not(edge))(copies[slot].wait)
            gather.arrive(slot, 0)
        shard = place ^ slot
        mine = pl.ds(pl.multiple_of(shard * rows, rows), rows)
        low = nt(buf[shard], e_ref[:groups].reshape(groups * rank, -1)).astype(bf16)
        l_ref[mine] = low
        for g in range(groups):
            band = slice(g * width, (g + 1) * width)
            value = nn(buf[shard], wv[:, band]) + nn(low[:, g * rank : (g + 1) * rank], a_ref[g])
            if g < groups - 1:
                value = turn(value, cos_ref[mine], sin_ref[mine])
            y_ref[g, mine] = value.astype(bf16)
    gather.drain(start=LINE - 1)


def project(x, weight, entries, exits, tables):
    _, rows, features = x.shape
    groups, rank, width = exits.shape
    return pl.pallas_call(
        project_body,
        in_specs=[IN_HBM, IN_HBM] + [IN_VMEM] * 4,
        out_specs=[IN_VMEM] * 3,
        out_shape=[
            jax.ShapeDtypeStruct((LINE, rows, features), bf16),
            jax.ShapeDtypeStruct((groups, LINE * rows, width), bf16),
            jax.ShapeDtypeStruct((LINE * rows, groups * rank), bf16),
        ],
        scratch_shapes=[
            pltpu.VMEM((features, groups * width), bf16),
            pltpu.SemaphoreType.DMA((LINE,)),
            pltpu.SemaphoreType.DMA((1,)),
        ]
        + line_sems(1),
        compiler_params=comm_params(4),
    )(x, weight, entries, exits, *tables)


def middle_body(
    chunks, d_ref, w_ref, c_ref, before_ref, after_ref, a_ref, e_ref, x_ref, gain_ref, mid_ref, buf, cbuf, low_ref,
    part, held, wv, wsem, s_send, s_recv, g_send, g_recv, c_send, c_recv,
):
    place = lax.axis_index("tensor")
    width = d_ref.shape[1]
    load, own = fetch([(w_ref.at[:, 3 * width :], wv), (c_ref, cbuf.at[place])], wsem)

    def neighbours(act):
        @pl.when(place > 0)
        def _():
            act(pltpu.make_async_copy(before_ref, cbuf.at[place - 1], wsem.at[2]))

        @pl.when(place < LINE - 1)
        def _():
            act(pltpu.make_async_copy(after_ref, cbuf.at[place + 1], wsem.at[3]))

    neighbours(lambda copy: copy.start())
    greet(place)
    load.wait()
    own.wait()
    cots = Gather(place, cbuf, c_send, c_recv, 1)
    rows = part.shape[1]
    summed = Sum(place, part, held, s_send, s_recv, chunks)
    gather = Gather(place, buf, g_send, g_recv, chunks)
    for slot in (3, 2, 1, 0):
        shard = place ^ slot
        mine = pl.ds(pl.multiple_of(shard * rows, rows), rows)
        d = d_ref[mine]
        low = nt(d, a_ref[...]).astype(bf16)
        low_ref[mine] = low
        part[shard] = (nt(d, wv[...]) + nn(low, e_ref[0])).astype(bf16)
        if slot == 3:
            for chunk in range(chunks):
                summed.send(1, chunk)
    neighbours(lambda copy: copy.wait())
    cots.send(2, 0)
    size = rows // chunks
    for turn_ in range(chunks + 2):
        if turn_ == 2:
            cots.arrive(2, 0)
            cots.send(3, 0)
        if turn_ < chunks:
            summed.send(2, turn_)
            summed.send(3, turn_)
            summed.total(turn_, mid_ref)
            here = chunk_rows(turn_, size)
            value = mid_ref[here] + x_ref[here].astype(f32)
            mid_ref[here] = value
            rms = lax.rsqrt(jnp.mean(value * value, axis=1, keepdims=True) + eps)
            buf[place, here] = (value * rms * gain_ref[...]).astype(bf16)
            gather.send(1, turn_)
        for step in (1, 2):
            chunk = turn_ - step
            if 0 <= chunk < chunks:
                gather.arrive(step, chunk)
                gather.send(step + 1, chunk)
    for chunk in range(chunks):
        gather.arrive(3, chunk)
    cots.arrive(3, 0)
    summed.drain()
    gather.drain()
    cots.drain(start=2)


def middle_rows(attended, weight, cot, before, after, exits, finals, x, gain, chunks=4):
    rows, features = x.shape
    width = attended.shape[1]
    return pl.pallas_call(
        functools.partial(middle_body, chunks),
        in_specs=[IN_VMEM] + [IN_HBM] * 4 + [IN_VMEM] * 4,
        out_specs=[IN_VMEM] * 4,
        out_shape=[
            jax.ShapeDtypeStruct((rows, features), f32),
            jax.ShapeDtypeStruct((LINE, rows, features), bf16),
            jax.ShapeDtypeStruct((LINE, rows, features), bf16),
            jax.ShapeDtypeStruct((LINE * rows, exits.shape[0]), bf16),
        ],
        scratch_shapes=[
            pltpu.VMEM((LINE, rows, features), bf16),
            pltpu.VMEM((2, LINE - 1, rows, features), bf16),
            pltpu.VMEM((features, width), bf16),
            pltpu.SemaphoreType.DMA((4,)),
        ]
        + line_sems(chunks)
        + line_sems(chunks)
        + line_sems(1),
        compiler_params=comm_params(1),
    )(attended, weight, cot, before, after, exits, finals, x, gain[None, :])


def branch_body(
    b_ref, w_ref, e_ref, a_ref, p_ref, buf, y_ref, l_ref, own_ref, right_ref, left_ref,
    part, held, wv, wsem, send, recv, s_send, s_recv,
):
    place = lax.axis_index("tensor")
    rows = b_ref.shape[0]
    load, parts = fetch([(w_ref.at[:, 3 * y_ref.shape[2] :], wv), (p_ref, part)], wsem)
    greet(place)
    buf[place] = b_ref[...]
    gather = Gather(place, buf, send, recv, 1)
    summed = Sum(place, part, held, s_send, s_recv, 1)
    gather.send(1, 0)
    parts.wait()
    summed.send(1, 0)
    load.wait()
    for slot in range(LINE):
        if slot:
            gather.arrive(slot, 0)
        if 0 < slot < LINE - 1:
            gather.send(slot + 1, 0)
        if slot == 1:
            summed.send(2, 0)
        if slot == 2:
            summed.add(3, 0)
            own_ref[...] = part[place]
            for out_ref, side in ((right_ref, 1), (left_ref, -1)):

                @pl.when(far_of(place, side) < LINE - 1)
                def _():
                    out_ref[...] = part[place + side]

                @pl.when(far_of(place, side) == LINE - 1)
                def _():
                    out_ref[...] = jnp.zeros_like(out_ref)

        shard = place ^ slot
        mine = pl.ds(pl.multiple_of(shard * rows, rows), rows)
        low = nt(buf[shard], e_ref[0]).astype(bf16)
        l_ref[mine] = low
        y_ref[0, mine] = (nn(buf[shard], wv[...]) + nn(low, a_ref[...])).astype(bf16)
    gather.drain()
    summed.drain(LINE - 1)


def branch_back(branch, weight, finals, exits, parts):
    rows, features = branch.shape
    rank, width = exits.shape
    return pl.pallas_call(
        branch_body,
        in_specs=[IN_VMEM, IN_HBM, IN_VMEM, IN_VMEM, IN_HBM],
        out_specs=[IN_VMEM] * 6,
        out_shape=[
            jax.ShapeDtypeStruct((LINE, rows, features), bf16),
            jax.ShapeDtypeStruct((1, LINE * rows, width), bf16),
            jax.ShapeDtypeStruct((LINE * rows, rank), bf16),
        ]
        + [jax.ShapeDtypeStruct((rows, features), bf16)] * 3,
        scratch_shapes=[
            pltpu.VMEM((LINE, rows, features), bf16),
            pltpu.VMEM((2, LINE - 1, rows, features), bf16),
            pltpu.VMEM((features, width), bf16),
            pltpu.SemaphoreType.DMA((2,)),
        ]
        + line_sems(1)
        + line_sems(1),
        compiler_params=comm_params(2),
    )(branch, weight, finals, exits, parts)


def tokens_body(
    chunks, d_ref, w_ref, a_ref, e_ref, x_ref, gain_ref, mid_ref, n_ref, b_ref, lone_ref, lo_ref, bo_ref, o_ref,
    out_ref, model_ref, head_ref,
    part, held, acc, dv, wv, midv, nv, bv, low, block, extra, wsem, send, recv, x_send, x_recv, t_send, t_recv,
):
    place = lax.axis_index("tensor")
    tree = lax.axis_index("dp")
    trees = Trees(tree, (model_ref, head_ref), t_send, t_recv)
    groups, total, width = d_ref.shape
    rank = a_ref.shape[1]
    loads = fetch(
        [(d_ref, dv), (w_ref.at[:, : groups * width], wv), (n_ref, nv), (b_ref, bv), (mid_ref, midv)],
        wsem,
    )
    block[...] = jnp.zeros_like(block)
    for g in range(groups):
        block[g * rank : (g + 1) * rank, g * width : (g + 1) * width] = a_ref[g]
    greet(place, trees.partners)
    for load in loads[:2]:
        load.wait()
    rows = part.shape[1]
    summed = Sum(place, part, held, send, recv, chunks)
    entry = e_ref[:groups].reshape(groups * rank, -1)
    for slot in (3, 2, 1, 0):
        shard = place ^ slot
        mine = pl.ds(pl.multiple_of(shard * rows, rows), rows)
        d = jnp.concatenate([dv[g, mine] for g in range(groups)], axis=1)
        mine_low = nt(d, block[...]).astype(bf16)
        low[mine] = mine_low
        part[shard] = (nt(d, wv[...]) + nn(mine_low, entry)).astype(bf16)
        if slot == 3:
            for chunk in range(chunks):
                summed.send(1, chunk)
    summed.send(2, 0)
    for load in loads[2:]:
        load.wait()

    def turned(value):
        return value.astype(f32).T.astype(bf16)

    joined = nn(turned(low[...]), nv[...].reshape(total, -1))
    final = nn(turned(lo_ref[...]), bv[...].reshape(total, -1))
    extra[place] = jnp.concatenate([joined, final], axis=0).astype(bf16)
    gather = Gather(place, extra, x_send, x_recv, 1)
    gather.send(1, 0)
    summed.send(3, 0)
    low_one = turned(lone_ref[...])
    for g in range(groups):
        band = slice(g * rank, (g + 1) * rank)
        head_ref[tree, band] = nn(low_one[band], dv[g]).astype(bf16)
    head_ref[tree, groups * rank :] = nn(turned(bo_ref[...]), o_ref[...]).astype(bf16)
    size = rows // chunks

    def finish(chunk):
        finish_tokens(summed, chunk, size, acc, x_ref, gain_ref, midv, out_ref)

    gather.arrive(1, 0)
    gather.send(2, 0)
    summed.send(2, 1)
    gather.arrive(2, 0)
    gather.send(3, 0)
    finish(0)
    summed.send(3, 1)
    gather.arrive(3, 0)
    model_ref[tree] = functools.reduce(
        jnp.add, [extra[shard].astype(f32) for shard in range(LINE)]
    ).astype(bf16)
    trees.send(0)
    for chunk in range(2, chunks):
        summed.send(2, chunk)
        summed.send(3, chunk)
        if chunk - 1 < trees.rounds:
            trees.arrive(chunk - 2)
            trees.send(chunk - 1)
        finish(chunk - 1)
    for number in range(chunks - 1, trees.rounds):
        trees.arrive(number - 1)
        trees.send(number)
    finish(chunks - 1)
    trees.arrive(trees.rounds - 1)
    summed.drain()
    gather.drain()
    trees.drain()


class Trees:
    def __init__(self, tree, refs, send, recv):
        self.tree, self.refs, self.sems = tree, refs, (send, recv)
        self.rounds = refs[0].shape[0].bit_length() - 1
        self.partners = [self.partner(number) for number in range(self.rounds)]

    def partner(self, number):
        size = 1 << number
        return self.tree + size - 2 * size * ((self.tree // size) % 2)

    def copies(self, number, owner):
        size = 1 << number
        here = pl.ds((owner // size) * size, size)
        return [
            pltpu.make_async_remote_copy(
                src_ref=ref.at[here],
                dst_ref=ref.at[here],
                send_sem=self.sems[0].at[number, k],
                recv_sem=self.sems[1].at[number, k],
                device_id={"dp": self.partner(number)},
                device_id_type=MESH,
            )
            for k, ref in enumerate(self.refs)
        ]

    def send(self, number):
        for copy in self.copies(number, self.tree):
            copy.start()

    def arrive(self, number):
        for copy in self.copies(number, self.partner(number)):
            copy.wait_recv()

    def drain(self):
        for number in range(self.rounds):
            for copy in self.copies(number, self.tree):
                copy.wait_send()


def finish_tokens(summed, chunk, size, acc, x_ref, gain_ref, mid_ref, out_ref):
    summed.total(chunk, acc)
    here = chunk_rows(chunk, size)
    rows = x_ref[here].astype(f32)
    rms = lax.rsqrt(jnp.mean(rows * rows, axis=1, keepdims=True) + eps)
    scaled = acc[here] * gain_ref[...]
    mean = jnp.mean(scaled * rows, axis=1, keepdims=True)
    out_ref[here] = (mid_ref[here] + rms * (scaled - rows * (rms * rms) * mean)).astype(bf16)


def tokens_back(
    head_grads, weight, exits, entries, x, gain, grad_middle, normed, branch, low_one, low_out, back_out, attended
):
    chunks = LINE
    rows, features = x.shape
    groups, total, width = head_grads.shape
    rank = exits.shape[1]
    deep = (groups + 1) * rank
    trees = lax.axis_size("dp")
    sems = pltpu.SemaphoreType.DMA((trees.bit_length() - 1, 2))
    return pl.pallas_call(
        functools.partial(tokens_body, chunks),
        in_specs=[IN_HBM, IN_HBM] + [IN_VMEM] * 4 + [IN_HBM] * 3 + [IN_VMEM] * 4,
        out_specs=[IN_VMEM] * 3,
        out_shape=[
            jax.ShapeDtypeStruct((rows, features), bf16),
            jax.ShapeDtypeStruct((trees, deep, features), bf16),
            jax.ShapeDtypeStruct((trees, deep, width), bf16),
        ],
        scratch_shapes=[
            pltpu.VMEM((LINE, rows, features), bf16),
            pltpu.VMEM((2, LINE - 1, rows, features), bf16),
            pltpu.VMEM((rows, features), f32),
            pltpu.VMEM((groups, total, width), bf16),
            pltpu.VMEM((features, groups * width), bf16),
            pltpu.VMEM((rows, features), f32),
            pltpu.VMEM((LINE, rows, features), bf16),
            pltpu.VMEM((LINE, rows, features), bf16),
            pltpu.VMEM((total, groups * rank), bf16),
            pltpu.VMEM((groups * rank, groups * width), bf16),
            pltpu.VMEM((LINE, deep, features), bf16),
            pltpu.SemaphoreType.DMA((5,)),
        ]
        + line_sems(chunks)
        + line_sems(1)
        + [sems, sems],
        compiler_params=comm_params(3),
    )(
        head_grads, weight, exits, entries, x, gain[None, :], grad_middle, normed, branch,
        low_one, low_out, back_out, attended,
    )


def tree_tiles(seg, rows, parent_row):
    trunk = TRUNK * seg
    leaves = trunk + BRANCHES * seg
    key = lax.broadcasted_iota(jnp.int32, (QT, QT), 0)
    query = lax.broadcasted_iota(jnp.int32, (QT, QT), 1)
    causal = key <= query
    own = causal & (key // seg == query // seg)
    tiles = []
    for start in range(0, trunk, QT):
        pieces = [(0, start, None)] if start else []
        tiles.append((start, pieces + [(start, QT, causal)]))
    tiles.append((trunk, [(0, trunk, None), (trunk, QT, own)]))
    branch = lax.broadcasted_iota(jnp.int32, (BRANCHES * seg, QT), 0) // seg
    for start in range(leaves, rows, QT):
        mine = branch == parent_row[:, start - leaves : start - leaves + QT]
        tiles.append(
            (start, [(0, trunk, None), (trunk, BRANCHES * seg, mine), (start, QT, own)])
        )
    return tiles


def attend_body(seg, q_ref, k_ref, v_ref, p_ref, o_ref, lse_ref):
    rows = q_ref.shape[1]
    value_t = v_ref[0].T
    lane = lax.broadcasted_iota(jnp.int32, (QT, 2 * HEAD_DIM), 1)
    for start, pieces in tree_tiles(seg, rows, p_ref[...]):
        query = q_ref[0, start : start + QT] * bf16(HEAD_DIM**-0.5)
        outs = []
        for h in range(2):
            own_query = jnp.where(lane // HEAD_DIM == h, query, bf16(0))
            scores = []
            for k0, count, mask in pieces:
                s = nt(k_ref[0, k0 : k0 + count], own_query)
                scores.append(s if mask is None else jnp.where(mask, s, -1e30))
            top = functools.reduce(
                jnp.maximum, [jnp.max(s, axis=0, keepdims=True) for s in scores]
            )
            summed, out = 0.0, 0.0
            for (k0, count, _), s in zip(pieces, scores):
                weights = jnp.exp(s - top)
                summed += jnp.sum(weights, axis=0, keepdims=True)
                out += nn(
                    value_t[h * HEAD_DIM : (h + 1) * HEAD_DIM, k0 : k0 + count],
                    weights.astype(bf16),
                )
            outs.append(out / summed)
            lse_ref[0, h : h + 1, start : start + QT] = top + jnp.log(summed)
        o_ref[0, start : start + QT] = jnp.concatenate(outs, axis=0).T.astype(bf16)


def attend(qkv, leaf_parent, seg):
    _, rows, width = qkv.shape
    pairs = width // (2 * HEAD_DIM)
    return pl.pallas_call(
        functools.partial(attend_body, seg),
        grid=(pairs,),
        in_specs=[
            pl.BlockSpec((1, rows, 2 * HEAD_DIM), lambda j, g=g: (g, 0, j)) for g in range(3)
        ]
        + [pl.BlockSpec(leaf_parent.shape, lambda j: (0, 0))],
        out_specs=[
            pl.BlockSpec((1, rows, 2 * HEAD_DIM), lambda j: (0, 0, j)),
            pl.BlockSpec((1, 2, rows), lambda j: (j, 0, 0)),
        ],
        out_shape=[
            jax.ShapeDtypeStruct((1, rows, width), bf16),
            jax.ShapeDtypeStruct((pairs, 2, rows), f32),
        ],
        compiler_params=pltpu.CompilerParams(vmem_limit_bytes=VMEM_LIMIT),
        cost_estimate=pl.CostEstimate(
            flops=8 * rows * rows * width, bytes_accessed=8 * rows * width, transcendentals=0
        ),
    )(qkv, qkv, qkv, leaf_parent)


def attend_back_body(
    seg, q_ref, k_ref, v_ref, o_ref, g_ref, lse_ref, p_ref, cos_ref, sin_ref, d_ref, dq_t, dk, dv
):
    rows = q_ref.shape[1]
    scale = bf16(HEAD_DIM**-0.5)
    key_t = k_ref[0].T
    weighed_t = (g_ref[0].astype(f32) * o_ref[0].astype(f32)).T
    lane = lax.broadcasted_iota(jnp.int32, (QT, 2 * HEAD_DIM), 1)
    dk[...] = jnp.zeros_like(dk)
    dv[...] = jnp.zeros_like(dv)
    for start, pieces in tree_tiles(seg, rows, p_ref[...]):
        query = q_ref[0, start : start + QT] * scale
        grad = g_ref[0, start : start + QT]
        for h in range(2):
            mine = lane // HEAD_DIM == h
            own_query = jnp.where(mine, query, bf16(0))
            own_grad = jnp.where(mine, grad, bf16(0))
            band = slice(h * HEAD_DIM, (h + 1) * HEAD_DIM)
            delta = jnp.sum(weighed_t[band, start : start + QT], axis=0, keepdims=True)
            lse = lse_ref[0, h : h + 1, start : start + QT]
            grad_q = 0.0
            for k0, count, mask in pieces:
                probs = jnp.exp(nt(k_ref[0, k0 : k0 + count], own_query) - lse)
                if mask is not None:
                    probs = jnp.where(mask, probs, 0.0)
                grad_probs = nt(v_ref[0, k0 : k0 + count], own_grad)
                grad_scores = (probs * (grad_probs - delta)).astype(bf16)
                dk[k0 : k0 + count] += nn(grad_scores, own_query)
                dv[k0 : k0 + count] += nn(probs.astype(bf16), own_grad)
                grad_q += nn(key_t[band, k0 : k0 + count], grad_scores)
            dq_t[band, start : start + QT] = grad_q
    cosine, sine = cos_ref[...], -sin_ref[...]
    d_ref[0] = turn(dq_t[...].T * HEAD_DIM**-0.5, cosine, sine).astype(bf16)
    d_ref[1] = turn(dk[...], cosine, sine).astype(bf16)
    d_ref[2] = dv[...].astype(bf16)


def attend_back(qkv, attended, grad, lse, leaf_parent, tables, seg):
    _, rows, width = qkv.shape
    pairs = width // (2 * HEAD_DIM)
    pair = 2 * HEAD_DIM
    return pl.pallas_call(
        functools.partial(attend_back_body, seg),
        grid=(pairs,),
        in_specs=[pl.BlockSpec((1, rows, pair), lambda j, g=g: (g, 0, j)) for g in range(3)]
        + [
            pl.BlockSpec((1, rows, pair), lambda j: (0, 0, j)),
            pl.BlockSpec((1, rows, pair), lambda j: (0, 0, j)),
            pl.BlockSpec((1, 2, rows), lambda j: (j, 0, 0)),
            pl.BlockSpec(leaf_parent.shape, lambda j: (0, 0)),
            pl.BlockSpec((rows, pair), lambda j: (0, 0)),
            pl.BlockSpec((rows, pair), lambda j: (0, 0)),
        ],
        out_specs=pl.BlockSpec((3, rows, pair), lambda j: (0, 0, j)),
        out_shape=jax.ShapeDtypeStruct((3, rows, width), bf16),
        scratch_shapes=[
            pltpu.VMEM((pair, rows), f32),
            pltpu.VMEM((rows, pair), f32),
            pltpu.VMEM((rows, pair), f32),
        ],
        compiler_params=pltpu.CompilerParams(vmem_limit_bytes=VMEM_LIMIT),
        cost_estimate=pl.CostEstimate(
            flops=20 * rows * rows * width, bytes_accessed=16 * rows * width, transcendentals=0
        ),
    )(qkv, qkv, qkv, attended, grad, lse, leaf_parent, *tables)


def feed_body(
    rank, tile, chunks,
    n_ref, c_ref, w_ref, mid_ref,
    xu_in, xd_in, e_in, f_in, gain_ref,
    grad_ref, low_grad_ref, res_ref, unit_ref, model_ref,
    x_ref, e_ref, f_ref, midv, nbuf, cbuf, wbuf, low, low_t, acc_res, acc_back, acc_low, part, held, resv,
    nsem, csem, wsem, rsem, msem, send, recv,
):
    place = lax.axis_index("tensor")
    units = unit_ref.shape[1]
    tiles = units // tile
    summed = Sum(place, part, held, send, recv, chunks)

    def load_rows(order, act):
        into = order % 2
        shard = place ^ (LINE - 1 - order)
        act(pltpu.make_async_copy(n_ref.at[shard], nbuf.at[into], nsem.at[into]))
        act(pltpu.make_async_copy(c_ref.at[shard], cbuf.at[into], csem.at[into]))

    def load_weights(index, into, act):
        for k in range(3):
            columns = pl.ds(pl.multiple_of(k * units + index * tile, tile), tile)
            act(pltpu.make_async_copy(w_ref.at[:, columns], wbuf.at[into, k], wsem.at[into, k]))

    def start(copy):
        copy.start()

    def wait(copy):
        copy.wait()

    load_rows(jnp.int32(0), start)
    load_weights(0, 0, start)
    (load_middle,) = fetch([(mid_ref, midv)], msem)
    for padded in (x_ref, e_ref, f_ref):
        padded[...] = jnp.zeros_like(padded)
    x_ref[0, :rank] = xu_in[0]
    x_ref[1, rank : 2 * rank] = xu_in[1]
    x_ref[2, 2 * rank :] = xd_in[...]
    e_ref[: 2 * rank] = e_in[3:].reshape(2 * rank, -1)
    f_ref[2 * rank :] = f_in[1]
    unit_ref[...] = jnp.zeros_like(unit_ref)
    model_ref[...] = jnp.zeros_like(model_ref)
    greet(place)

    def one_shard(order, carry):
        into = order % 2
        shard = place ^ (LINE - 1 - order)
        load_rows(order, wait)

        @pl.when(order < LINE - 1)
        def _():
            load_rows(order + 1, start)

        first = nt(nbuf[into], e_ref[...]) + nt(cbuf[into], f_ref[...])
        low[...] = first.astype(bf16)
        low_t[...] = first.T.astype(bf16)
        acc_res[...] = jnp.zeros_like(acc_res)
        acc_back[...] = jnp.zeros_like(acc_back)
        acc_low[...] = jnp.zeros_like(acc_low)

        def one_tile(index, carry):
            stage = order * tiles + index
            at = stage % 2
            load_weights(index, at, wait)

            @pl.when(stage < LINE * tiles - 1)
            def _():
                load_weights((index + 1) % tiles, 1 - at, start)

            columns = pl.ds(pl.multiple_of(index * tile, tile), tile)
            x_gate, x_rise, x_fall = x_ref[0, :, columns], x_ref[1, :, columns], x_ref[2, :, columns]
            gate = nn(nbuf[into], wbuf[at, 0]) + nn(low[...], x_gate)
            rise = nn(nbuf[into], wbuf[at, 1]) + nn(low[...], x_rise)
            grad_hidden = nn(cbuf[into], wbuf[at, 2]) + nn(low[...], x_fall)
            sigmoid = jax.nn.sigmoid(gate)
            silu = gate * sigmoid
            hidden = (silu * rise).astype(bf16)
            grad_gate = (grad_hidden * rise * sigmoid * (1.0 + gate * (1.0 - sigmoid))).astype(bf16)
            grad_rise = (grad_hidden * silu).astype(bf16)
            acc_back[...] += nt(grad_gate, wbuf[at, 0]) + nt(grad_rise, wbuf[at, 1])
            acc_res[...] += nt(hidden, wbuf[at, 2])
            acc_low[...] += nt(grad_gate, x_gate) + nt(grad_rise, x_rise) + nt(hidden, x_fall)
            unit_ref[:rank, columns] += nn(low_t[:rank], grad_gate)
            unit_ref[rank : 2 * rank, columns] += nn(low_t[rank : 2 * rank], grad_rise)
            unit_ref[2 * rank :, columns] += nn(low_t[2 * rank : 3 * rank], hidden)
            return carry

        lax.fori_loop(0, tiles, one_tile, 0)
        joined = acc_low[...].astype(bf16)
        joined_t = acc_low[...].T.astype(bf16)
        part[shard] = (acc_back[...] + nn(joined, e_ref[...])).astype(bf16)

        @pl.when(order > 0)
        def _():
            pltpu.make_async_copy(resv, res_ref.at[shard], rsem.at[0]).wait()

        resv[...] = (acc_res[...] + nn(joined, f_ref[...])).astype(bf16)
        pltpu.make_async_copy(resv, res_ref.at[shard], rsem.at[0]).start()
        for step in (1, 2, 3):

            @pl.when(order == step - 1)
            def _():
                for chunk in range(chunks):
                    summed.send(step, chunk)

        model_ref[: 2 * rank] += nn(joined_t[: 2 * rank], nbuf[into])
        model_ref[2 * rank :] += nn(joined_t[2 * rank : 3 * rank], cbuf[into])
        return carry

    lax.fori_loop(0, LINE, one_shard, 0)
    size = part.shape[1] // chunks
    last = (LINE - 1) % 2
    load_middle.wait()
    for chunk in range(chunks):
        summed.total(chunk, acc_back)
        here = chunk_rows(chunk, size)
        middle = midv[here]
        rms = lax.rsqrt(jnp.mean(middle * middle, axis=1, keepdims=True) + eps)
        scaled = acc_back[here] * gain_ref[...]
        mean = jnp.mean(scaled * middle, axis=1, keepdims=True)
        grad = cbuf[last, here].astype(f32) + rms * (scaled - middle * (rms * rms) * mean)
        grad_ref[here] = grad
        low_grad_ref[here] = grad.astype(bf16)
    pltpu.make_async_copy(resv, res_ref.at[place], rsem.at[0]).wait()
    summed.drain()


def feed(normed, cots, weight, middle, units_exit, fall_entry, entries, finals, gain, tile=512, chunks=4):
    _, rows, features = normed.shape
    units = weight.shape[1] // 3
    rank = fall_entry.shape[0]
    return pl.pallas_call(
        functools.partial(feed_body, rank, tile, chunks),
        in_specs=[IN_HBM] * 4 + [IN_VMEM] * 5,
        out_specs=[IN_VMEM, IN_VMEM, IN_HBM, IN_VMEM, IN_VMEM],
        out_shape=[
            jax.ShapeDtypeStruct((rows, features), f32),
            jax.ShapeDtypeStruct((rows, features), bf16),
            jax.ShapeDtypeStruct((LINE, rows, features), bf16),
            jax.ShapeDtypeStruct((3 * rank, units), f32),
            jax.ShapeDtypeStruct((3 * rank, features), f32),
        ],
        scratch_shapes=[
            pltpu.VMEM((3, 3 * rank, units), bf16),
            pltpu.VMEM((3 * rank, features), bf16),
            pltpu.VMEM((3 * rank, features), bf16),
            pltpu.VMEM((rows, features), f32),
            pltpu.VMEM((2, rows, features), bf16),
            pltpu.VMEM((2, rows, features), bf16),
            pltpu.VMEM((2, 3, features, tile), bf16),
            pltpu.VMEM((rows, 3 * rank), bf16),
            pltpu.VMEM((3 * rank, rows), bf16),
            pltpu.VMEM((rows, features), f32),
            pltpu.VMEM((rows, features), f32),
            pltpu.VMEM((rows, 3 * rank), f32),
            pltpu.VMEM((LINE, rows, features), bf16),
            pltpu.VMEM((2, LINE - 1, rows, features), bf16),
            pltpu.VMEM((rows, features), bf16),
            pltpu.SemaphoreType.DMA((2,)),
            pltpu.SemaphoreType.DMA((2,)),
            pltpu.SemaphoreType.DMA((2, 3)),
            pltpu.SemaphoreType.DMA((1,)),
            pltpu.SemaphoreType.DMA((1,)),
        ]
        + line_sems(chunks),
        compiler_params=comm_params(5),
    )(normed, cots, weight, middle, units_exit, fall_entry, entries, finals, gain[None, :])


def per_tree(block):
    return lax.all_gather(block, "dp", axis=0, tiled=False)


def combine_body(rank, pick_ref, early, model, late, head, entry_ref, final_ref, unit_ref, down_ref, exit_ref, out_ref):
    for ref in (entry_ref, final_ref, unit_ref, down_ref, exit_ref, out_ref):
        ref[...] = jnp.zeros_like(ref)

    def one_tree(tree, carry):
        pick = pick_ref[tree]

        def block(ref, index):
            return ref[tree, index * rank : (index + 1) * rank].astype(f32)

        for k in range(3):
            entry_ref[k, pick] += block(late, k)
            exit_ref[k, pick] += block(head, k)
        final_ref[0, pick] += block(late, 3)
        out_ref[pick] += block(head, 3)
        for k in range(2):
            entry_ref[3 + k, pick] += block(model, k)
            unit_ref[k, pick] += block(early, k)
        final_ref[1, pick] += block(model, 2)
        down_ref[pick] += block(early, 2)
        return carry

    lax.fori_loop(0, early.shape[0], one_tree, 0)


def combine(picks, early, model, late, head, adapters, steps=4):
    trees, _, features = early.shape
    rank = late.shape[1] // 4
    width = head.shape[2]
    wide, narrow = features // steps, width // steps

    def taken(array, tile):
        return pl.BlockSpec((trees, array.shape[1], tile), lambda i, p: (0, 0, i))

    def given(lead, tile):
        shape = lead + (adapters, rank, tile)
        return pl.BlockSpec(shape, lambda i, p: (0,) * (len(shape) - 1) + (i,))

    def shape(lead, full):
        return jax.ShapeDtypeStruct(lead + (adapters, rank, full), f32)

    return pl.pallas_call(
        functools.partial(combine_body, rank),
        grid_spec=pltpu.PrefetchScalarGridSpec(
            num_scalar_prefetch=1,
            grid=(steps,),
            in_specs=[taken(early, wide), taken(model, wide), taken(late, wide), taken(head, narrow)],
            out_specs=[
                given((5,), wide),
                given((2,), wide),
                given((2,), wide),
                given((), wide),
                given((3,), narrow),
                given((), narrow),
            ],
        ),
        out_shape=[
            shape((5,), features),
            shape((2,), features),
            shape((2,), features),
            shape((), features),
            shape((3,), width),
            shape((), width),
        ],
        compiler_params=pltpu.CompilerParams(vmem_limit_bytes=VMEM_LIMIT),
    )(picks, early, model, late, head)


def local(
    tokens,
    cotangent,
    attention_gain,
    feed_gain,
    query_weight,
    key_weight,
    value_weight,
    output_weight,
    gate_weight,
    up_weight,
    down_weight,
    entry_maps,
    head_exits,
    unit_exits,
    output_entry,
    down_entry,
    final_exits,
    parents,
    adapter_pick,
):
    pick = adapter_pick[0]
    adapters, rank = entry_maps.shape[1], entry_maps.shape[3]
    local_rows = tokens.shape[0]
    total = local_rows * lax.axis_size("tensor")
    blocks = parents.shape[1]
    seg = total // blocks
    tables = rope_tables(blocks, seg)
    leaf_parent = (jnp.repeat(parents[0, TRUNK + BRANCHES :], seg) - TRUNK)[None, :]
    gain_one = attention_gain.astype(f32)
    gain_two = feed_gain.astype(f32)

    w_heads = lax.all_gather(
        jnp.concatenate([query_weight, key_weight, value_weight, output_weight], axis=1),
        "dp",
        axis=0,
        tiled=True,
    )

    w_units = lax.all_gather(
        jnp.concatenate([gate_weight, up_weight, down_weight], axis=1), "dp", axis=0, tiled=True
    )
    entries = jnp.swapaxes(entry_maps, 2, 3)[:, pick]
    heads_exit = head_exits[:, pick]

    most_one = gather_norm(tokens, gain_one)
    full_one, qkv, low_one = project(most_one, w_heads, entries, heads_exit, tables)
    cot_tied, qkv = lax.optimization_barrier((cotangent, qkv))
    before = permute(cot_tied, [(0, 1), (1, 2), (2, 3)])
    after = permute(cot_tied, [(3, 2), (2, 1), (1, 0)])
    attended, lse = attend(qkv, leaf_parent, seg)
    late_pick, attended = lax.optimization_barrier((pick, attended))
    units_exit = unit_exits[:, late_pick]
    out_entry = jnp.swapaxes(output_entry, 1, 2)[late_pick]
    fall_entry = jnp.swapaxes(down_entry, 1, 2)[late_pick]
    finals = final_exits[:, late_pick]
    middle, full_two, full_cot, adapt_o = middle_rows(
        attended[0], w_heads, cotangent, before, after, out_entry, finals, tokens, gain_two
    )

    grad_middle, branch, res_parts, unit_grads, model_grads = feed(
        full_two, full_cot, w_units, middle, units_exit, fall_entry, entries, finals, gain_two
    )
    early = jnp.concatenate(
        [unit_grads.astype(bf16), jnp.full((rank, unit_grads.shape[1]), pick).astype(bf16)]
    )
    model_low = model_grads.astype(bf16)
    branch, early, model_low = lax.optimization_barrier((branch, early, model_low))
    early = per_tree(early)
    model_sum = lax.psum(model_low, "tensor")

    full_branch, grad_attended, back_o, res_own, res_right, res_left = branch_back(
        branch, w_heads, finals, out_entry, res_parts
    )
    grad_attended, res_right, res_left = lax.optimization_barrier((grad_attended, res_right, res_left))
    from_left = permute(res_right, [(0, 1), (1, 2), (2, 3)])
    from_right = permute(res_left, [(3, 2), (2, 1), (1, 0)])
    head_grads = attend_back(qkv, attended, grad_attended, lse, leaf_parent, tables, seg)
    head_grads, model_sum, from_left, from_right = lax.optimization_barrier(
        (head_grads, model_sum, from_left, from_right)
    )
    model_all = per_tree(model_sum)
    grad_tokens, late_model, late_head = tokens_back(
        head_grads, w_heads, heads_exit, entries, tokens, gain_one, grad_middle,
        full_one, full_branch, low_one, adapt_o, back_o, attended[0],
    )
    result = (
        middle
        + res_own.astype(f32)
        + from_left.astype(f32)
        + from_right.astype(f32)
    ).astype(bf16)

    picks = early[:, 3 * rank, 0].astype(jnp.int32)
    grad_entries, grad_finals, grad_units, grad_down, grad_heads, grad_output = combine(
        picks, early, model_all, late_model, late_head, adapters
    )
    grad_entries = grad_entries.swapaxes(2, 3)
    grad_output = grad_output.swapaxes(1, 2)
    grad_down = grad_down.swapaxes(1, 2)
    return (
        result,
        grad_tokens,
        grad_entries,
        grad_heads,
        grad_units,
        grad_output,
        grad_down,
        grad_finals,
    )


def solution(mesh):
    in_specs = (
        P(("dp", "tensor"), None),
        P(("dp", "tensor"), None),
        P(),
        P(),
        P("dp", "tensor"),
        P("dp", "tensor"),
        P("dp", "tensor"),
        P("dp", "tensor"),
        P("dp", "tensor"),
        P("dp", "tensor"),
        P("dp", "tensor"),
        P(),
        P(None, None, None, "tensor"),
        P(None, None, None, "tensor"),
        P(None, "tensor", None),
        P(None, "tensor", None),
        P(),
        P("dp", None),
        P("dp"),
    )
    out_specs = (
        P(("dp", "tensor"), None),
        P(("dp", "tensor"), None),
        P(),
        P(None, None, None, "tensor"),
        P(None, None, None, "tensor"),
        P(None, "tensor", None),
        P(None, "tensor", None),
        P(),
    )
    return jax.shard_map(local, mesh=mesh, in_specs=in_specs, out_specs=out_specs, check_vma=False)
```

```python
import functools

import jax
import jax.numpy as jnp
import numpy as np
from jax import lax
from jax.experimental import pallas as pl
from jax.experimental.pallas import tpu as pltpu
from jax.sharding import PartitionSpec as P

HEAD_DIM = 64
TRUNK, BRANCHES = 8, 4
QT = 256
VMEM_LIMIT = 60 * 1024 * 1024
LINE = 4
MESH = pl.DeviceIdType.MESH

eps = 1e-05
theta = 130000.0
bf16, f32 = jnp.bfloat16, jnp.float32


def nn(left, right):
    return jnp.dot(left, right, preferred_element_type=f32)


def nt(left, right):
    return lax.dot_general(left, right, (((1,), (1,)), ((), ())), preferred_element_type=f32)


def tn(left, right):
    return lax.dot_general(left, right, (((0,), (0,)), ((), ())), preferred_element_type=f32)


def permute(value, pairs):
    return lax.ppermute(value, "tensor", pairs)


def rope_tables(blocks, seg):
    depth = np.minimum(np.arange(blocks), TRUNK)
    depth[TRUNK + BRANCHES :] = TRUNK + 1
    position = (np.repeat(depth, seg) * seg + np.arange(blocks * seg) % seg).astype(np.float32)
    half = HEAD_DIM // 2
    freq = (np.float32(theta) ** (-np.arange(half, dtype=np.float32) / half)).astype(np.float32)
    angle = (position[:, None] * freq[None, :]).astype(np.float32)
    cosine = np.tile(np.cos(angle), (1, 4)).astype(np.float32)
    sine = np.sin(angle).astype(np.float32)
    sine = np.concatenate([-sine, sine, -sine, sine], axis=1)
    return jnp.asarray(cosine), jnp.asarray(sine)


def turn(values, cosine, sine):
    width = values.shape[1]
    reps = width // cosine.shape[1]
    if reps > 1:
        cosine = jnp.concatenate([cosine] * reps, axis=1)
        sine = jnp.concatenate([sine] * reps, axis=1)
    lane = lax.broadcasted_iota(jnp.int32, values.shape, 1)
    half = HEAD_DIM // 2
    other = jnp.where(
        lane % HEAD_DIM < half, pltpu.roll(values, width - half, 1), pltpu.roll(values, half, 1)
    )
    return values * cosine + other * sine


SIDES = (1, -1)


def far_of(place, side):
    return place if side == 1 else LINE - 1 - place


def greet(place, partners=()):
    barrier = pltpu.get_barrier_semaphore()
    for partner in partners:
        pl.semaphore_signal(barrier, inc=1, device_id={"dp": partner}, device_id_type=MESH)
    for side in SIDES:

        @pl.when(far_of(place, side) < LINE - 1)
        def _():
            pl.semaphore_signal(
                barrier, inc=1, device_id={"tensor": place + side}, device_id_type=MESH
            )

    edge = (place == 0) | (place == LINE - 1)

    @pl.when(edge)
    def _():
        pl.semaphore_wait(barrier, 1 + len(partners))

    @pl.when(jnp.logical_not(edge))
    def _():
        pl.semaphore_wait(barrier, 2 + len(partners))


def chunk_rows(chunk, rows):
    return pl.ds(chunk * rows, rows)


class Gather:
    def __init__(self, place, buf, send, recv, chunks, own=None):
        self.place, self.buf, self.sems, self.chunks = place, buf, (send, recv), chunks
        self.rows = buf.shape[1] // chunks
        self.own = own

    def copy(self, side, step, chunk, shard, target):
        rows = chunk_rows(chunk, self.rows)
        where = self.buf.at[shard, rows]
        spot = (0 if side == 1 else 1, step - 1, chunk)
        return pltpu.make_async_remote_copy(
            src_ref=where if self.own is None or step > 1 else self.own.at[rows],
            dst_ref=where,
            send_sem=self.sems[0].at[spot],
            recv_sem=self.sems[1].at[spot],
            device_id={"tensor": target},
            device_id_type=MESH,
        )

    def each_send(self, step, chunk, act):
        for side in SIDES:
            far = far_of(self.place, side)

            @pl.when((far < LINE - 1) & (far >= step - 1))
            def _():
                shard = self.place - side * (step - 1)
                act(self.copy(side, step, chunk, shard, self.place + side))

    def send(self, step, chunk):
        self.each_send(step, chunk, lambda copy: copy.start())

    def arrive(self, step, chunk):
        for side in SIDES:

            @pl.when(far_of(self.place, side) >= step)
            def _():
                shard = self.place - side * step
                self.copy(side, step, chunk, shard, self.place - side).wait_recv()

    def drain(self, stop=LINE, start=1):
        for step in range(start, stop):
            for chunk in range(self.chunks):
                self.each_send(step, chunk, lambda copy: copy.wait_send())


class Sum:
    def __init__(self, place, part, held, send, recv, chunks):
        self.place, self.part, self.held = place, part, held
        self.sems, self.chunks = (send, recv), chunks
        self.rows = part.shape[1] // chunks

    def copy(self, side, step, chunk, shard, target):
        rows = chunk_rows(chunk, self.rows)
        index = 0 if side == 1 else 1
        spot = (index, step - 1, chunk)
        return pltpu.make_async_remote_copy(
            src_ref=self.part.at[shard, rows],
            dst_ref=self.held.at[index, step - 1, rows],
            send_sem=self.sems[0].at[spot],
            recv_sem=self.sems[1].at[spot],
            device_id={"tensor": target},
            device_id_type=MESH,
        )

    def add(self, step, chunk):
        rows = chunk_rows(chunk, self.rows)
        for index, side in enumerate(SIDES):
            far = far_of(self.place, side)
            shard = self.place + side * (LINE - step)

            @pl.when((far >= 1) & (far <= step - 1))
            def _():
                self.copy(side, step - 1, chunk, self.place, self.place - side).wait_recv()
                self.part[shard, rows] = (
                    self.part[shard, rows].astype(f32)
                    + self.held[index, step - 2, rows].astype(f32)
                ).astype(bf16)

    def send(self, step, chunk):
        if step > 1:
            self.add(step, chunk)
        for side in SIDES:
            far = far_of(self.place, side)
            shard = self.place + side * (LINE - step)

            @pl.when(far <= step - 1)
            def _():
                self.copy(side, step, chunk, shard, self.place + side).start()

    def total(self, chunk, out):
        rows = chunk_rows(chunk, self.rows)
        out[rows] = self.part[self.place, rows].astype(f32)
        for index, side in enumerate(SIDES):

            @pl.when(far_of(self.place, side) >= 1)
            def _():
                self.copy(side, LINE - 1, chunk, self.place, self.place - side).wait_recv()
                out[rows] += self.held[index, LINE - 2, rows].astype(f32)

    def drain(self, stop=LINE):
        for step in range(1, stop):
            for chunk in range(self.chunks):
                for side in SIDES:
                    far = far_of(self.place, side)
                    shard = self.place + side * (LINE - step)

                    @pl.when(far <= step - 1)
                    def _():
                        self.copy(side, step, chunk, shard, self.place + side).wait_send()


def line_sems(chunks):
    return [pltpu.SemaphoreType.DMA((2, LINE - 1, chunks))] * 2


def fetch(pairs, sems):
    copies = [pltpu.make_async_copy(src, dst, sems.at[i]) for i, (src, dst) in enumerate(pairs)]
    for copy in copies:
        copy.start()
    return copies


IN_VMEM = pl.BlockSpec(memory_space=pltpu.VMEM)
IN_HBM = pl.BlockSpec(memory_space=pl.ANY)


def comm_params(number):
    return pltpu.CompilerParams(
        vmem_limit_bytes=VMEM_LIMIT, collective_id=number, has_side_effects=True
    )


def gather_norm_body(x_ref, gain_ref, buf, own, sem, send, recv):
    place = lax.axis_index("tensor")
    greet(place)
    rows = x_ref[...].astype(f32)
    rms = lax.rsqrt(jnp.mean(rows * rows, axis=1, keepdims=True) + eps)
    own[...] = (rows * rms * gain_ref[...]).astype(bf16)
    gather = Gather(place, buf, send, recv, 1, own)
    gather.send(1, 0)
    (kept,) = fetch([(own, buf.at[place])], sem)
    gather.arrive(1, 0)
    gather.send(2, 0)
    kept.wait()
    gather.arrive(2, 0)
    gather.drain(stop=LINE - 1)


def gather_norm(x, gain):
    rows, features = x.shape
    return pl.pallas_call(
        gather_norm_body,
        in_specs=[IN_VMEM, IN_VMEM],
        out_specs=IN_HBM,
        out_shape=jax.ShapeDtypeStruct((LINE, rows, features), bf16),
        scratch_shapes=[pltpu.VMEM((rows, features), bf16), pltpu.SemaphoreType.DMA((1,))]
        + line_sems(1),
        compiler_params=comm_params(0),
    )(x, gain[None, :])


def project_body(
    x_ref, w_ref, e_ref, a_ref, cos_ref, sin_ref, kept_ref, y_ref, l_ref,
    buf, yv, wv, xsem, wsem, ysem, send, recv,
):
    place = lax.axis_index("tensor")
    groups, _, width = y_ref.shape
    rows, rank = x_ref.shape[1], a_ref.shape[1]
    edge = (place == 0) | (place == LINE - 1)
    last = place ^ (LINE - 1)

    def passed(side):
        shard = place - side * (LINE - 2)
        index = 0 if side == 1 else 1
        return pltpu.make_async_remote_copy(
            src_ref=x_ref.at[shard],
            dst_ref=buf.at[shard],
            send_sem=send.at[index],
            recv_sem=recv.at[index],
            device_id={"tensor": place + side},
            device_id_type=MESH,
        )

    def came(side):
        index = 0 if side == 1 else 1
        return pltpu.make_async_remote_copy(
            src_ref=x_ref.at[last],
            dst_ref=buf.at[last],
            send_sem=send.at[index],
            recv_sem=recv.at[index],
            device_id={"tensor": place - side},
            device_id_type=MESH,
        )

    copies = []
    for slot in range(LINE):
        copy = pltpu.make_async_copy(x_ref.at[place ^ slot], buf.at[place ^ slot], xsem.at[slot])
        if slot < LINE - 1:
            copy.start()
        else:
            pl.when(jnp.logical_not(edge))(copy.start)
        copies.append(copy)
    (load,) = fetch([(w_ref.at[:, : groups * width], wv)], wsem)
    greet(place)
    for side in SIDES:
        pl.when(far_of(place, side) == LINE - 2)(passed(side).start)
    for copy in copies[:-1]:
        copy.wait()
    load.wait()
    outs = []
    for slot in range(LINE):
        shard = place ^ slot
        if slot == LINE - 1:
            pl.when(jnp.logical_not(edge))(copies[slot].wait)
            for side in SIDES:
                pl.when(far_of(place, side) == LINE - 1)(came(side).wait_recv)
            kept = pltpu.make_async_copy(buf.at[last], kept_ref.at[last], xsem.at[slot])
            pl.when(edge)(kept.start)
        mine = pl.ds(pl.multiple_of(shard * rows, rows), rows)
        low = nt(buf[shard], e_ref[:groups].reshape(groups * rank, -1)).astype(bf16)
        l_ref[mine] = low
        for g in range(groups):
            band = slice(g * width, (g + 1) * width)
            value = nn(buf[shard], wv[:, band]) + nn(low[:, g * rank : (g + 1) * rank], a_ref[g])
            if g < groups - 1:
                value = turn(value, cos_ref[mine], sin_ref[mine])
            yv[g, mine] = value.astype(bf16)
            out = pltpu.make_async_copy(yv.at[g, mine], y_ref.at[g, mine], ysem.at[slot, g])
            out.start()
            outs.append(out)
    pl.when(edge)(kept.wait)
    for out in outs:
        out.wait()
    for side in SIDES:
        pl.when(far_of(place, side) == LINE - 2)(passed(side).wait_send)


def project(x, weight, entries, exits, tables):
    _, rows, features = x.shape
    groups, rank, width = exits.shape
    return pl.pallas_call(
        project_body,
        in_specs=[IN_HBM, IN_HBM] + [IN_VMEM] * 4,
        out_specs=[IN_HBM, IN_HBM, IN_VMEM],
        out_shape=[
            jax.ShapeDtypeStruct((LINE, rows, features), bf16),
            jax.ShapeDtypeStruct((groups, LINE * rows, width), bf16),
            jax.ShapeDtypeStruct((LINE * rows, groups * rank), bf16),
        ],
        scratch_shapes=[
            pltpu.VMEM((LINE, rows, features), bf16),
            pltpu.VMEM((groups, LINE * rows, width), bf16),
            pltpu.VMEM((features, groups * width), bf16),
            pltpu.SemaphoreType.DMA((LINE,)),
            pltpu.SemaphoreType.DMA((1,)),
            pltpu.SemaphoreType.DMA((LINE, groups)),
            pltpu.SemaphoreType.DMA((2,)),
            pltpu.SemaphoreType.DMA((2,)),
        ],
        input_output_aliases={0: 0},
        compiler_params=comm_params(4),
    )(x, weight, entries, exits, *tables)


def middle_body(
    chunks, d_ref, w_ref, c_ref, before_ref, after_ref, a_ref, e_ref, x_ref, gain_ref, mid_ref, buf, cbuf, low_ref,
    part, held, own, wv, wsem, nsem, s_send, s_recv, g_send, g_recv, c_send, c_recv,
):
    place = lax.axis_index("tensor")
    width = d_ref.shape[1]
    load, own_cot = fetch([(w_ref.at[:, 3 * width :], wv), (c_ref, cbuf.at[place])], wsem)

    def neighbours(act):
        @pl.when(place > 0)
        def _():
            act(pltpu.make_async_copy(before_ref, cbuf.at[place - 1], wsem.at[2]))

        @pl.when(place < LINE - 1)
        def _():
            act(pltpu.make_async_copy(after_ref, cbuf.at[place + 1], wsem.at[3]))

    neighbours(lambda copy: copy.start())
    greet(place)
    load.wait()
    cots = Gather(place, cbuf, c_send, c_recv, chunks)
    rows = part.shape[1]
    summed = Sum(place, part, held, s_send, s_recv, chunks)
    gather = Gather(place, buf, g_send, g_recv, chunks, own)
    for slot in (3, 2, 1, 0):
        shard = place ^ slot
        mine = pl.ds(pl.multiple_of(shard * rows, rows), rows)
        d = d_ref[mine]
        low = nt(d, a_ref[...]).astype(bf16)
        low_ref[mine] = low
        part[shard] = (nt(d, wv[...]) + nn(low, e_ref[0])).astype(bf16)
        if slot == 3:
            summed.send(1, 0)
    neighbours(lambda copy: copy.wait())
    size = rows // chunks
    kept = []
    for now in range(chunks + 3):
        if now + 1 < chunks:
            summed.send(1, now + 1)
        if now < chunks:
            summed.send(2, now)
            summed.send(3, now)
            cots.send(2, now)
        chunk = now - 1
        if 0 <= chunk < chunks:
            summed.total(chunk, mid_ref)
            here = chunk_rows(chunk, size)
            value = mid_ref[here] + x_ref[here].astype(f32)
            mid_ref[here] = value
            rms = lax.rsqrt(jnp.mean(value * value, axis=1, keepdims=True) + eps)
            own[here] = (value * rms * gain_ref[...]).astype(bf16)
            gather.send(1, chunk)
            copy = pltpu.make_async_copy(own.at[here], buf.at[place, here], nsem.at[chunk])
            copy.start()
            kept.append(copy)
            cots.arrive(2, chunk)
            cots.send(3, chunk)
        for step in (1, 2):
            chunk = now - 1 - step
            if 0 <= chunk < chunks:
                gather.arrive(step, chunk)
                gather.send(step + 1, chunk)
    for chunk in range(chunks):
        cots.arrive(3, chunk)
        gather.arrive(3, chunk)
    own_cot.wait()
    for copy in kept:
        copy.wait()
    summed.drain()
    gather.drain()
    cots.drain(start=2)


def middle_rows(attended, weight, cot, before, after, exits, finals, x, gain, chunks=4):
    rows, features = x.shape
    width = attended.shape[1]
    return pl.pallas_call(
        functools.partial(middle_body, chunks),
        in_specs=[IN_VMEM] + [IN_HBM] * 4 + [IN_VMEM] * 4,
        out_specs=[IN_VMEM, IN_HBM, IN_HBM, IN_VMEM],
        out_shape=[
            jax.ShapeDtypeStruct((rows, features), f32),
            jax.ShapeDtypeStruct((LINE, rows, features), bf16),
            jax.ShapeDtypeStruct((LINE, rows, features), bf16),
            jax.ShapeDtypeStruct((LINE * rows, exits.shape[0]), bf16),
        ],
        scratch_shapes=[
            pltpu.VMEM((LINE, rows, features), bf16),
            pltpu.VMEM((2, LINE - 1, rows, features), bf16),
            pltpu.VMEM((rows, features), bf16),
            pltpu.VMEM((features, width), bf16),
            pltpu.SemaphoreType.DMA((4,)),
            pltpu.SemaphoreType.DMA((chunks,)),
        ]
        + line_sems(chunks)
        + line_sems(chunks)
        + line_sems(chunks),
        compiler_params=comm_params(1),
    )(attended, weight, cot, before, after, exits, finals, x, gain[None, :])


def branch_body(
    b_ref, w_ref, e_ref, a_ref, p_ref, kept_ref, y_ref, l_ref, own_ref, right_ref, left_ref,
    buf, part, held, wv, ksem, wsem, send, recv, s_send, s_recv,
):
    place = lax.axis_index("tensor")
    rows = b_ref.shape[0]
    load, parts = fetch([(w_ref.at[:, 3 * y_ref.shape[2] :], wv), (p_ref, part)], wsem)
    greet(place)
    buf[place] = b_ref[...]
    gather = Gather(place, buf, send, recv, 1)
    summed = Sum(place, part, held, s_send, s_recv, 1)
    gather.send(1, 0)
    parts.wait()
    summed.send(1, 0)
    load.wait()
    kept = []
    for slot in range(LINE):
        if slot:
            gather.arrive(slot, 0)
        if 0 < slot < LINE - 1:
            gather.send(slot + 1, 0)
        if slot == 1:
            summed.send(2, 0)
        if slot == 2:
            summed.add(3, 0)
            own_ref[...] = part[place]
            for out_ref, side in ((right_ref, 1), (left_ref, -1)):

                @pl.when(far_of(place, side) < LINE - 1)
                def _():
                    out_ref[...] = part[place + side]

                @pl.when(far_of(place, side) == LINE - 1)
                def _():
                    out_ref[...] = jnp.zeros_like(out_ref)

        shard = place ^ slot
        mine = pl.ds(pl.multiple_of(shard * rows, rows), rows)
        low = nt(buf[shard], e_ref[0]).astype(bf16)
        l_ref[mine] = low
        y_ref[0, mine] = (nn(buf[shard], wv[...]) + nn(low, a_ref[...])).astype(bf16)
        copy = pltpu.make_async_copy(buf.at[shard], kept_ref.at[shard], ksem.at[slot])
        copy.start()
        kept.append(copy)
    for copy in kept:
        copy.wait()
    gather.drain()
    summed.drain(LINE - 1)


def branch_back(branch, weight, finals, exits, parts):
    rows, features = branch.shape
    rank, width = exits.shape
    return pl.pallas_call(
        branch_body,
        in_specs=[IN_VMEM, IN_HBM, IN_VMEM, IN_VMEM, IN_HBM],
        out_specs=[IN_HBM] + [IN_VMEM] * 5,
        out_shape=[
            jax.ShapeDtypeStruct((LINE, rows, features), bf16),
            jax.ShapeDtypeStruct((1, LINE * rows, width), bf16),
            jax.ShapeDtypeStruct((LINE * rows, rank), bf16),
        ]
        + [jax.ShapeDtypeStruct((rows, features), bf16)] * 3,
        scratch_shapes=[
            pltpu.VMEM((LINE, rows, features), bf16),
            pltpu.VMEM((LINE, rows, features), bf16),
            pltpu.VMEM((2, LINE - 1, rows, features), bf16),
            pltpu.VMEM((features, width), bf16),
            pltpu.SemaphoreType.DMA((LINE,)),
            pltpu.SemaphoreType.DMA((2,)),
        ]
        + line_sems(1)
        + line_sems(1),
        compiler_params=comm_params(2),
    )(branch, weight, finals, exits, parts)


def tokens_body(
    chunks, d_ref, w_ref, a_ref, e_ref, x_ref, gain_ref, mid_ref, n_ref, b_ref, lone_ref, lo_ref, bo_ref, o_ref,
    out_ref, model_ref, head_ref,
    part, held, acc, dv, wv, midv, nv, bv, low, block, extra, wsem, send, recv, x_send, x_recv, t_send, t_recv, h_send, h_recv,
):
    place = lax.axis_index("tensor")
    tree = lax.axis_index("dp")
    trees = Trees(tree, model_ref, t_send, t_recv)
    heads = Trees(tree, head_ref, h_send, h_recv)
    groups, total, width = d_ref.shape
    rank = a_ref.shape[1]
    loads = fetch(
        [(d_ref, dv), (w_ref.at[:, : groups * width], wv), (n_ref, nv), (b_ref, bv), (mid_ref, midv)],
        wsem,
    )
    block[...] = jnp.zeros_like(block)
    for g in range(groups):
        block[g * rank : (g + 1) * rank, g * width : (g + 1) * width] = a_ref[g]
    greet(place, trees.partners)
    for load in loads[:2]:
        load.wait()
    rows = part.shape[1]
    summed = Sum(place, part, held, send, recv, chunks)
    gather = Gather(place, extra, x_send, x_recv, 1)
    entry = e_ref[:groups].reshape(groups * rank, -1)
    for slot in (3, 2, 1, 0):
        shard = place ^ slot
        mine = pl.ds(pl.multiple_of(shard * rows, rows), rows)
        d = jnp.concatenate([dv[g, mine] for g in range(groups)], axis=1)
        mine_low = nt(d, block[...]).astype(bf16)
        low[mine] = mine_low
        part[shard] = (nt(d, wv[...]) + nn(mine_low, entry)).astype(bf16)
        if slot == 3:
            for chunk in range(chunks):
                summed.send(1, chunk)
    for load in loads[2:]:
        load.wait()

    def turned(value):
        return value.astype(f32).T.astype(bf16)

    joined = nn(turned(low[...]), nv[...].reshape(total, -1))
    final = nn(turned(lo_ref[...]), bv[...].reshape(total, -1))
    extra[place] = jnp.concatenate([joined, final], axis=0).astype(bf16)
    gather.send(1, 0)
    for chunk in range(chunks):
        summed.send(2, chunk)
    low_one = turned(lone_ref[...])
    for g in range(groups):
        band = slice(g * rank, (g + 1) * rank)
        head_ref[tree, band] = nn(low_one[band], dv[g]).astype(bf16)
    head_ref[tree, groups * rank :] = nn(turned(bo_ref[...]), o_ref[...]).astype(bf16)
    heads.send(0)
    gather.arrive(1, 0)
    gather.send(2, 0)
    summed.send(3, 0)
    gather.arrive(2, 0)
    gather.send(3, 0)
    summed.send(3, 1)
    heads.advance(1)
    gather.arrive(3, 0)
    model_ref[tree] = functools.reduce(
        jnp.add, [extra[shard].astype(f32) for shard in range(LINE)]
    ).astype(bf16)
    trees.send(0)
    summed.send(3, 2)
    trees.advance(1)
    heads.advance(2)
    summed.send(3, 3)
    size = rows // chunks

    def finish(chunk):
        finish_tokens(summed, chunk, size, acc, x_ref, gain_ref, midv, out_ref)

    finish(0)
    trees.advance(2)
    finish(1)
    for number in range(3, trees.rounds):
        trees.advance(number)
        heads.advance(number)
    finish(2)
    finish(3)
    for blocks in (trees, heads):
        blocks.arrive(blocks.rounds - 1)
        blocks.drain()
    summed.drain()
    gather.drain()


class Trees:
    def __init__(self, tree, ref, send, recv):
        self.tree, self.ref, self.sems = tree, ref, (send, recv)
        self.rounds = ref.shape[0].bit_length() - 1
        self.partners = [self.partner(number) for number in range(self.rounds)]

    def partner(self, number):
        size = 1 << number
        return self.tree + size - 2 * size * ((self.tree // size) % 2)

    def copy(self, number, owner):
        size = 1 << number
        here = pl.ds((owner // size) * size, size)
        return pltpu.make_async_remote_copy(
            src_ref=self.ref.at[here],
            dst_ref=self.ref.at[here],
            send_sem=self.sems[0].at[number],
            recv_sem=self.sems[1].at[number],
            device_id={"dp": self.partner(number)},
            device_id_type=MESH,
        )

    def send(self, number):
        self.copy(number, self.tree).start()

    def arrive(self, number):
        self.copy(number, self.partner(number)).wait_recv()

    def advance(self, number):
        if number < self.rounds:
            self.arrive(number - 1)
            self.send(number)

    def drain(self):
        for number in range(self.rounds):
            self.copy(number, self.tree).wait_send()


def finish_tokens(summed, chunk, size, acc, x_ref, gain_ref, mid_ref, out_ref):
    summed.total(chunk, acc)
    here = chunk_rows(chunk, size)
    rows = x_ref[here].astype(f32)
    rms = lax.rsqrt(jnp.mean(rows * rows, axis=1, keepdims=True) + eps)
    scaled = acc[here] * gain_ref[...]
    mean = jnp.mean(scaled * rows, axis=1, keepdims=True)
    out_ref[here] = (mid_ref[here] + rms * (scaled - rows * (rms * rms) * mean)).astype(bf16)


def tokens_back(
    head_grads, weight, exits, entries, x, gain, grad_middle, normed, branch, low_one, low_out, back_out, attended
):
    chunks = LINE
    rows, features = x.shape
    groups, total, width = head_grads.shape
    rank = exits.shape[1]
    deep = (groups + 1) * rank
    trees = lax.axis_size("dp")
    sems = pltpu.SemaphoreType.DMA((trees.bit_length() - 1,))
    return pl.pallas_call(
        functools.partial(tokens_body, chunks),
        in_specs=[IN_HBM, IN_HBM] + [IN_VMEM] * 4 + [IN_HBM] * 3 + [IN_VMEM] * 4,
        out_specs=[IN_VMEM] * 3,
        out_shape=[
            jax.ShapeDtypeStruct((rows, features), bf16),
            jax.ShapeDtypeStruct((trees, deep, features), bf16),
            jax.ShapeDtypeStruct((trees, deep, width), bf16),
        ],
        scratch_shapes=[
            pltpu.VMEM((LINE, rows, features), bf16),
            pltpu.VMEM((2, LINE - 1, rows, features), bf16),
            pltpu.VMEM((rows, features), f32),
            pltpu.VMEM((groups, total, width), bf16),
            pltpu.VMEM((features, groups * width), bf16),
            pltpu.VMEM((rows, features), f32),
            pltpu.VMEM((LINE, rows, features), bf16),
            pltpu.VMEM((LINE, rows, features), bf16),
            pltpu.VMEM((total, groups * rank), bf16),
            pltpu.VMEM((groups * rank, groups * width), bf16),
            pltpu.VMEM((LINE, deep, features), bf16),
            pltpu.SemaphoreType.DMA((5,)),
        ]
        + line_sems(chunks)
        + line_sems(1)
        + [sems] * 4,
        compiler_params=comm_params(3),
    )(
        head_grads, weight, exits, entries, x, gain[None, :], grad_middle, normed, branch,
        low_one, low_out, back_out, attended,
    )


def tree_tiles(seg, rows, parent_row):
    trunk = TRUNK * seg
    leaves = trunk + BRANCHES * seg
    key = lax.broadcasted_iota(jnp.int32, (QT, QT), 0)
    query = lax.broadcasted_iota(jnp.int32, (QT, QT), 1)
    causal = key <= query
    own = causal & (key // seg == query // seg)
    tiles = []
    for start in range(0, trunk, QT):
        pieces = [(0, start, None)] if start else []
        tiles.append((start, pieces + [(start, QT, causal)]))
    tiles.append((trunk, [(0, trunk, None), (trunk, QT, own)]))
    branch = lax.broadcasted_iota(jnp.int32, (BRANCHES * seg, QT), 0) // seg
    for start in range(leaves, rows, QT):
        mine = branch == parent_row[:, start - leaves : start - leaves + QT]
        tiles.append(
            (start, [(0, trunk, None), (trunk, BRANCHES * seg, mine), (start, QT, own)])
        )
    return tiles


def attend_body(seg, q_ref, k_ref, v_ref, p_ref, o_ref, lse_ref):
    rows = q_ref.shape[1]
    value_t = v_ref[0].T
    lane = lax.broadcasted_iota(jnp.int32, (QT, 2 * HEAD_DIM), 1)
    for start, pieces in tree_tiles(seg, rows, p_ref[...]):
        query = q_ref[0, start : start + QT] * bf16(HEAD_DIM**-0.5)
        outs = []
        for h in range(2):
            own_query = jnp.where(lane // HEAD_DIM == h, query, bf16(0))
            scores = []
            for k0, count, mask in pieces:
                s = nt(k_ref[0, k0 : k0 + count], own_query)
                scores.append(s if mask is None else jnp.where(mask, s, -1e30))
            top = functools.reduce(
                jnp.maximum, [jnp.max(s, axis=0, keepdims=True) for s in scores]
            )
            summed, out = 0.0, 0.0
            for (k0, count, _), s in zip(pieces, scores):
                weights = jnp.exp(s - top)
                summed += jnp.sum(weights, axis=0, keepdims=True)
                out += nn(
                    value_t[h * HEAD_DIM : (h + 1) * HEAD_DIM, k0 : k0 + count],
                    weights.astype(bf16),
                )
            outs.append(out / summed)
            lse_ref[0, h : h + 1, start : start + QT] = top + jnp.log(summed)
        o_ref[0, start : start + QT] = jnp.concatenate(outs, axis=0).T.astype(bf16)


def attend(qkv, leaf_parent, seg):
    _, rows, width = qkv.shape
    pairs = width // (2 * HEAD_DIM)
    return pl.pallas_call(
        functools.partial(attend_body, seg),
        grid=(pairs,),
        in_specs=[
            pl.BlockSpec((1, rows, 2 * HEAD_DIM), lambda j, g=g: (g, 0, j)) for g in range(3)
        ]
        + [pl.BlockSpec(leaf_parent.shape, lambda j: (0, 0))],
        out_specs=[
            pl.BlockSpec((1, rows, 2 * HEAD_DIM), lambda j: (0, 0, j)),
            pl.BlockSpec((1, 2, rows), lambda j: (j, 0, 0)),
        ],
        out_shape=[
            jax.ShapeDtypeStruct((1, rows, width), bf16),
            jax.ShapeDtypeStruct((pairs, 2, rows), f32),
        ],
        compiler_params=pltpu.CompilerParams(vmem_limit_bytes=VMEM_LIMIT),
        cost_estimate=pl.CostEstimate(
            flops=8 * rows * rows * width, bytes_accessed=8 * rows * width, transcendentals=0
        ),
    )(qkv, qkv, qkv, leaf_parent)


def attend_back_body(
    seg, q_ref, k_ref, v_ref, o_ref, g_ref, lse_ref, p_ref, cos_ref, sin_ref, d_ref, dq_t, dk, dv
):
    rows = q_ref.shape[1]
    scale = bf16(HEAD_DIM**-0.5)
    key_t = k_ref[0].T
    weighed_t = (g_ref[0].astype(f32) * o_ref[0].astype(f32)).T
    lane = lax.broadcasted_iota(jnp.int32, (QT, 2 * HEAD_DIM), 1)
    dk[...] = jnp.zeros_like(dk)
    dv[...] = jnp.zeros_like(dv)
    for start, pieces in tree_tiles(seg, rows, p_ref[...]):
        query = q_ref[0, start : start + QT] * scale
        grad = g_ref[0, start : start + QT]
        for h in range(2):
            mine = lane // HEAD_DIM == h
            own_query = jnp.where(mine, query, bf16(0))
            own_grad = jnp.where(mine, grad, bf16(0))
            band = slice(h * HEAD_DIM, (h + 1) * HEAD_DIM)
            delta = jnp.sum(weighed_t[band, start : start + QT], axis=0, keepdims=True)
            lse = lse_ref[0, h : h + 1, start : start + QT]
            grad_q = 0.0
            for k0, count, mask in pieces:
                probs = jnp.exp(nt(k_ref[0, k0 : k0 + count], own_query) - lse)
                if mask is not None:
                    probs = jnp.where(mask, probs, 0.0)
                grad_probs = nt(v_ref[0, k0 : k0 + count], own_grad)
                grad_scores = (probs * (grad_probs - delta)).astype(bf16)
                dk[k0 : k0 + count] += nn(grad_scores, own_query)
                dv[k0 : k0 + count] += nn(probs.astype(bf16), own_grad)
                grad_q += nn(key_t[band, k0 : k0 + count], grad_scores)
            dq_t[band, start : start + QT] = grad_q
    cosine, sine = cos_ref[...], -sin_ref[...]
    d_ref[0] = turn(dq_t[...].T * HEAD_DIM**-0.5, cosine, sine).astype(bf16)
    d_ref[1] = turn(dk[...], cosine, sine).astype(bf16)
    d_ref[2] = dv[...].astype(bf16)


def attend_back(qkv, attended, grad, lse, leaf_parent, tables, seg):
    _, rows, width = qkv.shape
    pairs = width // (2 * HEAD_DIM)
    pair = 2 * HEAD_DIM
    return pl.pallas_call(
        functools.partial(attend_back_body, seg),
        grid=(pairs,),
        in_specs=[pl.BlockSpec((1, rows, pair), lambda j, g=g: (g, 0, j)) for g in range(3)]
        + [
            pl.BlockSpec((1, rows, pair), lambda j: (0, 0, j)),
            pl.BlockSpec((1, rows, pair), lambda j: (0, 0, j)),
            pl.BlockSpec((1, 2, rows), lambda j: (j, 0, 0)),
            pl.BlockSpec(leaf_parent.shape, lambda j: (0, 0)),
            pl.BlockSpec((rows, pair), lambda j: (0, 0)),
            pl.BlockSpec((rows, pair), lambda j: (0, 0)),
        ],
        out_specs=pl.BlockSpec((3, rows, pair), lambda j: (0, 0, j)),
        out_shape=jax.ShapeDtypeStruct((3, rows, width), bf16),
        scratch_shapes=[
            pltpu.VMEM((pair, rows), f32),
            pltpu.VMEM((rows, pair), f32),
            pltpu.VMEM((rows, pair), f32),
        ],
        compiler_params=pltpu.CompilerParams(vmem_limit_bytes=VMEM_LIMIT),
        cost_estimate=pl.CostEstimate(
            flops=20 * rows * rows * width, bytes_accessed=16 * rows * width, transcendentals=0
        ),
    )(qkv, qkv, qkv, attended, grad, lse, leaf_parent, *tables)


def feed_body(
    rank, tile, chunks,
    n_ref, c_ref, wg_ref, wu_ref, wd_ref, mid_ref,
    xu_in, xd_in, e_in, f_in, gain_ref,
    grad_ref, low_grad_ref, res_ref, unit_ref, model_ref,
    x_ref, e_ref, f_ref, midv, nbuf, cbuf, wbuf, low, low_t, acc_res, acc_back, acc_low, part, held, resv,
    nsem, csem, wsem, rsem, msem, send, recv,
):
    place = lax.axis_index("tensor")
    units = unit_ref.shape[1]
    tiles = units // tile
    summed = Sum(place, part, held, send, recv, chunks)

    def load_rows(order, act):
        into = order % 2
        shard = place ^ (LINE - 1 - order)
        act(pltpu.make_async_copy(n_ref.at[shard], nbuf.at[into], nsem.at[into]))
        act(pltpu.make_async_copy(c_ref.at[shard], cbuf.at[into], csem.at[into]))

    def load_weights(index, into, act):
        columns = pl.ds(pl.multiple_of(index * tile, tile), tile)
        for k, w_ref in enumerate((wg_ref, wu_ref, wd_ref)):
            act(pltpu.make_async_copy(w_ref.at[:, columns], wbuf.at[into, k], wsem.at[into, k]))

    def start(copy):
        copy.start()

    def wait(copy):
        copy.wait()

    load_rows(jnp.int32(0), start)
    load_weights(0, 0, start)
    (load_middle,) = fetch([(mid_ref, midv)], msem)
    for padded in (x_ref, e_ref, f_ref):
        padded[...] = jnp.zeros_like(padded)
    x_ref[0, :rank] = xu_in[0]
    x_ref[1, rank : 2 * rank] = xu_in[1]
    x_ref[2, 2 * rank :] = xd_in[...]
    e_ref[: 2 * rank] = e_in[3:].reshape(2 * rank, -1)
    f_ref[2 * rank :] = f_in[1]
    unit_ref[...] = jnp.zeros_like(unit_ref)
    model_ref[...] = jnp.zeros_like(model_ref)
    greet(place)

    def one_shard(order, carry):
        into = order % 2
        shard = place ^ (LINE - 1 - order)
        load_rows(order, wait)

        @pl.when(order < LINE - 1)
        def _():
            load_rows(order + 1, start)

        first = nt(nbuf[into], e_ref[...]) + nt(cbuf[into], f_ref[...])
        low[...] = first.astype(bf16)
        low_t[...] = first.T.astype(bf16)
        acc_res[...] = jnp.zeros_like(acc_res)
        acc_back[...] = jnp.zeros_like(acc_back)
        acc_low[...] = jnp.zeros_like(acc_low)

        def one_tile(index, carry):
            stage = order * tiles + index
            at = stage % 2
            load_weights(index, at, wait)

            @pl.when(stage < LINE * tiles - 1)
            def _():
                load_weights((index + 1) % tiles, 1 - at, start)

            columns = pl.ds(pl.multiple_of(index * tile, tile), tile)
            x_gate, x_rise, x_fall = x_ref[0, :, columns], x_ref[1, :, columns], x_ref[2, :, columns]
            gate = nn(nbuf[into], wbuf[at, 0]) + nn(low[...], x_gate)
            rise = nn(nbuf[into], wbuf[at, 1]) + nn(low[...], x_rise)
            grad_hidden = nn(cbuf[into], wbuf[at, 2]) + nn(low[...], x_fall)
            sigmoid = jax.nn.sigmoid(gate)
            silu = gate * sigmoid
            hidden = (silu * rise).astype(bf16)
            grad_gate = (grad_hidden * rise * sigmoid * (1.0 + gate * (1.0 - sigmoid))).astype(bf16)
            grad_rise = (grad_hidden * silu).astype(bf16)
            acc_back[...] += nt(grad_gate, wbuf[at, 0]) + nt(grad_rise, wbuf[at, 1])
            acc_res[...] += nt(hidden, wbuf[at, 2])
            acc_low[...] += nt(grad_gate, x_gate) + nt(grad_rise, x_rise) + nt(hidden, x_fall)
            unit_ref[:rank, columns] += nn(low_t[:rank], grad_gate)
            unit_ref[rank : 2 * rank, columns] += nn(low_t[rank : 2 * rank], grad_rise)
            unit_ref[2 * rank :, columns] += nn(low_t[2 * rank : 3 * rank], hidden)
            return carry

        lax.fori_loop(0, tiles, one_tile, 0)
        joined = acc_low[...].astype(bf16)
        joined_t = acc_low[...].T.astype(bf16)
        part[shard] = (acc_back[...] + nn(joined, e_ref[...])).astype(bf16)

        @pl.when(order > 0)
        def _():
            pltpu.make_async_copy(resv, res_ref.at[shard], rsem.at[0]).wait()

        resv[...] = (acc_res[...] + nn(joined, f_ref[...])).astype(bf16)
        pltpu.make_async_copy(resv, res_ref.at[shard], rsem.at[0]).start()
        for step in (1, 2, 3):

            @pl.when(order == step - 1)
            def _():
                for chunk in range(chunks):
                    summed.send(step, chunk)

        model_ref[: 2 * rank] += nn(joined_t[: 2 * rank], nbuf[into])
        model_ref[2 * rank :] += nn(joined_t[2 * rank : 3 * rank], cbuf[into])
        return carry

    lax.fori_loop(0, LINE, one_shard, 0)
    size = part.shape[1] // chunks
    last = (LINE - 1) % 2
    load_middle.wait()
    for chunk in range(chunks):
        summed.total(chunk, acc_back)
        here = chunk_rows(chunk, size)
        middle = midv[here]
        rms = lax.rsqrt(jnp.mean(middle * middle, axis=1, keepdims=True) + eps)
        scaled = acc_back[here] * gain_ref[...]
        mean = jnp.mean(scaled * middle, axis=1, keepdims=True)
        grad = cbuf[last, here].astype(f32) + rms * (scaled - middle * (rms * rms) * mean)
        grad_ref[here] = grad
        low_grad_ref[here] = grad.astype(bf16)
    pltpu.make_async_copy(resv, res_ref.at[place], rsem.at[0]).wait()
    summed.drain()


def feed(normed, cots, weights, middle, units_exit, fall_entry, entries, finals, gain, tile=512, chunks=4):
    _, rows, features = normed.shape
    units = weights[0].shape[1]
    rank = fall_entry.shape[0]
    return pl.pallas_call(
        functools.partial(feed_body, rank, tile, chunks),
        in_specs=[IN_HBM] * 6 + [IN_VMEM] * 5,
        out_specs=[IN_VMEM, IN_VMEM, IN_HBM, IN_VMEM, IN_VMEM],
        out_shape=[
            jax.ShapeDtypeStruct((rows, features), f32),
            jax.ShapeDtypeStruct((rows, features), bf16),
            jax.ShapeDtypeStruct((LINE, rows, features), bf16),
            jax.ShapeDtypeStruct((3 * rank, units), f32),
            jax.ShapeDtypeStruct((3 * rank, features), f32),
        ],
        scratch_shapes=[
            pltpu.VMEM((3, 3 * rank, units), bf16),
            pltpu.VMEM((3 * rank, features), bf16),
            pltpu.VMEM((3 * rank, features), bf16),
            pltpu.VMEM((rows, features), f32),
            pltpu.VMEM((2, rows, features), bf16),
            pltpu.VMEM((2, rows, features), bf16),
            pltpu.VMEM((2, 3, features, tile), bf16),
            pltpu.VMEM((rows, 3 * rank), bf16),
            pltpu.VMEM((3 * rank, rows), bf16),
            pltpu.VMEM((rows, features), f32),
            pltpu.VMEM((rows, features), f32),
            pltpu.VMEM((rows, 3 * rank), f32),
            pltpu.VMEM((LINE, rows, features), bf16),
            pltpu.VMEM((2, LINE - 1, rows, features), bf16),
            pltpu.VMEM((rows, features), bf16),
            pltpu.SemaphoreType.DMA((2,)),
            pltpu.SemaphoreType.DMA((2,)),
            pltpu.SemaphoreType.DMA((2, 3)),
            pltpu.SemaphoreType.DMA((1,)),
            pltpu.SemaphoreType.DMA((1,)),
        ]
        + line_sems(chunks),
        compiler_params=comm_params(5),
    )(normed, cots, *weights, middle, units_exit, fall_entry, entries, finals, gain[None, :])


def pick_body(pick_ref, *refs):
    count = len(refs) // 2
    for source, target in zip(refs[:count], refs[count:]):
        target[...] = source[...].reshape(target.shape)


def picked(pick, arrays):
    shapes = [a.shape[:1] + a.shape[2:] for a in arrays]
    return pl.pallas_call(
        pick_body,
        grid_spec=pltpu.PrefetchScalarGridSpec(
            num_scalar_prefetch=1,
            grid=(1,),
            in_specs=[
                pl.BlockSpec(a.shape[:1] + (1,) + a.shape[2:], lambda i, p: (0, p[0], 0, 0)) for a in arrays
            ],
            out_specs=[pl.BlockSpec(shape, lambda i, p: (0, 0, 0)) for shape in shapes],
        ),
        out_shape=[jax.ShapeDtypeStruct(shape, bf16) for shape in shapes],
    )(pick, *arrays)


def per_tree(block):
    return lax.all_gather(block, "dp", axis=0, tiled=False)


def combine_body(rank, pick_ref, early, model, late, head, entry_ref, final_ref, unit_ref, down_ref, exit_ref, out_ref):
    for ref in (entry_ref, final_ref, unit_ref, down_ref, exit_ref, out_ref):
        ref[...] = jnp.zeros_like(ref)

    def one_tree(tree, carry):
        pick = pick_ref[tree]

        def block(ref, index):
            return ref[tree, index * rank : (index + 1) * rank].astype(f32)

        for k in range(3):
            entry_ref[k, pick] += block(late, k)
            exit_ref[k, pick] += block(head, k)
        final_ref[0, pick] += block(late, 3)
        out_ref[pick] += block(head, 3)
        for k in range(2):
            entry_ref[3 + k, pick] += block(model, k)
            unit_ref[k, pick] += block(early, k)
        final_ref[1, pick] += block(model, 2)
        down_ref[pick] += block(early, 2)
        return carry

    lax.fori_loop(0, early.shape[0], one_tree, 0)


def combine(picks, early, model, late, head, adapters, steps=4):
    trees, _, features = early.shape
    rank = late.shape[1] // 4
    width = head.shape[2]
    wide, narrow = features // steps, width // steps

    def taken(array, tile):
        return pl.BlockSpec((trees, array.shape[1], tile), lambda i, p: (0, 0, i))

    def given(lead, tile):
        shape = lead + (adapters, rank, tile)
        return pl.BlockSpec(shape, lambda i, p: (0,) * (len(shape) - 1) + (i,))

    def shape(lead, full):
        return jax.ShapeDtypeStruct(lead + (adapters, rank, full), f32)

    return pl.pallas_call(
        functools.partial(combine_body, rank),
        grid_spec=pltpu.PrefetchScalarGridSpec(
            num_scalar_prefetch=1,
            grid=(steps,),
            in_specs=[taken(early, wide), taken(model, wide), taken(late, wide), taken(head, narrow)],
            out_specs=[
                given((5,), wide),
                given((2,), wide),
                given((2,), wide),
                given((), wide),
                given((3,), narrow),
                given((), narrow),
            ],
        ),
        out_shape=[
            shape((5,), features),
            shape((2,), features),
            shape((2,), features),
            shape((), features),
            shape((3,), width),
            shape((), width),
        ],
        compiler_params=pltpu.CompilerParams(vmem_limit_bytes=VMEM_LIMIT),
    )(picks, early, model, late, head)


def local(
    tokens,
    cotangent,
    attention_gain,
    feed_gain,
    query_weight,
    key_weight,
    value_weight,
    output_weight,
    gate_weight,
    up_weight,
    down_weight,
    entry_maps,
    head_exits,
    unit_exits,
    output_entry,
    down_entry,
    final_exits,
    parents,
    adapter_pick,
):
    pick = adapter_pick[0]
    adapters, rank = entry_maps.shape[1], entry_maps.shape[3]
    local_rows = tokens.shape[0]
    total = local_rows * lax.axis_size("tensor")
    blocks = parents.shape[1]
    seg = total // blocks
    tables = rope_tables(blocks, seg)
    leaf_parent = (jnp.repeat(parents[0, TRUNK + BRANCHES :], seg) - TRUNK)[None, :]
    gain_one = attention_gain.astype(f32)
    gain_two = feed_gain.astype(f32)

    w_heads = lax.all_gather(
        jnp.concatenate([query_weight, key_weight, value_weight, output_weight], axis=1),
        "dp",
        axis=0,
        tiled=True,
    )

    w_units = [
        lax.all_gather(w, "dp", axis=0, tiled=True) for w in (gate_weight, up_weight, down_weight)
    ]
    entries, heads_exit, units_exit, out_entry, fall_entry, finals = picked(
        adapter_pick,
        (
            jnp.swapaxes(entry_maps, 2, 3),
            head_exits,
            unit_exits,
            jnp.swapaxes(output_entry, 1, 2)[None],
            jnp.swapaxes(down_entry, 1, 2)[None],
            final_exits,
        ),
    )
    out_entry, fall_entry = out_entry[0], fall_entry[0]

    most_one = gather_norm(tokens, gain_one)
    full_one, qkv, low_one = project(most_one, w_heads, entries, heads_exit, tables)
    cot_tied, qkv = lax.optimization_barrier((cotangent, qkv))
    before = permute(cot_tied, [(0, 1), (1, 2), (2, 3)])
    after = permute(cot_tied, [(3, 2), (2, 1), (1, 0)])
    attended, lse = attend(qkv, leaf_parent, seg)
    middle, full_two, full_cot, adapt_o = middle_rows(
        attended[0], w_heads, cotangent, before, after, out_entry, finals, tokens, gain_two
    )

    grad_middle, branch, res_parts, unit_grads, model_grads = feed(
        full_two, full_cot, w_units, middle, units_exit, fall_entry, entries, finals, gain_two
    )
    early = jnp.concatenate(
        [unit_grads.astype(bf16), jnp.full((rank, unit_grads.shape[1]), pick).astype(bf16)]
    )
    model_low = model_grads.astype(bf16)
    branch, early, model_low = lax.optimization_barrier((branch, early, model_low))
    early = per_tree(early)
    model_sum = lax.psum(model_low, "tensor")

    full_branch, grad_attended, back_o, res_own, res_right, res_left = branch_back(
        branch, w_heads, finals, out_entry, res_parts
    )
    grad_attended, res_right, res_left = lax.optimization_barrier((grad_attended, res_right, res_left))
    from_left = permute(res_right, [(0, 1), (1, 2), (2, 3)])
    from_right = permute(res_left, [(3, 2), (2, 1), (1, 0)])
    head_grads = attend_back(qkv, attended, grad_attended, lse, leaf_parent, tables, seg)
    head_grads, model_sum, from_left, from_right = lax.optimization_barrier(
        (head_grads, model_sum, from_left, from_right)
    )
    model_all = per_tree(model_sum)
    grad_tokens, late_model, late_head = tokens_back(
        head_grads, w_heads, heads_exit, entries, tokens, gain_one, grad_middle,
        full_one, full_branch, low_one, adapt_o, back_o, attended[0],
    )
    result = (
        middle
        + res_own.astype(f32)
        + from_left.astype(f32)
        + from_right.astype(f32)
    ).astype(bf16)

    picks = early[:, 3 * rank, 0].astype(jnp.int32)
    grad_entries, grad_finals, grad_units, grad_down, grad_heads, grad_output = combine(
        picks, early, model_all, late_model, late_head, adapters
    )
    grad_entries = grad_entries.swapaxes(2, 3)
    grad_output = grad_output.swapaxes(1, 2)
    grad_down = grad_down.swapaxes(1, 2)
    return (
        result,
        grad_tokens,
        grad_entries,
        grad_heads,
        grad_units,
        grad_output,
        grad_down,
        grad_finals,
    )


def solution(mesh):
    in_specs = (
        P(("dp", "tensor"), None),
        P(("dp", "tensor"), None),
        P(),
        P(),
        P("dp", "tensor"),
        P("dp", "tensor"),
        P("dp", "tensor"),
        P("dp", "tensor"),
        P("dp", "tensor"),
        P("dp", "tensor"),
        P("dp", "tensor"),
        P(),
        P(None, None, None, "tensor"),
        P(None, None, None, "tensor"),
        P(None, "tensor", None),
        P(None, "tensor", None),
        P(),
        P("dp", None),
        P("dp"),
    )
    out_specs = (
        P(("dp", "tensor"), None),
        P(("dp", "tensor"), None),
        P(),
        P(None, None, None, "tensor"),
        P(None, None, None, "tensor"),
        P(None, "tensor", None),
        P(None, "tensor", None),
        P(),
    )
    return jax.shard_map(local, mesh=mesh, in_specs=in_specs, out_specs=out_specs, check_vma=False)
```

```python
import functools

import jax
import jax.numpy as jnp
import numpy as np
from jax import lax
from jax.experimental import pallas as pl
from jax.experimental.pallas import tpu as pltpu
from jax.sharding import PartitionSpec as P

HEAD_DIM = 64
TRUNK, BRANCHES = 8, 4
QT = 256
VMEM_LIMIT = 60 * 1024 * 1024
LINE = 4
MESH = pl.DeviceIdType.MESH

eps = 1e-05
theta = 130000.0
bf16, f32 = jnp.bfloat16, jnp.float32


def nn(left, right):
    return jnp.dot(left, right, preferred_element_type=f32)


def nt(left, right):
    return lax.dot_general(left, right, (((1,), (1,)), ((), ())), preferred_element_type=f32)


def tn(left, right):
    return lax.dot_general(left, right, (((0,), (0,)), ((), ())), preferred_element_type=f32)


def permute(value, pairs):
    return lax.ppermute(value, "tensor", pairs)


def rope_tables(blocks, seg):
    depth = np.minimum(np.arange(blocks), TRUNK)
    depth[TRUNK + BRANCHES :] = TRUNK + 1
    position = (np.repeat(depth, seg) * seg + np.arange(blocks * seg) % seg).astype(np.float32)
    half = HEAD_DIM // 2
    freq = (np.float32(theta) ** (-np.arange(half, dtype=np.float32) / half)).astype(np.float32)
    angle = (position[:, None] * freq[None, :]).astype(np.float32)
    cosine = np.tile(np.cos(angle), (1, 4)).astype(np.float32)
    sine = np.sin(angle).astype(np.float32)
    sine = np.concatenate([-sine, sine, -sine, sine], axis=1)
    return jnp.asarray(cosine), jnp.asarray(sine)


def turn(values, cosine, sine):
    width = values.shape[1]
    reps = width // cosine.shape[1]
    if reps > 1:
        cosine = jnp.concatenate([cosine] * reps, axis=1)
        sine = jnp.concatenate([sine] * reps, axis=1)
    lane = lax.broadcasted_iota(jnp.int32, values.shape, 1)
    half = HEAD_DIM // 2
    other = jnp.where(
        lane % HEAD_DIM < half, pltpu.roll(values, width - half, 1), pltpu.roll(values, half, 1)
    )
    return values * cosine + other * sine


SIDES = (1, -1)


def far_of(place, side):
    return place if side == 1 else LINE - 1 - place


def greet(place, partners=()):
    barrier = pltpu.get_barrier_semaphore()
    for partner in partners:
        pl.semaphore_signal(barrier, inc=1, device_id={"dp": partner}, device_id_type=MESH)
    for side in SIDES:

        @pl.when(far_of(place, side) < LINE - 1)
        def _():
            pl.semaphore_signal(
                barrier, inc=1, device_id={"tensor": place + side}, device_id_type=MESH
            )

    edge = (place == 0) | (place == LINE - 1)

    @pl.when(edge)
    def _():
        pl.semaphore_wait(barrier, 1 + len(partners))

    @pl.when(jnp.logical_not(edge))
    def _():
        pl.semaphore_wait(barrier, 2 + len(partners))


def chunk_rows(chunk, rows):
    return pl.ds(chunk * rows, rows)


class Gather:
    def __init__(self, place, buf, send, recv, chunks, own=None):
        self.place, self.buf, self.sems, self.chunks = place, buf, (send, recv), chunks
        self.rows = buf.shape[1] // chunks
        self.own = own

    def copy(self, side, step, chunk, shard, target):
        rows = chunk_rows(chunk, self.rows)
        where = self.buf.at[shard, rows]
        spot = (0 if side == 1 else 1, step - 1, chunk)
        return pltpu.make_async_remote_copy(
            src_ref=where if self.own is None or step > 1 else self.own.at[rows],
            dst_ref=where,
            send_sem=self.sems[0].at[spot],
            recv_sem=self.sems[1].at[spot],
            device_id={"tensor": target},
            device_id_type=MESH,
        )

    def each_send(self, step, chunk, act):
        for side in SIDES:
            far = far_of(self.place, side)

            @pl.when((far < LINE - 1) & (far >= step - 1))
            def _():
                shard = self.place - side * (step - 1)
                act(self.copy(side, step, chunk, shard, self.place + side))

    def send(self, step, chunk):
        self.each_send(step, chunk, lambda copy: copy.start())

    def arrive(self, step, chunk):
        for side in SIDES:

            @pl.when(far_of(self.place, side) >= step)
            def _():
                shard = self.place - side * step
                self.copy(side, step, chunk, shard, self.place - side).wait_recv()

    def drain(self, stop=LINE, start=1):
        for step in range(start, stop):
            for chunk in range(self.chunks):
                self.each_send(step, chunk, lambda copy: copy.wait_send())


class Sum:
    def __init__(self, place, part, held, send, recv, chunks):
        self.place, self.part, self.held = place, part, held
        self.sems, self.chunks = (send, recv), chunks
        self.rows = part.shape[1] // chunks

    def copy(self, side, step, chunk, shard, target):
        rows = chunk_rows(chunk, self.rows)
        index = 0 if side == 1 else 1
        spot = (index, step - 1, chunk)
        return pltpu.make_async_remote_copy(
            src_ref=self.part.at[shard, rows],
            dst_ref=self.held.at[index, step - 1, rows],
            send_sem=self.sems[0].at[spot],
            recv_sem=self.sems[1].at[spot],
            device_id={"tensor": target},
            device_id_type=MESH,
        )

    def add(self, step, chunk):
        rows = chunk_rows(chunk, self.rows)
        for index, side in enumerate(SIDES):
            far = far_of(self.place, side)
            shard = self.place + side * (LINE - step)

            @pl.when((far >= 1) & (far <= step - 1))
            def _():
                self.copy(side, step - 1, chunk, self.place, self.place - side).wait_recv()
                self.part[shard, rows] = (
                    self.part[shard, rows].astype(f32)
                    + self.held[index, step - 2, rows].astype(f32)
                ).astype(bf16)

    def send(self, step, chunk, least=0, most=LINE):
        if step > 1 and most > 0:
            self.add(step, chunk)
        for side in SIDES:
            far = far_of(self.place, side)
            shard = self.place + side * (LINE - step)

            @pl.when((far <= step - 1) & (far >= least) & (far <= most))
            def _():
                self.copy(side, step, chunk, shard, self.place + side).start()

    def begin(self, step, chunk):
        self.send(step, chunk, most=0)

    def relay(self, step, chunk):
        self.send(step, chunk, least=1)

    def total(self, chunk, out):
        rows = chunk_rows(chunk, self.rows)
        out[rows] = self.part[self.place, rows].astype(f32)
        for index, side in enumerate(SIDES):

            @pl.when(far_of(self.place, side) >= 1)
            def _():
                self.copy(side, LINE - 1, chunk, self.place, self.place - side).wait_recv()
                out[rows] += self.held[index, LINE - 2, rows].astype(f32)

    def drain(self, stop=LINE):
        for step in range(1, stop):
            for chunk in range(self.chunks):
                for side in SIDES:
                    far = far_of(self.place, side)
                    shard = self.place + side * (LINE - step)

                    @pl.when(far <= step - 1)
                    def _():
                        self.copy(side, step, chunk, shard, self.place + side).wait_send()


def line_sems(chunks):
    return [pltpu.SemaphoreType.DMA((2, LINE - 1, chunks))] * 2


def fetch(pairs, sems):
    copies = [pltpu.make_async_copy(src, dst, sems.at[i]) for i, (src, dst) in enumerate(pairs)]
    for copy in copies:
        copy.start()
    return copies


IN_VMEM = pl.BlockSpec(memory_space=pltpu.VMEM)
IN_HBM = pl.BlockSpec(memory_space=pl.ANY)


def comm_params(number):
    return pltpu.CompilerParams(
        vmem_limit_bytes=VMEM_LIMIT, collective_id=number, has_side_effects=True
    )


def gather_norm_body(x_ref, gain_ref, buf, own, sem, send, recv):
    place = lax.axis_index("tensor")
    greet(place)
    rows = x_ref[...].astype(f32)
    rms = lax.rsqrt(jnp.mean(rows * rows, axis=1, keepdims=True) + eps)
    own[...] = (rows * rms * gain_ref[...]).astype(bf16)
    gather = Gather(place, buf, send, recv, 1, own)
    gather.send(1, 0)
    (kept,) = fetch([(own, buf.at[place])], sem)
    gather.arrive(1, 0)
    gather.send(2, 0)
    kept.wait()
    gather.arrive(2, 0)
    gather.drain(stop=LINE - 1)


def gather_norm(x, gain):
    rows, features = x.shape
    return pl.pallas_call(
        gather_norm_body,
        in_specs=[IN_VMEM, IN_VMEM],
        out_specs=IN_HBM,
        out_shape=jax.ShapeDtypeStruct((LINE, rows, features), bf16),
        scratch_shapes=[pltpu.VMEM((rows, features), bf16), pltpu.SemaphoreType.DMA((1,))]
        + line_sems(1),
        compiler_params=comm_params(0),
    )(x, gain[None, :])


def project_body(
    x_ref, w_ref, e_ref, a_ref, cos_ref, sin_ref, kept_ref, y_ref, l_ref,
    buf, yv, wv, xsem, wsem, ysem, send, recv,
):
    place = lax.axis_index("tensor")
    groups, _, width = y_ref.shape
    rows, rank = x_ref.shape[1], a_ref.shape[1]
    edge = (place == 0) | (place == LINE - 1)
    last = place ^ (LINE - 1)

    def passed(side):
        shard = place - side * (LINE - 2)
        index = 0 if side == 1 else 1
        return pltpu.make_async_remote_copy(
            src_ref=x_ref.at[shard],
            dst_ref=buf.at[shard],
            send_sem=send.at[index],
            recv_sem=recv.at[index],
            device_id={"tensor": place + side},
            device_id_type=MESH,
        )

    def came(side):
        index = 0 if side == 1 else 1
        return pltpu.make_async_remote_copy(
            src_ref=x_ref.at[last],
            dst_ref=buf.at[last],
            send_sem=send.at[index],
            recv_sem=recv.at[index],
            device_id={"tensor": place - side},
            device_id_type=MESH,
        )

    copies = []
    for slot in range(LINE):
        copy = pltpu.make_async_copy(x_ref.at[place ^ slot], buf.at[place ^ slot], xsem.at[slot])
        if slot < LINE - 1:
            copy.start()
        else:
            pl.when(jnp.logical_not(edge))(copy.start)
        copies.append(copy)
    (load,) = fetch([(w_ref.at[:, : groups * width], wv)], wsem)
    greet(place)
    for side in SIDES:
        pl.when(far_of(place, side) == LINE - 2)(passed(side).start)
    for copy in copies[:-1]:
        copy.wait()
    load.wait()
    outs = []
    for slot in range(LINE):
        shard = place ^ slot
        if slot == LINE - 1:
            pl.when(jnp.logical_not(edge))(copies[slot].wait)
            for side in SIDES:
                pl.when(far_of(place, side) == LINE - 1)(came(side).wait_recv)
            kept = pltpu.make_async_copy(buf.at[last], kept_ref.at[last], xsem.at[slot])
            pl.when(edge)(kept.start)
        mine = pl.ds(pl.multiple_of(shard * rows, rows), rows)
        low = nt(buf[shard], e_ref[:groups].reshape(groups * rank, -1)).astype(bf16)
        l_ref[mine] = low
        for g in range(groups):
            band = slice(g * width, (g + 1) * width)
            value = nn(buf[shard], wv[:, band]) + nn(low[:, g * rank : (g + 1) * rank], a_ref[g])
            if g < groups - 1:
                value = turn(value, cos_ref[mine], sin_ref[mine])
            yv[g, mine] = value.astype(bf16)
            out = pltpu.make_async_copy(yv.at[g, mine], y_ref.at[g, mine], ysem.at[slot, g])
            out.start()
            outs.append(out)
    pl.when(edge)(kept.wait)
    for out in outs:
        out.wait()
    for side in SIDES:
        pl.when(far_of(place, side) == LINE - 2)(passed(side).wait_send)


def project(x, weight, entries, exits, tables):
    _, rows, features = x.shape
    groups, rank, width = exits.shape
    return pl.pallas_call(
        project_body,
        in_specs=[IN_HBM, IN_HBM] + [IN_VMEM] * 4,
        out_specs=[IN_HBM, IN_HBM, IN_VMEM],
        out_shape=[
            jax.ShapeDtypeStruct((LINE, rows, features), bf16),
            jax.ShapeDtypeStruct((groups, LINE * rows, width), bf16),
            jax.ShapeDtypeStruct((LINE * rows, groups * rank), bf16),
        ],
        scratch_shapes=[
            pltpu.VMEM((LINE, rows, features), bf16),
            pltpu.VMEM((groups, LINE * rows, width), bf16),
            pltpu.VMEM((features, groups * width), bf16),
            pltpu.SemaphoreType.DMA((LINE,)),
            pltpu.SemaphoreType.DMA((1,)),
            pltpu.SemaphoreType.DMA((LINE, groups)),
            pltpu.SemaphoreType.DMA((2,)),
            pltpu.SemaphoreType.DMA((2,)),
        ],
        input_output_aliases={0: 0},
        compiler_params=comm_params(4),
    )(x, weight, entries, exits, *tables)


def middle_body(
    chunks, d_ref, w_ref, c_ref, before_ref, after_ref, a_ref, e_ref, x_ref, gain_ref, mid_ref, buf, cbuf, low_ref,
    part, held, own, wv, wsem, nsem, s_send, s_recv, g_send, g_recv, c_send, c_recv,
):
    place = lax.axis_index("tensor")
    width = d_ref.shape[1]
    load, own_cot = fetch([(w_ref.at[:, 3 * width :], wv), (c_ref, cbuf.at[place])], wsem)

    def neighbours(act):
        @pl.when(place > 0)
        def _():
            act(pltpu.make_async_copy(before_ref, cbuf.at[place - 1], wsem.at[2]))

        @pl.when(place < LINE - 1)
        def _():
            act(pltpu.make_async_copy(after_ref, cbuf.at[place + 1], wsem.at[3]))

    neighbours(lambda copy: copy.start())
    greet(place)
    load.wait()
    cots = Gather(place, cbuf, c_send, c_recv, chunks)
    rows = part.shape[1]
    summed = Sum(place, part, held, s_send, s_recv, chunks)
    gather = Gather(place, buf, g_send, g_recv, chunks, own)
    for slot in (3, 2, 1, 0):
        shard = place ^ slot
        mine = pl.ds(pl.multiple_of(shard * rows, rows), rows)
        d = d_ref[mine]
        low = nt(d, a_ref[...]).astype(bf16)
        low_ref[mine] = low
        part[shard] = (nt(d, wv[...]) + nn(low, e_ref[0])).astype(bf16)
        if slot == 3:
            summed.begin(1, 0)
    for chunk in range(chunks):
        for step in (1, 2, 3):
            if chunk or step > 1:
                summed.begin(step, chunk)
    neighbours(lambda copy: copy.wait())
    size = rows // chunks
    kept = []
    for chunk in range(chunks):
        summed.relay(2, chunk)
        summed.relay(3, chunk)
        cots.send(2, chunk)
        if chunk:
            cots.arrive(2, chunk - 1)
            cots.send(3, chunk - 1)
        summed.total(chunk, mid_ref)
        here = chunk_rows(chunk, size)
        value = mid_ref[here] + x_ref[here].astype(f32)
        mid_ref[here] = value
        rms = lax.rsqrt(jnp.mean(value * value, axis=1, keepdims=True) + eps)
        own[here] = (value * rms * gain_ref[...]).astype(bf16)
        copy = pltpu.make_async_copy(own.at[here], buf.at[place, here], nsem.at[chunk])
        copy.start()
        kept.append(copy)
        if chunk == chunks - 1:
            for before in range(chunks):
                gather.send(1, before)
    cots.arrive(2, chunks - 1)
    cots.send(3, chunks - 1)
    for step in (1, 2):
        for chunk in range(chunks):
            gather.arrive(step, chunk)
            gather.send(step + 1, chunk)
    for chunk in range(chunks):
        cots.arrive(3, chunk)
        gather.arrive(3, chunk)
    own_cot.wait()
    for copy in kept:
        copy.wait()
    summed.drain()
    gather.drain()
    cots.drain(start=2)


def middle_rows(attended, weight, cot, before, after, exits, finals, x, gain, chunks=4):
    rows, features = x.shape
    width = attended.shape[1]
    return pl.pallas_call(
        functools.partial(middle_body, chunks),
        in_specs=[IN_VMEM] + [IN_HBM] * 4 + [IN_VMEM] * 4,
        out_specs=[IN_VMEM, IN_HBM, IN_HBM, IN_VMEM],
        out_shape=[
            jax.ShapeDtypeStruct((rows, features), f32),
            jax.ShapeDtypeStruct((LINE, rows, features), bf16),
            jax.ShapeDtypeStruct((LINE, rows, features), bf16),
            jax.ShapeDtypeStruct((LINE * rows, exits.shape[0]), bf16),
        ],
        scratch_shapes=[
            pltpu.VMEM((LINE, rows, features), bf16),
            pltpu.VMEM((2, LINE - 1, rows, features), bf16),
            pltpu.VMEM((rows, features), bf16),
            pltpu.VMEM((features, width), bf16),
            pltpu.SemaphoreType.DMA((4,)),
            pltpu.SemaphoreType.DMA((chunks,)),
        ]
        + line_sems(chunks)
        + line_sems(chunks)
        + line_sems(chunks),
        compiler_params=comm_params(1),
    )(attended, weight, cot, before, after, exits, finals, x, gain[None, :])


def branch_body(
    b_ref, w_ref, e_ref, a_ref, p_ref, d_ref, lo_ref, y_ref, own_ref, right_ref, left_ref,
    final_ref, exit_ref,
    buf, part, held, wv, wsem, send, recv, s_send, s_recv,
):
    place = lax.axis_index("tensor")
    rows = b_ref.shape[0]
    load, parts = fetch([(w_ref.at[:, 3 * y_ref.shape[2] :], wv), (p_ref, part)], wsem)
    greet(place)
    buf[place] = b_ref[...]
    gather = Gather(place, buf, send, recv, 1)
    summed = Sum(place, part, held, s_send, s_recv, 1)
    gather.send(1, 0)
    parts.wait()
    summed.send(1, 0)
    load.wait()
    for slot in range(LINE):
        if slot:
            gather.arrive(slot, 0)
        if 0 < slot < LINE - 1:
            gather.send(slot + 1, 0)
        if slot == 1:
            summed.send(2, 0)
        if slot == 2:
            summed.add(3, 0)
            own_ref[...] = part[place]
            for out_ref, side in ((right_ref, 1), (left_ref, -1)):

                @pl.when(far_of(place, side) < LINE - 1)
                def _():
                    out_ref[...] = part[place + side]

                @pl.when(far_of(place, side) == LINE - 1)
                def _():
                    out_ref[...] = jnp.zeros_like(out_ref)

        shard = place ^ slot
        mine = pl.ds(pl.multiple_of(shard * rows, rows), rows)
        low = nt(buf[shard], e_ref[0])
        y_ref[0, mine] = (nn(buf[shard], wv[...]) + nn(low.astype(bf16), a_ref[...])).astype(bf16)
        final = nn(lo_ref[mine].astype(f32).T.astype(bf16), buf[shard])
        leave = nn(low.T.astype(bf16), d_ref[mine])
        final_ref[...] = final if slot == 0 else final_ref[...] + final
        exit_ref[...] = leave if slot == 0 else exit_ref[...] + leave
    gather.drain()
    summed.drain(LINE - 1)


def branch_back(branch, weight, finals, exits, parts, attended, low_out):
    rows, features = branch.shape
    rank, width = exits.shape
    return pl.pallas_call(
        branch_body,
        in_specs=[IN_VMEM, IN_HBM, IN_VMEM, IN_VMEM, IN_HBM, IN_VMEM, IN_VMEM],
        out_specs=[IN_VMEM] * 6,
        out_shape=[jax.ShapeDtypeStruct((1, LINE * rows, width), bf16)]
        + [jax.ShapeDtypeStruct((rows, features), bf16)] * 3
        + [
            jax.ShapeDtypeStruct((rank, features), f32),
            jax.ShapeDtypeStruct((rank, width), f32),
        ],
        scratch_shapes=[
            pltpu.VMEM((LINE, rows, features), bf16),
            pltpu.VMEM((LINE, rows, features), bf16),
            pltpu.VMEM((2, LINE - 1, rows, features), bf16),
            pltpu.VMEM((features, width), bf16),
            pltpu.SemaphoreType.DMA((2,)),
        ]
        + line_sems(1)
        + line_sems(1),
        compiler_params=comm_params(2),
    )(branch, weight, finals, exits, parts, attended, low_out)


def tokens_body(
    chunks, d_ref, w_ref, a_ref, e_ref, x_ref, gain_ref, mid_ref, n_ref, lone_ref, final_ref, exit_ref,
    out_ref, model_ref, head_ref,
    part, held, acc, dv, wv, midv, nv, low, block, extra, wsem, send, recv, x_send, x_recv, t_send, t_recv, h_send, h_recv,
):
    place = lax.axis_index("tensor")
    tree = lax.axis_index("dp")
    trees = Trees(tree, model_ref, t_send, t_recv)
    heads = Trees(tree, head_ref, h_send, h_recv)
    groups, total, width = d_ref.shape
    rank = a_ref.shape[1]
    loads = fetch(
        [(d_ref, dv), (w_ref.at[:, : groups * width], wv), (n_ref, nv), (mid_ref, midv)],
        wsem,
    )
    block[...] = jnp.zeros_like(block)
    for g in range(groups):
        block[g * rank : (g + 1) * rank, g * width : (g + 1) * width] = a_ref[g]
    greet(place, trees.partners)
    for load in loads[:2]:
        load.wait()
    rows = part.shape[1]
    summed = Sum(place, part, held, send, recv, chunks)
    gather = Gather(place, extra, x_send, x_recv, 1)
    entry = e_ref[:groups].reshape(groups * rank, -1)

    def rows_of(slot):
        shard = place ^ slot
        mine = pl.ds(pl.multiple_of(shard * rows, rows), rows)
        return shard, mine, jnp.concatenate([dv[g, mine] for g in range(groups)], axis=1)

    def lower(slot):
        _, mine, d = rows_of(slot)
        low[mine] = nt(d, block[...]).astype(bf16)

    def partial(slot):
        shard, mine, d = rows_of(slot)
        part[shard] = (nt(d, wv[...]) + nn(low[mine], entry)).astype(bf16)

    lower(3)
    partial(3)
    summed.begin(1, 0)
    summed.begin(1, 1)
    for slot in (2, 1, 0):
        lower(slot)
    for load in loads[2:]:
        load.wait()

    def turned(value):
        return value.astype(f32).T.astype(bf16)

    joined = nn(turned(low[...]), nv[...].reshape(total, -1))
    extra[place] = jnp.concatenate([joined, final_ref[...]], axis=0).astype(bf16)
    gather.send(1, 0)
    for chunk in range(2, chunks):
        summed.begin(1, chunk)
    for slot in (2, 1, 0):
        partial(slot)
    for step in (2, 3):
        for chunk in range(chunks):
            summed.begin(step, chunk)
    summed.relay(2, 0)
    summed.relay(2, 1)
    gather.arrive(1, 0)
    gather.send(2, 0)
    summed.relay(2, 2)
    low_one = turned(lone_ref[...])
    for g in range(groups):
        band = slice(g * rank, (g + 1) * rank)
        head_ref[tree, band] = nn(low_one[band], dv[g]).astype(bf16)
    head_ref[tree, groups * rank :] = exit_ref[...].astype(bf16)
    heads.send(0)
    summed.relay(2, 3)
    gather.arrive(2, 0)
    gather.send(3, 0)
    heads.advance(1)
    summed.relay(3, 0)
    gather.arrive(3, 0)
    model_ref[tree] = functools.reduce(
        jnp.add, [extra[shard].astype(f32) for shard in range(LINE)]
    ).astype(bf16)
    trees.send(0)
    heads.advance(2)
    summed.relay(3, 1)
    trees.advance(1)
    summed.relay(3, 2)
    summed.relay(3, 3)
    trees.advance(2)
    size = rows // chunks

    def finish(chunk):
        finish_tokens(summed, chunk, size, acc, x_ref, gain_ref, midv, out_ref)

    finish(0)
    finish(1)
    for number in range(3, trees.rounds):
        trees.advance(number)
        heads.advance(number)
    finish(2)
    finish(3)
    for blocks in (trees, heads):
        blocks.arrive(blocks.rounds - 1)
        blocks.drain()
    summed.drain()
    gather.drain()


class Trees:
    def __init__(self, tree, ref, send, recv):
        self.tree, self.ref, self.sems = tree, ref, (send, recv)
        self.rounds = ref.shape[0].bit_length() - 1
        self.partners = [self.partner(number) for number in range(self.rounds)]

    def partner(self, number):
        size = 1 << number
        return self.tree + size - 2 * size * ((self.tree // size) % 2)

    def copy(self, number, owner):
        size = 1 << number
        here = pl.ds((owner // size) * size, size)
        return pltpu.make_async_remote_copy(
            src_ref=self.ref.at[here],
            dst_ref=self.ref.at[here],
            send_sem=self.sems[0].at[number],
            recv_sem=self.sems[1].at[number],
            device_id={"dp": self.partner(number)},
            device_id_type=MESH,
        )

    def send(self, number):
        self.copy(number, self.tree).start()

    def arrive(self, number):
        self.copy(number, self.partner(number)).wait_recv()

    def advance(self, number):
        if number < self.rounds:
            self.arrive(number - 1)
            self.send(number)

    def drain(self):
        for number in range(self.rounds):
            self.copy(number, self.tree).wait_send()


def finish_tokens(summed, chunk, size, acc, x_ref, gain_ref, mid_ref, out_ref):
    summed.total(chunk, acc)
    here = chunk_rows(chunk, size)
    rows = x_ref[here].astype(f32)
    rms = lax.rsqrt(jnp.mean(rows * rows, axis=1, keepdims=True) + eps)
    scaled = acc[here] * gain_ref[...]
    mean = jnp.mean(scaled * rows, axis=1, keepdims=True)
    out_ref[here] = (mid_ref[here] + rms * (scaled - rows * (rms * rms) * mean)).astype(bf16)


def tokens_back(
    head_grads, weight, exits, entries, x, gain, grad_middle, normed, low_one, final_grads, exit_grads
):
    chunks = LINE
    rows, features = x.shape
    groups, total, width = head_grads.shape
    rank = exits.shape[1]
    deep = (groups + 1) * rank
    trees = lax.axis_size("dp")
    sems = pltpu.SemaphoreType.DMA((trees.bit_length() - 1,))
    return pl.pallas_call(
        functools.partial(tokens_body, chunks),
        in_specs=[IN_HBM, IN_HBM] + [IN_VMEM] * 4 + [IN_HBM] * 2 + [IN_VMEM] * 3,
        out_specs=[IN_VMEM] * 3,
        out_shape=[
            jax.ShapeDtypeStruct((rows, features), bf16),
            jax.ShapeDtypeStruct((trees, deep, features), bf16),
            jax.ShapeDtypeStruct((trees, deep, width), bf16),
        ],
        scratch_shapes=[
            pltpu.VMEM((LINE, rows, features), bf16),
            pltpu.VMEM((2, LINE - 1, rows, features), bf16),
            pltpu.VMEM((rows, features), f32),
            pltpu.VMEM((groups, total, width), bf16),
            pltpu.VMEM((features, groups * width), bf16),
            pltpu.VMEM((rows, features), f32),
            pltpu.VMEM((LINE, rows, features), bf16),
            pltpu.VMEM((total, groups * rank), bf16),
            pltpu.VMEM((groups * rank, groups * width), bf16),
            pltpu.VMEM((LINE, deep, features), bf16),
            pltpu.SemaphoreType.DMA((4,)),
        ]
        + line_sems(chunks)
        + line_sems(1)
        + [sems] * 4,
        compiler_params=comm_params(3),
    )(
        head_grads, weight, exits, entries, x, gain[None, :], grad_middle, normed,
        low_one, final_grads, exit_grads,
    )


def tree_tiles(seg, rows, parent_row):
    trunk = TRUNK * seg
    leaves = trunk + BRANCHES * seg
    key = lax.broadcasted_iota(jnp.int32, (QT, QT), 0)
    query = lax.broadcasted_iota(jnp.int32, (QT, QT), 1)
    causal = key <= query
    own = causal & (key // seg == query // seg)
    tiles = []
    for start in range(0, trunk, QT):
        pieces = [(0, start, None)] if start else []
        tiles.append((start, pieces + [(start, QT, causal)]))
    tiles.append((trunk, [(0, trunk, None), (trunk, QT, own)]))
    branch = lax.broadcasted_iota(jnp.int32, (BRANCHES * seg, QT), 0) // seg
    for start in range(leaves, rows, QT):
        mine = branch == parent_row[:, start - leaves : start - leaves + QT]
        tiles.append(
            (start, [(0, trunk, None), (trunk, BRANCHES * seg, mine), (start, QT, own)])
        )
    return tiles


def attend_body(seg, q_ref, k_ref, v_ref, p_ref, o_ref, lse_ref):
    rows = q_ref.shape[1]
    value_t = v_ref[0].T
    lane = lax.broadcasted_iota(jnp.int32, (QT, 2 * HEAD_DIM), 1)
    for start, pieces in tree_tiles(seg, rows, p_ref[...]):
        query = q_ref[0, start : start + QT] * bf16(HEAD_DIM**-0.5)
        outs = []
        for h in range(2):
            own_query = jnp.where(lane // HEAD_DIM == h, query, bf16(0))
            scores = []
            for k0, count, mask in pieces:
                s = nt(k_ref[0, k0 : k0 + count], own_query)
                scores.append(s if mask is None else jnp.where(mask, s, -1e30))
            top = functools.reduce(
                jnp.maximum, [jnp.max(s, axis=0, keepdims=True) for s in scores]
            )
            summed, out = 0.0, 0.0
            for (k0, count, _), s in zip(pieces, scores):
                weights = jnp.exp(s - top)
                summed += jnp.sum(weights, axis=0, keepdims=True)
                out += nn(
                    value_t[h * HEAD_DIM : (h + 1) * HEAD_DIM, k0 : k0 + count],
                    weights.astype(bf16),
                )
            outs.append(out / summed)
            lse_ref[0, h : h + 1, start : start + QT] = top + jnp.log(summed)
        o_ref[0, start : start + QT] = jnp.concatenate(outs, axis=0).T.astype(bf16)


def attend(qkv, leaf_parent, seg):
    _, rows, width = qkv.shape
    pairs = width // (2 * HEAD_DIM)
    return pl.pallas_call(
        functools.partial(attend_body, seg),
        grid=(pairs,),
        in_specs=[
            pl.BlockSpec((1, rows, 2 * HEAD_DIM), lambda j, g=g: (g, 0, j)) for g in range(3)
        ]
        + [pl.BlockSpec(leaf_parent.shape, lambda j: (0, 0))],
        out_specs=[
            pl.BlockSpec((1, rows, 2 * HEAD_DIM), lambda j: (0, 0, j)),
            pl.BlockSpec((1, 2, rows), lambda j: (j, 0, 0)),
        ],
        out_shape=[
            jax.ShapeDtypeStruct((1, rows, width), bf16),
            jax.ShapeDtypeStruct((pairs, 2, rows), f32),
        ],
        compiler_params=pltpu.CompilerParams(vmem_limit_bytes=VMEM_LIMIT),
        cost_estimate=pl.CostEstimate(
            flops=8 * rows * rows * width, bytes_accessed=8 * rows * width, transcendentals=0
        ),
    )(qkv, qkv, qkv, leaf_parent)


def attend_back_body(
    seg, q_ref, k_ref, v_ref, o_ref, g_ref, lse_ref, p_ref, cos_ref, sin_ref, d_ref, dq_t, dk, dv
):
    rows = q_ref.shape[1]
    scale = bf16(HEAD_DIM**-0.5)
    key_t = k_ref[0].T
    weighed_t = (g_ref[0].astype(f32) * o_ref[0].astype(f32)).T
    lane = lax.broadcasted_iota(jnp.int32, (QT, 2 * HEAD_DIM), 1)
    dk[...] = jnp.zeros_like(dk)
    dv[...] = jnp.zeros_like(dv)
    for start, pieces in tree_tiles(seg, rows, p_ref[...]):
        query = q_ref[0, start : start + QT] * scale
        grad = g_ref[0, start : start + QT]
        for h in range(2):
            mine = lane // HEAD_DIM == h
            own_query = jnp.where(mine, query, bf16(0))
            own_grad = jnp.where(mine, grad, bf16(0))
            band = slice(h * HEAD_DIM, (h + 1) * HEAD_DIM)
            delta = jnp.sum(weighed_t[band, start : start + QT], axis=0, keepdims=True)
            lse = lse_ref[0, h : h + 1, start : start + QT]
            grad_q = 0.0
            for k0, count, mask in pieces:
                probs = jnp.exp(nt(k_ref[0, k0 : k0 + count], own_query) - lse)
                if mask is not None:
                    probs = jnp.where(mask, probs, 0.0)
                grad_probs = nt(v_ref[0, k0 : k0 + count], own_grad)
                grad_scores = (probs * (grad_probs - delta)).astype(bf16)
                dk[k0 : k0 + count] += nn(grad_scores, own_query)
                dv[k0 : k0 + count] += nn(probs.astype(bf16), own_grad)
                grad_q += nn(key_t[band, k0 : k0 + count], grad_scores)
            dq_t[band, start : start + QT] = grad_q
    cosine, sine = cos_ref[...], -sin_ref[...]
    d_ref[0] = turn(dq_t[...].T * HEAD_DIM**-0.5, cosine, sine).astype(bf16)
    d_ref[1] = turn(dk[...], cosine, sine).astype(bf16)
    d_ref[2] = dv[...].astype(bf16)


def attend_back(qkv, attended, grad, lse, leaf_parent, tables, seg):
    _, rows, width = qkv.shape
    pairs = width // (2 * HEAD_DIM)
    pair = 2 * HEAD_DIM
    return pl.pallas_call(
        functools.partial(attend_back_body, seg),
        grid=(pairs,),
        in_specs=[pl.BlockSpec((1, rows, pair), lambda j, g=g: (g, 0, j)) for g in range(3)]
        + [
            pl.BlockSpec((1, rows, pair), lambda j: (0, 0, j)),
            pl.BlockSpec((1, rows, pair), lambda j: (0, 0, j)),
            pl.BlockSpec((1, 2, rows), lambda j: (j, 0, 0)),
            pl.BlockSpec(leaf_parent.shape, lambda j: (0, 0)),
            pl.BlockSpec((rows, pair), lambda j: (0, 0)),
            pl.BlockSpec((rows, pair), lambda j: (0, 0)),
        ],
        out_specs=pl.BlockSpec((3, rows, pair), lambda j: (0, 0, j)),
        out_shape=jax.ShapeDtypeStruct((3, rows, width), bf16),
        scratch_shapes=[
            pltpu.VMEM((pair, rows), f32),
            pltpu.VMEM((rows, pair), f32),
            pltpu.VMEM((rows, pair), f32),
        ],
        compiler_params=pltpu.CompilerParams(vmem_limit_bytes=VMEM_LIMIT),
        cost_estimate=pl.CostEstimate(
            flops=20 * rows * rows * width, bytes_accessed=16 * rows * width, transcendentals=0
        ),
    )(qkv, qkv, qkv, attended, grad, lse, leaf_parent, *tables)


def feed_body(
    rank, tile, chunks,
    n_ref, c_ref, wg_ref, wu_ref, wd_ref, mid_ref,
    xu_in, xd_in, e_in, f_in, gain_ref,
    grad_ref, low_grad_ref, res_ref, unit_ref, model_ref,
    x_ref, e_ref, f_ref, midv, nbuf, cbuf, wbuf, low, low_t, acc_res, acc_back, acc_low, part, held, resv,
    nsem, csem, wsem, rsem, msem, send, recv,
):
    place = lax.axis_index("tensor")
    units = unit_ref.shape[1]
    tiles = units // tile
    summed = Sum(place, part, held, send, recv, chunks)

    def load_rows(order, act):
        into = order % 2
        shard = place ^ (LINE - 1 - order)
        act(pltpu.make_async_copy(n_ref.at[shard], nbuf.at[into], nsem.at[into]))
        act(pltpu.make_async_copy(c_ref.at[shard], cbuf.at[into], csem.at[into]))

    def load_weights(index, into, act):
        columns = pl.ds(pl.multiple_of(index * tile, tile), tile)
        for k, w_ref in enumerate((wg_ref, wu_ref, wd_ref)):
            act(pltpu.make_async_copy(w_ref.at[:, columns], wbuf.at[into, k], wsem.at[into, k]))

    def start(copy):
        copy.start()

    def wait(copy):
        copy.wait()

    load_rows(jnp.int32(0), start)
    load_weights(0, 0, start)
    (load_middle,) = fetch([(mid_ref, midv)], msem)
    for padded in (x_ref, e_ref, f_ref):
        padded[...] = jnp.zeros_like(padded)
    x_ref[0, :rank] = xu_in[0]
    x_ref[1, rank : 2 * rank] = xu_in[1]
    x_ref[2, 2 * rank :] = xd_in[...]
    e_ref[: 2 * rank] = e_in[3:].reshape(2 * rank, -1)
    f_ref[2 * rank :] = f_in[1]
    unit_ref[...] = jnp.zeros_like(unit_ref)
    model_ref[...] = jnp.zeros_like(model_ref)
    greet(place)

    def one_shard(order, carry):
        into = order % 2
        shard = place ^ (LINE - 1 - order)
        load_rows(order, wait)

        @pl.when(order < LINE - 1)
        def _():
            load_rows(order + 1, start)

        first = nt(nbuf[into], e_ref[...]) + nt(cbuf[into], f_ref[...])
        low[...] = first.astype(bf16)
        low_t[...] = first.T.astype(bf16)
        acc_res[...] = jnp.zeros_like(acc_res)
        acc_back[...] = jnp.zeros_like(acc_back)
        acc_low[...] = jnp.zeros_like(acc_low)

        def one_tile(index, carry):
            stage = order * tiles + index
            at = stage % 2
            load_weights(index, at, wait)

            @pl.when(stage < LINE * tiles - 1)
            def _():
                load_weights((index + 1) % tiles, 1 - at, start)

            columns = pl.ds(pl.multiple_of(index * tile, tile), tile)
            x_gate, x_rise, x_fall = x_ref[0, :, columns], x_ref[1, :, columns], x_ref[2, :, columns]
            gate = nn(nbuf[into], wbuf[at, 0]) + nn(low[...], x_gate)
            rise = nn(nbuf[into], wbuf[at, 1]) + nn(low[...], x_rise)
            grad_hidden = nn(cbuf[into], wbuf[at, 2]) + nn(low[...], x_fall)
            sigmoid = jax.nn.sigmoid(gate)
            silu = gate * sigmoid
            hidden = (silu * rise).astype(bf16)
            grad_gate = (grad_hidden * rise * sigmoid * (1.0 + gate * (1.0 - sigmoid))).astype(bf16)
            grad_rise = (grad_hidden * silu).astype(bf16)
            acc_back[...] += nt(grad_gate, wbuf[at, 0]) + nt(grad_rise, wbuf[at, 1])
            acc_res[...] += nt(hidden, wbuf[at, 2])
            acc_low[...] += nt(grad_gate, x_gate) + nt(grad_rise, x_rise) + nt(hidden, x_fall)
            unit_ref[:rank, columns] += nn(low_t[:rank], grad_gate)
            unit_ref[rank : 2 * rank, columns] += nn(low_t[rank : 2 * rank], grad_rise)
            unit_ref[2 * rank :, columns] += nn(low_t[2 * rank : 3 * rank], hidden)
            return carry

        lax.fori_loop(0, tiles, one_tile, 0)
        joined = acc_low[...].astype(bf16)
        joined_t = acc_low[...].T.astype(bf16)
        part[shard] = (acc_back[...] + nn(joined, e_ref[...])).astype(bf16)

        @pl.when(order > 0)
        def _():
            pltpu.make_async_copy(resv, res_ref.at[shard], rsem.at[0]).wait()

        resv[...] = (acc_res[...] + nn(joined, f_ref[...])).astype(bf16)
        pltpu.make_async_copy(resv, res_ref.at[shard], rsem.at[0]).start()
        for step in (1, 2, 3):

            @pl.when(order == step - 1)
            def _():
                for chunk in range(chunks):
                    summed.send(step, chunk)

        model_ref[: 2 * rank] += nn(joined_t[: 2 * rank], nbuf[into])
        model_ref[2 * rank :] += nn(joined_t[2 * rank : 3 * rank], cbuf[into])
        return carry

    lax.fori_loop(0, LINE, one_shard, 0)
    size = part.shape[1] // chunks
    last = (LINE - 1) % 2
    load_middle.wait()
    for chunk in range(chunks):
        summed.total(chunk, acc_back)
        here = chunk_rows(chunk, size)
        middle = midv[here]
        rms = lax.rsqrt(jnp.mean(middle * middle, axis=1, keepdims=True) + eps)
        scaled = acc_back[here] * gain_ref[...]
        mean = jnp.mean(scaled * middle, axis=1, keepdims=True)
        grad = cbuf[last, here].astype(f32) + rms * (scaled - middle * (rms * rms) * mean)
        grad_ref[here] = grad
        low_grad_ref[here] = grad.astype(bf16)
    pltpu.make_async_copy(resv, res_ref.at[place], rsem.at[0]).wait()
    summed.drain()


def feed(normed, cots, weights, middle, units_exit, fall_entry, entries, finals, gain, tile=512, chunks=4):
    _, rows, features = normed.shape
    units = weights[0].shape[1]
    rank = fall_entry.shape[0]
    return pl.pallas_call(
        functools.partial(feed_body, rank, tile, chunks),
        in_specs=[IN_HBM] * 6 + [IN_VMEM] * 5,
        out_specs=[IN_VMEM, IN_VMEM, IN_HBM, IN_VMEM, IN_VMEM],
        out_shape=[
            jax.ShapeDtypeStruct((rows, features), f32),
            jax.ShapeDtypeStruct((rows, features), bf16),
            jax.ShapeDtypeStruct((LINE, rows, features), bf16),
            jax.ShapeDtypeStruct((3 * rank, units), f32),
            jax.ShapeDtypeStruct((3 * rank, features), f32),
        ],
        scratch_shapes=[
            pltpu.VMEM((3, 3 * rank, units), bf16),
            pltpu.VMEM((3 * rank, features), bf16),
            pltpu.VMEM((3 * rank, features), bf16),
            pltpu.VMEM((rows, features), f32),
            pltpu.VMEM((2, rows, features), bf16),
            pltpu.VMEM((2, rows, features), bf16),
            pltpu.VMEM((2, 3, features, tile), bf16),
            pltpu.VMEM((rows, 3 * rank), bf16),
            pltpu.VMEM((3 * rank, rows), bf16),
            pltpu.VMEM((rows, features), f32),
            pltpu.VMEM((rows, features), f32),
            pltpu.VMEM((rows, 3 * rank), f32),
            pltpu.VMEM((LINE, rows, features), bf16),
            pltpu.VMEM((2, LINE - 1, rows, features), bf16),
            pltpu.VMEM((rows, features), bf16),
            pltpu.SemaphoreType.DMA((2,)),
            pltpu.SemaphoreType.DMA((2,)),
            pltpu.SemaphoreType.DMA((2, 3)),
            pltpu.SemaphoreType.DMA((1,)),
            pltpu.SemaphoreType.DMA((1,)),
        ]
        + line_sems(chunks),
        compiler_params=comm_params(5),
    )(normed, cots, *weights, middle, units_exit, fall_entry, entries, finals, gain[None, :])


def pick_body(pick_ref, *refs):
    count = len(refs) // 2
    for source, target in zip(refs[:count], refs[count:]):
        target[...] = source[...].reshape(target.shape)


def picked(pick, arrays):
    shapes = [a.shape[:1] + a.shape[2:] for a in arrays]
    return pl.pallas_call(
        pick_body,
        grid_spec=pltpu.PrefetchScalarGridSpec(
            num_scalar_prefetch=1,
            grid=(1,),
            in_specs=[
                pl.BlockSpec(a.shape[:1] + (1,) + a.shape[2:], lambda i, p: (0, p[0], 0, 0)) for a in arrays
            ],
            out_specs=[pl.BlockSpec(shape, lambda i, p: (0, 0, 0)) for shape in shapes],
        ),
        out_shape=[jax.ShapeDtypeStruct(shape, bf16) for shape in shapes],
    )(pick, *arrays)


def per_tree(block):
    return lax.all_gather(block, "dp", axis=0, tiled=False)


def combine_body(rank, pick_ref, early, model, late, head, entry_ref, final_ref, unit_ref, down_ref, exit_ref, out_ref):
    for ref in (entry_ref, final_ref, unit_ref, down_ref, exit_ref, out_ref):
        ref[...] = jnp.zeros_like(ref)

    def one_tree(tree, carry):
        pick = pick_ref[tree]

        def block(ref, index):
            return ref[tree, index * rank : (index + 1) * rank].astype(f32)

        for k in range(3):
            entry_ref[k, pick] += block(late, k)
            exit_ref[k, pick] += block(head, k)
        final_ref[0, pick] += block(late, 3)
        out_ref[pick] += block(head, 3)
        for k in range(2):
            entry_ref[3 + k, pick] += block(model, k)
            unit_ref[k, pick] += block(early, k)
        final_ref[1, pick] += block(model, 2)
        down_ref[pick] += block(early, 2)
        return carry

    lax.fori_loop(0, early.shape[0], one_tree, 0)


def combine(picks, early, model, late, head, adapters, steps=4):
    trees, _, features = early.shape
    rank = late.shape[1] // 4
    width = head.shape[2]
    wide, narrow = features // steps, width // steps

    def taken(array, tile):
        return pl.BlockSpec((trees, array.shape[1], tile), lambda i, p: (0, 0, i))

    def given(lead, tile):
        shape = lead + (adapters, rank, tile)
        return pl.BlockSpec(shape, lambda i, p: (0,) * (len(shape) - 1) + (i,))

    def shape(lead, full):
        return jax.ShapeDtypeStruct(lead + (adapters, rank, full), f32)

    return pl.pallas_call(
        functools.partial(combine_body, rank),
        grid_spec=pltpu.PrefetchScalarGridSpec(
            num_scalar_prefetch=1,
            grid=(steps,),
            in_specs=[taken(early, wide), taken(model, wide), taken(late, wide), taken(head, narrow)],
            out_specs=[
                given((5,), wide),
                given((2,), wide),
                given((2,), wide),
                given((), wide),
                given((3,), narrow),
                given((), narrow),
            ],
        ),
        out_shape=[
            shape((5,), features),
            shape((2,), features),
            shape((2,), features),
            shape((), features),
            shape((3,), width),
            shape((), width),
        ],
        compiler_params=pltpu.CompilerParams(vmem_limit_bytes=VMEM_LIMIT),
    )(picks, early, model, late, head)


def local(
    tokens,
    cotangent,
    attention_gain,
    feed_gain,
    query_weight,
    key_weight,
    value_weight,
    output_weight,
    gate_weight,
    up_weight,
    down_weight,
    entry_maps,
    head_exits,
    unit_exits,
    output_entry,
    down_entry,
    final_exits,
    parents,
    adapter_pick,
):
    pick = adapter_pick[0]
    adapters, rank = entry_maps.shape[1], entry_maps.shape[3]
    local_rows = tokens.shape[0]
    total = local_rows * lax.axis_size("tensor")
    blocks = parents.shape[1]
    seg = total // blocks
    tables = rope_tables(blocks, seg)
    leaf_parent = (jnp.repeat(parents[0, TRUNK + BRANCHES :], seg) - TRUNK)[None, :]
    gain_one = attention_gain.astype(f32)
    gain_two = feed_gain.astype(f32)

    w_heads = lax.all_gather(
        jnp.concatenate([query_weight, key_weight, value_weight, output_weight], axis=1),
        "dp",
        axis=0,
        tiled=True,
    )

    w_units = [
        lax.all_gather(w, "dp", axis=0, tiled=True) for w in (gate_weight, up_weight, down_weight)
    ]
    entries, heads_exit, units_exit, out_entry, fall_entry, finals = picked(
        adapter_pick,
        (
            jnp.swapaxes(entry_maps, 2, 3),
            head_exits,
            unit_exits,
            jnp.swapaxes(output_entry, 1, 2)[None],
            jnp.swapaxes(down_entry, 1, 2)[None],
            final_exits,
        ),
    )
    out_entry, fall_entry = out_entry[0], fall_entry[0]

    most_one = gather_norm(tokens, gain_one)
    full_one, qkv, low_one = project(most_one, w_heads, entries, heads_exit, tables)
    cot_tied, qkv = lax.optimization_barrier((cotangent, qkv))
    before = permute(cot_tied, [(0, 1), (1, 2), (2, 3)])
    after = permute(cot_tied, [(3, 2), (2, 1), (1, 0)])
    attended, lse = attend(qkv, leaf_parent, seg)
    middle, full_two, full_cot, adapt_o = middle_rows(
        attended[0], w_heads, cotangent, before, after, out_entry, finals, tokens, gain_two
    )

    grad_middle, branch, res_parts, unit_grads, model_grads = feed(
        full_two, full_cot, w_units, middle, units_exit, fall_entry, entries, finals, gain_two
    )
    early = jnp.concatenate(
        [unit_grads.astype(bf16), jnp.full((rank, unit_grads.shape[1]), pick).astype(bf16)]
    )
    model_low = model_grads.astype(bf16)
    branch, early, model_low = lax.optimization_barrier((branch, early, model_low))
    early = per_tree(early)
    model_sum = lax.psum(model_low, "tensor")

    grad_attended, res_own, res_right, res_left, final_grads, exit_grads = branch_back(
        branch, w_heads, finals, out_entry, res_parts, attended[0], adapt_o
    )
    grad_attended, res_right, res_left = lax.optimization_barrier((grad_attended, res_right, res_left))
    from_left = permute(res_right, [(0, 1), (1, 2), (2, 3)])
    from_right = permute(res_left, [(3, 2), (2, 1), (1, 0)])
    head_grads = attend_back(qkv, attended, grad_attended, lse, leaf_parent, tables, seg)
    head_grads, model_sum, from_left, from_right = lax.optimization_barrier(
        (head_grads, model_sum, from_left, from_right)
    )
    model_all = per_tree(model_sum)
    grad_tokens, late_model, late_head = tokens_back(
        head_grads, w_heads, heads_exit, entries, tokens, gain_one, grad_middle,
        full_one, low_one, final_grads, exit_grads,
    )
    result = (
        middle
        + res_own.astype(f32)
        + from_left.astype(f32)
        + from_right.astype(f32)
    ).astype(bf16)

    picks = early[:, 3 * rank, 0].astype(jnp.int32)
    grad_entries, grad_finals, grad_units, grad_down, grad_heads, grad_output = combine(
        picks, early, model_all, late_model, late_head, adapters
    )
    grad_entries = grad_entries.swapaxes(2, 3)
    grad_output = grad_output.swapaxes(1, 2)
    grad_down = grad_down.swapaxes(1, 2)
    return (
        result,
        grad_tokens,
        grad_entries,
        grad_heads,
        grad_units,
        grad_output,
        grad_down,
        grad_finals,
    )


def solution(mesh):
    in_specs = (
        P(("dp", "tensor"), None),
        P(("dp", "tensor"), None),
        P(),
        P(),
        P("dp", "tensor"),
        P("dp", "tensor"),
        P("dp", "tensor"),
        P("dp", "tensor"),
        P("dp", "tensor"),
        P("dp", "tensor"),
        P("dp", "tensor"),
        P(),
        P(None, None, None, "tensor"),
        P(None, None, None, "tensor"),
        P(None, "tensor", None),
        P(None, "tensor", None),
        P(),
        P("dp", None),
        P("dp"),
    )
    out_specs = (
        P(("dp", "tensor"), None),
        P(("dp", "tensor"), None),
        P(),
        P(None, None, None, "tensor"),
        P(None, None, None, "tensor"),
        P(None, "tensor", None),
        P(None, "tensor", None),
        P(),
    )
    return jax.shard_map(local, mesh=mesh, in_specs=in_specs, out_specs=out_specs, check_vma=False)
```

```python
import functools

import jax
import jax.numpy as jnp
import numpy as np
from jax import lax
from jax.experimental import pallas as pl
from jax.experimental.pallas import tpu as pltpu
from jax.sharding import PartitionSpec as P

HEAD_DIM = 64
TRUNK, BRANCHES = 8, 4
QT = 256
VMEM_LIMIT = 60 * 1024 * 1024
LINE = 4
MESH = pl.DeviceIdType.MESH

eps = 1e-05
theta = 130000.0
bf16, f32 = jnp.bfloat16, jnp.float32


def nn(left, right):
    return jnp.dot(left, right, preferred_element_type=f32)


def nt(left, right):
    return lax.dot_general(left, right, (((1,), (1,)), ((), ())), preferred_element_type=f32)


def tn(left, right):
    return lax.dot_general(left, right, (((0,), (0,)), ((), ())), preferred_element_type=f32)


def permute(value, pairs):
    return lax.ppermute(value, "tensor", pairs)


def rope_tables(blocks, seg):
    depth = np.minimum(np.arange(blocks), TRUNK)
    depth[TRUNK + BRANCHES :] = TRUNK + 1
    position = (np.repeat(depth, seg) * seg + np.arange(blocks * seg) % seg).astype(np.float32)
    half = HEAD_DIM // 2
    freq = (np.float32(theta) ** (-np.arange(half, dtype=np.float32) / half)).astype(np.float32)
    angle = (position[:, None] * freq[None, :]).astype(np.float32)
    cosine = np.tile(np.cos(angle), (1, 4)).astype(np.float32)
    sine = np.sin(angle).astype(np.float32)
    sine = np.concatenate([-sine, sine, -sine, sine], axis=1)
    return jnp.asarray(cosine), jnp.asarray(sine)


def turn(values, cosine, sine):
    width = values.shape[1]
    reps = width // cosine.shape[1]
    if reps > 1:
        cosine = jnp.concatenate([cosine] * reps, axis=1)
        sine = jnp.concatenate([sine] * reps, axis=1)
    lane = lax.broadcasted_iota(jnp.int32, values.shape, 1)
    half = HEAD_DIM // 2
    other = jnp.where(
        lane % HEAD_DIM < half, pltpu.roll(values, width - half, 1), pltpu.roll(values, half, 1)
    )
    return values * cosine + other * sine


SIDES = (1, -1)


def far_of(place, side):
    return place if side == 1 else LINE - 1 - place


def greet(place, partners=()):
    barrier = pltpu.get_barrier_semaphore()
    for partner in partners:
        pl.semaphore_signal(barrier, inc=1, device_id={"dp": partner}, device_id_type=MESH)
    for side in SIDES:

        @pl.when(far_of(place, side) < LINE - 1)
        def _():
            pl.semaphore_signal(
                barrier, inc=1, device_id={"tensor": place + side}, device_id_type=MESH
            )

    edge = (place == 0) | (place == LINE - 1)

    @pl.when(edge)
    def _():
        pl.semaphore_wait(barrier, 1 + len(partners))

    @pl.when(jnp.logical_not(edge))
    def _():
        pl.semaphore_wait(barrier, 2 + len(partners))


def chunk_rows(chunk, rows):
    return pl.ds(chunk * rows, rows)


class Gather:
    def __init__(self, place, buf, send, recv, chunks, own=None, beside=None):
        self.place, self.buf, self.sems, self.chunks = place, buf, (send, recv), chunks
        self.rows = buf.shape[1] // chunks
        self.own, self.beside = own, beside

    def copy(self, side, step, chunk, shard, target):
        rows = chunk_rows(chunk, self.rows)
        where = self.buf.at[shard, rows]
        index = 0 if side == 1 else 1
        spot = (index, step - 1, chunk)
        source = where
        if step == 1 and self.own is not None:
            source = self.own.at[rows]
        if step == 2 and self.beside is not None:
            source = self.beside[index].at[rows]
        return pltpu.make_async_remote_copy(
            src_ref=source,
            dst_ref=where,
            send_sem=self.sems[0].at[spot],
            recv_sem=self.sems[1].at[spot],
            device_id={"tensor": target},
            device_id_type=MESH,
        )

    def each_send(self, step, chunk, act):
        for side in SIDES:
            far = far_of(self.place, side)

            @pl.when((far < LINE - 1) & (far >= step - 1))
            def _():
                shard = self.place - side * (step - 1)
                act(self.copy(side, step, chunk, shard, self.place + side))

    def send(self, step, chunk):
        self.each_send(step, chunk, lambda copy: copy.start())

    def arrive(self, step, chunk):
        for side in SIDES:

            @pl.when(far_of(self.place, side) >= step)
            def _():
                shard = self.place - side * step
                self.copy(side, step, chunk, shard, self.place - side).wait_recv()

    def drain(self, stop=LINE, start=1):
        for step in range(start, stop):
            for chunk in range(self.chunks):
                self.each_send(step, chunk, lambda copy: copy.wait_send())


class Sum:
    def __init__(self, place, part, held, send, recv, chunks):
        self.place, self.part, self.held = place, part, held
        self.sems, self.chunks = (send, recv), chunks
        self.rows = part.shape[1] // chunks

    def copy(self, side, step, chunk, shard, target):
        rows = chunk_rows(chunk, self.rows)
        index = 0 if side == 1 else 1
        spot = (index, step - 1, chunk)
        return pltpu.make_async_remote_copy(
            src_ref=self.part.at[shard, rows],
            dst_ref=self.held.at[index, step - 1, rows],
            send_sem=self.sems[0].at[spot],
            recv_sem=self.sems[1].at[spot],
            device_id={"tensor": target},
            device_id_type=MESH,
        )

    def add(self, step, chunk):
        rows = chunk_rows(chunk, self.rows)
        for index, side in enumerate(SIDES):
            far = far_of(self.place, side)
            shard = self.place + side * (LINE - step)

            @pl.when((far >= 1) & (far <= step - 1))
            def _():
                self.copy(side, step - 1, chunk, self.place, self.place - side).wait_recv()
                self.part[shard, rows] = (
                    self.part[shard, rows].astype(f32)
                    + self.held[index, step - 2, rows].astype(f32)
                ).astype(bf16)

    def send(self, step, chunk, least=0, most=LINE):
        if step > 1 and most > 0:
            self.add(step, chunk)
        for side in SIDES:
            far = far_of(self.place, side)
            shard = self.place + side * (LINE - step)

            @pl.when((far <= step - 1) & (far >= least) & (far <= most))
            def _():
                self.copy(side, step, chunk, shard, self.place + side).start()

    def begin(self, step, chunk):
        self.send(step, chunk, most=0)

    def relay(self, step, chunk):
        self.send(step, chunk, least=1)

    def total(self, chunk, out):
        rows = chunk_rows(chunk, self.rows)
        out[rows] = self.part[self.place, rows].astype(f32)
        for index, side in enumerate(SIDES):

            @pl.when(far_of(self.place, side) >= 1)
            def _():
                self.copy(side, LINE - 1, chunk, self.place, self.place - side).wait_recv()
                out[rows] += self.held[index, LINE - 2, rows].astype(f32)

    def drain(self, stop=LINE):
        for step in range(1, stop):
            for chunk in range(self.chunks):
                for side in SIDES:
                    far = far_of(self.place, side)
                    shard = self.place + side * (LINE - step)

                    @pl.when(far <= step - 1)
                    def _():
                        self.copy(side, step, chunk, shard, self.place + side).wait_send()


def line_sems(chunks):
    return [pltpu.SemaphoreType.DMA((2, LINE - 1, chunks))] * 2


def fetch(pairs, sems):
    copies = [pltpu.make_async_copy(src, dst, sems.at[i]) for i, (src, dst) in enumerate(pairs)]
    for copy in copies:
        copy.start()
    return copies


IN_VMEM = pl.BlockSpec(memory_space=pltpu.VMEM)
IN_HBM = pl.BlockSpec(memory_space=pl.ANY)


def comm_params(number):
    return pltpu.CompilerParams(
        vmem_limit_bytes=VMEM_LIMIT, collective_id=number, has_side_effects=True
    )


def gather_norm_body(x_ref, gain_ref, buf, own, sem, send, recv):
    place = lax.axis_index("tensor")
    greet(place)
    rows = x_ref[...].astype(f32)
    rms = lax.rsqrt(jnp.mean(rows * rows, axis=1, keepdims=True) + eps)
    own[...] = (rows * rms * gain_ref[...]).astype(bf16)
    gather = Gather(place, buf, send, recv, 1, own)
    gather.send(1, 0)
    (kept,) = fetch([(own, buf.at[place])], sem)
    gather.arrive(1, 0)
    gather.send(2, 0)
    kept.wait()
    gather.arrive(2, 0)
    gather.drain(stop=LINE - 1)


def gather_norm(x, gain):
    rows, features = x.shape
    return pl.pallas_call(
        gather_norm_body,
        in_specs=[IN_VMEM, IN_VMEM],
        out_specs=IN_HBM,
        out_shape=jax.ShapeDtypeStruct((LINE, rows, features), bf16),
        scratch_shapes=[pltpu.VMEM((rows, features), bf16), pltpu.SemaphoreType.DMA((1,))]
        + line_sems(1),
        compiler_params=comm_params(0),
    )(x, gain[None, :])


def project_body(
    x_ref, w_ref, e_ref, a_ref, cos_ref, sin_ref, kept_ref, y_ref, l_ref,
    buf, yv, wv, xsem, wsem, ysem, send, recv,
):
    place = lax.axis_index("tensor")
    groups, _, width = y_ref.shape
    rows, rank = x_ref.shape[1], a_ref.shape[1]
    edge = (place == 0) | (place == LINE - 1)
    last = place ^ (LINE - 1)

    def passed(side):
        shard = place - side * (LINE - 2)
        index = 0 if side == 1 else 1
        return pltpu.make_async_remote_copy(
            src_ref=x_ref.at[shard],
            dst_ref=buf.at[shard],
            send_sem=send.at[index],
            recv_sem=recv.at[index],
            device_id={"tensor": place + side},
            device_id_type=MESH,
        )

    def came(side):
        index = 0 if side == 1 else 1
        return pltpu.make_async_remote_copy(
            src_ref=x_ref.at[last],
            dst_ref=buf.at[last],
            send_sem=send.at[index],
            recv_sem=recv.at[index],
            device_id={"tensor": place - side},
            device_id_type=MESH,
        )

    copies = []
    for slot in range(LINE):
        copy = pltpu.make_async_copy(x_ref.at[place ^ slot], buf.at[place ^ slot], xsem.at[slot])
        if slot < LINE - 1:
            copy.start()
        else:
            pl.when(jnp.logical_not(edge))(copy.start)
        copies.append(copy)
    (load,) = fetch([(w_ref.at[:, : groups * width], wv)], wsem)
    greet(place)
    for side in SIDES:
        pl.when(far_of(place, side) == LINE - 2)(passed(side).start)
    for copy in copies[:-1]:
        copy.wait()
    load.wait()
    outs = []
    for slot in range(LINE):
        shard = place ^ slot
        if slot == LINE - 1:
            pl.when(jnp.logical_not(edge))(copies[slot].wait)
            for side in SIDES:
                pl.when(far_of(place, side) == LINE - 1)(came(side).wait_recv)
            kept = pltpu.make_async_copy(buf.at[last], kept_ref.at[last], xsem.at[slot])
            pl.when(edge)(kept.start)
        mine = pl.ds(pl.multiple_of(shard * rows, rows), rows)
        low = nt(buf[shard], e_ref[:groups].reshape(groups * rank, -1)).astype(bf16)
        l_ref[mine] = low
        for g in range(groups):
            band = slice(g * width, (g + 1) * width)
            value = nn(buf[shard], wv[:, band]) + nn(low[:, g * rank : (g + 1) * rank], a_ref[g])
            if g < groups - 1:
                value = turn(value, cos_ref[mine], sin_ref[mine])
            yv[g, mine] = value.astype(bf16)
            out = pltpu.make_async_copy(yv.at[g, mine], y_ref.at[g, mine], ysem.at[slot, g])
            out.start()
            outs.append(out)
    pl.when(edge)(kept.wait)
    for out in outs:
        out.wait()
    for side in SIDES:
        pl.when(far_of(place, side) == LINE - 2)(passed(side).wait_send)


def project(x, weight, entries, exits, tables):
    _, rows, features = x.shape
    groups, rank, width = exits.shape
    return pl.pallas_call(
        project_body,
        in_specs=[IN_HBM, IN_HBM] + [IN_VMEM] * 4,
        out_specs=[IN_HBM, IN_HBM, IN_VMEM],
        out_shape=[
            jax.ShapeDtypeStruct((LINE, rows, features), bf16),
            jax.ShapeDtypeStruct((groups, LINE * rows, width), bf16),
            jax.ShapeDtypeStruct((LINE * rows, groups * rank), bf16),
        ],
        scratch_shapes=[
            pltpu.VMEM((LINE, rows, features), bf16),
            pltpu.VMEM((groups, LINE * rows, width), bf16),
            pltpu.VMEM((features, groups * width), bf16),
            pltpu.SemaphoreType.DMA((LINE,)),
            pltpu.SemaphoreType.DMA((1,)),
            pltpu.SemaphoreType.DMA((LINE, groups)),
            pltpu.SemaphoreType.DMA((2,)),
            pltpu.SemaphoreType.DMA((2,)),
        ],
        input_output_aliases={0: 0},
        compiler_params=comm_params(4),
    )(x, weight, entries, exits, *tables)


def middle_body(
    chunks, d_ref, w_ref, before_ref, after_ref, a_ref, e_ref, x_ref, gain_ref, mid_ref, buf, cbuf, low_ref,
    part, held, own, wv, wsem, nsem, s_send, s_recv, g_send, g_recv, c_send, c_recv,
):
    place = lax.axis_index("tensor")
    width = d_ref.shape[1]
    (load,) = fetch([(w_ref.at[:, 3 * width :], wv)], wsem)
    greet(place)
    load.wait()
    cots = Gather(place, cbuf, c_send, c_recv, chunks, beside=(before_ref, after_ref))
    rows = part.shape[1]
    summed = Sum(place, part, held, s_send, s_recv, chunks)
    gather = Gather(place, buf, g_send, g_recv, chunks, own)
    for slot in (3, 2, 1, 0):
        shard = place ^ slot
        mine = pl.ds(pl.multiple_of(shard * rows, rows), rows)
        d = d_ref[mine]
        low = nt(d, a_ref[...]).astype(bf16)
        low_ref[mine] = low
        part[shard] = (nt(d, wv[...]) + nn(low, e_ref[0])).astype(bf16)
        if slot == 3:
            summed.begin(1, 0)
    for chunk in range(chunks):
        for step in (1, 2, 3):
            if chunk or step > 1:
                summed.begin(step, chunk)
    size = rows // chunks
    kept = []
    for chunk in range(chunks):
        summed.relay(2, chunk)
        summed.relay(3, chunk)
        cots.send(2, chunk)
        if chunk:
            cots.arrive(2, chunk - 1)
            cots.send(3, chunk - 1)
        summed.total(chunk, mid_ref)
        here = chunk_rows(chunk, size)
        value = mid_ref[here] + x_ref[here].astype(f32)
        mid_ref[here] = value
        rms = lax.rsqrt(jnp.mean(value * value, axis=1, keepdims=True) + eps)
        own[here] = (value * rms * gain_ref[...]).astype(bf16)
        copy = pltpu.make_async_copy(own.at[here], buf.at[place, here], nsem.at[chunk])
        copy.start()
        kept.append(copy)
        if chunk == chunks - 1:
            for before in range(chunks):
                gather.send(1, before)
    cots.arrive(2, chunks - 1)
    cots.send(3, chunks - 1)
    for step in (1, 2):
        for chunk in range(chunks):
            gather.arrive(step, chunk)
            gather.send(step + 1, chunk)
    for chunk in range(chunks):
        cots.arrive(3, chunk)
        gather.arrive(3, chunk)
    for copy in kept:
        copy.wait()
    summed.drain()
    gather.drain()
    cots.drain(start=2)


def middle_rows(attended, weight, before, after, exits, finals, x, gain, chunks=4):
    rows, features = x.shape
    width = attended.shape[1]
    return pl.pallas_call(
        functools.partial(middle_body, chunks),
        in_specs=[IN_VMEM] + [IN_HBM] * 3 + [IN_VMEM] * 4,
        out_specs=[IN_VMEM, IN_HBM, IN_HBM, IN_VMEM],
        out_shape=[
            jax.ShapeDtypeStruct((rows, features), f32),
            jax.ShapeDtypeStruct((LINE, rows, features), bf16),
            jax.ShapeDtypeStruct((LINE, rows, features), bf16),
            jax.ShapeDtypeStruct((LINE * rows, exits.shape[0]), bf16),
        ],
        scratch_shapes=[
            pltpu.VMEM((LINE, rows, features), bf16),
            pltpu.VMEM((2, LINE - 1, rows, features), bf16),
            pltpu.VMEM((rows, features), bf16),
            pltpu.VMEM((features, width), bf16),
            pltpu.SemaphoreType.DMA((1,)),
            pltpu.SemaphoreType.DMA((chunks,)),
        ]
        + line_sems(chunks)
        + line_sems(chunks)
        + line_sems(chunks),
        compiler_params=comm_params(1),
    )(attended, weight, before, after, exits, finals, x, gain[None, :])


def branch_body(
    b_ref, w_ref, e_ref, a_ref, p_ref, d_ref, lo_ref, y_ref, own_ref, right_ref, left_ref,
    final_ref, exit_ref,
    buf, part, held, wv, wsem, send, recv, s_send, s_recv,
):
    place = lax.axis_index("tensor")
    rows = b_ref.shape[0]
    load, parts = fetch([(w_ref.at[:, 3 * y_ref.shape[2] :], wv), (p_ref, part)], wsem)
    greet(place)
    buf[place] = b_ref[...]
    gather = Gather(place, buf, send, recv, 1)
    summed = Sum(place, part, held, s_send, s_recv, 1)
    gather.send(1, 0)
    parts.wait()
    summed.send(1, 0)
    load.wait()
    for slot in range(LINE):
        if slot:
            gather.arrive(slot, 0)
        if 0 < slot < LINE - 1:
            gather.send(slot + 1, 0)
        if slot == 1:
            summed.send(2, 0)
        if slot == 2:
            summed.add(3, 0)
            own_ref[...] = part[place]
            for out_ref, side in ((right_ref, 1), (left_ref, -1)):

                @pl.when(far_of(place, side) < LINE - 1)
                def _():
                    out_ref[...] = part[place + side]

                @pl.when(far_of(place, side) == LINE - 1)
                def _():
                    out_ref[...] = jnp.zeros_like(out_ref)

        shard = place ^ slot
        mine = pl.ds(pl.multiple_of(shard * rows, rows), rows)
        low = nt(buf[shard], e_ref[0])
        y_ref[0, mine] = (nn(buf[shard], wv[...]) + nn(low.astype(bf16), a_ref[...])).astype(bf16)
        final = nn(lo_ref[mine].astype(f32).T.astype(bf16), buf[shard])
        leave = nn(low.T.astype(bf16), d_ref[mine])
        final_ref[...] = final if slot == 0 else final_ref[...] + final
        exit_ref[...] = leave if slot == 0 else exit_ref[...] + leave
    gather.drain()
    summed.drain(LINE - 1)


def branch_back(branch, weight, finals, exits, parts, attended, low_out):
    rows, features = branch.shape
    rank, width = exits.shape
    return pl.pallas_call(
        branch_body,
        in_specs=[IN_VMEM, IN_HBM, IN_VMEM, IN_VMEM, IN_HBM, IN_VMEM, IN_VMEM],
        out_specs=[IN_VMEM] * 6,
        out_shape=[jax.ShapeDtypeStruct((1, LINE * rows, width), bf16)]
        + [jax.ShapeDtypeStruct((rows, features), bf16)] * 3
        + [
            jax.ShapeDtypeStruct((rank, features), f32),
            jax.ShapeDtypeStruct((rank, width), f32),
        ],
        scratch_shapes=[
            pltpu.VMEM((LINE, rows, features), bf16),
            pltpu.VMEM((LINE, rows, features), bf16),
            pltpu.VMEM((2, LINE - 1, rows, features), bf16),
            pltpu.VMEM((features, width), bf16),
            pltpu.SemaphoreType.DMA((2,)),
        ]
        + line_sems(1)
        + line_sems(1),
        compiler_params=comm_params(2),
    )(branch, weight, finals, exits, parts, attended, low_out)


def tokens_body(
    chunks, d_ref, w_ref, a_ref, e_ref, x_ref, gain_ref, mid_ref, n_ref, lone_ref, final_ref, exit_ref,
    out_ref, model_ref, head_ref,
    part, held, acc, dv, wv, midv, nv, low, block, extra, wsem, send, recv, x_send, x_recv, t_send, t_recv, h_send, h_recv,
):
    place = lax.axis_index("tensor")
    tree = lax.axis_index("dp")
    trees = Trees(tree, model_ref, t_send, t_recv)
    heads = Trees(tree, head_ref, h_send, h_recv)
    groups, total, width = d_ref.shape
    rank = a_ref.shape[1]
    loads = fetch(
        [(d_ref, dv), (w_ref.at[:, : groups * width], wv), (n_ref, nv), (mid_ref, midv)],
        wsem,
    )
    block[...] = jnp.zeros_like(block)
    for g in range(groups):
        block[g * rank : (g + 1) * rank, g * width : (g + 1) * width] = a_ref[g]
    greet(place, trees.partners)
    for load in loads[:2]:
        load.wait()
    rows = part.shape[1]
    summed = Sum(place, part, held, send, recv, chunks)
    gather = Gather(place, extra, x_send, x_recv, 1)
    entry = e_ref[:groups].reshape(groups * rank, -1)

    def rows_of(slot):
        shard = place ^ slot
        mine = pl.ds(pl.multiple_of(shard * rows, rows), rows)
        return shard, mine, jnp.concatenate([dv[g, mine] for g in range(groups)], axis=1)

    def lower(slot):
        _, mine, d = rows_of(slot)
        low[mine] = nt(d, block[...]).astype(bf16)

    def partial(slot):
        shard, mine, d = rows_of(slot)
        part[shard] = (nt(d, wv[...]) + nn(low[mine], entry)).astype(bf16)

    lower(3)
    partial(3)
    summed.begin(1, 0)
    summed.begin(1, 1)
    for slot in (2, 1, 0):
        lower(slot)
    for load in loads[2:]:
        load.wait()

    def turned(value):
        return value.astype(f32).T.astype(bf16)

    joined = nn(turned(low[...]), nv[...].reshape(total, -1))
    extra[place] = jnp.concatenate([joined, final_ref[...]], axis=0).astype(bf16)
    gather.send(1, 0)
    for chunk in range(2, chunks):
        summed.begin(1, chunk)
    for slot in (2, 1, 0):
        partial(slot)
    for step in (2, 3):
        for chunk in range(chunks):
            summed.begin(step, chunk)
    summed.relay(2, 0)
    summed.relay(2, 1)
    gather.arrive(1, 0)
    gather.send(2, 0)
    summed.relay(2, 2)
    low_one = turned(lone_ref[...])
    for g in range(groups):
        band = slice(g * rank, (g + 1) * rank)
        head_ref[tree, band] = nn(low_one[band], dv[g]).astype(bf16)
    head_ref[tree, groups * rank :] = exit_ref[...].astype(bf16)
    heads.send(0)
    summed.relay(2, 3)
    gather.arrive(2, 0)
    gather.send(3, 0)
    heads.advance(1)
    summed.relay(3, 0)
    gather.arrive(3, 0)
    model_ref[tree] = functools.reduce(
        jnp.add, [extra[shard].astype(f32) for shard in range(LINE)]
    ).astype(bf16)
    trees.send(0)
    heads.advance(2)
    summed.relay(3, 1)
    trees.advance(1)
    summed.relay(3, 2)
    summed.relay(3, 3)
    trees.advance(2)
    size = rows // chunks

    def finish(chunk):
        finish_tokens(summed, chunk, size, acc, x_ref, gain_ref, midv, out_ref)

    finish(0)
    finish(1)
    for number in range(3, trees.rounds):
        trees.advance(number)
        heads.advance(number)
    finish(2)
    finish(3)
    for blocks in (trees, heads):
        blocks.arrive(blocks.rounds - 1)
        blocks.drain()
    summed.drain()
    gather.drain()


class Trees:
    def __init__(self, tree, ref, send, recv):
        self.tree, self.ref, self.sems = tree, ref, (send, recv)
        self.rounds = ref.shape[0].bit_length() - 1
        self.partners = [self.partner(number) for number in range(self.rounds)]

    def partner(self, number):
        size = 1 << number
        return self.tree + size - 2 * size * ((self.tree // size) % 2)

    def copy(self, number, owner):
        size = 1 << number
        here = pl.ds((owner // size) * size, size)
        return pltpu.make_async_remote_copy(
            src_ref=self.ref.at[here],
            dst_ref=self.ref.at[here],
            send_sem=self.sems[0].at[number],
            recv_sem=self.sems[1].at[number],
            device_id={"dp": self.partner(number)},
            device_id_type=MESH,
        )

    def send(self, number):
        self.copy(number, self.tree).start()

    def arrive(self, number):
        self.copy(number, self.partner(number)).wait_recv()

    def advance(self, number):
        if number < self.rounds:
            self.arrive(number - 1)
            self.send(number)

    def drain(self):
        for number in range(self.rounds):
            self.copy(number, self.tree).wait_send()


def finish_tokens(summed, chunk, size, acc, x_ref, gain_ref, mid_ref, out_ref):
    summed.total(chunk, acc)
    here = chunk_rows(chunk, size)
    rows = x_ref[here].astype(f32)
    rms = lax.rsqrt(jnp.mean(rows * rows, axis=1, keepdims=True) + eps)
    scaled = acc[here] * gain_ref[...]
    mean = jnp.mean(scaled * rows, axis=1, keepdims=True)
    out_ref[here] = (mid_ref[here] + rms * (scaled - rows * (rms * rms) * mean)).astype(bf16)


def tokens_back(
    head_grads, weight, exits, entries, x, gain, grad_middle, normed, low_one, final_grads, exit_grads
):
    chunks = LINE
    rows, features = x.shape
    groups, total, width = head_grads.shape
    rank = exits.shape[1]
    deep = (groups + 1) * rank
    trees = lax.axis_size("dp")
    sems = pltpu.SemaphoreType.DMA((trees.bit_length() - 1,))
    return pl.pallas_call(
        functools.partial(tokens_body, chunks),
        in_specs=[IN_HBM, IN_HBM] + [IN_VMEM] * 4 + [IN_HBM] * 2 + [IN_VMEM] * 3,
        out_specs=[IN_VMEM] * 3,
        out_shape=[
            jax.ShapeDtypeStruct((rows, features), bf16),
            jax.ShapeDtypeStruct((trees, deep, features), bf16),
            jax.ShapeDtypeStruct((trees, deep, width), bf16),
        ],
        scratch_shapes=[
            pltpu.VMEM((LINE, rows, features), bf16),
            pltpu.VMEM((2, LINE - 1, rows, features), bf16),
            pltpu.VMEM((rows, features), f32),
            pltpu.VMEM((groups, total, width), bf16),
            pltpu.VMEM((features, groups * width), bf16),
            pltpu.VMEM((rows, features), f32),
            pltpu.VMEM((LINE, rows, features), bf16),
            pltpu.VMEM((total, groups * rank), bf16),
            pltpu.VMEM((groups * rank, groups * width), bf16),
            pltpu.VMEM((LINE, deep, features), bf16),
            pltpu.SemaphoreType.DMA((4,)),
        ]
        + line_sems(chunks)
        + line_sems(1)
        + [sems] * 4,
        compiler_params=comm_params(3),
    )(
        head_grads, weight, exits, entries, x, gain[None, :], grad_middle, normed,
        low_one, final_grads, exit_grads,
    )


def tree_tiles(seg, rows, parent_row):
    trunk = TRUNK * seg
    leaves = trunk + BRANCHES * seg
    key = lax.broadcasted_iota(jnp.int32, (QT, QT), 0)
    query = lax.broadcasted_iota(jnp.int32, (QT, QT), 1)
    causal = key <= query
    own = causal & (key // seg == query // seg)
    tiles = []
    for start in range(0, trunk, QT):
        pieces = [(0, start, None)] if start else []
        tiles.append((start, pieces + [(start, QT, causal)]))
    tiles.append((trunk, [(0, trunk, None), (trunk, QT, own)]))
    branch = lax.broadcasted_iota(jnp.int32, (BRANCHES * seg, QT), 0) // seg
    for start in range(leaves, rows, QT):
        mine = branch == parent_row[:, start - leaves : start - leaves + QT]
        tiles.append(
            (start, [(0, trunk, None), (trunk, BRANCHES * seg, mine), (start, QT, own)])
        )
    return tiles


def attend_body(seg, q_ref, k_ref, v_ref, p_ref, o_ref, lse_ref):
    rows = q_ref.shape[1]
    value_t = v_ref[0].T
    lane = lax.broadcasted_iota(jnp.int32, (QT, 2 * HEAD_DIM), 1)
    for start, pieces in tree_tiles(seg, rows, p_ref[...]):
        query = q_ref[0, start : start + QT] * bf16(HEAD_DIM**-0.5)
        outs = []
        for h in range(2):
            own_query = jnp.where(lane // HEAD_DIM == h, query, bf16(0))
            scores = []
            for k0, count, mask in pieces:
                s = nt(k_ref[0, k0 : k0 + count], own_query)
                scores.append(s if mask is None else jnp.where(mask, s, -1e30))
            top = functools.reduce(
                jnp.maximum, [jnp.max(s, axis=0, keepdims=True) for s in scores]
            )
            summed, out = 0.0, 0.0
            for (k0, count, _), s in zip(pieces, scores):
                weights = jnp.exp(s - top)
                summed += jnp.sum(weights, axis=0, keepdims=True)
                out += nn(
                    value_t[h * HEAD_DIM : (h + 1) * HEAD_DIM, k0 : k0 + count],
                    weights.astype(bf16),
                )
            outs.append(out / summed)
            lse_ref[0, h : h + 1, start : start + QT] = top + jnp.log(summed)
        o_ref[0, start : start + QT] = jnp.concatenate(outs, axis=0).T.astype(bf16)


def attend(qkv, leaf_parent, seg):
    _, rows, width = qkv.shape
    pairs = width // (2 * HEAD_DIM)
    return pl.pallas_call(
        functools.partial(attend_body, seg),
        grid=(pairs,),
        in_specs=[
            pl.BlockSpec((1, rows, 2 * HEAD_DIM), lambda j, g=g: (g, 0, j)) for g in range(3)
        ]
        + [pl.BlockSpec(leaf_parent.shape, lambda j: (0, 0))],
        out_specs=[
            pl.BlockSpec((1, rows, 2 * HEAD_DIM), lambda j: (0, 0, j)),
            pl.BlockSpec((1, 2, rows), lambda j: (j, 0, 0)),
        ],
        out_shape=[
            jax.ShapeDtypeStruct((1, rows, width), bf16),
            jax.ShapeDtypeStruct((pairs, 2, rows), f32),
        ],
        compiler_params=pltpu.CompilerParams(vmem_limit_bytes=VMEM_LIMIT),
        cost_estimate=pl.CostEstimate(
            flops=8 * rows * rows * width, bytes_accessed=8 * rows * width, transcendentals=0
        ),
    )(qkv, qkv, qkv, leaf_parent)


def attend_back_body(
    seg, q_ref, k_ref, v_ref, o_ref, g_ref, lse_ref, p_ref, cos_ref, sin_ref, d_ref, dq_t, dk, dv
):
    rows = q_ref.shape[1]
    scale = bf16(HEAD_DIM**-0.5)
    key_t = k_ref[0].T
    weighed_t = (g_ref[0].astype(f32) * o_ref[0].astype(f32)).T
    lane = lax.broadcasted_iota(jnp.int32, (QT, 2 * HEAD_DIM), 1)
    dk[...] = jnp.zeros_like(dk)
    dv[...] = jnp.zeros_like(dv)
    for start, pieces in tree_tiles(seg, rows, p_ref[...]):
        query = q_ref[0, start : start + QT] * scale
        grad = g_ref[0, start : start + QT]
        for h in range(2):
            mine = lane // HEAD_DIM == h
            own_query = jnp.where(mine, query, bf16(0))
            own_grad = jnp.where(mine, grad, bf16(0))
            band = slice(h * HEAD_DIM, (h + 1) * HEAD_DIM)
            delta = jnp.sum(weighed_t[band, start : start + QT], axis=0, keepdims=True)
            lse = lse_ref[0, h : h + 1, start : start + QT]
            grad_q = 0.0
            for k0, count, mask in pieces:
                probs = jnp.exp(nt(k_ref[0, k0 : k0 + count], own_query) - lse)
                if mask is not None:
                    probs = jnp.where(mask, probs, 0.0)
                grad_probs = nt(v_ref[0, k0 : k0 + count], own_grad)
                grad_scores = (probs * (grad_probs - delta)).astype(bf16)
                dk[k0 : k0 + count] += nn(grad_scores, own_query)
                dv[k0 : k0 + count] += nn(probs.astype(bf16), own_grad)
                grad_q += nn(key_t[band, k0 : k0 + count], grad_scores)
            dq_t[band, start : start + QT] = grad_q
    cosine, sine = cos_ref[...], -sin_ref[...]
    d_ref[0] = turn(dq_t[...].T * HEAD_DIM**-0.5, cosine, sine).astype(bf16)
    d_ref[1] = turn(dk[...], cosine, sine).astype(bf16)
    d_ref[2] = dv[...].astype(bf16)


def attend_back(qkv, attended, grad, lse, leaf_parent, tables, seg):
    _, rows, width = qkv.shape
    pairs = width // (2 * HEAD_DIM)
    pair = 2 * HEAD_DIM
    return pl.pallas_call(
        functools.partial(attend_back_body, seg),
        grid=(pairs,),
        in_specs=[pl.BlockSpec((1, rows, pair), lambda j, g=g: (g, 0, j)) for g in range(3)]
        + [
            pl.BlockSpec((1, rows, pair), lambda j: (0, 0, j)),
            pl.BlockSpec((1, rows, pair), lambda j: (0, 0, j)),
            pl.BlockSpec((1, 2, rows), lambda j: (j, 0, 0)),
            pl.BlockSpec(leaf_parent.shape, lambda j: (0, 0)),
            pl.BlockSpec((rows, pair), lambda j: (0, 0)),
            pl.BlockSpec((rows, pair), lambda j: (0, 0)),
        ],
        out_specs=pl.BlockSpec((3, rows, pair), lambda j: (0, 0, j)),
        out_shape=jax.ShapeDtypeStruct((3, rows, width), bf16),
        scratch_shapes=[
            pltpu.VMEM((pair, rows), f32),
            pltpu.VMEM((rows, pair), f32),
            pltpu.VMEM((rows, pair), f32),
        ],
        compiler_params=pltpu.CompilerParams(vmem_limit_bytes=VMEM_LIMIT),
        cost_estimate=pl.CostEstimate(
            flops=20 * rows * rows * width, bytes_accessed=16 * rows * width, transcendentals=0
        ),
    )(qkv, qkv, qkv, attended, grad, lse, leaf_parent, *tables)


def feed_body(
    rank, tile, chunks,
    n_ref, c_ref, before_ref, after_ref, far_ref, wg_ref, wu_ref, wd_ref, mid_ref,
    xu_in, xd_in, e_in, f_in, gain_ref,
    grad_ref, low_grad_ref, res_ref, unit_ref, model_ref,
    x_ref, e_ref, f_ref, midv, nbuf, cbuf, wbuf, low, low_t, acc_res, acc_back, acc_low, part, held, resv,
    nsem, csem, wsem, rsem, msem, send, recv,
):
    place = lax.axis_index("tensor")
    units = unit_ref.shape[1]
    tiles = units // tile
    summed = Sum(place, part, held, send, recv, chunks)

    def load_rows(order, act):
        into = order % 2
        shard = place ^ (LINE - 1 - order)
        act(pltpu.make_async_copy(n_ref.at[shard], nbuf.at[into], nsem.at[into]))

        def take(source):
            act(pltpu.make_async_copy(source, cbuf.at[into], csem.at[into]))

        pl.when(shard == place)(lambda: take(c_ref))
        pl.when(shard == place - 1)(lambda: take(before_ref))
        pl.when(shard == place + 1)(lambda: take(after_ref))
        pl.when((shard > place + 1) | (shard < place - 1))(lambda: take(far_ref.at[shard]))

    def load_weights(index, into, act):
        columns = pl.ds(pl.multiple_of(index * tile, tile), tile)
        for k, w_ref in enumerate((wg_ref, wu_ref, wd_ref)):
            act(pltpu.make_async_copy(w_ref.at[:, columns], wbuf.at[into, k], wsem.at[into, k]))

    def start(copy):
        copy.start()

    def wait(copy):
        copy.wait()

    load_rows(jnp.int32(0), start)
    load_weights(0, 0, start)
    (load_middle,) = fetch([(mid_ref, midv)], msem)
    for padded in (x_ref, e_ref, f_ref):
        padded[...] = jnp.zeros_like(padded)
    x_ref[0, :rank] = xu_in[0]
    x_ref[1, rank : 2 * rank] = xu_in[1]
    x_ref[2, 2 * rank :] = xd_in[...]
    e_ref[: 2 * rank] = e_in[3:].reshape(2 * rank, -1)
    f_ref[2 * rank :] = f_in[1]
    unit_ref[...] = jnp.zeros_like(unit_ref)
    model_ref[...] = jnp.zeros_like(model_ref)
    greet(place)

    def one_shard(order, carry):
        into = order % 2
        shard = place ^ (LINE - 1 - order)
        load_rows(order, wait)

        @pl.when(order < LINE - 1)
        def _():
            load_rows(order + 1, start)

        first = nt(nbuf[into], e_ref[...]) + nt(cbuf[into], f_ref[...])
        low[...] = first.astype(bf16)
        low_t[...] = first.T.astype(bf16)
        acc_res[...] = jnp.zeros_like(acc_res)
        acc_back[...] = jnp.zeros_like(acc_back)
        acc_low[...] = jnp.zeros_like(acc_low)

        def one_tile(index, carry):
            stage = order * tiles + index
            at = stage % 2
            load_weights(index, at, wait)

            @pl.when(stage < LINE * tiles - 1)
            def _():
                load_weights((index + 1) % tiles, 1 - at, start)

            columns = pl.ds(pl.multiple_of(index * tile, tile), tile)
            x_gate, x_rise, x_fall = x_ref[0, :, columns], x_ref[1, :, columns], x_ref[2, :, columns]
            gate = nn(nbuf[into], wbuf[at, 0]) + nn(low[...], x_gate)
            rise = nn(nbuf[into], wbuf[at, 1]) + nn(low[...], x_rise)
            grad_hidden = nn(cbuf[into], wbuf[at, 2]) + nn(low[...], x_fall)
            sigmoid = jax.nn.sigmoid(gate)
            silu = gate * sigmoid
            hidden = (silu * rise).astype(bf16)
            grad_gate = (grad_hidden * rise * sigmoid * (1.0 + gate * (1.0 - sigmoid))).astype(bf16)
            grad_rise = (grad_hidden * silu).astype(bf16)
            acc_back[...] += nt(grad_gate, wbuf[at, 0]) + nt(grad_rise, wbuf[at, 1])
            acc_res[...] += nt(hidden, wbuf[at, 2])
            acc_low[...] += nt(grad_gate, x_gate) + nt(grad_rise, x_rise) + nt(hidden, x_fall)
            unit_ref[:rank, columns] += nn(low_t[:rank], grad_gate)
            unit_ref[rank : 2 * rank, columns] += nn(low_t[rank : 2 * rank], grad_rise)
            unit_ref[2 * rank :, columns] += nn(low_t[2 * rank : 3 * rank], hidden)
            return carry

        lax.fori_loop(0, tiles, one_tile, 0)
        joined = acc_low[...].astype(bf16)
        joined_t = acc_low[...].T.astype(bf16)
        part[shard] = (acc_back[...] + nn(joined, e_ref[...])).astype(bf16)

        @pl.when(order > 0)
        def _():
            pltpu.make_async_copy(resv, res_ref.at[shard], rsem.at[0]).wait()

        resv[...] = (acc_res[...] + nn(joined, f_ref[...])).astype(bf16)
        pltpu.make_async_copy(resv, res_ref.at[shard], rsem.at[0]).start()
        for step in (1, 2, 3):

            @pl.when(order == step - 1)
            def _():
                for chunk in range(chunks):
                    summed.send(step, chunk)

        model_ref[: 2 * rank] += nn(joined_t[: 2 * rank], nbuf[into])
        model_ref[2 * rank :] += nn(joined_t[2 * rank : 3 * rank], cbuf[into])
        return carry

    lax.fori_loop(0, LINE, one_shard, 0)
    size = part.shape[1] // chunks
    last = (LINE - 1) % 2
    load_middle.wait()
    for chunk in range(chunks):
        summed.total(chunk, acc_back)
        here = chunk_rows(chunk, size)
        middle = midv[here]
        rms = lax.rsqrt(jnp.mean(middle * middle, axis=1, keepdims=True) + eps)
        scaled = acc_back[here] * gain_ref[...]
        mean = jnp.mean(scaled * middle, axis=1, keepdims=True)
        grad = cbuf[last, here].astype(f32) + rms * (scaled - middle * (rms * rms) * mean)
        grad_ref[here] = grad
        low_grad_ref[here] = grad.astype(bf16)
    pltpu.make_async_copy(resv, res_ref.at[place], rsem.at[0]).wait()
    summed.drain()


def feed(normed, cots, weights, middle, units_exit, fall_entry, entries, finals, gain, tile=512, chunks=4):
    _, rows, features = normed.shape
    units = weights[0].shape[1]
    rank = fall_entry.shape[0]
    return pl.pallas_call(
        functools.partial(feed_body, rank, tile, chunks),
        in_specs=[IN_HBM] * 9 + [IN_VMEM] * 5,
        out_specs=[IN_VMEM, IN_VMEM, IN_HBM, IN_VMEM, IN_VMEM],
        out_shape=[
            jax.ShapeDtypeStruct((rows, features), f32),
            jax.ShapeDtypeStruct((rows, features), bf16),
            jax.ShapeDtypeStruct((LINE, rows, features), bf16),
            jax.ShapeDtypeStruct((3 * rank, units), f32),
            jax.ShapeDtypeStruct((3 * rank, features), f32),
        ],
        scratch_shapes=[
            pltpu.VMEM((3, 3 * rank, units), bf16),
            pltpu.VMEM((3 * rank, features), bf16),
            pltpu.VMEM((3 * rank, features), bf16),
            pltpu.VMEM((rows, features), f32),
            pltpu.VMEM((2, rows, features), bf16),
            pltpu.VMEM((2, rows, features), bf16),
            pltpu.VMEM((2, 3, features, tile), bf16),
            pltpu.VMEM((rows, 3 * rank), bf16),
            pltpu.VMEM((3 * rank, rows), bf16),
            pltpu.VMEM((rows, features), f32),
            pltpu.VMEM((rows, features), f32),
            pltpu.VMEM((rows, 3 * rank), f32),
            pltpu.VMEM((LINE, rows, features), bf16),
            pltpu.VMEM((2, LINE - 1, rows, features), bf16),
            pltpu.VMEM((rows, features), bf16),
            pltpu.SemaphoreType.DMA((2,)),
            pltpu.SemaphoreType.DMA((2,)),
            pltpu.SemaphoreType.DMA((2, 3)),
            pltpu.SemaphoreType.DMA((1,)),
            pltpu.SemaphoreType.DMA((1,)),
        ]
        + line_sems(chunks),
        compiler_params=comm_params(5),
    )(normed, *cots, *weights, middle, units_exit, fall_entry, entries, finals, gain[None, :])


def pick_body(pick_ref, *refs):
    count = len(refs) // 2
    for source, target in zip(refs[:count], refs[count:]):
        target[...] = source[...].reshape(target.shape)


def picked(pick, arrays):
    shapes = [a.shape[:1] + a.shape[2:] for a in arrays]
    return pl.pallas_call(
        pick_body,
        grid_spec=pltpu.PrefetchScalarGridSpec(
            num_scalar_prefetch=1,
            grid=(1,),
            in_specs=[
                pl.BlockSpec(a.shape[:1] + (1,) + a.shape[2:], lambda i, p: (0, p[0], 0, 0)) for a in arrays
            ],
            out_specs=[pl.BlockSpec(shape, lambda i, p: (0, 0, 0)) for shape in shapes],
        ),
        out_shape=[jax.ShapeDtypeStruct(shape, bf16) for shape in shapes],
    )(pick, *arrays)


def per_tree(block):
    return lax.all_gather(block, "dp", axis=0, tiled=False)


def combine_body(rank, pick_ref, early, model, late, head, entry_ref, final_ref, unit_ref, down_ref, exit_ref, out_ref):
    for ref in (entry_ref, final_ref, unit_ref, down_ref, exit_ref, out_ref):
        ref[...] = jnp.zeros_like(ref)

    def one_tree(tree, carry):
        pick = pick_ref[tree]

        def block(ref, index):
            return ref[tree, index * rank : (index + 1) * rank].astype(f32)

        for k in range(3):
            entry_ref[k, pick] += block(late, k)
            exit_ref[k, pick] += block(head, k)
        final_ref[0, pick] += block(late, 3)
        out_ref[pick] += block(head, 3)
        for k in range(2):
            entry_ref[3 + k, pick] += block(model, k)
            unit_ref[k, pick] += block(early, k)
        final_ref[1, pick] += block(model, 2)
        down_ref[pick] += block(early, 2)
        return carry

    lax.fori_loop(0, early.shape[0], one_tree, 0)


def combine(picks, early, model, late, head, adapters, steps=4):
    trees, _, features = early.shape
    rank = late.shape[1] // 4
    width = head.shape[2]
    wide, narrow = features // steps, width // steps

    def taken(array, tile):
        return pl.BlockSpec((trees, array.shape[1], tile), lambda i, p: (0, 0, i))

    def given(lead, tile):
        shape = lead + (adapters, rank, tile)
        return pl.BlockSpec(shape, lambda i, p: (0,) * (len(shape) - 1) + (i,))

    def shape(lead, full):
        return jax.ShapeDtypeStruct(lead + (adapters, rank, full), f32)

    return pl.pallas_call(
        functools.partial(combine_body, rank),
        grid_spec=pltpu.PrefetchScalarGridSpec(
            num_scalar_prefetch=1,
            grid=(steps,),
            in_specs=[taken(early, wide), taken(model, wide), taken(late, wide), taken(head, narrow)],
            out_specs=[
                given((5,), wide),
                given((2,), wide),
                given((2,), wide),
                given((), wide),
                given((3,), narrow),
                given((), narrow),
            ],
        ),
        out_shape=[
            shape((5,), features),
            shape((2,), features),
            shape((2,), features),
            shape((), features),
            shape((3,), width),
            shape((), width),
        ],
        compiler_params=pltpu.CompilerParams(vmem_limit_bytes=VMEM_LIMIT),
    )(picks, early, model, late, head)


def local(
    tokens,
    cotangent,
    attention_gain,
    feed_gain,
    query_weight,
    key_weight,
    value_weight,
    output_weight,
    gate_weight,
    up_weight,
    down_weight,
    entry_maps,
    head_exits,
    unit_exits,
    output_entry,
    down_entry,
    final_exits,
    parents,
    adapter_pick,
):
    pick = adapter_pick[0]
    adapters, rank = entry_maps.shape[1], entry_maps.shape[3]
    local_rows = tokens.shape[0]
    total = local_rows * lax.axis_size("tensor")
    blocks = parents.shape[1]
    seg = total // blocks
    tables = rope_tables(blocks, seg)
    leaf_parent = (jnp.repeat(parents[0, TRUNK + BRANCHES :], seg) - TRUNK)[None, :]
    gain_one = attention_gain.astype(f32)
    gain_two = feed_gain.astype(f32)

    w_heads = lax.all_gather(
        jnp.concatenate([query_weight, key_weight, value_weight, output_weight], axis=1),
        "dp",
        axis=0,
        tiled=True,
    )

    w_units = [
        lax.all_gather(w, "dp", axis=0, tiled=True) for w in (gate_weight, up_weight, down_weight)
    ]
    entries, heads_exit, units_exit, out_entry, fall_entry, finals = picked(
        adapter_pick,
        (
            jnp.swapaxes(entry_maps, 2, 3),
            head_exits,
            unit_exits,
            jnp.swapaxes(output_entry, 1, 2)[None],
            jnp.swapaxes(down_entry, 1, 2)[None],
            final_exits,
        ),
    )
    out_entry, fall_entry = out_entry[0], fall_entry[0]

    most_one = gather_norm(tokens, gain_one)
    full_one, qkv, low_one = project(most_one, w_heads, entries, heads_exit, tables)
    cot_tied, qkv = lax.optimization_barrier((cotangent, qkv))
    before = permute(cot_tied, [(0, 1), (1, 2), (2, 3)])
    after = permute(cot_tied, [(3, 2), (2, 1), (1, 0)])
    attended, lse = attend(qkv, leaf_parent, seg)
    middle, full_two, far_cot, adapt_o = middle_rows(
        attended[0], w_heads, before, after, out_entry, finals, tokens, gain_two
    )

    grad_middle, branch, res_parts, unit_grads, model_grads = feed(
        full_two, (cotangent, before, after, far_cot), w_units, middle, units_exit, fall_entry, entries, finals, gain_two
    )
    early = jnp.concatenate(
        [unit_grads.astype(bf16), jnp.full((rank, unit_grads.shape[1]), pick).astype(bf16)]
    )
    model_low = model_grads.astype(bf16)
    branch, early, model_low = lax.optimization_barrier((branch, early, model_low))
    early = per_tree(early)
    model_sum = lax.psum(model_low, "tensor")

    grad_attended, res_own, res_right, res_left, final_grads, exit_grads = branch_back(
        branch, w_heads, finals, out_entry, res_parts, attended[0], adapt_o
    )
    grad_attended, res_right, res_left = lax.optimization_barrier((grad_attended, res_right, res_left))
    from_left = permute(res_right, [(0, 1), (1, 2), (2, 3)])
    from_right = permute(res_left, [(3, 2), (2, 1), (1, 0)])
    head_grads = attend_back(qkv, attended, grad_attended, lse, leaf_parent, tables, seg)
    head_grads, model_sum, from_left, from_right = lax.optimization_barrier(
        (head_grads, model_sum, from_left, from_right)
    )
    model_all = per_tree(model_sum)
    grad_tokens, late_model, late_head = tokens_back(
        head_grads, w_heads, heads_exit, entries, tokens, gain_one, grad_middle,
        full_one, low_one, final_grads, exit_grads,
    )
    result = (
        middle
        + res_own.astype(f32)
        + from_left.astype(f32)
        + from_right.astype(f32)
    ).astype(bf16)

    picks = early[:, 3 * rank, 0].astype(jnp.int32)
    grad_entries, grad_finals, grad_units, grad_down, grad_heads, grad_output = combine(
        picks, early, model_all, late_model, late_head, adapters
    )
    grad_entries = grad_entries.swapaxes(2, 3)
    grad_output = grad_output.swapaxes(1, 2)
    grad_down = grad_down.swapaxes(1, 2)
    return (
        result,
        grad_tokens,
        grad_entries,
        grad_heads,
        grad_units,
        grad_output,
        grad_down,
        grad_finals,
    )


def solution(mesh):
    in_specs = (
        P(("dp", "tensor"), None),
        P(("dp", "tensor"), None),
        P(),
        P(),
        P("dp", "tensor"),
        P("dp", "tensor"),
        P("dp", "tensor"),
        P("dp", "tensor"),
        P("dp", "tensor"),
        P("dp", "tensor"),
        P("dp", "tensor"),
        P(),
        P(None, None, None, "tensor"),
        P(None, None, None, "tensor"),
        P(None, "tensor", None),
        P(None, "tensor", None),
        P(),
        P("dp", None),
        P("dp"),
    )
    out_specs = (
        P(("dp", "tensor"), None),
        P(("dp", "tensor"), None),
        P(),
        P(None, None, None, "tensor"),
        P(None, None, None, "tensor"),
        P(None, "tensor", None),
        P(None, "tensor", None),
        P(),
    )
    return jax.shard_map(local, mesh=mesh, in_specs=in_specs, out_specs=out_specs, check_vma=False)
```

```python
import functools

import jax
import jax.numpy as jnp
import numpy as np
from jax import lax
from jax.experimental import pallas as pl
from jax.experimental.pallas import tpu as pltpu
from jax.sharding import PartitionSpec as P

HEAD_DIM = 64
TRUNK, BRANCHES = 8, 4
QT = 256
VMEM_LIMIT = 60 * 1024 * 1024
LINE = 4
MESH = pl.DeviceIdType.MESH

eps = 1e-05
theta = 130000.0
bf16, f32 = jnp.bfloat16, jnp.float32


def nn(left, right):
    return jnp.dot(left, right, preferred_element_type=f32)


def nt(left, right):
    return lax.dot_general(left, right, (((1,), (1,)), ((), ())), preferred_element_type=f32)


def tn(left, right):
    return lax.dot_general(left, right, (((0,), (0,)), ((), ())), preferred_element_type=f32)


def permute(value, pairs):
    return lax.ppermute(value, "tensor", pairs)


def rope_tables(blocks, seg):
    depth = np.minimum(np.arange(blocks), TRUNK)
    depth[TRUNK + BRANCHES :] = TRUNK + 1
    position = (np.repeat(depth, seg) * seg + np.arange(blocks * seg) % seg).astype(np.float32)
    half = HEAD_DIM // 2
    freq = (np.float32(theta) ** (-np.arange(half, dtype=np.float32) / half)).astype(np.float32)
    angle = (position[:, None] * freq[None, :]).astype(np.float32)
    cosine = np.tile(np.cos(angle), (1, 4)).astype(np.float32)
    sine = np.sin(angle).astype(np.float32)
    sine = np.concatenate([-sine, sine, -sine, sine], axis=1)
    return jnp.asarray(cosine), jnp.asarray(sine)


def turn(values, cosine, sine):
    width = values.shape[1]
    reps = width // cosine.shape[1]
    if reps > 1:
        cosine = jnp.concatenate([cosine] * reps, axis=1)
        sine = jnp.concatenate([sine] * reps, axis=1)
    lane = lax.broadcasted_iota(jnp.int32, values.shape, 1)
    half = HEAD_DIM // 2
    other = jnp.where(
        lane % HEAD_DIM < half, pltpu.roll(values, width - half, 1), pltpu.roll(values, half, 1)
    )
    return values * cosine + other * sine


SIDES = (1, -1)


def far_of(place, side):
    return place if side == 1 else LINE - 1 - place


def greet(place, partners=()):
    barrier = pltpu.get_barrier_semaphore()
    for partner in partners:
        pl.semaphore_signal(barrier, inc=1, device_id={"dp": partner}, device_id_type=MESH)
    for side in SIDES:

        @pl.when(far_of(place, side) < LINE - 1)
        def _():
            pl.semaphore_signal(
                barrier, inc=1, device_id={"tensor": place + side}, device_id_type=MESH
            )

    edge = (place == 0) | (place == LINE - 1)

    @pl.when(edge)
    def _():
        pl.semaphore_wait(barrier, 1 + len(partners))

    @pl.when(jnp.logical_not(edge))
    def _():
        pl.semaphore_wait(barrier, 2 + len(partners))


def chunk_rows(chunk, rows):
    return pl.ds(chunk * rows, rows)


class Gather:
    def __init__(self, place, buf, send, recv, chunks, own=None):
        self.place, self.buf, self.sems, self.chunks = place, buf, (send, recv), chunks
        self.rows = buf.shape[1] // chunks
        self.own = own

    def copy(self, side, step, chunk, shard, target):
        rows = chunk_rows(chunk, self.rows)
        where = self.buf.at[shard, rows]
        index = 0 if side == 1 else 1
        spot = (index, step - 1, chunk)
        source = where
        if step == 1 and self.own is not None:
            source = self.own.at[rows]
        return pltpu.make_async_remote_copy(
            src_ref=source,
            dst_ref=where,
            send_sem=self.sems[0].at[spot],
            recv_sem=self.sems[1].at[spot],
            device_id={"tensor": target},
            device_id_type=MESH,
        )

    def each_send(self, step, chunk, act, least=0, most=LINE):
        for side in SIDES:
            far = far_of(self.place, side)

            @pl.when((far < LINE - 1) & (far >= step - 1) & (far >= least) & (far <= most))
            def _():
                shard = self.place - side * (step - 1)
                act(self.copy(side, step, chunk, shard, self.place + side))

    def send(self, step, chunk, least=0, most=LINE):
        self.each_send(step, chunk, lambda copy: copy.start(), least, most)

    def arrive(self, step, chunk):
        for side in SIDES:

            @pl.when(far_of(self.place, side) >= step)
            def _():
                shard = self.place - side * step
                self.copy(side, step, chunk, shard, self.place - side).wait_recv()

    def relay(self, step, chunk):
        for side in SIDES:
            far = far_of(self.place, side)

            @pl.when((far < LINE - 1) & (far >= step - 1))
            def _():
                before = self.place - side * (step - 1)
                self.copy(side, step - 1, chunk, before, self.place - side).wait_recv()
                self.copy(side, step, chunk, before, self.place + side).start()

    def close(self):
        for side in SIDES:

            @pl.when(far_of(self.place, side) == LINE - 1)
            def _():
                for step in range(1, LINE):
                    for chunk in range(self.chunks):
                        shard = self.place - side * step
                        self.copy(side, step, chunk, shard, self.place - side).wait_recv()

    def drain(self, stop=LINE, start=1):
        for step in range(start, stop):
            for chunk in range(self.chunks):
                self.each_send(step, chunk, lambda copy: copy.wait_send())


class Sum:
    def __init__(self, place, part, held, send, recv, chunks):
        self.place, self.part, self.held = place, part, held
        self.sems, self.chunks = (send, recv), chunks
        self.rows = part.shape[1] // chunks

    def copy(self, side, step, chunk, shard, target):
        rows = chunk_rows(chunk, self.rows)
        index = 0 if side == 1 else 1
        spot = (index, step - 1, chunk)
        return pltpu.make_async_remote_copy(
            src_ref=self.part.at[shard, rows],
            dst_ref=self.held.at[index, step - 1, rows],
            send_sem=self.sems[0].at[spot],
            recv_sem=self.sems[1].at[spot],
            device_id={"tensor": target},
            device_id_type=MESH,
        )

    def add(self, step, chunk):
        rows = chunk_rows(chunk, self.rows)
        for index, side in enumerate(SIDES):
            far = far_of(self.place, side)
            shard = self.place + side * (LINE - step)

            @pl.when((far >= 1) & (far <= step - 1))
            def _():
                self.copy(side, step - 1, chunk, self.place, self.place - side).wait_recv()
                self.part[shard, rows] = (
                    self.part[shard, rows].astype(f32)
                    + self.held[index, step - 2, rows].astype(f32)
                ).astype(bf16)

    def send(self, step, chunk, least=0, most=LINE):
        if step > 1 and most > 0:
            self.add(step, chunk)
        for side in SIDES:
            far = far_of(self.place, side)
            shard = self.place + side * (LINE - step)

            @pl.when((far <= step - 1) & (far >= least) & (far <= most))
            def _():
                self.copy(side, step, chunk, shard, self.place + side).start()

    def begin(self, step, chunk):
        self.send(step, chunk, most=0)

    def relay(self, step, chunk):
        self.send(step, chunk, least=1)

    def total(self, chunk, out):
        rows = chunk_rows(chunk, self.rows)
        out[rows] = self.part[self.place, rows].astype(f32)
        for index, side in enumerate(SIDES):

            @pl.when(far_of(self.place, side) >= 1)
            def _():
                self.copy(side, LINE - 1, chunk, self.place, self.place - side).wait_recv()
                out[rows] += self.held[index, LINE - 2, rows].astype(f32)

    def drain(self, stop=LINE):
        for step in range(1, stop):
            for chunk in range(self.chunks):
                for side in SIDES:
                    far = far_of(self.place, side)
                    shard = self.place + side * (LINE - step)

                    @pl.when(far <= step - 1)
                    def _():
                        self.copy(side, step, chunk, shard, self.place + side).wait_send()


def line_sems(chunks):
    return [pltpu.SemaphoreType.DMA((2, LINE - 1, chunks))] * 2


def fetch(pairs, sems):
    copies = [pltpu.make_async_copy(src, dst, sems.at[i]) for i, (src, dst) in enumerate(pairs)]
    for copy in copies:
        copy.start()
    return copies


IN_VMEM = pl.BlockSpec(memory_space=pltpu.VMEM)
IN_HBM = pl.BlockSpec(memory_space=pl.ANY)


def comm_params(number):
    return pltpu.CompilerParams(
        vmem_limit_bytes=VMEM_LIMIT, collective_id=number, has_side_effects=True
    )


def gather_norm_body(x_ref, gain_ref, buf, own, sem, send, recv):
    place = lax.axis_index("tensor")
    greet(place)
    rows = x_ref[...].astype(f32)
    rms = lax.rsqrt(jnp.mean(rows * rows, axis=1, keepdims=True) + eps)
    own[...] = (rows * rms * gain_ref[...]).astype(bf16)
    gather = Gather(place, buf, send, recv, 1, own)
    gather.send(1, 0)
    (kept,) = fetch([(own, buf.at[place])], sem)
    gather.arrive(1, 0)
    gather.send(2, 0)
    kept.wait()
    gather.arrive(2, 0)
    gather.drain(stop=LINE - 1)


def gather_norm(x, gain):
    rows, features = x.shape
    return pl.pallas_call(
        gather_norm_body,
        in_specs=[IN_VMEM, IN_VMEM],
        out_specs=IN_HBM,
        out_shape=jax.ShapeDtypeStruct((LINE, rows, features), bf16),
        scratch_shapes=[pltpu.VMEM((rows, features), bf16), pltpu.SemaphoreType.DMA((1,))]
        + line_sems(1),
        compiler_params=comm_params(0),
    )(x, gain[None, :])


def front_body(
    chunks, seg,
    x_ref, w_ref, c_ref, e_ref, a_ref, cos_ref, sin_ref, p_ref, oe_ref, f_ref, tok_ref, gain_ref,
    kept_ref, y_ref, mid_ref, n_ref, cot_ref, l_ref, att_ref, lse_ref, lo_ref,
    buf, yv, wv, wo, part, held, own, midv, xsem, wsem, ysem, nsem, msem, send, recv,
    s_send, s_recv, g_send, g_recv, c_send, c_recv,
):
    place = lax.axis_index("tensor")
    groups, total, width = y_ref.shape
    rows, rank = x_ref.shape[1], a_ref.shape[1]
    edge = (place == 0) | (place == LINE - 1)
    last = place ^ (LINE - 1)

    def passed(side):
        shard = place - side * (LINE - 2)
        index = 0 if side == 1 else 1
        return pltpu.make_async_remote_copy(
            src_ref=x_ref.at[shard],
            dst_ref=buf.at[shard],
            send_sem=send.at[index],
            recv_sem=recv.at[index],
            device_id={"tensor": place + side},
            device_id_type=MESH,
        )

    def came(side):
        index = 0 if side == 1 else 1
        return pltpu.make_async_remote_copy(
            src_ref=x_ref.at[last],
            dst_ref=buf.at[last],
            send_sem=send.at[index],
            recv_sem=recv.at[index],
            device_id={"tensor": place - side},
            device_id_type=MESH,
        )

    copies = []
    for slot in range(LINE):
        copy = pltpu.make_async_copy(x_ref.at[place ^ slot], buf.at[place ^ slot], xsem.at[slot])
        if slot < LINE - 1:
            copy.start()
        else:
            pl.when(jnp.logical_not(edge))(copy.start)
        copies.append(copy)
    load, load_out = fetch(
        [(w_ref.at[:, : groups * width], wv), (w_ref.at[:, groups * width :], wo)], wsem
    )
    greet(place)
    cots = Gather(place, cot_ref, c_send, c_recv, chunks, c_ref)
    summed = Sum(place, part, held, s_send, s_recv, chunks)
    gather = Gather(place, n_ref, g_send, g_recv, chunks, own)
    for side in SIDES:
        pl.when(far_of(place, side) == LINE - 2)(passed(side).start)
    for chunk in range(chunks):
        cots.send(1, chunk)

    for copy in copies[:-1]:
        copy.wait()
    load.wait()
    outs = []
    for slot in range(LINE):
        shard = place ^ slot
        if slot == LINE - 1:
            pl.when(jnp.logical_not(edge))(copies[slot].wait)
            for side in SIDES:
                pl.when(far_of(place, side) == LINE - 1)(came(side).wait_recv)
            kept = pltpu.make_async_copy(buf.at[last], kept_ref.at[last], xsem.at[slot])
            pl.when(edge)(kept.start)
        mine = pl.ds(pl.multiple_of(shard * rows, rows), rows)
        low = nt(buf[shard], e_ref[:groups].reshape(groups * rank, -1)).astype(bf16)
        l_ref[mine] = low
        for g in range(groups):
            band = slice(g * width, (g + 1) * width)
            value = nn(buf[shard], wv[:, band]) + nn(low[:, g * rank : (g + 1) * rank], a_ref[g])
            if g < groups - 1:
                value = turn(value, cos_ref[mine], sin_ref[mine])
            yv[g, mine] = value.astype(bf16)
            out = pltpu.make_async_copy(yv.at[g, mine], y_ref.at[g, mine], ysem.at[slot, g])
            out.start()
            outs.append(out)

    pair = 2 * HEAD_DIM

    def one_pair(j, carry):
        lanes = pl.ds(pl.multiple_of(j * pair, pair), pair)
        attend_pair(seg, yv, lanes, p_ref[...], j, att_ref, lse_ref)

        @pl.when(j == 0)
        def _():
            for chunk in range(chunks):
                cots.relay(2, chunk)

        return carry

    lax.fori_loop(0, width // pair, one_pair, 0)

    load_out.wait()
    for slot in (3, 2, 1, 0):
        shard = place ^ slot
        mine = pl.ds(pl.multiple_of(shard * rows, rows), rows)
        d = att_ref[mine]
        low = nt(d, oe_ref[...]).astype(bf16)
        lo_ref[mine] = low
        part[shard] = (nt(d, wo[...]) + nn(low, f_ref[0])).astype(bf16)
        if slot == 3:
            summed.begin(1, 0)
    for chunk in range(chunks):
        for step in (1, 2, 3):
            if chunk or step > 1:
                summed.begin(step, chunk)
    size = rows // chunks
    stores = []
    for chunk in range(chunks):
        summed.relay(2, chunk)
        summed.relay(3, chunk)
        cots.relay(3, chunk)
        summed.total(chunk, midv)
        here = chunk_rows(chunk, size)
        value = midv[here] + tok_ref[here].astype(f32)
        midv[here] = value
        rms = lax.rsqrt(jnp.mean(value * value, axis=1, keepdims=True) + eps)
        own[here] = (value * rms * gain_ref[...]).astype(bf16)
        stores.append(pltpu.make_async_copy(own.at[here], n_ref.at[place, here], nsem.at[chunk]))
        stores.append(pltpu.make_async_copy(midv.at[here], mid_ref.at[here], msem.at[chunk]))
        gather.send(1, chunk, least=1)
        for store in stores[-2:]:
            store.start()
    for chunk in range(chunks):
        gather.send(1, chunk, most=0)
    for step in (2, 3):
        for chunk in range(chunks):
            gather.relay(step, chunk)
    cots.close()
    gather.close()
    pl.when(edge)(kept.wait)
    for out in outs + stores:
        out.wait()
    for side in SIDES:
        pl.when(far_of(place, side) == LINE - 2)(passed(side).wait_send)
    summed.drain()
    gather.drain()
    cots.drain()


def front(x, weight, cot, entries, exits, tables, leaf_parent, out_entry, finals, tokens, gain, seg, chunks=4):
    _, rows, features = x.shape
    groups, rank, width = exits.shape
    total = LINE * rows
    shards = jax.ShapeDtypeStruct((LINE, rows, features), bf16)
    return pl.pallas_call(
        functools.partial(front_body, chunks, seg),
        in_specs=[IN_HBM] * 3 + [IN_VMEM] * 9,
        out_specs=[IN_HBM] * 5 + [IN_VMEM] * 4,
        out_shape=[
            shards,
            jax.ShapeDtypeStruct((groups, total, width), bf16),
            jax.ShapeDtypeStruct((rows, features), f32),
            shards,
            shards,
            jax.ShapeDtypeStruct((total, groups * rank), bf16),
            jax.ShapeDtypeStruct((total, width), bf16),
            jax.ShapeDtypeStruct((width // (2 * HEAD_DIM), 2, total), f32),
            jax.ShapeDtypeStruct((total, rank), bf16),
        ],
        scratch_shapes=[
            pltpu.VMEM((LINE, rows, features), bf16),
            pltpu.VMEM((groups, total, width), bf16),
            pltpu.VMEM((features, groups * width), bf16),
            pltpu.VMEM((features, width), bf16),
            pltpu.VMEM((LINE, rows, features), bf16),
            pltpu.VMEM((2, LINE - 1, rows, features), bf16),
            pltpu.VMEM((rows, features), bf16),
            pltpu.VMEM((rows, features), f32),
            pltpu.SemaphoreType.DMA((LINE,)),
            pltpu.SemaphoreType.DMA((2,)),
            pltpu.SemaphoreType.DMA((LINE, groups)),
            pltpu.SemaphoreType.DMA((chunks,)),
            pltpu.SemaphoreType.DMA((chunks,)),
            pltpu.SemaphoreType.DMA((2,)),
            pltpu.SemaphoreType.DMA((2,)),
        ]
        + line_sems(chunks)
        + line_sems(chunks)
        + line_sems(chunks),
        input_output_aliases={0: 0},
        compiler_params=comm_params(1),
    )(x, weight, cot, entries, exits, *tables, leaf_parent, out_entry, finals, tokens, gain[None, :])


def branch_body(
    b_ref, w_ref, e_ref, a_ref, p_ref, d_ref, lo_ref, y_ref, own_ref, right_ref, left_ref,
    final_ref, exit_ref,
    buf, part, held, wv, wsem, send, recv, s_send, s_recv,
):
    place = lax.axis_index("tensor")
    rows = b_ref.shape[0]
    load, parts = fetch([(w_ref.at[:, 3 * y_ref.shape[2] :], wv), (p_ref, part)], wsem)
    greet(place)
    buf[place] = b_ref[...]
    gather = Gather(place, buf, send, recv, 1)
    summed = Sum(place, part, held, s_send, s_recv, 1)
    gather.send(1, 0)
    parts.wait()
    summed.send(1, 0)
    load.wait()
    for slot in range(LINE):
        if slot:
            gather.arrive(slot, 0)
        if 0 < slot < LINE - 1:
            gather.send(slot + 1, 0)
        if slot == 1:
            summed.send(2, 0)
        if slot == 2:
            summed.add(3, 0)
            own_ref[...] = part[place]
            for out_ref, side in ((right_ref, 1), (left_ref, -1)):

                @pl.when(far_of(place, side) < LINE - 1)
                def _():
                    out_ref[...] = part[place + side]

                @pl.when(far_of(place, side) == LINE - 1)
                def _():
                    out_ref[...] = jnp.zeros_like(out_ref)

        shard = place ^ slot
        mine = pl.ds(pl.multiple_of(shard * rows, rows), rows)
        low = nt(buf[shard], e_ref[0])
        y_ref[0, mine] = (nn(buf[shard], wv[...]) + nn(low.astype(bf16), a_ref[...])).astype(bf16)
        final = nn(lo_ref[mine].astype(f32).T.astype(bf16), buf[shard])
        leave = nn(low.T.astype(bf16), d_ref[mine])
        final_ref[...] = final if slot == 0 else final_ref[...] + final
        exit_ref[...] = leave if slot == 0 else exit_ref[...] + leave
    gather.drain()
    summed.drain(LINE - 1)


def branch_back(branch, weight, finals, exits, parts, attended, low_out):
    rows, features = branch.shape
    rank, width = exits.shape
    return pl.pallas_call(
        branch_body,
        in_specs=[IN_VMEM, IN_HBM, IN_VMEM, IN_VMEM, IN_HBM, IN_VMEM, IN_VMEM],
        out_specs=[IN_VMEM] * 6,
        out_shape=[jax.ShapeDtypeStruct((1, LINE * rows, width), bf16)]
        + [jax.ShapeDtypeStruct((rows, features), bf16)] * 3
        + [
            jax.ShapeDtypeStruct((rank, features), f32),
            jax.ShapeDtypeStruct((rank, width), f32),
        ],
        scratch_shapes=[
            pltpu.VMEM((LINE, rows, features), bf16),
            pltpu.VMEM((LINE, rows, features), bf16),
            pltpu.VMEM((2, LINE - 1, rows, features), bf16),
            pltpu.VMEM((features, width), bf16),
            pltpu.SemaphoreType.DMA((2,)),
        ]
        + line_sems(1)
        + line_sems(1),
        compiler_params=comm_params(2),
    )(branch, weight, finals, exits, parts, attended, low_out)


def tokens_body(
    chunks, d_ref, w_ref, a_ref, e_ref, x_ref, gain_ref, mid_ref, n_ref, lone_ref, final_ref, exit_ref,
    out_ref, model_ref, head_ref,
    part, held, acc, dv, wv, midv, nv, low, block, extra, wsem, send, recv, x_send, x_recv, t_send, t_recv, h_send, h_recv,
):
    place = lax.axis_index("tensor")
    tree = lax.axis_index("dp")
    trees = Trees(tree, model_ref, t_send, t_recv)
    heads = Trees(tree, head_ref, h_send, h_recv)
    groups, total, width = d_ref.shape
    rank = a_ref.shape[1]
    loads = fetch(
        [(d_ref, dv), (w_ref.at[:, : groups * width], wv), (n_ref, nv), (mid_ref, midv)],
        wsem,
    )
    block[...] = jnp.zeros_like(block)
    for g in range(groups):
        block[g * rank : (g + 1) * rank, g * width : (g + 1) * width] = a_ref[g]
    greet(place, trees.partners)
    for load in loads[:2]:
        load.wait()
    rows = part.shape[1]
    summed = Sum(place, part, held, send, recv, chunks)
    gather = Gather(place, extra, x_send, x_recv, 1)
    entry = e_ref[:groups].reshape(groups * rank, -1)

    def rows_of(slot):
        shard = place ^ slot
        mine = pl.ds(pl.multiple_of(shard * rows, rows), rows)
        return shard, mine, jnp.concatenate([dv[g, mine] for g in range(groups)], axis=1)

    def lower(slot):
        _, mine, d = rows_of(slot)
        low[mine] = nt(d, block[...]).astype(bf16)

    def partial(slot):
        shard, mine, d = rows_of(slot)
        part[shard] = (nt(d, wv[...]) + nn(low[mine], entry)).astype(bf16)

    lower(3)
    partial(3)
    summed.begin(1, 0)
    summed.begin(1, 1)
    for slot in (2, 1, 0):
        lower(slot)
    for load in loads[2:]:
        load.wait()

    def turned(value):
        return value.astype(f32).T.astype(bf16)

    joined = nn(turned(low[...]), nv[...].reshape(total, -1))
    extra[place] = jnp.concatenate([joined, final_ref[...]], axis=0).astype(bf16)
    gather.send(1, 0)
    for chunk in range(2, chunks):
        summed.begin(1, chunk)
    for slot in (2, 1, 0):
        partial(slot)
    for step in (2, 3):
        for chunk in range(chunks):
            summed.begin(step, chunk)
    summed.relay(2, 0)
    summed.relay(2, 1)
    gather.arrive(1, 0)
    gather.send(2, 0)
    summed.relay(2, 2)
    low_one = turned(lone_ref[...])
    for g in range(groups):
        band = slice(g * rank, (g + 1) * rank)
        head_ref[tree, band] = nn(low_one[band], dv[g]).astype(bf16)
    head_ref[tree, groups * rank :] = exit_ref[...].astype(bf16)
    heads.send(0)
    summed.relay(2, 3)
    gather.arrive(2, 0)
    gather.send(3, 0)
    heads.advance(1)
    summed.relay(3, 0)
    gather.arrive(3, 0)
    model_ref[tree] = functools.reduce(
        jnp.add, [extra[shard].astype(f32) for shard in range(LINE)]
    ).astype(bf16)
    trees.send(0)
    heads.advance(2)
    summed.relay(3, 1)
    trees.advance(1)
    summed.relay(3, 2)
    summed.relay(3, 3)
    trees.advance(2)
    size = rows // chunks

    def finish(chunk):
        finish_tokens(summed, chunk, size, acc, x_ref, gain_ref, midv, out_ref)

    finish(0)
    finish(1)
    for number in range(3, trees.rounds):
        trees.advance(number)
        heads.advance(number)
    finish(2)
    finish(3)
    for blocks in (trees, heads):
        blocks.arrive(blocks.rounds - 1)
        blocks.drain()
    summed.drain()
    gather.drain()


class Trees:
    def __init__(self, tree, ref, send, recv):
        self.tree, self.ref, self.sems = tree, ref, (send, recv)
        self.rounds = ref.shape[0].bit_length() - 1
        self.partners = [self.partner(number) for number in range(self.rounds)]

    def partner(self, number):
        size = 1 << number
        return self.tree + size - 2 * size * ((self.tree // size) % 2)

    def copy(self, number, owner):
        size = 1 << number
        here = pl.ds((owner // size) * size, size)
        return pltpu.make_async_remote_copy(
            src_ref=self.ref.at[here],
            dst_ref=self.ref.at[here],
            send_sem=self.sems[0].at[number],
            recv_sem=self.sems[1].at[number],
            device_id={"dp": self.partner(number)},
            device_id_type=MESH,
        )

    def send(self, number):
        self.copy(number, self.tree).start()

    def arrive(self, number):
        self.copy(number, self.partner(number)).wait_recv()

    def advance(self, number):
        if number < self.rounds:
            self.arrive(number - 1)
            self.send(number)

    def drain(self):
        for number in range(self.rounds):
            self.copy(number, self.tree).wait_send()


def finish_tokens(summed, chunk, size, acc, x_ref, gain_ref, mid_ref, out_ref):
    summed.total(chunk, acc)
    here = chunk_rows(chunk, size)
    rows = x_ref[here].astype(f32)
    rms = lax.rsqrt(jnp.mean(rows * rows, axis=1, keepdims=True) + eps)
    scaled = acc[here] * gain_ref[...]
    mean = jnp.mean(scaled * rows, axis=1, keepdims=True)
    out_ref[here] = (mid_ref[here] + rms * (scaled - rows * (rms * rms) * mean)).astype(bf16)


def tokens_back(
    head_grads, weight, exits, entries, x, gain, grad_middle, normed, low_one, final_grads, exit_grads
):
    chunks = LINE
    rows, features = x.shape
    groups, total, width = head_grads.shape
    rank = exits.shape[1]
    deep = (groups + 1) * rank
    trees = lax.axis_size("dp")
    sems = pltpu.SemaphoreType.DMA((trees.bit_length() - 1,))
    return pl.pallas_call(
        functools.partial(tokens_body, chunks),
        in_specs=[IN_HBM, IN_HBM] + [IN_VMEM] * 4 + [IN_HBM] * 2 + [IN_VMEM] * 3,
        out_specs=[IN_VMEM] * 3,
        out_shape=[
            jax.ShapeDtypeStruct((rows, features), bf16),
            jax.ShapeDtypeStruct((trees, deep, features), bf16),
            jax.ShapeDtypeStruct((trees, deep, width), bf16),
        ],
        scratch_shapes=[
            pltpu.VMEM((LINE, rows, features), bf16),
            pltpu.VMEM((2, LINE - 1, rows, features), bf16),
            pltpu.VMEM((rows, features), f32),
            pltpu.VMEM((groups, total, width), bf16),
            pltpu.VMEM((features, groups * width), bf16),
            pltpu.VMEM((rows, features), f32),
            pltpu.VMEM((LINE, rows, features), bf16),
            pltpu.VMEM((total, groups * rank), bf16),
            pltpu.VMEM((groups * rank, groups * width), bf16),
            pltpu.VMEM((LINE, deep, features), bf16),
            pltpu.SemaphoreType.DMA((4,)),
        ]
        + line_sems(chunks)
        + line_sems(1)
        + [sems] * 4,
        compiler_params=comm_params(3),
    )(
        head_grads, weight, exits, entries, x, gain[None, :], grad_middle, normed,
        low_one, final_grads, exit_grads,
    )


def tree_tiles(seg, rows, parent_row):
    trunk = TRUNK * seg
    leaves = trunk + BRANCHES * seg
    key = lax.broadcasted_iota(jnp.int32, (QT, QT), 0)
    query = lax.broadcasted_iota(jnp.int32, (QT, QT), 1)
    causal = key <= query
    own = causal & (key // seg == query // seg)
    tiles = []
    for start in range(0, trunk, QT):
        pieces = [(0, start, None)] if start else []
        tiles.append((start, pieces + [(start, QT, causal)]))
    tiles.append((trunk, [(0, trunk, None), (trunk, QT, own)]))
    branch = lax.broadcasted_iota(jnp.int32, (BRANCHES * seg, QT), 0) // seg
    for start in range(leaves, rows, QT):
        mine = branch == parent_row[:, start - leaves : start - leaves + QT]
        tiles.append(
            (start, [(0, trunk, None), (trunk, BRANCHES * seg, mine), (start, QT, own)])
        )
    return tiles


def attend_pair(seg, qkv_ref, lanes, parent_row, pair, o_ref, lse_ref):
    rows = qkv_ref.shape[1]
    value_t = qkv_ref[2, :, lanes].T
    lane = lax.broadcasted_iota(jnp.int32, (QT, 2 * HEAD_DIM), 1)
    for start, pieces in tree_tiles(seg, rows, parent_row):
        query = qkv_ref[0, start : start + QT, lanes] * bf16(HEAD_DIM**-0.5)
        outs = []
        for h in range(2):
            own_query = jnp.where(lane // HEAD_DIM == h, query, bf16(0))
            scores = []
            for k0, count, mask in pieces:
                s = nt(qkv_ref[1, k0 : k0 + count, lanes], own_query)
                scores.append(s if mask is None else jnp.where(mask, s, -1e30))
            top = functools.reduce(
                jnp.maximum, [jnp.max(s, axis=0, keepdims=True) for s in scores]
            )
            summed, out = 0.0, 0.0
            for (k0, count, _), s in zip(pieces, scores):
                weights = jnp.exp(s - top)
                summed += jnp.sum(weights, axis=0, keepdims=True)
                out += nn(
                    value_t[h * HEAD_DIM : (h + 1) * HEAD_DIM, k0 : k0 + count],
                    weights.astype(bf16),
                )
            outs.append(out / summed)
            lse_ref[pair, h : h + 1, start : start + QT] = top + jnp.log(summed)
        o_ref[start : start + QT, lanes] = jnp.concatenate(outs, axis=0).T.astype(bf16)


def attend_back_body(
    seg, q_ref, k_ref, v_ref, o_ref, g_ref, lse_ref, p_ref, cos_ref, sin_ref, d_ref, dq_t, dk, dv
):
    rows = q_ref.shape[1]
    scale = bf16(HEAD_DIM**-0.5)
    key_t = k_ref[0].T
    weighed_t = (g_ref[0].astype(f32) * o_ref[...].astype(f32)).T
    lane = lax.broadcasted_iota(jnp.int32, (QT, 2 * HEAD_DIM), 1)
    dk[...] = jnp.zeros_like(dk)
    dv[...] = jnp.zeros_like(dv)
    for start, pieces in tree_tiles(seg, rows, p_ref[...]):
        query = q_ref[0, start : start + QT] * scale
        grad = g_ref[0, start : start + QT]
        for h in range(2):
            mine = lane // HEAD_DIM == h
            own_query = jnp.where(mine, query, bf16(0))
            own_grad = jnp.where(mine, grad, bf16(0))
            band = slice(h * HEAD_DIM, (h + 1) * HEAD_DIM)
            delta = jnp.sum(weighed_t[band, start : start + QT], axis=0, keepdims=True)
            lse = lse_ref[0, h : h + 1, start : start + QT]
            grad_q = 0.0
            for k0, count, mask in pieces:
                probs = jnp.exp(nt(k_ref[0, k0 : k0 + count], own_query) - lse)
                if mask is not None:
                    probs = jnp.where(mask, probs, 0.0)
                grad_probs = nt(v_ref[0, k0 : k0 + count], own_grad)
                grad_scores = (probs * (grad_probs - delta)).astype(bf16)
                dk[k0 : k0 + count] += nn(grad_scores, own_query)
                dv[k0 : k0 + count] += nn(probs.astype(bf16), own_grad)
                grad_q += nn(key_t[band, k0 : k0 + count], grad_scores)
            dq_t[band, start : start + QT] = grad_q
    cosine, sine = cos_ref[...], -sin_ref[...]
    d_ref[0] = turn(dq_t[...].T * HEAD_DIM**-0.5, cosine, sine).astype(bf16)
    d_ref[1] = turn(dk[...], cosine, sine).astype(bf16)
    d_ref[2] = dv[...].astype(bf16)


def attend_back(qkv, attended, grad, lse, leaf_parent, tables, seg):
    _, rows, width = qkv.shape
    pairs = width // (2 * HEAD_DIM)
    pair = 2 * HEAD_DIM
    return pl.pallas_call(
        functools.partial(attend_back_body, seg),
        grid=(pairs,),
        in_specs=[pl.BlockSpec((1, rows, pair), lambda j, g=g: (g, 0, j)) for g in range(3)]
        + [
            pl.BlockSpec((rows, pair), lambda j: (0, j)),
            pl.BlockSpec((1, rows, pair), lambda j: (0, 0, j)),
            pl.BlockSpec((1, 2, rows), lambda j: (j, 0, 0)),
            pl.BlockSpec(leaf_parent.shape, lambda j: (0, 0)),
            pl.BlockSpec((rows, pair), lambda j: (0, 0)),
            pl.BlockSpec((rows, pair), lambda j: (0, 0)),
        ],
        out_specs=pl.BlockSpec((3, rows, pair), lambda j: (0, 0, j)),
        out_shape=jax.ShapeDtypeStruct((3, rows, width), bf16),
        scratch_shapes=[
            pltpu.VMEM((pair, rows), f32),
            pltpu.VMEM((rows, pair), f32),
            pltpu.VMEM((rows, pair), f32),
        ],
        compiler_params=pltpu.CompilerParams(vmem_limit_bytes=VMEM_LIMIT),
        cost_estimate=pl.CostEstimate(
            flops=20 * rows * rows * width, bytes_accessed=16 * rows * width, transcendentals=0
        ),
    )(qkv, qkv, qkv, attended, grad, lse, leaf_parent, *tables)


def feed_body(
    rank, tile, chunks,
    n_ref, c_ref, far_ref, wg_ref, wu_ref, wd_ref, mid_ref,
    xu_in, xd_in, e_in, f_in, gain_ref,
    grad_ref, low_grad_ref, res_ref, unit_ref, model_ref,
    x_ref, e_ref, f_ref, midv, nbuf, cbuf, wbuf, low, low_t, acc_res, acc_back, acc_low, part, held, resv,
    nsem, csem, wsem, rsem, msem, send, recv,
):
    place = lax.axis_index("tensor")
    units = unit_ref.shape[1]
    tiles = units // tile
    summed = Sum(place, part, held, send, recv, chunks)

    def load_rows(order, act):
        into = order % 2
        shard = place ^ (LINE - 1 - order)
        act(pltpu.make_async_copy(n_ref.at[shard], nbuf.at[into], nsem.at[into]))

        def take(source):
            act(pltpu.make_async_copy(source, cbuf.at[into], csem.at[into]))

        pl.when(order == LINE - 1)(lambda: take(c_ref))
        pl.when(order < LINE - 1)(lambda: take(far_ref.at[shard]))

    def load_weights(index, into, act):
        columns = pl.ds(pl.multiple_of(index * tile, tile), tile)
        for k, w_ref in enumerate((wg_ref, wu_ref, wd_ref)):
            act(pltpu.make_async_copy(w_ref.at[:, columns], wbuf.at[into, k], wsem.at[into, k]))

    def start(copy):
        copy.start()

    def wait(copy):
        copy.wait()

    load_rows(jnp.int32(0), start)
    load_weights(0, 0, start)
    (load_middle,) = fetch([(mid_ref, midv)], msem)
    for padded in (x_ref, e_ref, f_ref):
        padded[...] = jnp.zeros_like(padded)
    x_ref[0, :rank] = xu_in[0]
    x_ref[1, rank : 2 * rank] = xu_in[1]
    x_ref[2, 2 * rank :] = xd_in[...]
    e_ref[: 2 * rank] = e_in[3:].reshape(2 * rank, -1)
    f_ref[2 * rank :] = f_in[1]
    unit_ref[...] = jnp.zeros_like(unit_ref)
    model_ref[...] = jnp.zeros_like(model_ref)
    greet(place)

    def one_shard(order, carry):
        into = order % 2
        shard = place ^ (LINE - 1 - order)
        load_rows(order, wait)

        @pl.when(order < LINE - 1)
        def _():
            load_rows(order + 1, start)

        first = nt(nbuf[into], e_ref[...]) + nt(cbuf[into], f_ref[...])
        low[...] = first.astype(bf16)
        low_t[...] = first.T.astype(bf16)
        acc_res[...] = jnp.zeros_like(acc_res)
        acc_back[...] = jnp.zeros_like(acc_back)
        acc_low[...] = jnp.zeros_like(acc_low)

        def one_tile(index, carry):
            stage = order * tiles + index
            at = stage % 2
            load_weights(index, at, wait)

            @pl.when(stage < LINE * tiles - 1)
            def _():
                load_weights((index + 1) % tiles, 1 - at, start)

            columns = pl.ds(pl.multiple_of(index * tile, tile), tile)
            x_gate, x_rise, x_fall = x_ref[0, :, columns], x_ref[1, :, columns], x_ref[2, :, columns]
            gate = nn(nbuf[into], wbuf[at, 0]) + nn(low[...], x_gate)
            rise = nn(nbuf[into], wbuf[at, 1]) + nn(low[...], x_rise)
            grad_hidden = nn(cbuf[into], wbuf[at, 2]) + nn(low[...], x_fall)
            sigmoid = jax.nn.sigmoid(gate)
            silu = gate * sigmoid
            hidden = (silu * rise).astype(bf16)
            grad_gate = (grad_hidden * rise * sigmoid * (1.0 + gate * (1.0 - sigmoid))).astype(bf16)
            grad_rise = (grad_hidden * silu).astype(bf16)
            acc_back[...] += nt(grad_gate, wbuf[at, 0]) + nt(grad_rise, wbuf[at, 1])
            acc_res[...] += nt(hidden, wbuf[at, 2])
            acc_low[...] += nt(grad_gate, x_gate) + nt(grad_rise, x_rise) + nt(hidden, x_fall)
            unit_ref[:rank, columns] += nn(low_t[:rank], grad_gate)
            unit_ref[rank : 2 * rank, columns] += nn(low_t[rank : 2 * rank], grad_rise)
            unit_ref[2 * rank :, columns] += nn(low_t[2 * rank : 3 * rank], hidden)
            return carry

        lax.fori_loop(0, tiles, one_tile, 0)
        joined = acc_low[...].astype(bf16)
        joined_t = acc_low[...].T.astype(bf16)
        part[shard] = (acc_back[...] + nn(joined, e_ref[...])).astype(bf16)

        @pl.when(order > 0)
        def _():
            pltpu.make_async_copy(resv, res_ref.at[shard], rsem.at[0]).wait()

        resv[...] = (acc_res[...] + nn(joined, f_ref[...])).astype(bf16)
        pltpu.make_async_copy(resv, res_ref.at[shard], rsem.at[0]).start()
        for step in (1, 2, 3):

            @pl.when(order == step - 1)
            def _():
                for chunk in range(chunks):
                    summed.send(step, chunk)

        model_ref[: 2 * rank] += nn(joined_t[: 2 * rank], nbuf[into])
        model_ref[2 * rank :] += nn(joined_t[2 * rank : 3 * rank], cbuf[into])
        return carry

    lax.fori_loop(0, LINE, one_shard, 0)
    size = part.shape[1] // chunks
    last = (LINE - 1) % 2
    load_middle.wait()
    for chunk in range(chunks):
        summed.total(chunk, acc_back)
        here = chunk_rows(chunk, size)
        middle = midv[here]
        rms = lax.rsqrt(jnp.mean(middle * middle, axis=1, keepdims=True) + eps)
        scaled = acc_back[here] * gain_ref[...]
        mean = jnp.mean(scaled * middle, axis=1, keepdims=True)
        grad = cbuf[last, here].astype(f32) + rms * (scaled - middle * (rms * rms) * mean)
        grad_ref[here] = grad
        low_grad_ref[here] = grad.astype(bf16)
    pltpu.make_async_copy(resv, res_ref.at[place], rsem.at[0]).wait()
    summed.drain()


def feed(normed, cots, weights, middle, units_exit, fall_entry, entries, finals, gain, tile=512, chunks=4):
    _, rows, features = normed.shape
    units = weights[0].shape[1]
    rank = fall_entry.shape[0]
    return pl.pallas_call(
        functools.partial(feed_body, rank, tile, chunks),
        in_specs=[IN_HBM] * 7 + [IN_VMEM] * 5,
        out_specs=[IN_VMEM, IN_VMEM, IN_HBM, IN_VMEM, IN_VMEM],
        out_shape=[
            jax.ShapeDtypeStruct((rows, features), f32),
            jax.ShapeDtypeStruct((rows, features), bf16),
            jax.ShapeDtypeStruct((LINE, rows, features), bf16),
            jax.ShapeDtypeStruct((3 * rank, units), f32),
            jax.ShapeDtypeStruct((3 * rank, features), f32),
        ],
        scratch_shapes=[
            pltpu.VMEM((3, 3 * rank, units), bf16),
            pltpu.VMEM((3 * rank, features), bf16),
            pltpu.VMEM((3 * rank, features), bf16),
            pltpu.VMEM((rows, features), f32),
            pltpu.VMEM((2, rows, features), bf16),
            pltpu.VMEM((2, rows, features), bf16),
            pltpu.VMEM((2, 3, features, tile), bf16),
            pltpu.VMEM((rows, 3 * rank), bf16),
            pltpu.VMEM((3 * rank, rows), bf16),
            pltpu.VMEM((rows, features), f32),
            pltpu.VMEM((rows, features), f32),
            pltpu.VMEM((rows, 3 * rank), f32),
            pltpu.VMEM((LINE, rows, features), bf16),
            pltpu.VMEM((2, LINE - 1, rows, features), bf16),
            pltpu.VMEM((rows, features), bf16),
            pltpu.SemaphoreType.DMA((2,)),
            pltpu.SemaphoreType.DMA((2,)),
            pltpu.SemaphoreType.DMA((2, 3)),
            pltpu.SemaphoreType.DMA((1,)),
            pltpu.SemaphoreType.DMA((1,)),
        ]
        + line_sems(chunks),
        compiler_params=comm_params(5),
    )(normed, *cots, *weights, middle, units_exit, fall_entry, entries, finals, gain[None, :])


def pick_body(pick_ref, *refs):
    count = len(refs) // 2
    for source, target in zip(refs[:count], refs[count:]):
        target[...] = source[...].reshape(target.shape)


def picked(pick, arrays):
    shapes = [a.shape[:1] + a.shape[2:] for a in arrays]
    return pl.pallas_call(
        pick_body,
        grid_spec=pltpu.PrefetchScalarGridSpec(
            num_scalar_prefetch=1,
            grid=(1,),
            in_specs=[
                pl.BlockSpec(a.shape[:1] + (1,) + a.shape[2:], lambda i, p: (0, p[0], 0, 0)) for a in arrays
            ],
            out_specs=[pl.BlockSpec(shape, lambda i, p: (0, 0, 0)) for shape in shapes],
        ),
        out_shape=[jax.ShapeDtypeStruct(shape, bf16) for shape in shapes],
    )(pick, *arrays)


def per_tree(block):
    return lax.all_gather(block, "dp", axis=0, tiled=False)


def combine_body(rank, pick_ref, early, model, late, head, entry_ref, final_ref, unit_ref, down_ref, exit_ref, out_ref):
    for ref in (entry_ref, final_ref, unit_ref, down_ref, exit_ref, out_ref):
        ref[...] = jnp.zeros_like(ref)

    def one_tree(tree, carry):
        pick = pick_ref[tree]

        def block(ref, index):
            return ref[tree, index * rank : (index + 1) * rank].astype(f32)

        for k in range(3):
            entry_ref[k, pick] += block(late, k)
            exit_ref[k, pick] += block(head, k)
        final_ref[0, pick] += block(late, 3)
        out_ref[pick] += block(head, 3)
        for k in range(2):
            entry_ref[3 + k, pick] += block(model, k)
            unit_ref[k, pick] += block(early, k)
        final_ref[1, pick] += block(model, 2)
        down_ref[pick] += block(early, 2)
        return carry

    lax.fori_loop(0, early.shape[0], one_tree, 0)


def combine(picks, early, model, late, head, adapters, steps=4):
    trees, _, features = early.shape
    rank = late.shape[1] // 4
    width = head.shape[2]
    wide, narrow = features // steps, width // steps

    def taken(array, tile):
        return pl.BlockSpec((trees, array.shape[1], tile), lambda i, p: (0, 0, i))

    def given(lead, tile):
        shape = lead + (adapters, rank, tile)
        return pl.BlockSpec(shape, lambda i, p: (0,) * (len(shape) - 1) + (i,))

    def shape(lead, full):
        return jax.ShapeDtypeStruct(lead + (adapters, rank, full), f32)

    return pl.pallas_call(
        functools.partial(combine_body, rank),
        grid_spec=pltpu.PrefetchScalarGridSpec(
            num_scalar_prefetch=1,
            grid=(steps,),
            in_specs=[taken(early, wide), taken(model, wide), taken(late, wide), taken(head, narrow)],
            out_specs=[
                given((5,), wide),
                given((2,), wide),
                given((2,), wide),
                given((), wide),
                given((3,), narrow),
                given((), narrow),
            ],
        ),
        out_shape=[
            shape((5,), features),
            shape((2,), features),
            shape((2,), features),
            shape((), features),
            shape((3,), width),
            shape((), width),
        ],
        compiler_params=pltpu.CompilerParams(vmem_limit_bytes=VMEM_LIMIT),
    )(picks, early, model, late, head)


def local(
    tokens,
    cotangent,
    attention_gain,
    feed_gain,
    query_weight,
    key_weight,
    value_weight,
    output_weight,
    gate_weight,
    up_weight,
    down_weight,
    entry_maps,
    head_exits,
    unit_exits,
    output_entry,
    down_entry,
    final_exits,
    parents,
    adapter_pick,
):
    pick = adapter_pick[0]
    adapters, rank = entry_maps.shape[1], entry_maps.shape[3]
    local_rows = tokens.shape[0]
    total = local_rows * lax.axis_size("tensor")
    blocks = parents.shape[1]
    seg = total // blocks
    tables = rope_tables(blocks, seg)
    leaf_parent = (jnp.repeat(parents[0, TRUNK + BRANCHES :], seg) - TRUNK)[None, :]
    gain_one = attention_gain.astype(f32)
    gain_two = feed_gain.astype(f32)

    w_heads = lax.all_gather(
        jnp.concatenate([query_weight, key_weight, value_weight, output_weight], axis=1),
        "dp",
        axis=0,
        tiled=True,
    )

    w_units = [
        lax.all_gather(w, "dp", axis=0, tiled=True) for w in (gate_weight, up_weight, down_weight)
    ]
    entries, heads_exit, units_exit, out_entry, fall_entry, finals = picked(
        adapter_pick,
        (
            jnp.swapaxes(entry_maps, 2, 3),
            head_exits,
            unit_exits,
            jnp.swapaxes(output_entry, 1, 2)[None],
            jnp.swapaxes(down_entry, 1, 2)[None],
            final_exits,
        ),
    )
    out_entry, fall_entry = out_entry[0], fall_entry[0]

    most_one = gather_norm(tokens, gain_one)
    full_one, qkv, middle, full_two, full_cot, low_one, attended, lse, adapt_o = front(
        most_one, w_heads, cotangent, entries, heads_exit, tables, leaf_parent, out_entry, finals, tokens, gain_two, seg
    )

    grad_middle, branch, res_parts, unit_grads, model_grads = feed(
        full_two, (cotangent, full_cot), w_units, middle, units_exit, fall_entry, entries, finals, gain_two
    )
    early = jnp.concatenate(
        [unit_grads.astype(bf16), jnp.full((rank, unit_grads.shape[1]), pick).astype(bf16)]
    )
    model_low = model_grads.astype(bf16)
    branch, early, model_low = lax.optimization_barrier((branch, early, model_low))
    early = per_tree(early)
    model_sum = lax.psum(model_low, "tensor")

    grad_attended, res_own, res_right, res_left, final_grads, exit_grads = branch_back(
        branch, w_heads, finals, out_entry, res_parts, attended, adapt_o
    )
    grad_attended, res_right, res_left = lax.optimization_barrier((grad_attended, res_right, res_left))
    from_left = permute(res_right, [(0, 1), (1, 2), (2, 3)])
    from_right = permute(res_left, [(3, 2), (2, 1), (1, 0)])
    head_grads = attend_back(qkv, attended, grad_attended, lse, leaf_parent, tables, seg)
    head_grads, model_sum, from_left, from_right = lax.optimization_barrier(
        (head_grads, model_sum, from_left, from_right)
    )
    model_all = per_tree(model_sum)
    grad_tokens, late_model, late_head = tokens_back(
        head_grads, w_heads, heads_exit, entries, tokens, gain_one, grad_middle,
        full_one, low_one, final_grads, exit_grads,
    )
    result = (
        middle
        + res_own.astype(f32)
        + from_left.astype(f32)
        + from_right.astype(f32)
    ).astype(bf16)

    picks = early[:, 3 * rank, 0].astype(jnp.int32)
    grad_entries, grad_finals, grad_units, grad_down, grad_heads, grad_output = combine(
        picks, early, model_all, late_model, late_head, adapters
    )
    grad_entries = grad_entries.swapaxes(2, 3)
    grad_output = grad_output.swapaxes(1, 2)
    grad_down = grad_down.swapaxes(1, 2)
    return (
        result,
        grad_tokens,
        grad_entries,
        grad_heads,
        grad_units,
        grad_output,
        grad_down,
        grad_finals,
    )


def solution(mesh):
    in_specs = (
        P(("dp", "tensor"), None),
        P(("dp", "tensor"), None),
        P(),
        P(),
        P("dp", "tensor"),
        P("dp", "tensor"),
        P("dp", "tensor"),
        P("dp", "tensor"),
        P("dp", "tensor"),
        P("dp", "tensor"),
        P("dp", "tensor"),
        P(),
        P(None, None, None, "tensor"),
        P(None, None, None, "tensor"),
        P(None, "tensor", None),
        P(None, "tensor", None),
        P(),
        P("dp", None),
        P("dp"),
    )
    out_specs = (
        P(("dp", "tensor"), None),
        P(("dp", "tensor"), None),
        P(),
        P(None, None, None, "tensor"),
        P(None, None, None, "tensor"),
        P(None, "tensor", None),
        P(None, "tensor", None),
        P(),
    )
    return jax.shard_map(local, mesh=mesh, in_specs=in_specs, out_specs=out_specs, check_vma=False)
```

```python
import functools

import jax
import jax.numpy as jnp
import numpy as np
from jax import lax
from jax.experimental import pallas as pl
from jax.experimental.pallas import tpu as pltpu
from jax.sharding import PartitionSpec as P

HEAD_DIM = 64
TRUNK, BRANCHES = 8, 4
QT = 256
VMEM_LIMIT = 60 * 1024 * 1024
LINE = 4
MESH = pl.DeviceIdType.MESH

eps = 1e-05
theta = 130000.0
bf16, f32 = jnp.bfloat16, jnp.float32


def nn(left, right):
    return jnp.dot(left, right, preferred_element_type=f32)


def nt(left, right):
    return lax.dot_general(left, right, (((1,), (1,)), ((), ())), preferred_element_type=f32)


def tn(left, right):
    return lax.dot_general(left, right, (((0,), (0,)), ((), ())), preferred_element_type=f32)


def rope_tables(blocks, seg):
    depth = np.minimum(np.arange(blocks), TRUNK)
    depth[TRUNK + BRANCHES :] = TRUNK + 1
    position = (np.repeat(depth, seg) * seg + np.arange(blocks * seg) % seg).astype(np.float32)
    half = HEAD_DIM // 2
    freq = (np.float32(theta) ** (-np.arange(half, dtype=np.float32) / half)).astype(np.float32)
    angle = (position[:, None] * freq[None, :]).astype(np.float32)
    cosine = np.tile(np.cos(angle), (1, 4)).astype(np.float32)
    sine = np.sin(angle).astype(np.float32)
    sine = np.concatenate([-sine, sine, -sine, sine], axis=1)
    return jnp.asarray(cosine), jnp.asarray(sine)


def turn(values, cosine, sine):
    width = values.shape[1]
    reps = width // cosine.shape[1]
    if reps > 1:
        cosine = jnp.concatenate([cosine] * reps, axis=1)
        sine = jnp.concatenate([sine] * reps, axis=1)
    lane = lax.broadcasted_iota(jnp.int32, values.shape, 1)
    half = HEAD_DIM // 2
    other = jnp.where(
        lane % HEAD_DIM < half, pltpu.roll(values, width - half, 1), pltpu.roll(values, half, 1)
    )
    return values * cosine + other * sine


SIDES = (1, -1)


def far_of(place, side):
    return place if side == 1 else LINE - 1 - place


def greet(place, partners=()):
    barrier = pltpu.get_barrier_semaphore()
    for partner in partners:
        pl.semaphore_signal(barrier, inc=1, device_id={"dp": partner}, device_id_type=MESH)
    for side in SIDES:

        @pl.when(far_of(place, side) < LINE - 1)
        def _():
            pl.semaphore_signal(
                barrier, inc=1, device_id={"tensor": place + side}, device_id_type=MESH
            )

    edge = (place == 0) | (place == LINE - 1)

    @pl.when(edge)
    def _():
        pl.semaphore_wait(barrier, 1 + len(partners))

    @pl.when(jnp.logical_not(edge))
    def _():
        pl.semaphore_wait(barrier, 2 + len(partners))


def chunk_rows(chunk, rows):
    return pl.ds(chunk * rows, rows)


class Gather:
    def __init__(self, place, buf, send, recv, chunks, own=None):
        self.place, self.buf, self.sems, self.chunks = place, buf, (send, recv), chunks
        self.rows = buf.shape[1] // chunks
        self.own = own

    def copy(self, side, step, chunk, shard, target):
        rows = chunk_rows(chunk, self.rows)
        where = self.buf.at[shard, rows]
        index = 0 if side == 1 else 1
        spot = (index, step - 1, chunk)
        source = where
        if step == 1 and self.own is not None:
            source = self.own.at[rows]
        return pltpu.make_async_remote_copy(
            src_ref=source,
            dst_ref=where,
            send_sem=self.sems[0].at[spot],
            recv_sem=self.sems[1].at[spot],
            device_id={"tensor": target},
            device_id_type=MESH,
        )

    def each_send(self, step, chunk, act, least=0, most=LINE):
        for side in SIDES:
            far = far_of(self.place, side)

            @pl.when((far < LINE - 1) & (far >= step - 1) & (far >= least) & (far <= most))
            def _():
                shard = self.place - side * (step - 1)
                act(self.copy(side, step, chunk, shard, self.place + side))

    def send(self, step, chunk, least=0, most=LINE):
        self.each_send(step, chunk, lambda copy: copy.start(), least, most)

    def arrive(self, step, chunk):
        for side in SIDES:

            @pl.when(far_of(self.place, side) >= step)
            def _():
                shard = self.place - side * step
                self.copy(side, step, chunk, shard, self.place - side).wait_recv()

    def relay(self, step, chunk):
        for side in SIDES:
            far = far_of(self.place, side)

            @pl.when((far < LINE - 1) & (far >= step - 1))
            def _():
                before = self.place - side * (step - 1)
                self.copy(side, step - 1, chunk, before, self.place - side).wait_recv()
                self.copy(side, step, chunk, before, self.place + side).start()

    def close(self):
        for side in SIDES:

            @pl.when(far_of(self.place, side) == LINE - 1)
            def _():
                for step in range(1, LINE):
                    for chunk in range(self.chunks):
                        shard = self.place - side * step
                        self.copy(side, step, chunk, shard, self.place - side).wait_recv()

    def drain(self, stop=LINE, start=1):
        for step in range(start, stop):
            for chunk in range(self.chunks):
                self.each_send(step, chunk, lambda copy: copy.wait_send())


class Sum:
    def __init__(self, place, part, held, send, recv, chunks):
        self.place, self.part, self.held = place, part, held
        self.sems, self.chunks = (send, recv), chunks
        self.rows = part.shape[1] // chunks

    def copy(self, side, step, chunk, shard, target):
        rows = chunk_rows(chunk, self.rows)
        index = 0 if side == 1 else 1
        spot = (index, step - 1, chunk)
        return pltpu.make_async_remote_copy(
            src_ref=self.part.at[shard, rows],
            dst_ref=self.held.at[index, step - 1, rows],
            send_sem=self.sems[0].at[spot],
            recv_sem=self.sems[1].at[spot],
            device_id={"tensor": target},
            device_id_type=MESH,
        )

    def add(self, step, chunk):
        rows = chunk_rows(chunk, self.rows)
        for index, side in enumerate(SIDES):
            far = far_of(self.place, side)
            shard = self.place + side * (LINE - step)

            @pl.when((far >= 1) & (far <= step - 1))
            def _():
                self.copy(side, step - 1, chunk, self.place, self.place - side).wait_recv()
                self.part[shard, rows] = (
                    self.part[shard, rows].astype(f32)
                    + self.held[index, step - 2, rows].astype(f32)
                ).astype(bf16)

    def send(self, step, chunk, least=0, most=LINE):
        if step > 1 and most > 0:
            self.add(step, chunk)
        for side in SIDES:
            far = far_of(self.place, side)
            shard = self.place + side * (LINE - step)

            @pl.when((far <= step - 1) & (far >= least) & (far <= most))
            def _():
                self.copy(side, step, chunk, shard, self.place + side).start()

    def begin(self, step, chunk):
        self.send(step, chunk, most=0)

    def relay(self, step, chunk):
        self.send(step, chunk, least=1)

    def total(self, chunk, out):
        rows = chunk_rows(chunk, self.rows)
        out[rows] = self.part[self.place, rows].astype(f32)
        for index, side in enumerate(SIDES):

            @pl.when(far_of(self.place, side) >= 1)
            def _():
                self.copy(side, LINE - 1, chunk, self.place, self.place - side).wait_recv()
                out[rows] += self.held[index, LINE - 2, rows].astype(f32)

    def drain(self, stop=LINE):
        for step in range(1, stop):
            for chunk in range(self.chunks):
                for side in SIDES:
                    far = far_of(self.place, side)
                    shard = self.place + side * (LINE - step)

                    @pl.when(far <= step - 1)
                    def _():
                        self.copy(side, step, chunk, shard, self.place + side).wait_send()


def line_sems(chunks):
    return [pltpu.SemaphoreType.DMA((2, LINE - 1, chunks))] * 2


def fetch(pairs, sems):
    copies = [pltpu.make_async_copy(src, dst, sems.at[i]) for i, (src, dst) in enumerate(pairs)]
    for copy in copies:
        copy.start()
    return copies


IN_VMEM = pl.BlockSpec(memory_space=pltpu.VMEM)
IN_HBM = pl.BlockSpec(memory_space=pl.ANY)


def comm_params(number):
    return pltpu.CompilerParams(
        vmem_limit_bytes=VMEM_LIMIT, collective_id=number, has_side_effects=True
    )


def gather_norm_body(x_ref, gain_ref, buf, own, sem, send, recv):
    place = lax.axis_index("tensor")
    greet(place)
    rows = x_ref[...].astype(f32)
    rms = lax.rsqrt(jnp.mean(rows * rows, axis=1, keepdims=True) + eps)
    own[...] = (rows * rms * gain_ref[...]).astype(bf16)
    gather = Gather(place, buf, send, recv, 1, own)
    gather.send(1, 0)
    (kept,) = fetch([(own, buf.at[place])], sem)
    gather.arrive(1, 0)
    gather.send(2, 0)
    kept.wait()
    gather.arrive(2, 0)
    gather.drain(stop=LINE - 1)


def gather_norm(x, gain):
    rows, features = x.shape
    return pl.pallas_call(
        gather_norm_body,
        in_specs=[IN_VMEM, IN_VMEM],
        out_specs=IN_HBM,
        out_shape=jax.ShapeDtypeStruct((LINE, rows, features), bf16),
        scratch_shapes=[pltpu.VMEM((rows, features), bf16), pltpu.SemaphoreType.DMA((1,))]
        + line_sems(1),
        compiler_params=comm_params(0),
    )(x, gain[None, :])


def front_body(
    chunks, seg,
    x_ref, w_ref, c_ref, e_ref, a_ref, cos_ref, sin_ref, p_ref, oe_ref, f_ref, tok_ref, gain_ref,
    kept_ref, y_ref, mid_ref, n_ref, cot_ref, l_ref, att_ref, lse_ref, lo_ref,
    buf, yv, wv, wo, part, held, own, midv, xsem, wsem, ysem, nsem, msem, send, recv,
    s_send, s_recv, g_send, g_recv, c_send, c_recv,
):
    place = lax.axis_index("tensor")
    groups, total, width = y_ref.shape
    rows, rank = x_ref.shape[1], a_ref.shape[1]
    edge = (place == 0) | (place == LINE - 1)
    last = place ^ (LINE - 1)

    def passed(side):
        shard = place - side * (LINE - 2)
        index = 0 if side == 1 else 1
        return pltpu.make_async_remote_copy(
            src_ref=x_ref.at[shard],
            dst_ref=buf.at[shard],
            send_sem=send.at[index],
            recv_sem=recv.at[index],
            device_id={"tensor": place + side},
            device_id_type=MESH,
        )

    def came(side):
        index = 0 if side == 1 else 1
        return pltpu.make_async_remote_copy(
            src_ref=x_ref.at[last],
            dst_ref=buf.at[last],
            send_sem=send.at[index],
            recv_sem=recv.at[index],
            device_id={"tensor": place - side},
            device_id_type=MESH,
        )

    copies = []
    for slot in range(LINE):
        copy = pltpu.make_async_copy(x_ref.at[place ^ slot], buf.at[place ^ slot], xsem.at[slot])
        if slot < LINE - 1:
            copy.start()
        else:
            pl.when(jnp.logical_not(edge))(copy.start)
        copies.append(copy)
    load, load_out = fetch(
        [(w_ref.at[:, : groups * width], wv), (w_ref.at[:, groups * width :], wo)], wsem
    )
    greet(place)
    cots = Gather(place, cot_ref, c_send, c_recv, chunks, c_ref)
    summed = Sum(place, part, held, s_send, s_recv, chunks)
    gather = Gather(place, n_ref, g_send, g_recv, chunks, own)
    for side in SIDES:
        pl.when(far_of(place, side) == LINE - 2)(passed(side).start)
    for chunk in range(chunks):
        cots.send(1, chunk)

    for copy in copies[:-1]:
        copy.wait()
    load.wait()
    outs = []
    for slot in range(LINE):
        shard = place ^ slot
        if slot == LINE - 1:
            pl.when(jnp.logical_not(edge))(copies[slot].wait)
            for side in SIDES:
                pl.when(far_of(place, side) == LINE - 1)(came(side).wait_recv)
            kept = pltpu.make_async_copy(buf.at[last], kept_ref.at[last], xsem.at[slot])
            pl.when(edge)(kept.start)
        mine = pl.ds(pl.multiple_of(shard * rows, rows), rows)
        low = nt(buf[shard], e_ref[:groups].reshape(groups * rank, -1)).astype(bf16)
        l_ref[mine] = low
        for g in range(groups):
            band = slice(g * width, (g + 1) * width)
            value = nn(buf[shard], wv[:, band]) + nn(low[:, g * rank : (g + 1) * rank], a_ref[g])
            if g < groups - 1:
                value = turn(value, cos_ref[mine], sin_ref[mine])
            yv[g, mine] = value.astype(bf16)
            out = pltpu.make_async_copy(yv.at[g, mine], y_ref.at[g, mine], ysem.at[slot, g])
            out.start()
            outs.append(out)

    pair = 2 * HEAD_DIM

    def one_pair(j, carry):
        lanes = pl.ds(pl.multiple_of(j * pair, pair), pair)
        attend_pair(seg, yv, lanes, p_ref[...], j, att_ref, lse_ref)

        @pl.when(j == 0)
        def _():
            for chunk in range(chunks):
                cots.relay(2, chunk)

        return carry

    lax.fori_loop(0, width // pair, one_pair, 0)

    load_out.wait()
    for slot in (3, 2, 1, 0):
        shard = place ^ slot
        mine = pl.ds(pl.multiple_of(shard * rows, rows), rows)
        d = att_ref[mine]
        low = nt(d, oe_ref[...]).astype(bf16)
        lo_ref[mine] = low
        part[shard] = (nt(d, wo[...]) + nn(low, f_ref[0])).astype(bf16)
        if slot == 3:
            summed.begin(1, 0)
    for chunk in range(chunks):
        for step in (1, 2, 3):
            if chunk or step > 1:
                summed.begin(step, chunk)
    size = rows // chunks
    stores = []
    for chunk in range(chunks):
        summed.relay(2, chunk)
        summed.relay(3, chunk)
        cots.relay(3, chunk)
        summed.total(chunk, midv)
        here = chunk_rows(chunk, size)
        value = midv[here] + tok_ref[here].astype(f32)
        midv[here] = value
        rms = lax.rsqrt(jnp.mean(value * value, axis=1, keepdims=True) + eps)
        own[here] = (value * rms * gain_ref[...]).astype(bf16)
        stores.append(pltpu.make_async_copy(own.at[here], n_ref.at[place, here], nsem.at[chunk]))
        stores.append(pltpu.make_async_copy(midv.at[here], mid_ref.at[here], msem.at[chunk]))
        gather.send(1, chunk, least=1)
        for store in stores[-2:]:
            store.start()
    for chunk in range(chunks):
        gather.send(1, chunk, most=0)
    for step in (2, 3):
        for chunk in range(chunks):
            gather.relay(step, chunk)
    cots.close()
    gather.close()
    pl.when(edge)(kept.wait)
    for out in outs + stores:
        out.wait()
    for side in SIDES:
        pl.when(far_of(place, side) == LINE - 2)(passed(side).wait_send)
    summed.drain()
    gather.drain()
    cots.drain()


def front(x, weight, cot, entries, exits, tables, leaf_parent, out_entry, finals, tokens, gain, seg, chunks=4):
    _, rows, features = x.shape
    groups, rank, width = exits.shape
    total = LINE * rows
    shards = jax.ShapeDtypeStruct((LINE, rows, features), bf16)
    return pl.pallas_call(
        functools.partial(front_body, chunks, seg),
        in_specs=[IN_HBM] * 3 + [IN_VMEM] * 9,
        out_specs=[IN_HBM] * 5 + [IN_VMEM] * 4,
        out_shape=[
            shards,
            jax.ShapeDtypeStruct((groups, total, width), bf16),
            jax.ShapeDtypeStruct((rows, features), f32),
            shards,
            shards,
            jax.ShapeDtypeStruct((total, groups * rank), bf16),
            jax.ShapeDtypeStruct((total, width), bf16),
            jax.ShapeDtypeStruct((width // (2 * HEAD_DIM), 2, total), f32),
            jax.ShapeDtypeStruct((total, rank), bf16),
        ],
        scratch_shapes=[
            pltpu.VMEM((LINE, rows, features), bf16),
            pltpu.VMEM((groups, total, width), bf16),
            pltpu.VMEM((features, groups * width), bf16),
            pltpu.VMEM((features, width), bf16),
            pltpu.VMEM((LINE, rows, features), bf16),
            pltpu.VMEM((2, LINE - 1, rows, features), bf16),
            pltpu.VMEM((rows, features), bf16),
            pltpu.VMEM((rows, features), f32),
            pltpu.SemaphoreType.DMA((LINE,)),
            pltpu.SemaphoreType.DMA((2,)),
            pltpu.SemaphoreType.DMA((LINE, groups)),
            pltpu.SemaphoreType.DMA((chunks,)),
            pltpu.SemaphoreType.DMA((chunks,)),
            pltpu.SemaphoreType.DMA((2,)),
            pltpu.SemaphoreType.DMA((2,)),
        ]
        + line_sems(chunks)
        + line_sems(chunks)
        + line_sems(chunks),
        input_output_aliases={0: 0},
        compiler_params=comm_params(1),
    )(x, weight, cot, entries, exits, *tables, leaf_parent, out_entry, finals, tokens, gain[None, :])


def branch_body(
    b_ref, w_ref, e_ref, a_ref, p_ref, d_ref, lo_ref, y_ref, own_ref, right_ref, left_ref,
    final_ref, exit_ref,
    buf, part, held, wv, wsem, send, recv, s_send, s_recv,
):
    place = lax.axis_index("tensor")
    rows = b_ref.shape[0]
    load, parts = fetch([(w_ref.at[:, 3 * y_ref.shape[2] :], wv), (p_ref, part)], wsem)
    greet(place)
    buf[place] = b_ref[...]
    gather = Gather(place, buf, send, recv, 1)
    summed = Sum(place, part, held, s_send, s_recv, 1)
    gather.send(1, 0)
    parts.wait()
    summed.send(1, 0)
    load.wait()
    for slot in range(LINE):
        if slot:
            gather.arrive(slot, 0)
        if 0 < slot < LINE - 1:
            gather.send(slot + 1, 0)
        if slot == 1:
            summed.send(2, 0)
        if slot == 2:
            summed.add(3, 0)
            own_ref[...] = part[place]
            for out_ref, side in ((right_ref, 1), (left_ref, -1)):

                @pl.when(far_of(place, side) < LINE - 1)
                def _():
                    out_ref[...] = part[place + side]

                @pl.when(far_of(place, side) == LINE - 1)
                def _():
                    out_ref[...] = jnp.zeros_like(out_ref)

        shard = place ^ slot
        mine = pl.ds(pl.multiple_of(shard * rows, rows), rows)
        low = nt(buf[shard], e_ref[0])
        y_ref[0, mine] = (nn(buf[shard], wv[...]) + nn(low.astype(bf16), a_ref[...])).astype(bf16)
        final = nn(lo_ref[mine].astype(f32).T.astype(bf16), buf[shard])
        leave = nn(low.T.astype(bf16), d_ref[mine])
        final_ref[...] = final if slot == 0 else final_ref[...] + final
        exit_ref[...] = leave if slot == 0 else exit_ref[...] + leave
    gather.drain()
    summed.drain(LINE - 1)


def branch_back(branch, weight, finals, exits, parts, attended, low_out):
    rows, features = branch.shape
    rank, width = exits.shape
    return pl.pallas_call(
        branch_body,
        in_specs=[IN_VMEM, IN_HBM, IN_VMEM, IN_VMEM, IN_HBM, IN_VMEM, IN_VMEM],
        out_specs=[IN_VMEM] * 6,
        out_shape=[jax.ShapeDtypeStruct((1, LINE * rows, width), bf16)]
        + [jax.ShapeDtypeStruct((rows, features), bf16)] * 3
        + [
            jax.ShapeDtypeStruct((rank, features), f32),
            jax.ShapeDtypeStruct((rank, width), f32),
        ],
        scratch_shapes=[
            pltpu.VMEM((LINE, rows, features), bf16),
            pltpu.VMEM((LINE, rows, features), bf16),
            pltpu.VMEM((2, LINE - 1, rows, features), bf16),
            pltpu.VMEM((features, width), bf16),
            pltpu.SemaphoreType.DMA((2,)),
        ]
        + line_sems(1)
        + line_sems(1),
        compiler_params=comm_params(2),
    )(branch, weight, finals, exits, parts, attended, low_out)


def tokens_body(
    chunks, d_ref, w_ref, a_ref, e_ref, x_ref, gain_ref, mid_ref, n_ref, lone_ref, final_ref, exit_ref,
    middle_ref, own_ref, left_ref, right_ref,
    out_ref, model_ref, head_ref, res_ref,
    part, held, acc, dv, wv, midv, nv, terms, low, block, extra, wsem, send, recv, x_send, x_recv, t_send, t_recv, h_send, h_recv,
):
    place = lax.axis_index("tensor")
    tree = lax.axis_index("dp")
    trees = Trees(tree, model_ref, t_send, t_recv)
    heads = Trees(tree, head_ref, h_send, h_recv)
    groups, total, width = d_ref.shape
    rank = a_ref.shape[1]
    loads = fetch(
        [
            (d_ref, dv),
            (w_ref.at[:, : groups * width], wv),
            (n_ref, nv),
            (mid_ref, midv),
            (middle_ref, acc),
            (own_ref, terms.at[0]),
            (left_ref, terms.at[1]),
            (right_ref, terms.at[2]),
        ],
        wsem,
    )
    block[...] = jnp.zeros_like(block)
    for g in range(groups):
        block[g * rank : (g + 1) * rank, g * width : (g + 1) * width] = a_ref[g]
    greet(place, trees.partners)
    for load in loads[:2]:
        load.wait()
    rows = part.shape[1]
    summed = Sum(place, part, held, send, recv, chunks)
    gather = Gather(place, extra, x_send, x_recv, 1)
    entry = e_ref[:groups].reshape(groups * rank, -1)

    def rows_of(slot):
        shard = place ^ slot
        mine = pl.ds(pl.multiple_of(shard * rows, rows), rows)
        return shard, mine, jnp.concatenate([dv[g, mine] for g in range(groups)], axis=1)

    def lower(slot):
        _, mine, d = rows_of(slot)
        low[mine] = nt(d, block[...]).astype(bf16)

    def partial(slot):
        shard, mine, d = rows_of(slot)
        part[shard] = (nt(d, wv[...]) + nn(low[mine], entry)).astype(bf16)

    lower(3)
    partial(3)
    summed.begin(1, 0)
    summed.begin(1, 1)
    for slot in (2, 1, 0):
        lower(slot)
    for load in loads[2:]:
        load.wait()

    def turned(value):
        return value.astype(f32).T.astype(bf16)

    joined = nn(turned(low[...]), nv[...].reshape(total, -1))
    extra[place] = jnp.concatenate([joined, final_ref[...]], axis=0).astype(bf16)
    gather.send(1, 0)
    for chunk in range(2, chunks):
        summed.begin(1, chunk)
    for slot in (2, 1, 0):
        partial(slot)
    for step in (2, 3):
        for chunk in range(chunks):
            summed.begin(step, chunk)
    summed.relay(2, 0)
    summed.relay(2, 1)
    gather.arrive(1, 0)
    gather.send(2, 0)
    summed.relay(2, 2)
    low_one = turned(lone_ref[...])
    for g in range(groups):
        band = slice(g * rank, (g + 1) * rank)
        head_ref[tree, band] = nn(low_one[band], dv[g]).astype(bf16)
    head_ref[tree, groups * rank :] = exit_ref[...].astype(bf16)
    heads.send(0)
    value = acc[...] + terms[0].astype(f32)
    for index, side in enumerate(SIDES):
        value += jnp.where(far_of(place, side) > 0, terms[index + 1].astype(f32), 0.0)
    res_ref[...] = value.astype(bf16)
    summed.relay(2, 3)
    gather.arrive(2, 0)
    gather.send(3, 0)
    heads.advance(1)
    summed.relay(3, 0)
    gather.arrive(3, 0)
    model_ref[tree] = functools.reduce(
        jnp.add, [extra[shard].astype(f32) for shard in range(LINE)]
    ).astype(bf16)
    trees.send(0)
    heads.advance(2)
    summed.relay(3, 1)
    trees.advance(1)
    summed.relay(3, 2)
    summed.relay(3, 3)
    trees.advance(2)
    size = rows // chunks

    def finish(chunk):
        finish_tokens(summed, chunk, size, acc, x_ref, gain_ref, midv, out_ref)

    finish(0)
    finish(1)
    for number in range(3, trees.rounds):
        trees.advance(number)
        heads.advance(number)
    finish(2)
    finish(3)
    for blocks in (trees, heads):
        blocks.arrive(blocks.rounds - 1)
        blocks.drain()
    summed.drain()
    gather.drain()


class Trees:
    def __init__(self, tree, ref, send, recv):
        self.tree, self.ref, self.sems = tree, ref, (send, recv)
        self.rounds = ref.shape[0].bit_length() - 1
        self.partners = [self.partner(number) for number in range(self.rounds)]

    def partner(self, number):
        size = 1 << number
        return self.tree + size - 2 * size * ((self.tree // size) % 2)

    def copy(self, number, owner):
        size = 1 << number
        here = pl.ds((owner // size) * size, size)
        return pltpu.make_async_remote_copy(
            src_ref=self.ref.at[here],
            dst_ref=self.ref.at[here],
            send_sem=self.sems[0].at[number],
            recv_sem=self.sems[1].at[number],
            device_id={"dp": self.partner(number)},
            device_id_type=MESH,
        )

    def send(self, number):
        self.copy(number, self.tree).start()

    def arrive(self, number):
        self.copy(number, self.partner(number)).wait_recv()

    def advance(self, number):
        if number < self.rounds:
            self.arrive(number - 1)
            self.send(number)

    def drain(self):
        for number in range(self.rounds):
            self.copy(number, self.tree).wait_send()


def finish_tokens(summed, chunk, size, acc, x_ref, gain_ref, mid_ref, out_ref):
    summed.total(chunk, acc)
    here = chunk_rows(chunk, size)
    rows = x_ref[here].astype(f32)
    rms = lax.rsqrt(jnp.mean(rows * rows, axis=1, keepdims=True) + eps)
    scaled = acc[here] * gain_ref[...]
    mean = jnp.mean(scaled * rows, axis=1, keepdims=True)
    out_ref[here] = (mid_ref[here] + rms * (scaled - rows * (rms * rms) * mean)).astype(bf16)


def tokens_back(
    head_grads, weight, exits, entries, x, gain, grad_middle, normed, low_one, final_grads, exit_grads,
    middle, own, from_left, from_right,
):
    chunks = LINE
    rows, features = x.shape
    groups, total, width = head_grads.shape
    rank = exits.shape[1]
    deep = (groups + 1) * rank
    trees = lax.axis_size("dp")
    sems = pltpu.SemaphoreType.DMA((trees.bit_length() - 1,))
    return pl.pallas_call(
        functools.partial(tokens_body, chunks),
        in_specs=[IN_HBM, IN_HBM] + [IN_VMEM] * 4 + [IN_HBM] * 2 + [IN_VMEM] * 3 + [IN_HBM] * 4,
        out_specs=[IN_VMEM] * 4,
        out_shape=[
            jax.ShapeDtypeStruct((rows, features), bf16),
            jax.ShapeDtypeStruct((trees, deep, features), bf16),
            jax.ShapeDtypeStruct((trees, deep, width), bf16),
            jax.ShapeDtypeStruct((rows, features), bf16),
        ],
        scratch_shapes=[
            pltpu.VMEM((LINE, rows, features), bf16),
            pltpu.VMEM((2, LINE - 1, rows, features), bf16),
            pltpu.VMEM((rows, features), f32),
            pltpu.VMEM((groups, total, width), bf16),
            pltpu.VMEM((features, groups * width), bf16),
            pltpu.VMEM((rows, features), f32),
            pltpu.VMEM((LINE, rows, features), bf16),
            pltpu.VMEM((3, rows, features), bf16),
            pltpu.VMEM((total, groups * rank), bf16),
            pltpu.VMEM((groups * rank, groups * width), bf16),
            pltpu.VMEM((LINE, deep, features), bf16),
            pltpu.SemaphoreType.DMA((8,)),
        ]
        + line_sems(chunks)
        + line_sems(1)
        + [sems] * 4,
        compiler_params=comm_params(3),
    )(
        head_grads, weight, exits, entries, x, gain[None, :], grad_middle, normed,
        low_one, final_grads, exit_grads, middle, own, from_left, from_right,
    )


def tree_tiles(seg, rows, parent_row):
    trunk = TRUNK * seg
    leaves = trunk + BRANCHES * seg
    key = lax.broadcasted_iota(jnp.int32, (QT, QT), 0)
    query = lax.broadcasted_iota(jnp.int32, (QT, QT), 1)
    causal = key <= query
    own = causal & (key // seg == query // seg)
    tiles = []
    for start in range(0, trunk, QT):
        pieces = [(0, start, None)] if start else []
        tiles.append((start, pieces + [(start, QT, causal)]))
    tiles.append((trunk, [(0, trunk, None), (trunk, QT, own)]))
    branch = lax.broadcasted_iota(jnp.int32, (BRANCHES * seg, QT), 0) // seg
    for start in range(leaves, rows, QT):
        mine = branch == parent_row[:, start - leaves : start - leaves + QT]
        tiles.append(
            (start, [(0, trunk, None), (trunk, BRANCHES * seg, mine), (start, QT, own)])
        )
    return tiles


def attend_pair(seg, qkv_ref, lanes, parent_row, pair, o_ref, lse_ref):
    rows = qkv_ref.shape[1]
    value_t = qkv_ref[2, :, lanes].T
    lane = lax.broadcasted_iota(jnp.int32, (QT, 2 * HEAD_DIM), 1)
    for start, pieces in tree_tiles(seg, rows, parent_row):
        query = qkv_ref[0, start : start + QT, lanes] * bf16(HEAD_DIM**-0.5)
        outs = []
        for h in range(2):
            own_query = jnp.where(lane // HEAD_DIM == h, query, bf16(0))
            scores = []
            for k0, count, mask in pieces:
                s = nt(qkv_ref[1, k0 : k0 + count, lanes], own_query)
                scores.append(s if mask is None else jnp.where(mask, s, -1e30))
            top = functools.reduce(
                jnp.maximum, [jnp.max(s, axis=0, keepdims=True) for s in scores]
            )
            summed, out = 0.0, 0.0
            for (k0, count, _), s in zip(pieces, scores):
                weights = jnp.exp(s - top)
                summed += jnp.sum(weights, axis=0, keepdims=True)
                out += nn(
                    value_t[h * HEAD_DIM : (h + 1) * HEAD_DIM, k0 : k0 + count],
                    weights.astype(bf16),
                )
            outs.append(out / summed)
            lse_ref[pair, h : h + 1, start : start + QT] = top + jnp.log(summed)
        o_ref[start : start + QT, lanes] = jnp.concatenate(outs, axis=0).T.astype(bf16)


def attend_back_body(
    seg, q_ref, k_ref, v_ref, o_ref, g_ref, lse_ref, p_ref, cos_ref, sin_ref, right_ref, left_ref,
    d_ref, from_left_ref, from_right_ref, dq_t, dk, dv, send, recv,
):
    place = lax.axis_index("tensor")

    def exchange(side, target):
        index = 0 if side == 1 else 1
        return pltpu.make_async_remote_copy(
            src_ref=(right_ref, left_ref)[index],
            dst_ref=(from_left_ref, from_right_ref)[index],
            send_sem=send.at[index],
            recv_sem=recv.at[index],
            device_id={"tensor": target},
            device_id_type=MESH,
        )

    @pl.when(pl.program_id(0) == 0)
    def _():
        greet(place)
        for side in SIDES:
            pl.when(far_of(place, side) < LINE - 1)(exchange(side, place + side).start)

    rows = q_ref.shape[1]
    scale = bf16(HEAD_DIM**-0.5)
    key_t = k_ref[0].T
    weighed_t = (g_ref[0].astype(f32) * o_ref[...].astype(f32)).T
    lane = lax.broadcasted_iota(jnp.int32, (QT, 2 * HEAD_DIM), 1)
    dk[...] = jnp.zeros_like(dk)
    dv[...] = jnp.zeros_like(dv)
    for start, pieces in tree_tiles(seg, rows, p_ref[...]):
        query = q_ref[0, start : start + QT] * scale
        grad = g_ref[0, start : start + QT]
        for h in range(2):
            mine = lane // HEAD_DIM == h
            own_query = jnp.where(mine, query, bf16(0))
            own_grad = jnp.where(mine, grad, bf16(0))
            band = slice(h * HEAD_DIM, (h + 1) * HEAD_DIM)
            delta = jnp.sum(weighed_t[band, start : start + QT], axis=0, keepdims=True)
            lse = lse_ref[0, h : h + 1, start : start + QT]
            grad_q = 0.0
            for k0, count, mask in pieces:
                probs = jnp.exp(nt(k_ref[0, k0 : k0 + count], own_query) - lse)
                if mask is not None:
                    probs = jnp.where(mask, probs, 0.0)
                grad_probs = nt(v_ref[0, k0 : k0 + count], own_grad)
                grad_scores = (probs * (grad_probs - delta)).astype(bf16)
                dk[k0 : k0 + count] += nn(grad_scores, own_query)
                dv[k0 : k0 + count] += nn(probs.astype(bf16), own_grad)
                grad_q += nn(key_t[band, k0 : k0 + count], grad_scores)
            dq_t[band, start : start + QT] = grad_q
    cosine, sine = cos_ref[...], -sin_ref[...]
    d_ref[0] = turn(dq_t[...].T * HEAD_DIM**-0.5, cosine, sine).astype(bf16)
    d_ref[1] = turn(dk[...], cosine, sine).astype(bf16)
    d_ref[2] = dv[...].astype(bf16)

    @pl.when(pl.program_id(0) == pl.num_programs(0) - 1)
    def _():
        for side in SIDES:
            pl.when(far_of(place, side) < LINE - 1)(exchange(side, place + side).wait_send)
            pl.when(far_of(place, side) > 0)(exchange(side, place - side).wait_recv)


def attend_back(qkv, attended, grad, lse, leaf_parent, tables, seg, right, left):
    _, rows, width = qkv.shape
    pairs = width // (2 * HEAD_DIM)
    pair = 2 * HEAD_DIM
    return pl.pallas_call(
        functools.partial(attend_back_body, seg),
        grid=(pairs,),
        in_specs=[pl.BlockSpec((1, rows, pair), lambda j, g=g: (g, 0, j)) for g in range(3)]
        + [
            pl.BlockSpec((rows, pair), lambda j: (0, j)),
            pl.BlockSpec((1, rows, pair), lambda j: (0, 0, j)),
            pl.BlockSpec((1, 2, rows), lambda j: (j, 0, 0)),
            pl.BlockSpec(leaf_parent.shape, lambda j: (0, 0)),
            pl.BlockSpec((rows, pair), lambda j: (0, 0)),
            pl.BlockSpec((rows, pair), lambda j: (0, 0)),
            IN_HBM,
            IN_HBM,
        ],
        out_specs=[pl.BlockSpec((3, rows, pair), lambda j: (0, 0, j)), IN_HBM, IN_HBM],
        out_shape=[
            jax.ShapeDtypeStruct((3, rows, width), bf16),
            jax.ShapeDtypeStruct(right.shape, bf16),
            jax.ShapeDtypeStruct(left.shape, bf16),
        ],
        scratch_shapes=[
            pltpu.VMEM((pair, rows), f32),
            pltpu.VMEM((rows, pair), f32),
            pltpu.VMEM((rows, pair), f32),
            pltpu.SemaphoreType.DMA((2,)),
            pltpu.SemaphoreType.DMA((2,)),
        ],
        compiler_params=comm_params(4),
    )(qkv, qkv, qkv, attended, grad, lse, leaf_parent, *tables, right, left)


def feed_body(
    rank, tile, chunks,
    n_ref, c_ref, far_ref, wg_ref, wu_ref, wd_ref, mid_ref,
    pick_ref, xu_in, xd_in, e_in, f_in, gain_ref,
    grad_ref, low_grad_ref, res_ref, unit_out, model_out,
    unit_ref, model_ref, x_ref, e_ref, f_ref, midv, nbuf, cbuf, wbuf, low, low_t, half_t, acc_res, acc_back, acc_low,
    part, held, resv, nsem, csem, wsem, rsem, msem, send, recv,
):
    place = lax.axis_index("tensor")
    units = unit_ref.shape[1]
    tiles = units // tile
    rows = part.shape[1]
    half = rows // 2
    summed = Sum(place, part, held, send, recv, chunks)

    def load_rows(order, act):
        into = order % 2
        shard = place ^ (LINE - 1 - order)
        act(pltpu.make_async_copy(n_ref.at[shard], nbuf.at[into], nsem.at[into]))

        def take(source):
            act(pltpu.make_async_copy(source, cbuf.at[into], csem.at[into]))

        pl.when(order == LINE - 1)(lambda: take(c_ref))
        pl.when(order < LINE - 1)(lambda: take(far_ref.at[shard]))

    def load_weights(index, into, act):
        columns = pl.ds(pl.multiple_of(index * tile, tile), tile)
        for k, w_ref in enumerate((wg_ref, wu_ref, wd_ref)):
            act(pltpu.make_async_copy(w_ref.at[:, columns], wbuf.at[into, k], wsem.at[into, k]))

    def start(copy):
        copy.start()

    def wait(copy):
        copy.wait()

    load_rows(jnp.int32(0), start)
    load_weights(0, 0, start)
    (load_middle,) = fetch([(mid_ref, midv)], msem)
    for padded in (x_ref, e_ref, f_ref):
        padded[...] = jnp.zeros_like(padded)
    x_ref[0, :rank] = xu_in[0]
    x_ref[1, rank : 2 * rank] = xu_in[1]
    x_ref[2, 2 * rank :] = xd_in[...]
    e_ref[: 2 * rank] = e_in[3:].reshape(2 * rank, -1)
    f_ref[2 * rank :] = f_in[1]
    unit_ref[...] = jnp.zeros_like(unit_ref)
    model_ref[...] = jnp.zeros_like(model_ref)
    greet(place)

    def one_block(n_rows, c_rows, count, turned, stage0, shard, here):
        first = nt(n_rows(), e_ref[...]) + nt(c_rows(), f_ref[...])
        low[:count] = first.astype(bf16)
        turned[...] = first.T.astype(bf16)
        acc_res[:count] = jnp.zeros((count, acc_res.shape[1]), f32)
        acc_back[:count] = jnp.zeros((count, acc_back.shape[1]), f32)
        acc_low[:count] = jnp.zeros((count, acc_low.shape[1]), f32)

        def one_tile(index, carry):
            stage = stage0 + index
            at = stage % 2
            load_weights(index, at, wait)

            @pl.when(stage < (LINE + 1) * tiles - 1)
            def _():
                load_weights((index + 1) % tiles, 1 - at, start)

            columns = pl.ds(pl.multiple_of(index * tile, tile), tile)
            x_gate, x_rise, x_fall = x_ref[0, :, columns], x_ref[1, :, columns], x_ref[2, :, columns]
            gate = nn(n_rows(), wbuf[at, 0]) + nn(low[:count], x_gate)
            rise = nn(n_rows(), wbuf[at, 1]) + nn(low[:count], x_rise)
            grad_hidden = nn(c_rows(), wbuf[at, 2]) + nn(low[:count], x_fall)
            sigmoid = jax.nn.sigmoid(gate)
            silu = gate * sigmoid
            hidden = (silu * rise).astype(bf16)
            grad_gate = (grad_hidden * rise * sigmoid * (1.0 + gate * (1.0 - sigmoid))).astype(bf16)
            grad_rise = (grad_hidden * silu).astype(bf16)
            acc_back[:count] += nt(grad_gate, wbuf[at, 0]) + nt(grad_rise, wbuf[at, 1])
            acc_res[:count] += nt(hidden, wbuf[at, 2])
            acc_low[:count] += nt(grad_gate, x_gate) + nt(grad_rise, x_rise) + nt(hidden, x_fall)
            unit_ref[:rank, columns] += nn(turned[:rank], grad_gate)
            unit_ref[rank : 2 * rank, columns] += nn(turned[rank : 2 * rank], grad_rise)
            unit_ref[2 * rank :, columns] += nn(turned[2 * rank : 3 * rank], hidden)
            return carry

        lax.fori_loop(0, tiles, one_tile, 0)
        joined = acc_low[:count].astype(bf16)
        joined_t = acc_low[:count].T.astype(bf16)
        part[shard, here] = (acc_back[:count] + nn(joined, e_ref[...])).astype(bf16)
        return joined, joined_t

    def model_grads(joined_t, n_rows, c_rows):
        model_ref[: 2 * rank] += nn(joined_t[: 2 * rank], n_rows())
        model_ref[2 * rank :] += nn(joined_t[2 * rank : 3 * rank], c_rows())

    load_rows(jnp.int32(0), wait)
    load_rows(jnp.int32(1), start)

    def one_half(number, carry):
        here = pl.ds(pl.multiple_of(number * half, half), half)

        def n_rows():
            return nbuf[0, here]

        def c_rows():
            return cbuf[0, here]

        joined, joined_t = one_block(
            n_rows, c_rows, half, half_t, number * tiles, place ^ (LINE - 1), here
        )
        for which in range(2):

            @pl.when(number == which)
            def _():
                for chunk in range(which * chunks // 2, (which + 1) * chunks // 2):
                    summed.begin(1, chunk)

        resv[here] = (acc_res[:half] + nn(joined, f_ref[...])).astype(bf16)
        model_grads(joined_t, n_rows, c_rows)
        return carry

    lax.fori_loop(0, 2, one_half, 0)
    pltpu.make_async_copy(resv, res_ref.at[place ^ (LINE - 1)], rsem.at[0]).start()

    def one_shard(order, carry):
        into = order % 2
        shard = place ^ (LINE - 1 - order)
        load_rows(order, wait)

        @pl.when(order < LINE - 1)
        def _():
            load_rows(order + 1, start)

        def n_rows():
            return nbuf[into]

        def c_rows():
            return cbuf[into]

        joined, joined_t = one_block(
            n_rows, c_rows, rows, low_t, (order + 1) * tiles, shard, slice(0, rows)
        )
        for step in (2, 3):

            @pl.when(order == step - 1)
            def _():
                for chunk in range(chunks):
                    summed.send(step, chunk)

        pltpu.make_async_copy(resv, res_ref.at[shard], rsem.at[0]).wait()
        resv[...] = (acc_res[...] + nn(joined, f_ref[...])).astype(bf16)
        pltpu.make_async_copy(resv, res_ref.at[shard], rsem.at[0]).start()
        model_grads(joined_t, n_rows, c_rows)
        return carry

    lax.fori_loop(1, LINE, one_shard, 0)
    unit_out[: 3 * rank] = unit_ref[...].astype(bf16)
    unit_out[3 * rank :] = jnp.full((rank, units), pick_ref[0, 0], f32).astype(bf16)
    model_out[...] = model_ref[...].astype(bf16)
    size = rows // chunks
    last = (LINE - 1) % 2
    load_middle.wait()
    for chunk in range(chunks):
        summed.total(chunk, acc_back)
        here = chunk_rows(chunk, size)
        middle = midv[here]
        rms = lax.rsqrt(jnp.mean(middle * middle, axis=1, keepdims=True) + eps)
        scaled = acc_back[here] * gain_ref[...]
        mean = jnp.mean(scaled * middle, axis=1, keepdims=True)
        grad = cbuf[last, here].astype(f32) + rms * (scaled - middle * (rms * rms) * mean)
        grad_ref[here] = grad
        low_grad_ref[here] = grad.astype(bf16)
    pltpu.make_async_copy(resv, res_ref.at[place], rsem.at[0]).wait()
    summed.drain()


def feed(normed, cots, weights, middle, pick, units_exit, fall_entry, entries, finals, gain, tile=512, chunks=4):
    _, rows, features = normed.shape
    units = weights[0].shape[1]
    rank = fall_entry.shape[0]
    return pl.pallas_call(
        functools.partial(feed_body, rank, tile, chunks),
        in_specs=[IN_HBM] * 7 + [pl.BlockSpec(memory_space=pltpu.SMEM)] + [IN_VMEM] * 5,
        out_specs=[IN_VMEM, IN_VMEM, IN_HBM, IN_VMEM, IN_VMEM],
        out_shape=[
            jax.ShapeDtypeStruct((rows, features), f32),
            jax.ShapeDtypeStruct((rows, features), bf16),
            jax.ShapeDtypeStruct((LINE, rows, features), bf16),
            jax.ShapeDtypeStruct((4 * rank, units), bf16),
            jax.ShapeDtypeStruct((3 * rank, features), bf16),
        ],
        scratch_shapes=[
            pltpu.VMEM((3 * rank, units), f32),
            pltpu.VMEM((3 * rank, features), f32),
            pltpu.VMEM((3, 3 * rank, units), bf16),
            pltpu.VMEM((3 * rank, features), bf16),
            pltpu.VMEM((3 * rank, features), bf16),
            pltpu.VMEM((rows, features), f32),
            pltpu.VMEM((2, rows, features), bf16),
            pltpu.VMEM((2, rows, features), bf16),
            pltpu.VMEM((2, 3, features, tile), bf16),
            pltpu.VMEM((rows, 3 * rank), bf16),
            pltpu.VMEM((3 * rank, rows), bf16),
            pltpu.VMEM((3 * rank, rows // 2), bf16),
            pltpu.VMEM((rows, features), f32),
            pltpu.VMEM((rows, features), f32),
            pltpu.VMEM((rows, 3 * rank), f32),
            pltpu.VMEM((LINE, rows, features), bf16),
            pltpu.VMEM((2, LINE - 1, rows, features), bf16),
            pltpu.VMEM((rows, features), bf16),
            pltpu.SemaphoreType.DMA((2,)),
            pltpu.SemaphoreType.DMA((2,)),
            pltpu.SemaphoreType.DMA((2, 3)),
            pltpu.SemaphoreType.DMA((1,)),
            pltpu.SemaphoreType.DMA((1,)),
        ]
        + line_sems(chunks),
        compiler_params=comm_params(5),
    )(normed, *cots, *weights, middle, pick, units_exit, fall_entry, entries, finals, gain[None, :])


def pick_body(pick_ref, *refs):
    count = len(refs) // 2
    for source, target in zip(refs[:count], refs[count:]):
        target[...] = source[...].reshape(target.shape)


def picked(pick, arrays):
    shapes = [a.shape[:1] + a.shape[2:] for a in arrays]
    return pl.pallas_call(
        pick_body,
        grid_spec=pltpu.PrefetchScalarGridSpec(
            num_scalar_prefetch=1,
            grid=(1,),
            in_specs=[
                pl.BlockSpec(a.shape[:1] + (1,) + a.shape[2:], lambda i, p: (0, p[0], 0, 0)) for a in arrays
            ],
            out_specs=[pl.BlockSpec(shape, lambda i, p: (0, 0, 0)) for shape in shapes],
        ),
        out_shape=[jax.ShapeDtypeStruct(shape, bf16) for shape in shapes],
    )(pick, *arrays)


def per_tree(block):
    return lax.all_gather(block, "dp", axis=0, tiled=False)


def combine_body(rank, pick_ref, early, model, late, head, entry_ref, final_ref, unit_ref, down_ref, exit_ref, out_ref):
    for ref in (entry_ref, final_ref, unit_ref, down_ref, exit_ref, out_ref):
        ref[...] = jnp.zeros_like(ref)

    def one_tree(tree, carry):
        pick = pick_ref[tree]

        def block(ref, index):
            return ref[tree, index * rank : (index + 1) * rank].astype(f32)

        for k in range(3):
            entry_ref[k, pick] += block(late, k)
            exit_ref[k, pick] += block(head, k)
        final_ref[0, pick] += block(late, 3)
        out_ref[pick] += block(head, 3)
        for k in range(2):
            entry_ref[3 + k, pick] += block(model, k)
            unit_ref[k, pick] += block(early, k)
        final_ref[1, pick] += block(model, 2)
        down_ref[pick] += block(early, 2)
        return carry

    lax.fori_loop(0, early.shape[0], one_tree, 0)


def combine(picks, early, model, late, head, adapters, steps=4):
    trees, _, features = early.shape
    rank = late.shape[1] // 4
    width = head.shape[2]
    wide, narrow = features // steps, width // steps

    def taken(array, tile):
        return pl.BlockSpec((trees, array.shape[1], tile), lambda i, p: (0, 0, i))

    def given(lead, tile):
        shape = lead + (adapters, rank, tile)
        return pl.BlockSpec(shape, lambda i, p: (0,) * (len(shape) - 1) + (i,))

    def shape(lead, full):
        return jax.ShapeDtypeStruct(lead + (adapters, rank, full), f32)

    return pl.pallas_call(
        functools.partial(combine_body, rank),
        grid_spec=pltpu.PrefetchScalarGridSpec(
            num_scalar_prefetch=1,
            grid=(steps,),
            in_specs=[taken(early, wide), taken(model, wide), taken(late, wide), taken(head, narrow)],
            out_specs=[
                given((5,), wide),
                given((2,), wide),
                given((2,), wide),
                given((), wide),
                given((3,), narrow),
                given((), narrow),
            ],
        ),
        out_shape=[
            shape((5,), features),
            shape((2,), features),
            shape((2,), features),
            shape((), features),
            shape((3,), width),
            shape((), width),
        ],
        compiler_params=pltpu.CompilerParams(vmem_limit_bytes=VMEM_LIMIT),
    )(picks, early, model, late, head)


def local(
    tokens,
    cotangent,
    attention_gain,
    feed_gain,
    query_weight,
    key_weight,
    value_weight,
    output_weight,
    gate_weight,
    up_weight,
    down_weight,
    entry_maps,
    head_exits,
    unit_exits,
    output_entry,
    down_entry,
    final_exits,
    parents,
    adapter_pick,
):
    adapters, rank = entry_maps.shape[1], entry_maps.shape[3]
    local_rows = tokens.shape[0]
    total = local_rows * lax.axis_size("tensor")
    blocks = parents.shape[1]
    seg = total // blocks
    tables = rope_tables(blocks, seg)
    leaf_parent = (jnp.repeat(parents[0, TRUNK + BRANCHES :], seg) - TRUNK)[None, :]
    gain_one = attention_gain.astype(f32)
    gain_two = feed_gain.astype(f32)

    w_heads = lax.all_gather(
        jnp.concatenate([query_weight, key_weight, value_weight, output_weight], axis=1),
        "dp",
        axis=0,
        tiled=True,
    )

    w_units = [
        lax.all_gather(w, "dp", axis=0, tiled=True) for w in (gate_weight, up_weight, down_weight)
    ]
    entries, heads_exit, units_exit, out_entry, fall_entry, finals = picked(
        adapter_pick,
        (
            jnp.swapaxes(entry_maps, 2, 3),
            head_exits,
            unit_exits,
            jnp.swapaxes(output_entry, 1, 2)[None],
            jnp.swapaxes(down_entry, 1, 2)[None],
            final_exits,
        ),
    )
    out_entry, fall_entry = out_entry[0], fall_entry[0]

    most_one = gather_norm(tokens, gain_one)
    full_one, qkv, middle, full_two, full_cot, low_one, attended, lse, adapt_o = front(
        most_one, w_heads, cotangent, entries, heads_exit, tables, leaf_parent, out_entry, finals, tokens, gain_two, seg
    )

    grad_middle, branch, res_parts, early, model_low = feed(
        full_two, (cotangent, full_cot), w_units, middle, adapter_pick.astype(f32)[None, :],
        units_exit, fall_entry, entries, finals, gain_two,
    )
    early = per_tree(early)
    model_sum = lax.psum(model_low, "tensor")

    grad_attended, res_own, res_right, res_left, final_grads, exit_grads = branch_back(
        branch, w_heads, finals, out_entry, res_parts, attended, adapt_o
    )
    head_grads, from_left, from_right = attend_back(
        qkv, attended, grad_attended, lse, leaf_parent, tables, seg, res_right, res_left
    )
    head_grads, model_sum = lax.optimization_barrier((head_grads, model_sum))
    model_all = per_tree(model_sum)
    grad_tokens, late_model, late_head, result = tokens_back(
        head_grads, w_heads, heads_exit, entries, tokens, gain_one, grad_middle,
        full_one, low_one, final_grads, exit_grads, middle, res_own, from_left, from_right,
    )

    picks = early[:, 3 * rank, 0].astype(jnp.int32)
    grad_entries, grad_finals, grad_units, grad_down, grad_heads, grad_output = combine(
        picks, early, model_all, late_model, late_head, adapters
    )
    grad_entries = grad_entries.swapaxes(2, 3)
    grad_output = grad_output.swapaxes(1, 2)
    grad_down = grad_down.swapaxes(1, 2)
    return (
        result,
        grad_tokens,
        grad_entries,
        grad_heads,
        grad_units,
        grad_output,
        grad_down,
        grad_finals,
    )


def solution(mesh):
    in_specs = (
        P(("dp", "tensor"), None),
        P(("dp", "tensor"), None),
        P(),
        P(),
        P("dp", "tensor"),
        P("dp", "tensor"),
        P("dp", "tensor"),
        P("dp", "tensor"),
        P("dp", "tensor"),
        P("dp", "tensor"),
        P("dp", "tensor"),
        P(),
        P(None, None, None, "tensor"),
        P(None, None, None, "tensor"),
        P(None, "tensor", None),
        P(None, "tensor", None),
        P(),
        P("dp", None),
        P("dp"),
    )
    out_specs = (
        P(("dp", "tensor"), None),
        P(("dp", "tensor"), None),
        P(),
        P(None, None, None, "tensor"),
        P(None, None, None, "tensor"),
        P(None, "tensor", None),
        P(None, "tensor", None),
        P(),
    )
    return jax.shard_map(local, mesh=mesh, in_specs=in_specs, out_specs=out_specs, check_vma=False)
```

```python
import functools

import jax
import jax.numpy as jnp
import numpy as np
from jax import lax
from jax.experimental import pallas as pl
from jax.experimental.pallas import tpu as pltpu
from jax.sharding import PartitionSpec as P

HEAD_DIM = 64
TRUNK, BRANCHES = 8, 4
QT = 256
VMEM_LIMIT = 60 * 1024 * 1024
LINE = 4
MESH = pl.DeviceIdType.MESH

eps = 1e-05
theta = 130000.0
bf16, f32 = jnp.bfloat16, jnp.float32


def nn(left, right):
    return jnp.dot(left, right, preferred_element_type=f32)


def nt(left, right):
    return lax.dot_general(left, right, (((1,), (1,)), ((), ())), preferred_element_type=f32)


def tn(left, right):
    return lax.dot_general(left, right, (((0,), (0,)), ((), ())), preferred_element_type=f32)


def rope_tables(blocks, seg):
    depth = np.minimum(np.arange(blocks), TRUNK)
    depth[TRUNK + BRANCHES :] = TRUNK + 1
    position = (np.repeat(depth, seg) * seg + np.arange(blocks * seg) % seg).astype(np.float32)
    half = HEAD_DIM // 2
    freq = (np.float32(theta) ** (-np.arange(half, dtype=np.float32) / half)).astype(np.float32)
    angle = (position[:, None] * freq[None, :]).astype(np.float32)
    cosine = np.tile(np.cos(angle), (1, 4)).astype(np.float32)
    sine = np.sin(angle).astype(np.float32)
    sine = np.concatenate([-sine, sine, -sine, sine], axis=1)
    return jnp.asarray(cosine), jnp.asarray(sine)


def turn(values, cosine, sine):
    width = values.shape[1]
    reps = width // cosine.shape[1]
    if reps > 1:
        cosine = jnp.concatenate([cosine] * reps, axis=1)
        sine = jnp.concatenate([sine] * reps, axis=1)
    lane = lax.broadcasted_iota(jnp.int32, values.shape, 1)
    half = HEAD_DIM // 2
    other = jnp.where(
        lane % HEAD_DIM < half, pltpu.roll(values, width - half, 1), pltpu.roll(values, half, 1)
    )
    return values * cosine + other * sine


SIDES = (1, -1)


def far_of(place, side):
    return place if side == 1 else LINE - 1 - place


def greet(place, partners=()):
    barrier = pltpu.get_barrier_semaphore()
    for partner in partners:
        pl.semaphore_signal(barrier, inc=1, device_id={"dp": partner}, device_id_type=MESH)
    for side in SIDES:

        @pl.when(far_of(place, side) < LINE - 1)
        def _():
            pl.semaphore_signal(
                barrier, inc=1, device_id={"tensor": place + side}, device_id_type=MESH
            )

    edge = (place == 0) | (place == LINE - 1)

    @pl.when(edge)
    def _():
        pl.semaphore_wait(barrier, 1 + len(partners))

    @pl.when(jnp.logical_not(edge))
    def _():
        pl.semaphore_wait(barrier, 2 + len(partners))


def chunk_rows(chunk, rows):
    return pl.ds(chunk * rows, rows)


class Gather:
    def __init__(self, place, buf, send, recv, chunks, own=None):
        self.place, self.buf, self.sems, self.chunks = place, buf, (send, recv), chunks
        self.rows = buf.shape[1] // chunks
        self.own = own

    def copy(self, side, step, chunk, shard, target):
        rows = chunk_rows(chunk, self.rows)
        where = self.buf.at[shard, rows]
        index = 0 if side == 1 else 1
        spot = (index, step - 1, chunk)
        source = where
        if step == 1 and self.own is not None:
            source = self.own.at[rows]
        return pltpu.make_async_remote_copy(
            src_ref=source,
            dst_ref=where,
            send_sem=self.sems[0].at[spot],
            recv_sem=self.sems[1].at[spot],
            device_id={"tensor": target},
            device_id_type=MESH,
        )

    def each_send(self, step, chunk, act, least=0, most=LINE):
        for side in SIDES:
            far = far_of(self.place, side)

            @pl.when((far < LINE - 1) & (far >= step - 1) & (far >= least) & (far <= most))
            def _():
                shard = self.place - side * (step - 1)
                act(self.copy(side, step, chunk, shard, self.place + side))

    def send(self, step, chunk, least=0, most=LINE):
        self.each_send(step, chunk, lambda copy: copy.start(), least, most)

    def arrive(self, step, chunk):
        for side in SIDES:

            @pl.when(far_of(self.place, side) >= step)
            def _():
                shard = self.place - side * step
                self.copy(side, step, chunk, shard, self.place - side).wait_recv()

    def relay(self, step, chunk):
        for side in SIDES:
            far = far_of(self.place, side)

            @pl.when((far < LINE - 1) & (far >= step - 1))
            def _():
                before = self.place - side * (step - 1)
                self.copy(side, step - 1, chunk, before, self.place - side).wait_recv()
                self.copy(side, step, chunk, before, self.place + side).start()

    def close(self):
        for side in SIDES:

            @pl.when(far_of(self.place, side) == LINE - 1)
            def _():
                for step in range(1, LINE):
                    for chunk in range(self.chunks):
                        shard = self.place - side * step
                        self.copy(side, step, chunk, shard, self.place - side).wait_recv()

    def drain(self, stop=LINE, start=1):
        for step in range(start, stop):
            for chunk in range(self.chunks):
                self.each_send(step, chunk, lambda copy: copy.wait_send())


class Sum:
    def __init__(self, place, part, held, send, recv, chunks):
        self.place, self.part, self.held = place, part, held
        self.sems, self.chunks = (send, recv), chunks
        self.rows = part.shape[1] // chunks

    def copy(self, side, step, chunk, shard, target):
        rows = chunk_rows(chunk, self.rows)
        index = 0 if side == 1 else 1
        spot = (index, step - 1, chunk)
        return pltpu.make_async_remote_copy(
            src_ref=self.part.at[shard, rows],
            dst_ref=self.held.at[index, step - 1, rows],
            send_sem=self.sems[0].at[spot],
            recv_sem=self.sems[1].at[spot],
            device_id={"tensor": target},
            device_id_type=MESH,
        )

    def add(self, step, chunk):
        rows = chunk_rows(chunk, self.rows)
        for index, side in enumerate(SIDES):
            far = far_of(self.place, side)
            shard = self.place + side * (LINE - step)

            @pl.when((far >= 1) & (far <= step - 1))
            def _():
                self.copy(side, step - 1, chunk, self.place, self.place - side).wait_recv()
                self.part[shard, rows] = (
                    self.part[shard, rows].astype(f32)
                    + self.held[index, step - 2, rows].astype(f32)
                ).astype(bf16)

    def send(self, step, chunk, least=0, most=LINE):
        if step > 1 and most > 0:
            self.add(step, chunk)
        for side in SIDES:
            far = far_of(self.place, side)
            shard = self.place + side * (LINE - step)

            @pl.when((far <= step - 1) & (far >= least) & (far <= most))
            def _():
                self.copy(side, step, chunk, shard, self.place + side).start()

    def begin(self, step, chunk):
        self.send(step, chunk, most=0)

    def relay(self, step, chunk):
        self.send(step, chunk, least=1)

    def total(self, chunk, out):
        rows = chunk_rows(chunk, self.rows)
        out[rows] = self.part[self.place, rows].astype(f32)
        for index, side in enumerate(SIDES):

            @pl.when(far_of(self.place, side) >= 1)
            def _():
                self.copy(side, LINE - 1, chunk, self.place, self.place - side).wait_recv()
                out[rows] += self.held[index, LINE - 2, rows].astype(f32)

    def drain(self, stop=LINE):
        for step in range(1, stop):
            for chunk in range(self.chunks):
                for side in SIDES:
                    far = far_of(self.place, side)
                    shard = self.place + side * (LINE - step)

                    @pl.when(far <= step - 1)
                    def _():
                        self.copy(side, step, chunk, shard, self.place + side).wait_send()


def line_sems(chunks):
    return [pltpu.SemaphoreType.DMA((2, LINE - 1, chunks))] * 2


def fetch(pairs, sems):
    copies = [pltpu.make_async_copy(src, dst, sems.at[i]) for i, (src, dst) in enumerate(pairs)]
    for copy in copies:
        copy.start()
    return copies


IN_VMEM = pl.BlockSpec(memory_space=pltpu.VMEM)
IN_HBM = pl.BlockSpec(memory_space=pl.ANY)


def comm_params(number):
    return pltpu.CompilerParams(
        vmem_limit_bytes=VMEM_LIMIT, collective_id=number, has_side_effects=True
    )


def gather_norm_body(x_ref, gain_ref, buf, own, sem, send, recv):
    place = lax.axis_index("tensor")
    greet(place)
    rows = x_ref[...].astype(f32)
    rms = lax.rsqrt(jnp.mean(rows * rows, axis=1, keepdims=True) + eps)
    own[...] = (rows * rms * gain_ref[...]).astype(bf16)
    gather = Gather(place, buf, send, recv, 1, own)
    gather.send(1, 0)
    (kept,) = fetch([(own, buf.at[place])], sem)
    gather.arrive(1, 0)
    gather.send(2, 0)
    kept.wait()
    gather.arrive(2, 0)
    gather.drain(stop=LINE - 1)


def gather_norm(x, gain):
    rows, features = x.shape
    return pl.pallas_call(
        gather_norm_body,
        in_specs=[IN_VMEM, IN_VMEM],
        out_specs=IN_HBM,
        out_shape=jax.ShapeDtypeStruct((LINE, rows, features), bf16),
        scratch_shapes=[pltpu.VMEM((rows, features), bf16), pltpu.SemaphoreType.DMA((1,))]
        + line_sems(1),
        compiler_params=comm_params(0),
    )(x, gain[None, :])


def front_body(
    chunks, seg,
    x_ref, w_ref, c_ref, e_ref, a_ref, cos_ref, sin_ref, p_ref, oe_ref, f_ref, tok_ref, gain_ref,
    kept_ref, y_ref, mid_ref, n_ref, cot_ref, l_ref, att_ref, lse_ref, lo_ref,
    buf, yv, wv, wo, part, held, own, midv, xsem, wsem, ysem, nsem, msem, send, recv,
    s_send, s_recv, g_send, g_recv, c_send, c_recv,
):
    place = lax.axis_index("tensor")
    groups, total, width = y_ref.shape
    rows, rank = x_ref.shape[1], a_ref.shape[1]
    edge = (place == 0) | (place == LINE - 1)
    last = place ^ (LINE - 1)

    def passed(side):
        shard = place - side * (LINE - 2)
        index = 0 if side == 1 else 1
        return pltpu.make_async_remote_copy(
            src_ref=x_ref.at[shard],
            dst_ref=buf.at[shard],
            send_sem=send.at[index],
            recv_sem=recv.at[index],
            device_id={"tensor": place + side},
            device_id_type=MESH,
        )

    def came(side):
        index = 0 if side == 1 else 1
        return pltpu.make_async_remote_copy(
            src_ref=x_ref.at[last],
            dst_ref=buf.at[last],
            send_sem=send.at[index],
            recv_sem=recv.at[index],
            device_id={"tensor": place - side},
            device_id_type=MESH,
        )

    copies = []
    for slot in range(LINE):
        copy = pltpu.make_async_copy(x_ref.at[place ^ slot], buf.at[place ^ slot], xsem.at[slot])
        if slot < LINE - 1:
            copy.start()
        else:
            pl.when(jnp.logical_not(edge))(copy.start)
        copies.append(copy)
    load, load_out = fetch(
        [(w_ref.at[:, : groups * width], wv), (w_ref.at[:, groups * width :], wo)], wsem
    )
    greet(place)
    cots = Gather(place, cot_ref, c_send, c_recv, chunks, c_ref)
    summed = Sum(place, part, held, s_send, s_recv, chunks)
    gather = Gather(place, n_ref, g_send, g_recv, chunks, own)
    for side in SIDES:
        pl.when(far_of(place, side) == LINE - 2)(passed(side).start)
    for chunk in range(chunks):
        cots.send(1, chunk)

    for copy in copies[:-1]:
        copy.wait()
    load.wait()
    outs = []
    for slot in range(LINE):
        shard = place ^ slot
        if slot == LINE - 1:
            pl.when(jnp.logical_not(edge))(copies[slot].wait)
            for side in SIDES:
                pl.when(far_of(place, side) == LINE - 1)(came(side).wait_recv)
            kept = pltpu.make_async_copy(buf.at[last], kept_ref.at[last], xsem.at[slot])
            pl.when(edge)(kept.start)
        mine = pl.ds(pl.multiple_of(shard * rows, rows), rows)
        low = nt(buf[shard], e_ref[:groups].reshape(groups * rank, -1)).astype(bf16)
        l_ref[mine] = low
        for g in range(groups):
            band = slice(g * width, (g + 1) * width)
            value = nn(buf[shard], wv[:, band]) + nn(low[:, g * rank : (g + 1) * rank], a_ref[g])
            if g < groups - 1:
                value = turn(value, cos_ref[mine], sin_ref[mine])
            yv[g, mine] = value.astype(bf16)
            out = pltpu.make_async_copy(yv.at[g, mine], y_ref.at[g, mine], ysem.at[slot, g])
            out.start()
            outs.append(out)

    pair = 2 * HEAD_DIM

    def one_pair(j, carry):
        lanes = pl.ds(pl.multiple_of(j * pair, pair), pair)
        attend_pair(seg, yv, lanes, p_ref[...], j, att_ref, lse_ref)

        @pl.when(j == 0)
        def _():
            for chunk in range(chunks):
                cots.relay(2, chunk)

        return carry

    lax.fori_loop(0, width // pair, one_pair, 0)

    load_out.wait()
    for slot in (3, 2, 1, 0):
        shard = place ^ slot
        mine = pl.ds(pl.multiple_of(shard * rows, rows), rows)
        d = att_ref[mine]
        low = nt(d, oe_ref[...]).astype(bf16)
        lo_ref[mine] = low
        part[shard] = (nt(d, wo[...]) + nn(low, f_ref[0])).astype(bf16)
        if slot == 3:
            summed.begin(1, 0)
    for chunk in range(chunks):
        for step in (1, 2, 3):
            if chunk or step > 1:
                summed.begin(step, chunk)
    size = rows // chunks
    stores = []
    for chunk in range(chunks):
        summed.relay(2, chunk)
        summed.relay(3, chunk)
        cots.relay(3, chunk)
        summed.total(chunk, midv)
        here = chunk_rows(chunk, size)
        value = midv[here] + tok_ref[here].astype(f32)
        midv[here] = value
        rms = lax.rsqrt(jnp.mean(value * value, axis=1, keepdims=True) + eps)
        own[here] = (value * rms * gain_ref[...]).astype(bf16)
        stores.append(pltpu.make_async_copy(own.at[here], n_ref.at[place, here], nsem.at[chunk]))
        stores.append(pltpu.make_async_copy(midv.at[here], mid_ref.at[here], msem.at[chunk]))
        gather.send(1, chunk, least=1)
        for store in stores[-2:]:
            store.start()
    for chunk in range(chunks):
        gather.send(1, chunk, most=0)
    for step in (2, 3):
        for chunk in range(chunks):
            gather.relay(step, chunk)
    cots.close()
    gather.close()
    pl.when(edge)(kept.wait)
    for out in outs + stores:
        out.wait()
    for side in SIDES:
        pl.when(far_of(place, side) == LINE - 2)(passed(side).wait_send)
    summed.drain()
    gather.drain()
    cots.drain()


def front(x, weight, cot, entries, exits, tables, leaf_parent, out_entry, finals, tokens, gain, seg, chunks=4):
    _, rows, features = x.shape
    groups, rank, width = exits.shape
    total = LINE * rows
    shards = jax.ShapeDtypeStruct((LINE, rows, features), bf16)
    return pl.pallas_call(
        functools.partial(front_body, chunks, seg),
        in_specs=[IN_HBM] * 3 + [IN_VMEM] * 9,
        out_specs=[IN_HBM] * 5 + [IN_VMEM] * 4,
        out_shape=[
            shards,
            jax.ShapeDtypeStruct((groups, total, width), bf16),
            jax.ShapeDtypeStruct((rows, features), f32),
            shards,
            shards,
            jax.ShapeDtypeStruct((total, groups * rank), bf16),
            jax.ShapeDtypeStruct((total, width), bf16),
            jax.ShapeDtypeStruct((width // (2 * HEAD_DIM), 2, total), f32),
            jax.ShapeDtypeStruct((total, rank), bf16),
        ],
        scratch_shapes=[
            pltpu.VMEM((LINE, rows, features), bf16),
            pltpu.VMEM((groups, total, width), bf16),
            pltpu.VMEM((features, groups * width), bf16),
            pltpu.VMEM((features, width), bf16),
            pltpu.VMEM((LINE, rows, features), bf16),
            pltpu.VMEM((2, LINE - 1, rows, features), bf16),
            pltpu.VMEM((rows, features), bf16),
            pltpu.VMEM((rows, features), f32),
            pltpu.SemaphoreType.DMA((LINE,)),
            pltpu.SemaphoreType.DMA((2,)),
            pltpu.SemaphoreType.DMA((LINE, groups)),
            pltpu.SemaphoreType.DMA((chunks,)),
            pltpu.SemaphoreType.DMA((chunks,)),
            pltpu.SemaphoreType.DMA((2,)),
            pltpu.SemaphoreType.DMA((2,)),
        ]
        + line_sems(chunks)
        + line_sems(chunks)
        + line_sems(chunks),
        input_output_aliases={0: 0},
        compiler_params=comm_params(1),
    )(x, weight, cot, entries, exits, *tables, leaf_parent, out_entry, finals, tokens, gain[None, :])


def tokens_body(
    chunks, d_ref, w_ref, a_ref, e_ref, x_ref, gain_ref, mid_ref, n_ref, lone_ref, final_ref, exit_ref,
    middle_ref, own_ref, left_ref, right_ref,
    out_ref, model_ref, head_ref, res_ref,
    part, held, acc, dv, wv, midv, nv, terms, low, block, extra, wsem, send, recv, x_send, x_recv, t_send, t_recv, h_send, h_recv,
):
    place = lax.axis_index("tensor")
    tree = lax.axis_index("dp")
    trees = Trees(tree, model_ref, t_send, t_recv)
    heads = Trees(tree, head_ref, h_send, h_recv)
    groups, total, width = d_ref.shape
    rank = a_ref.shape[1]
    loads = fetch(
        [
            (d_ref, dv),
            (w_ref.at[:, : groups * width], wv),
            (n_ref, nv),
            (mid_ref, midv),
            (middle_ref, acc),
            (own_ref.at[place], terms.at[0]),
            (left_ref, terms.at[1]),
            (right_ref, terms.at[2]),
        ],
        wsem,
    )
    block[...] = jnp.zeros_like(block)
    for g in range(groups):
        block[g * rank : (g + 1) * rank, g * width : (g + 1) * width] = a_ref[g]
    greet(place, trees.partners)
    for load in loads[:2]:
        load.wait()
    rows = part.shape[1]
    summed = Sum(place, part, held, send, recv, chunks)
    gather = Gather(place, extra, x_send, x_recv, 1)
    entry = e_ref[:groups].reshape(groups * rank, -1)

    def rows_of(slot):
        shard = place ^ slot
        mine = pl.ds(pl.multiple_of(shard * rows, rows), rows)
        return shard, mine, jnp.concatenate([dv[g, mine] for g in range(groups)], axis=1)

    def lower(slot):
        _, mine, d = rows_of(slot)
        low[mine] = nt(d, block[...]).astype(bf16)

    def partial(slot):
        shard, mine, d = rows_of(slot)
        part[shard] = (nt(d, wv[...]) + nn(low[mine], entry)).astype(bf16)

    lower(3)
    partial(3)
    summed.begin(1, 0)
    summed.begin(1, 1)
    for slot in (2, 1, 0):
        lower(slot)
    for load in loads[2:]:
        load.wait()

    def turned(value):
        return value.astype(f32).T.astype(bf16)

    joined = nn(turned(low[...]), nv[...].reshape(total, -1))
    extra[place] = jnp.concatenate([joined, final_ref[...]], axis=0).astype(bf16)
    gather.send(1, 0)
    for chunk in range(2, chunks):
        summed.begin(1, chunk)
    for slot in (2, 1, 0):
        partial(slot)
    for step in (2, 3):
        for chunk in range(chunks):
            summed.begin(step, chunk)
    summed.relay(2, 0)
    summed.relay(2, 1)
    gather.arrive(1, 0)
    gather.send(2, 0)
    summed.relay(2, 2)
    low_one = turned(lone_ref[...])
    for g in range(groups):
        band = slice(g * rank, (g + 1) * rank)
        head_ref[tree, band] = nn(low_one[band], dv[g]).astype(bf16)
    head_ref[tree, groups * rank :] = exit_ref[...].astype(bf16)
    heads.send(0)
    value = acc[...] + terms[0].astype(f32)
    for index, side in enumerate(SIDES):
        value += jnp.where(far_of(place, side) > 0, terms[index + 1].astype(f32), 0.0)
    res_ref[...] = value.astype(bf16)
    summed.relay(2, 3)
    gather.arrive(2, 0)
    gather.send(3, 0)
    heads.advance(1)
    summed.relay(3, 0)
    gather.arrive(3, 0)
    model_ref[tree] = functools.reduce(
        jnp.add, [extra[shard].astype(f32) for shard in range(LINE)]
    ).astype(bf16)
    trees.send(0)
    heads.advance(2)
    summed.relay(3, 1)
    trees.advance(1)
    summed.relay(3, 2)
    summed.relay(3, 3)
    trees.advance(2)
    size = rows // chunks

    def finish(chunk):
        finish_tokens(summed, chunk, size, acc, x_ref, gain_ref, midv, out_ref)

    finish(0)
    finish(1)
    for number in range(3, trees.rounds):
        trees.advance(number)
        heads.advance(number)
    finish(2)
    finish(3)
    for blocks in (trees, heads):
        blocks.arrive(blocks.rounds - 1)
        blocks.drain()
    summed.drain()
    gather.drain()


class Trees:
    def __init__(self, tree, ref, send, recv):
        self.tree, self.ref, self.sems = tree, ref, (send, recv)
        self.rounds = ref.shape[0].bit_length() - 1
        self.partners = [self.partner(number) for number in range(self.rounds)]

    def partner(self, number):
        size = 1 << number
        return self.tree + size - 2 * size * ((self.tree // size) % 2)

    def copy(self, number, owner):
        size = 1 << number
        here = pl.ds((owner // size) * size, size)
        return pltpu.make_async_remote_copy(
            src_ref=self.ref.at[here],
            dst_ref=self.ref.at[here],
            send_sem=self.sems[0].at[number],
            recv_sem=self.sems[1].at[number],
            device_id={"dp": self.partner(number)},
            device_id_type=MESH,
        )

    def send(self, number):
        self.copy(number, self.tree).start()

    def arrive(self, number):
        self.copy(number, self.partner(number)).wait_recv()

    def advance(self, number):
        if number < self.rounds:
            self.arrive(number - 1)
            self.send(number)

    def drain(self):
        for number in range(self.rounds):
            self.copy(number, self.tree).wait_send()


def finish_tokens(summed, chunk, size, acc, x_ref, gain_ref, mid_ref, out_ref):
    summed.total(chunk, acc)
    here = chunk_rows(chunk, size)
    rows = x_ref[here].astype(f32)
    rms = lax.rsqrt(jnp.mean(rows * rows, axis=1, keepdims=True) + eps)
    scaled = acc[here] * gain_ref[...]
    mean = jnp.mean(scaled * rows, axis=1, keepdims=True)
    out_ref[here] = (mid_ref[here] + rms * (scaled - rows * (rms * rms) * mean)).astype(bf16)


def tokens_back(
    head_grads, weight, exits, entries, x, gain, grad_middle, normed, low_one, final_grads, exit_grads,
    middle, own, from_left, from_right,
):
    chunks = LINE
    rows, features = x.shape
    groups, total, width = head_grads.shape
    rank = exits.shape[1]
    deep = (groups + 1) * rank
    trees = lax.axis_size("dp")
    sems = pltpu.SemaphoreType.DMA((trees.bit_length() - 1,))
    return pl.pallas_call(
        functools.partial(tokens_body, chunks),
        in_specs=[IN_HBM, IN_HBM] + [IN_VMEM] * 4 + [IN_HBM] * 2 + [IN_VMEM] * 3 + [IN_HBM] * 4,
        out_specs=[IN_VMEM] * 4,
        out_shape=[
            jax.ShapeDtypeStruct((rows, features), bf16),
            jax.ShapeDtypeStruct((trees, deep, features), bf16),
            jax.ShapeDtypeStruct((trees, deep, width), bf16),
            jax.ShapeDtypeStruct((rows, features), bf16),
        ],
        scratch_shapes=[
            pltpu.VMEM((LINE, rows, features), bf16),
            pltpu.VMEM((2, LINE - 1, rows, features), bf16),
            pltpu.VMEM((rows, features), f32),
            pltpu.VMEM((groups, total, width), bf16),
            pltpu.VMEM((features, groups * width), bf16),
            pltpu.VMEM((rows, features), f32),
            pltpu.VMEM((LINE, rows, features), bf16),
            pltpu.VMEM((3, rows, features), bf16),
            pltpu.VMEM((total, groups * rank), bf16),
            pltpu.VMEM((groups * rank, groups * width), bf16),
            pltpu.VMEM((LINE, deep, features), bf16),
            pltpu.SemaphoreType.DMA((8,)),
        ]
        + line_sems(chunks)
        + line_sems(1)
        + [sems] * 4,
        compiler_params=comm_params(3),
    )(
        head_grads, weight, exits, entries, x, gain[None, :], grad_middle, normed,
        low_one, final_grads, exit_grads, middle, own, from_left, from_right,
    )


def tree_tiles(seg, rows, parent_row):
    trunk = TRUNK * seg
    leaves = trunk + BRANCHES * seg
    key = lax.broadcasted_iota(jnp.int32, (QT, QT), 0)
    query = lax.broadcasted_iota(jnp.int32, (QT, QT), 1)
    causal = key <= query
    own = causal & (key // seg == query // seg)
    tiles = []
    for start in range(0, trunk, QT):
        pieces = [(0, start, None)] if start else []
        tiles.append((start, pieces + [(start, QT, causal)]))
    tiles.append((trunk, [(0, trunk, None), (trunk, QT, own)]))
    branch = lax.broadcasted_iota(jnp.int32, (BRANCHES * seg, QT), 0) // seg
    for start in range(leaves, rows, QT):
        mine = branch == parent_row[:, start - leaves : start - leaves + QT]
        tiles.append(
            (start, [(0, trunk, None), (trunk, BRANCHES * seg, mine), (start, QT, own)])
        )
    return tiles


def attend_pair(seg, qkv_ref, lanes, parent_row, pair, o_ref, lse_ref):
    rows = qkv_ref.shape[1]
    value_t = qkv_ref[2, :, lanes].T
    lane = lax.broadcasted_iota(jnp.int32, (QT, 2 * HEAD_DIM), 1)
    for start, pieces in tree_tiles(seg, rows, parent_row):
        query = qkv_ref[0, start : start + QT, lanes] * bf16(HEAD_DIM**-0.5)
        outs = []
        for h in range(2):
            own_query = jnp.where(lane // HEAD_DIM == h, query, bf16(0))
            scores = []
            for k0, count, mask in pieces:
                s = nt(qkv_ref[1, k0 : k0 + count, lanes], own_query)
                scores.append(s if mask is None else jnp.where(mask, s, -1e30))
            top = functools.reduce(
                jnp.maximum, [jnp.max(s, axis=0, keepdims=True) for s in scores]
            )
            summed, out = 0.0, 0.0
            for (k0, count, _), s in zip(pieces, scores):
                weights = jnp.exp(s - top)
                summed += jnp.sum(weights, axis=0, keepdims=True)
                out += nn(
                    value_t[h * HEAD_DIM : (h + 1) * HEAD_DIM, k0 : k0 + count],
                    weights.astype(bf16),
                )
            outs.append(out / summed)
            lse_ref[pair, h : h + 1, start : start + QT] = top + jnp.log(summed)
        o_ref[start : start + QT, lanes] = jnp.concatenate(outs, axis=0).T.astype(bf16)


def attend_back_body(
    seg, q_ref, k_ref, v_ref, o_ref, g_ref, lse_ref, p_ref, cos_ref, sin_ref, right_ref, left_ref,
    d_ref, from_left_ref, from_right_ref, dq_t, dk, dv, send, recv,
):
    place = lax.axis_index("tensor")

    def exchange(side, target):
        index = 0 if side == 1 else 1
        return pltpu.make_async_remote_copy(
            src_ref=(right_ref, left_ref)[index],
            dst_ref=(from_left_ref, from_right_ref)[index],
            send_sem=send.at[index],
            recv_sem=recv.at[index],
            device_id={"tensor": target},
            device_id_type=MESH,
        )

    @pl.when(pl.program_id(0) == 0)
    def _():
        greet(place)
        for side in SIDES:
            pl.when(far_of(place, side) < LINE - 1)(exchange(side, place + side).start)

    rows = q_ref.shape[1]
    scale = bf16(HEAD_DIM**-0.5)
    key_t = k_ref[0].T
    weighed_t = (g_ref[0].astype(f32) * o_ref[...].astype(f32)).T
    lane = lax.broadcasted_iota(jnp.int32, (QT, 2 * HEAD_DIM), 1)
    dk[...] = jnp.zeros_like(dk)
    dv[...] = jnp.zeros_like(dv)
    for start, pieces in tree_tiles(seg, rows, p_ref[...]):
        query = q_ref[0, start : start + QT] * scale
        grad = g_ref[0, start : start + QT]
        for h in range(2):
            mine = lane // HEAD_DIM == h
            own_query = jnp.where(mine, query, bf16(0))
            own_grad = jnp.where(mine, grad, bf16(0))
            band = slice(h * HEAD_DIM, (h + 1) * HEAD_DIM)
            delta = jnp.sum(weighed_t[band, start : start + QT], axis=0, keepdims=True)
            lse = lse_ref[0, h : h + 1, start : start + QT]
            grad_q = 0.0
            for k0, count, mask in pieces:
                probs = jnp.exp(nt(k_ref[0, k0 : k0 + count], own_query) - lse)
                if mask is not None:
                    probs = jnp.where(mask, probs, 0.0)
                grad_probs = nt(v_ref[0, k0 : k0 + count], own_grad)
                grad_scores = (probs * (grad_probs - delta)).astype(bf16)
                dk[k0 : k0 + count] += nn(grad_scores, own_query)
                dv[k0 : k0 + count] += nn(probs.astype(bf16), own_grad)
                grad_q += nn(key_t[band, k0 : k0 + count], grad_scores)
            dq_t[band, start : start + QT] = grad_q
    cosine, sine = cos_ref[...], -sin_ref[...]
    d_ref[0] = turn(dq_t[...].T * HEAD_DIM**-0.5, cosine, sine).astype(bf16)
    d_ref[1] = turn(dk[...], cosine, sine).astype(bf16)
    d_ref[2] = dv[...].astype(bf16)

    @pl.when(pl.program_id(0) == pl.num_programs(0) - 1)
    def _():
        for side in SIDES:
            pl.when(far_of(place, side) < LINE - 1)(exchange(side, place + side).wait_send)
            pl.when(far_of(place, side) > 0)(exchange(side, place - side).wait_recv)


def attend_back(qkv, attended, grad, lse, leaf_parent, tables, seg, right, left):
    _, rows, width = qkv.shape
    pairs = width // (2 * HEAD_DIM)
    pair = 2 * HEAD_DIM
    return pl.pallas_call(
        functools.partial(attend_back_body, seg),
        grid=(pairs,),
        in_specs=[pl.BlockSpec((1, rows, pair), lambda j, g=g: (g, 0, j)) for g in range(3)]
        + [
            pl.BlockSpec((rows, pair), lambda j: (0, j)),
            pl.BlockSpec((1, rows, pair), lambda j: (0, 0, j)),
            pl.BlockSpec((1, 2, rows), lambda j: (j, 0, 0)),
            pl.BlockSpec(leaf_parent.shape, lambda j: (0, 0)),
            pl.BlockSpec((rows, pair), lambda j: (0, 0)),
            pl.BlockSpec((rows, pair), lambda j: (0, 0)),
            IN_HBM,
            IN_HBM,
        ],
        out_specs=[pl.BlockSpec((3, rows, pair), lambda j: (0, 0, j)), IN_HBM, IN_HBM],
        out_shape=[
            jax.ShapeDtypeStruct((3, rows, width), bf16),
            jax.ShapeDtypeStruct(right.shape, bf16),
            jax.ShapeDtypeStruct(left.shape, bf16),
        ],
        scratch_shapes=[
            pltpu.VMEM((pair, rows), f32),
            pltpu.VMEM((rows, pair), f32),
            pltpu.VMEM((rows, pair), f32),
            pltpu.SemaphoreType.DMA((2,)),
            pltpu.SemaphoreType.DMA((2,)),
        ],
        compiler_params=comm_params(4),
    )(qkv, qkv, qkv, attended, grad, lse, leaf_parent, *tables, right, left)


def feed_body(
    rank, tile, chunks,
    n_ref, c_ref, far_ref, wg_ref, wu_ref, wd_ref, mid_ref, wo_ref,
    pick_ref, xu_in, xd_in, e_in, f_in, gain_ref, oe_ref, att_ref, lo_ref,
    grad_ref, res_ref, right_ref, left_ref, b_ref, held_ref, unit_out, model_out, y_ref, final_ref, exit_ref,
    unit_ref, model_ref, x_ref, e_ref, f_ref, midv, nbuf, cbuf, wbuf, low, low_t, acc_res, acc_back, acc_low,
    part, held, resv, own, extra, wo, nsem, csem, wsem, rsem, msem,
    send, recv, g_send, g_recv, x_send, x_recv, r_send, r_recv,
):
    place = lax.axis_index("tensor")
    units = unit_ref.shape[1]
    tiles = units // tile
    rows = part.shape[1]
    summed = Sum(place, part, held, send, recv, chunks)
    gather = Gather(place, b_ref, g_send, g_recv, chunks, own)
    joint = Gather(place, extra, x_send, x_recv, 1)

    def load_rows(order, act):
        into = order % 2
        shard = place ^ (LINE - 1 - order)
        act(pltpu.make_async_copy(n_ref.at[shard], nbuf.at[into], nsem.at[into]))

        def take(source):
            act(pltpu.make_async_copy(source, cbuf.at[into], csem.at[into]))

        pl.when(order == LINE - 1)(lambda: take(c_ref))
        pl.when(order < LINE - 1)(lambda: take(far_ref.at[shard]))

    def load_weights(index, into, act):
        columns = pl.ds(pl.multiple_of(index * tile, tile), tile)
        for k, w_ref in enumerate((wg_ref, wu_ref, wd_ref)):
            act(pltpu.make_async_copy(w_ref.at[:, columns], wbuf.at[into, k], wsem.at[into, k]))

    def start(copy):
        copy.start()

    def wait(copy):
        copy.wait()

    load_rows(jnp.int32(0), start)
    load_weights(0, 0, start)
    width = wo.shape[1]
    load_middle, load_out = fetch([(mid_ref, midv), (wo_ref.at[:, 3 * width :], wo)], msem)
    for padded in (x_ref, e_ref, f_ref):
        padded[...] = jnp.zeros_like(padded)
    x_ref[0, :rank] = xu_in[0]
    x_ref[1, rank : 2 * rank] = xu_in[1]
    x_ref[2, 2 * rank :] = xd_in[...]
    e_ref[: 2 * rank] = e_in[3:].reshape(2 * rank, -1)
    f_ref[2 * rank :] = f_in[1]
    unit_ref[...] = jnp.zeros_like(unit_ref)
    model_ref[...] = jnp.zeros_like(model_ref)
    greet(place)

    def one_shard(order, carry):
        into = order % 2
        shard = place ^ (LINE - 1 - order)
        load_rows(order, wait)

        @pl.when(order < LINE - 1)
        def _():
            load_rows(order + 1, start)

        first = nt(nbuf[into], e_ref[...]) + nt(cbuf[into], f_ref[...])
        low[...] = first.astype(bf16)
        low_t[...] = first.T.astype(bf16)
        acc_res[...] = jnp.zeros_like(acc_res)
        acc_back[...] = jnp.zeros_like(acc_back)
        acc_low[...] = jnp.zeros_like(acc_low)

        def one_tile(index, carry):
            stage = order * tiles + index
            at = stage % 2
            load_weights(index, at, wait)

            @pl.when(stage < LINE * tiles - 1)
            def _():
                load_weights((index + 1) % tiles, 1 - at, start)

            columns = pl.ds(pl.multiple_of(index * tile, tile), tile)
            x_gate, x_rise, x_fall = x_ref[0, :, columns], x_ref[1, :, columns], x_ref[2, :, columns]
            gate = nn(nbuf[into], wbuf[at, 0]) + nn(low[...], x_gate)
            rise = nn(nbuf[into], wbuf[at, 1]) + nn(low[...], x_rise)
            grad_hidden = nn(cbuf[into], wbuf[at, 2]) + nn(low[...], x_fall)
            sigmoid = jax.nn.sigmoid(gate)
            silu = gate * sigmoid
            hidden = (silu * rise).astype(bf16)
            grad_gate = (grad_hidden * rise * sigmoid * (1.0 + gate * (1.0 - sigmoid))).astype(bf16)
            grad_rise = (grad_hidden * silu).astype(bf16)
            acc_back[...] += nt(grad_gate, wbuf[at, 0]) + nt(grad_rise, wbuf[at, 1])
            acc_res[...] += nt(hidden, wbuf[at, 2])
            acc_low[...] += nt(grad_gate, x_gate) + nt(grad_rise, x_rise) + nt(hidden, x_fall)
            unit_ref[:rank, columns] += nn(low_t[:rank], grad_gate)
            unit_ref[rank : 2 * rank, columns] += nn(low_t[rank : 2 * rank], grad_rise)
            unit_ref[2 * rank :, columns] += nn(low_t[2 * rank : 3 * rank], hidden)
            return carry

        lax.fori_loop(0, tiles, one_tile, 0)
        joined = acc_low[...].astype(bf16)
        joined_t = acc_low[...].T.astype(bf16)
        part[shard] = (acc_back[...] + nn(joined, e_ref[...])).astype(bf16)
        for step in (1, 2, 3):

            @pl.when(order == step - 1)
            def _():
                for chunk in range(chunks):
                    summed.send(step, chunk)

        @pl.when(order > 0)
        def _():
            pltpu.make_async_copy(resv, res_ref.at[shard], rsem.at[0]).wait()

        resv[...] = (acc_res[...] + nn(joined, f_ref[...])).astype(bf16)
        pltpu.make_async_copy(resv, res_ref.at[shard], rsem.at[0]).start()
        model_ref[: 2 * rank] += nn(joined_t[: 2 * rank], nbuf[into])
        model_ref[2 * rank :] += nn(joined_t[2 * rank : 3 * rank], cbuf[into])
        return carry

    lax.fori_loop(0, LINE, one_shard, 0)
    extra[place] = model_ref[...].astype(bf16)
    joint.send(1, 0)
    size = rows // chunks
    last = (LINE - 1) % 2
    load_middle.wait()
    stores = []
    for chunk in range(chunks):
        summed.total(chunk, acc_back)
        here = chunk_rows(chunk, size)
        middle = midv[here]
        rms = lax.rsqrt(jnp.mean(middle * middle, axis=1, keepdims=True) + eps)
        scaled = acc_back[here] * gain_ref[...]
        mean = jnp.mean(scaled * middle, axis=1, keepdims=True)
        grad = cbuf[last, here].astype(f32) + rms * (scaled - middle * (rms * rms) * mean)
        own[here] = grad.astype(bf16)
        gather.send(1, chunk, least=1)
        midv[here] = grad
        store = pltpu.make_async_copy(midv.at[here], grad_ref.at[here], nsem.at[chunk % 2])
        if chunk >= 2:
            stores[chunk - 2].wait()
        store.start()
        stores.append(store)
    for chunk in range(chunks):
        gather.send(1, chunk, most=0)
    pltpu.make_async_copy(resv, res_ref.at[place], rsem.at[0]).wait()

    def pass_on(side, step, source, target):
        index = 0 if side == 1 else 1
        return pltpu.make_async_remote_copy(
            src_ref=source,
            dst_ref=held_ref.at[index, step - 1],
            send_sem=r_send.at[index, step - 1],
            recv_sem=r_recv.at[index, step - 1],
            device_id={"tensor": target},
            device_id_type=MESH,
        )

    def at_far(side, number, act):
        pl.when(far_of(place, side) == number)(act)

    def ready(side, step, shard):
        index = 0 if side == 1 else 1
        pass_on(side, step, resv, place - side).wait_recv()
        copies = [
            pltpu.make_async_copy(res_ref.at[shard], cbuf.at[0], csem.at[0]),
            pltpu.make_async_copy(held_ref.at[index, step - 1], cbuf.at[1], csem.at[1]),
        ]
        for copy in copies:
            copy.start()
        for copy in copies:
            copy.wait()
        cbuf[0] = (cbuf[0].astype(f32) + cbuf[1].astype(f32)).astype(bf16)

    for side in SIDES:
        for step in (1, 2):
            at_far(
                side,
                0,
                lambda: pass_on(side, step, res_ref.at[place + side * (LINE - step)], place + side).start(),
            )

    load_out.wait()
    for store in stores[-2:]:
        store.wait()

    def through(number, rows_ref, shard):
        mine = pl.ds(pl.multiple_of(shard * rows, rows), rows)
        value = rows_ref[...]
        reduced = nt(value, f_in[0])
        y_ref[0, mine] = (nn(value, wo[...]) + nn(reduced.astype(bf16), oe_ref[...])).astype(bf16)
        final = nn(lo_ref[mine].astype(f32).T.astype(bf16), value)
        leave = nn(reduced.T.astype(bf16), att_ref[mine])
        final_ref[...] = final if number == 0 else final_ref[...] + final
        exit_ref[...] = leave if number == 0 else exit_ref[...] + leave

    def take(number, shard):
        copy = pltpu.make_async_copy(b_ref.at[shard], nbuf.at[number % 2], nsem.at[number % 2])
        copy.start()
        copy.wait()
        through(number, nbuf.at[number % 2], shard)

    def edge_got(step):
        for side in SIDES:

            @pl.when(far_of(place, side) == LINE - 1)
            def _():
                for chunk in range(chunks):
                    gather.copy(side, step, chunk, place - side * step, place - side).wait_recv()

    inside = ((place + 1) // 2) % 2
    joint.relay(2, 0)
    through(0, own, place)
    unit_out[: 3 * rank] = unit_ref[...].astype(bf16)
    unit_out[3 * rank :] = jnp.full((rank, units), pick_ref[0, 0], f32).astype(bf16)
    for chunk in range(chunks):
        gather.relay(2, chunk)
    edge_got(1)
    joint.relay(3, 0)
    take(1, place ^ (1 + 2 * inside))
    for chunk in range(chunks):
        gather.relay(3, chunk)
    for side in SIDES:

        @pl.when(far_of(place, side) == 1)
        def _():
            ready(side, 1, place + side * 2)
            resv[...] = cbuf[0]
            pass_on(side, 2, resv, place + side).start()

    edge_got(2)
    take(2, place ^ (2 - inside))
    joint.close()
    model_out[...] = functools.reduce(
        jnp.add, [extra[shard].astype(f32) for shard in range(LINE)]
    ).astype(bf16)
    edge_got(3)
    take(3, place ^ (3 - inside))
    for index, side in enumerate(SIDES):
        target = (right_ref, left_ref)[index]

        @pl.when(far_of(place, side) == 0)
        def _():
            copy = pltpu.make_async_copy(res_ref.at[place + side], nbuf.at[index], nsem.at[index])
            copy.start()
            copy.wait()

        @pl.when((far_of(place, side) > 0) & (far_of(place, side) < LINE - 1))
        def _():
            ready(side, 2, place + side)
            nbuf[index] = cbuf[0]

        copy = pltpu.make_async_copy(nbuf.at[index], target, nsem.at[index])
        copy.start()
        copy.wait()
    for side in SIDES:
        for step in (1, 2):
            at_far(
                side,
                0,
                lambda: pass_on(side, step, res_ref.at[place + side * (LINE - step)], place + side).wait_send(),
            )
        at_far(side, 1, lambda: pass_on(side, 2, resv, place + side).wait_send())
    summed.drain()
    gather.drain()
    joint.drain()


def feed(
    normed, cots, weights, middle, w_heads, pick, units_exit, fall_entry, entries, finals, gain, out_entry,
    attended, low_out, tile=512, chunks=4,
):
    _, rows, features = normed.shape
    units = weights[0].shape[1]
    rank, width = out_entry.shape
    total = LINE * rows
    one = jax.ShapeDtypeStruct((rows, features), bf16)
    return pl.pallas_call(
        functools.partial(feed_body, rank, tile, chunks),
        in_specs=[IN_HBM] * 8 + [pl.BlockSpec(memory_space=pltpu.SMEM)] + [IN_VMEM] * 8,
        out_specs=[IN_HBM] * 6 + [IN_VMEM] * 5,
        out_shape=[
            jax.ShapeDtypeStruct((rows, features), f32),
            jax.ShapeDtypeStruct((LINE, rows, features), bf16),
            one,
            one,
            jax.ShapeDtypeStruct((LINE, rows, features), bf16),
            jax.ShapeDtypeStruct((2, LINE - 2, rows, features), bf16),
            jax.ShapeDtypeStruct((4 * rank, units), bf16),
            jax.ShapeDtypeStruct((3 * rank, features), bf16),
            jax.ShapeDtypeStruct((1, total, width), bf16),
            jax.ShapeDtypeStruct((rank, features), f32),
            jax.ShapeDtypeStruct((rank, width), f32),
        ],
        scratch_shapes=[
            pltpu.VMEM((3 * rank, units), f32),
            pltpu.VMEM((3 * rank, features), f32),
            pltpu.VMEM((3, 3 * rank, units), bf16),
            pltpu.VMEM((3 * rank, features), bf16),
            pltpu.VMEM((3 * rank, features), bf16),
            pltpu.VMEM((rows, features), f32),
            pltpu.VMEM((2, rows, features), bf16),
            pltpu.VMEM((2, rows, features), bf16),
            pltpu.VMEM((2, 3, features, tile), bf16),
            pltpu.VMEM((rows, 3 * rank), bf16),
            pltpu.VMEM((3 * rank, rows), bf16),
            pltpu.VMEM((rows, features), f32),
            pltpu.VMEM((rows, features), f32),
            pltpu.VMEM((rows, 3 * rank), f32),
            pltpu.VMEM((LINE, rows, features), bf16),
            pltpu.VMEM((2, LINE - 1, rows, features), bf16),
            pltpu.VMEM((rows, features), bf16),
            pltpu.VMEM((rows, features), bf16),
            pltpu.VMEM((LINE, 3 * rank, features), bf16),
            pltpu.VMEM((features, width), bf16),
            pltpu.SemaphoreType.DMA((2,)),
            pltpu.SemaphoreType.DMA((2,)),
            pltpu.SemaphoreType.DMA((2, 3)),
            pltpu.SemaphoreType.DMA((1,)),
            pltpu.SemaphoreType.DMA((2,)),
        ]
        + line_sems(chunks)
        + line_sems(chunks)
        + line_sems(1)
        + [pltpu.SemaphoreType.DMA((2, LINE - 2))] * 2,
        compiler_params=comm_params(5),
    )(
        normed, *cots, *weights, middle, w_heads, pick, units_exit, fall_entry, entries, finals, gain[None, :], out_entry,
        attended, low_out,
    )


def pick_body(pick_ref, *refs):
    count = len(refs) // 2
    for source, target in zip(refs[:count], refs[count:]):
        target[...] = source[...].reshape(target.shape)


def picked(pick, arrays):
    shapes = [a.shape[:1] + a.shape[2:] for a in arrays]
    return pl.pallas_call(
        pick_body,
        grid_spec=pltpu.PrefetchScalarGridSpec(
            num_scalar_prefetch=1,
            grid=(1,),
            in_specs=[
                pl.BlockSpec(a.shape[:1] + (1,) + a.shape[2:], lambda i, p: (0, p[0], 0, 0)) for a in arrays
            ],
            out_specs=[pl.BlockSpec(shape, lambda i, p: (0, 0, 0)) for shape in shapes],
        ),
        out_shape=[jax.ShapeDtypeStruct(shape, bf16) for shape in shapes],
    )(pick, *arrays)


def per_tree(block):
    return lax.all_gather(block, "dp", axis=0, tiled=False)


def combine_body(rank, pick_ref, early, model, late, head, entry_ref, final_ref, unit_ref, down_ref, exit_ref, out_ref):
    for ref in (entry_ref, final_ref, unit_ref, down_ref, exit_ref, out_ref):
        ref[...] = jnp.zeros_like(ref)

    def one_tree(tree, carry):
        pick = pick_ref[tree]

        def block(ref, index):
            return ref[tree, index * rank : (index + 1) * rank].astype(f32)

        for k in range(3):
            entry_ref[k, pick] += block(late, k)
            exit_ref[k, pick] += block(head, k)
        final_ref[0, pick] += block(late, 3)
        out_ref[pick] += block(head, 3)
        for k in range(2):
            entry_ref[3 + k, pick] += block(model, k)
            unit_ref[k, pick] += block(early, k)
        final_ref[1, pick] += block(model, 2)
        down_ref[pick] += block(early, 2)
        return carry

    lax.fori_loop(0, early.shape[0], one_tree, 0)


def combine(picks, early, model, late, head, adapters, steps=4):
    trees, _, features = early.shape
    rank = late.shape[1] // 4
    width = head.shape[2]
    wide, narrow = features // steps, width // steps

    def taken(array, tile):
        return pl.BlockSpec((trees, array.shape[1], tile), lambda i, p: (0, 0, i))

    def given(lead, tile):
        shape = lead + (adapters, rank, tile)
        return pl.BlockSpec(shape, lambda i, p: (0,) * (len(shape) - 1) + (i,))

    def shape(lead, full):
        return jax.ShapeDtypeStruct(lead + (adapters, rank, full), f32)

    return pl.pallas_call(
        functools.partial(combine_body, rank),
        grid_spec=pltpu.PrefetchScalarGridSpec(
            num_scalar_prefetch=1,
            grid=(steps,),
            in_specs=[taken(early, wide), taken(model, wide), taken(late, wide), taken(head, narrow)],
            out_specs=[
                given((5,), wide),
                given((2,), wide),
                given((2,), wide),
                given((), wide),
                given((3,), narrow),
                given((), narrow),
            ],
        ),
        out_shape=[
            shape((5,), features),
            shape((2,), features),
            shape((2,), features),
            shape((), features),
            shape((3,), width),
            shape((), width),
        ],
        compiler_params=pltpu.CompilerParams(vmem_limit_bytes=VMEM_LIMIT),
    )(picks, early, model, late, head)


def local(
    tokens,
    cotangent,
    attention_gain,
    feed_gain,
    query_weight,
    key_weight,
    value_weight,
    output_weight,
    gate_weight,
    up_weight,
    down_weight,
    entry_maps,
    head_exits,
    unit_exits,
    output_entry,
    down_entry,
    final_exits,
    parents,
    adapter_pick,
):
    adapters, rank = entry_maps.shape[1], entry_maps.shape[3]
    local_rows = tokens.shape[0]
    total = local_rows * lax.axis_size("tensor")
    blocks = parents.shape[1]
    seg = total // blocks
    tables = rope_tables(blocks, seg)
    leaf_parent = (jnp.repeat(parents[0, TRUNK + BRANCHES :], seg) - TRUNK)[None, :]
    gain_one = attention_gain.astype(f32)
    gain_two = feed_gain.astype(f32)

    w_heads = lax.all_gather(
        jnp.concatenate([query_weight, key_weight, value_weight, output_weight], axis=1),
        "dp",
        axis=0,
        tiled=True,
    )

    w_units = [
        lax.all_gather(w, "dp", axis=0, tiled=True) for w in (gate_weight, up_weight, down_weight)
    ]
    entries, heads_exit, units_exit, out_entry, fall_entry, finals = picked(
        adapter_pick,
        (
            jnp.swapaxes(entry_maps, 2, 3),
            head_exits,
            unit_exits,
            jnp.swapaxes(output_entry, 1, 2)[None],
            jnp.swapaxes(down_entry, 1, 2)[None],
            final_exits,
        ),
    )
    out_entry, fall_entry = out_entry[0], fall_entry[0]

    most_one = gather_norm(tokens, gain_one)
    full_one, qkv, middle, full_two, full_cot, low_one, attended, lse, adapt_o = front(
        most_one, w_heads, cotangent, entries, heads_exit, tables, leaf_parent, out_entry, finals, tokens, gain_two, seg
    )

    (
        grad_middle, res_parts, res_right, res_left, _, _, early, model_sum, grad_attended, final_grads, exit_grads,
    ) = feed(
        full_two, (cotangent, full_cot), w_units, middle, w_heads, adapter_pick.astype(f32)[None, :],
        units_exit, fall_entry, entries, finals, gain_two, out_entry, attended, adapt_o,
    )
    early = per_tree(early)
    model_all = per_tree(model_sum)

    head_grads, from_left, from_right = attend_back(
        qkv, attended, grad_attended, lse, leaf_parent, tables, seg, res_right, res_left
    )
    grad_tokens, late_model, late_head, result = tokens_back(
        head_grads, w_heads, heads_exit, entries, tokens, gain_one, grad_middle,
        full_one, low_one, final_grads, exit_grads, middle, res_parts, from_left, from_right,
    )

    picks = early[:, 3 * rank, 0].astype(jnp.int32)
    grad_entries, grad_finals, grad_units, grad_down, grad_heads, grad_output = combine(
        picks, early, model_all, late_model, late_head, adapters
    )
    grad_entries = grad_entries.swapaxes(2, 3)
    grad_output = grad_output.swapaxes(1, 2)
    grad_down = grad_down.swapaxes(1, 2)
    return (
        result,
        grad_tokens,
        grad_entries,
        grad_heads,
        grad_units,
        grad_output,
        grad_down,
        grad_finals,
    )


def solution(mesh):
    in_specs = (
        P(("dp", "tensor"), None),
        P(("dp", "tensor"), None),
        P(),
        P(),
        P("dp", "tensor"),
        P("dp", "tensor"),
        P("dp", "tensor"),
        P("dp", "tensor"),
        P("dp", "tensor"),
        P("dp", "tensor"),
        P("dp", "tensor"),
        P(),
        P(None, None, None, "tensor"),
        P(None, None, None, "tensor"),
        P(None, "tensor", None),
        P(None, "tensor", None),
        P(),
        P("dp", None),
        P("dp"),
    )
    out_specs = (
        P(("dp", "tensor"), None),
        P(("dp", "tensor"), None),
        P(),
        P(None, None, None, "tensor"),
        P(None, None, None, "tensor"),
        P(None, "tensor", None),
        P(None, "tensor", None),
        P(),
    )
    return jax.shard_map(local, mesh=mesh, in_specs=in_specs, out_specs=out_specs, check_vma=False)
```

```python
import functools

import jax
import jax.numpy as jnp
import numpy as np
from jax import lax
from jax.experimental import pallas as pl
from jax.experimental.pallas import tpu as pltpu
from jax.sharding import PartitionSpec as P

HEAD_DIM = 64
TRUNK, BRANCHES = 8, 4
QT = 256
VMEM_LIMIT = 60 * 1024 * 1024
LINE = 4
MESH = pl.DeviceIdType.MESH

eps = 1e-05
theta = 130000.0
bf16, f32 = jnp.bfloat16, jnp.float32


def nn(left, right):
    return jnp.dot(left, right, preferred_element_type=f32)


def nt(left, right):
    return lax.dot_general(left, right, (((1,), (1,)), ((), ())), preferred_element_type=f32)


def tn(left, right):
    return lax.dot_general(left, right, (((0,), (0,)), ((), ())), preferred_element_type=f32)


def rope_tables(blocks, seg):
    depth = np.minimum(np.arange(blocks), TRUNK)
    depth[TRUNK + BRANCHES :] = TRUNK + 1
    position = (np.repeat(depth, seg) * seg + np.arange(blocks * seg) % seg).astype(np.float32)
    half = HEAD_DIM // 2
    freq = (np.float32(theta) ** (-np.arange(half, dtype=np.float32) / half)).astype(np.float32)
    angle = (position[:, None] * freq[None, :]).astype(np.float32)
    cosine = np.tile(np.cos(angle), (1, 4)).astype(np.float32)
    sine = np.sin(angle).astype(np.float32)
    sine = np.concatenate([-sine, sine, -sine, sine], axis=1)
    return jnp.asarray(cosine), jnp.asarray(sine)


def turn(values, cosine, sine):
    width = values.shape[1]
    reps = width // cosine.shape[1]
    if reps > 1:
        cosine = jnp.concatenate([cosine] * reps, axis=1)
        sine = jnp.concatenate([sine] * reps, axis=1)
    lane = lax.broadcasted_iota(jnp.int32, values.shape, 1)
    half = HEAD_DIM // 2
    other = jnp.where(
        lane % HEAD_DIM < half, pltpu.roll(values, width - half, 1), pltpu.roll(values, half, 1)
    )
    return values * cosine + other * sine


SIDES = (1, -1)


def far_of(place, side):
    return place if side == 1 else LINE - 1 - place


def greet(place, partners=()):
    barrier = pltpu.get_barrier_semaphore()
    for partner in partners:
        pl.semaphore_signal(barrier, inc=1, device_id={"dp": partner}, device_id_type=MESH)
    for side in SIDES:

        @pl.when(far_of(place, side) < LINE - 1)
        def _():
            pl.semaphore_signal(
                barrier, inc=1, device_id={"tensor": place + side}, device_id_type=MESH
            )

    edge = (place == 0) | (place == LINE - 1)

    @pl.when(edge)
    def _():
        pl.semaphore_wait(barrier, 1 + len(partners))

    @pl.when(jnp.logical_not(edge))
    def _():
        pl.semaphore_wait(barrier, 2 + len(partners))


def chunk_rows(chunk, rows):
    return pl.ds(chunk * rows, rows)


class Gather:
    def __init__(self, place, buf, send, recv, chunks, own=None):
        self.place, self.buf, self.sems, self.chunks = place, buf, (send, recv), chunks
        self.rows = buf.shape[1] // chunks
        self.own = own

    def copy(self, side, step, chunk, shard, target):
        rows = chunk_rows(chunk, self.rows)
        where = self.buf.at[shard, rows]
        index = 0 if side == 1 else 1
        spot = (index, step - 1, chunk)
        source = where
        if step == 1 and self.own is not None:
            source = self.own.at[rows]
        return pltpu.make_async_remote_copy(
            src_ref=source,
            dst_ref=where,
            send_sem=self.sems[0].at[spot],
            recv_sem=self.sems[1].at[spot],
            device_id={"tensor": target},
            device_id_type=MESH,
        )

    def each_send(self, step, chunk, act, least=0, most=LINE):
        for side in SIDES:
            far = far_of(self.place, side)

            @pl.when((far < LINE - 1) & (far >= step - 1) & (far >= least) & (far <= most))
            def _():
                shard = self.place - side * (step - 1)
                act(self.copy(side, step, chunk, shard, self.place + side))

    def send(self, step, chunk, least=0, most=LINE):
        self.each_send(step, chunk, lambda copy: copy.start(), least, most)

    def arrive(self, step, chunk):
        for side in SIDES:

            @pl.when(far_of(self.place, side) >= step)
            def _():
                shard = self.place - side * step
                self.copy(side, step, chunk, shard, self.place - side).wait_recv()

    def relay(self, step, chunk):
        for side in SIDES:
            far = far_of(self.place, side)

            @pl.when((far < LINE - 1) & (far >= step - 1))
            def _():
                before = self.place - side * (step - 1)
                self.copy(side, step - 1, chunk, before, self.place - side).wait_recv()
                self.copy(side, step, chunk, before, self.place + side).start()

    def close(self):
        for side in SIDES:

            @pl.when(far_of(self.place, side) == LINE - 1)
            def _():
                for step in range(1, LINE):
                    for chunk in range(self.chunks):
                        shard = self.place - side * step
                        self.copy(side, step, chunk, shard, self.place - side).wait_recv()

    def drain(self, stop=LINE, start=1):
        for step in range(start, stop):
            for chunk in range(self.chunks):
                self.each_send(step, chunk, lambda copy: copy.wait_send())


class Sum:
    def __init__(self, place, part, held, send, recv, chunks):
        self.place, self.part, self.held = place, part, held
        self.sems, self.chunks = (send, recv), chunks
        self.rows = part.shape[1] // chunks

    def copy(self, side, step, chunk, shard, target):
        rows = chunk_rows(chunk, self.rows)
        index = 0 if side == 1 else 1
        spot = (index, step - 1, chunk)
        return pltpu.make_async_remote_copy(
            src_ref=self.part.at[shard, rows],
            dst_ref=self.held.at[index, step - 1, rows],
            send_sem=self.sems[0].at[spot],
            recv_sem=self.sems[1].at[spot],
            device_id={"tensor": target},
            device_id_type=MESH,
        )

    def add(self, step, chunk):
        rows = chunk_rows(chunk, self.rows)
        for index, side in enumerate(SIDES):
            far = far_of(self.place, side)
            shard = self.place + side * (LINE - step)

            @pl.when((far >= 1) & (far <= step - 1))
            def _():
                self.copy(side, step - 1, chunk, self.place, self.place - side).wait_recv()
                self.part[shard, rows] = (
                    self.part[shard, rows].astype(f32)
                    + self.held[index, step - 2, rows].astype(f32)
                ).astype(bf16)

    def send(self, step, chunk, least=0, most=LINE):
        if step > 1 and most > 0:
            self.add(step, chunk)
        for side in SIDES:
            far = far_of(self.place, side)
            shard = self.place + side * (LINE - step)

            @pl.when((far <= step - 1) & (far >= least) & (far <= most))
            def _():
                self.copy(side, step, chunk, shard, self.place + side).start()

    def begin(self, step, chunk):
        self.send(step, chunk, most=0)

    def relay(self, step, chunk):
        self.send(step, chunk, least=1)

    def total(self, chunk, out):
        rows = chunk_rows(chunk, self.rows)
        out[rows] = self.part[self.place, rows].astype(f32)
        for index, side in enumerate(SIDES):

            @pl.when(far_of(self.place, side) >= 1)
            def _():
                self.copy(side, LINE - 1, chunk, self.place, self.place - side).wait_recv()
                out[rows] += self.held[index, LINE - 2, rows].astype(f32)

    def drain(self, stop=LINE):
        for step in range(1, stop):
            for chunk in range(self.chunks):
                for side in SIDES:
                    far = far_of(self.place, side)
                    shard = self.place + side * (LINE - step)

                    @pl.when(far <= step - 1)
                    def _():
                        self.copy(side, step, chunk, shard, self.place + side).wait_send()


def line_sems(chunks):
    return [pltpu.SemaphoreType.DMA((2, LINE - 1, chunks))] * 2


def fetch(pairs, sems):
    copies = [pltpu.make_async_copy(src, dst, sems.at[i]) for i, (src, dst) in enumerate(pairs)]
    for copy in copies:
        copy.start()
    return copies


IN_VMEM = pl.BlockSpec(memory_space=pltpu.VMEM)
IN_HBM = pl.BlockSpec(memory_space=pl.ANY)


def comm_params(number):
    return pltpu.CompilerParams(
        vmem_limit_bytes=VMEM_LIMIT, collective_id=number, has_side_effects=True
    )


def gather_norm_body(chunks, x_ref, gain_ref, buf, own, sem, send, recv):
    place = lax.axis_index("tensor")
    greet(place)
    rows = x_ref[...].astype(f32)
    rms = lax.rsqrt(jnp.mean(rows * rows, axis=1, keepdims=True) + eps)
    own[...] = (rows * rms * gain_ref[...].astype(f32)).astype(bf16)
    gather = Gather(place, buf, send, recv, chunks, own)
    for chunk in range(chunks):
        gather.send(1, chunk)
    (kept,) = fetch([(own, buf.at[place])], sem)
    for chunk in range(chunks):
        gather.arrive(1, chunk)
        gather.send(2, chunk)
    kept.wait()
    for chunk in range(chunks):
        gather.arrive(2, chunk)
    gather.drain(stop=LINE - 1)


def gather_norm(x, gain, chunks=2):
    rows, features = x.shape
    return pl.pallas_call(
        functools.partial(gather_norm_body, chunks),
        in_specs=[IN_VMEM, IN_VMEM],
        out_specs=IN_HBM,
        out_shape=jax.ShapeDtypeStruct((LINE, rows, features), bf16),
        scratch_shapes=[pltpu.VMEM((rows, features), bf16), pltpu.SemaphoreType.DMA((1,))]
        + line_sems(chunks),
        compiler_params=comm_params(0),
    )(x, gain[None, :])


def front_body(
    chunks, seg,
    x_ref, w_ref, c_ref, e_ref, a_ref, cos_ref, sin_ref, p_ref, oe_ref, f_ref, tok_ref, gain_ref,
    kept_ref, y_ref, mid_ref, n_ref, cot_ref, l_ref, att_ref, lse_ref, lo_ref,
    buf, yv, wv, wo, part, held, own, midv, xsem, wsem, ysem, nsem, msem, send, recv,
    s_send, s_recv, g_send, g_recv, c_send, c_recv,
):
    place = lax.axis_index("tensor")
    groups, total, width = y_ref.shape
    rows, rank = x_ref.shape[1], a_ref.shape[1]
    edge = (place == 0) | (place == LINE - 1)
    last = place ^ (LINE - 1)

    def passed(side):
        shard = place - side * (LINE - 2)
        index = 0 if side == 1 else 1
        return pltpu.make_async_remote_copy(
            src_ref=x_ref.at[shard],
            dst_ref=buf.at[shard],
            send_sem=send.at[index],
            recv_sem=recv.at[index],
            device_id={"tensor": place + side},
            device_id_type=MESH,
        )

    def came(side):
        index = 0 if side == 1 else 1
        return pltpu.make_async_remote_copy(
            src_ref=x_ref.at[last],
            dst_ref=buf.at[last],
            send_sem=send.at[index],
            recv_sem=recv.at[index],
            device_id={"tensor": place - side},
            device_id_type=MESH,
        )

    copies = []
    for slot in range(LINE):
        copy = pltpu.make_async_copy(x_ref.at[place ^ slot], buf.at[place ^ slot], xsem.at[slot])
        if slot < LINE - 1:
            copy.start()
        else:
            pl.when(jnp.logical_not(edge))(copy.start)
        copies.append(copy)
    load, load_out = fetch(
        [(w_ref.at[:, : groups * width], wv), (w_ref.at[:, groups * width :], wo)], wsem
    )
    greet(place)
    cots = Gather(place, cot_ref, c_send, c_recv, chunks, c_ref)
    summed = Sum(place, part, held, s_send, s_recv, chunks)
    gather = Gather(place, n_ref, g_send, g_recv, chunks, own)
    for side in SIDES:
        pl.when(far_of(place, side) == LINE - 2)(passed(side).start)
    for chunk in range(chunks):
        cots.send(1, chunk)

    for copy in copies[:-1]:
        copy.wait()
    load.wait()
    outs = []
    for slot in range(LINE):
        shard = place ^ slot
        if slot == LINE - 1:
            pl.when(jnp.logical_not(edge))(copies[slot].wait)
            for side in SIDES:
                pl.when(far_of(place, side) == LINE - 1)(came(side).wait_recv)
            kept = pltpu.make_async_copy(buf.at[last], kept_ref.at[last], xsem.at[slot])
            pl.when(edge)(kept.start)
        mine = pl.ds(pl.multiple_of(shard * rows, rows), rows)
        low = nt(buf[shard], e_ref[:groups].reshape(groups * rank, -1)).astype(bf16)
        l_ref[mine] = low
        for g in range(groups):
            band = slice(g * width, (g + 1) * width)
            value = nn(buf[shard], wv[:, band]) + nn(low[:, g * rank : (g + 1) * rank], a_ref[g])
            if g < groups - 1:
                value = turn(value, cos_ref[mine], sin_ref[mine])
            yv[g, mine] = value.astype(bf16)
            out = pltpu.make_async_copy(yv.at[g, mine], y_ref.at[g, mine], ysem.at[slot, g])
            out.start()
            outs.append(out)

    pair = 2 * HEAD_DIM

    def one_pair(j, carry):
        lanes = pl.ds(pl.multiple_of(j * pair, pair), pair)
        attend_pair(seg, yv, lanes, p_ref[...], j, att_ref, lse_ref)

        @pl.when(j == 0)
        def _():
            for chunk in range(chunks):
                cots.relay(2, chunk)

        return carry

    lax.fori_loop(0, width // pair, one_pair, 0)

    load_out.wait()
    for slot in (3, 2, 1, 0):
        shard = place ^ slot
        mine = pl.ds(pl.multiple_of(shard * rows, rows), rows)
        d = att_ref[mine]
        low = nt(d, oe_ref[...]).astype(bf16)
        lo_ref[mine] = low
        part[shard] = (nt(d, wo[...]) + nn(low, f_ref[0])).astype(bf16)
        if slot == 3:
            summed.begin(1, 0)
    for chunk in range(chunks):
        for step in (1, 2, 3):
            if chunk or step > 1:
                summed.begin(step, chunk)
    size = rows // chunks
    stores = []
    for chunk in range(chunks):
        summed.relay(2, chunk)
        summed.relay(3, chunk)
        cots.relay(3, chunk)
        summed.total(chunk, midv)
        here = chunk_rows(chunk, size)
        value = midv[here] + tok_ref[here].astype(f32)
        midv[here] = value
        rms = lax.rsqrt(jnp.mean(value * value, axis=1, keepdims=True) + eps)
        own[here] = (value * rms * gain_ref[...].astype(f32)).astype(bf16)
        stores.append(pltpu.make_async_copy(own.at[here], n_ref.at[place, here], nsem.at[chunk]))
        stores.append(pltpu.make_async_copy(midv.at[here], mid_ref.at[here], msem.at[chunk]))
        gather.send(1, chunk, least=1)
        for store in stores[-2:]:
            store.start()
    for chunk in range(chunks):
        gather.send(1, chunk, most=0)
    for step in (2, 3):
        for chunk in range(chunks):
            gather.relay(step, chunk)
    cots.close()
    gather.close()
    pl.when(edge)(kept.wait)
    for out in outs + stores:
        out.wait()
    for side in SIDES:
        pl.when(far_of(place, side) == LINE - 2)(passed(side).wait_send)
    summed.drain()
    gather.drain()
    cots.drain()


def front(x, weight, cot, entries, exits, tables, leaf_parent, out_entry, finals, tokens, gain, seg, chunks=4):
    _, rows, features = x.shape
    groups, rank, width = exits.shape
    total = LINE * rows
    shards = jax.ShapeDtypeStruct((LINE, rows, features), bf16)
    return pl.pallas_call(
        functools.partial(front_body, chunks, seg),
        in_specs=[IN_HBM] * 3 + [IN_VMEM] * 9,
        out_specs=[IN_HBM] * 5 + [IN_VMEM] * 4,
        out_shape=[
            shards,
            jax.ShapeDtypeStruct((groups, total, width), bf16),
            jax.ShapeDtypeStruct((rows, features), f32),
            shards,
            shards,
            jax.ShapeDtypeStruct((total, groups * rank), bf16),
            jax.ShapeDtypeStruct((total, width), bf16),
            jax.ShapeDtypeStruct((width // (2 * HEAD_DIM), 2, total), f32),
            jax.ShapeDtypeStruct((total, rank), bf16),
        ],
        scratch_shapes=[
            pltpu.VMEM((LINE, rows, features), bf16),
            pltpu.VMEM((groups, total, width), bf16),
            pltpu.VMEM((features, groups * width), bf16),
            pltpu.VMEM((features, width), bf16),
            pltpu.VMEM((LINE, rows, features), bf16),
            pltpu.VMEM((2, LINE - 1, rows, features), bf16),
            pltpu.VMEM((rows, features), bf16),
            pltpu.VMEM((rows, features), f32),
            pltpu.SemaphoreType.DMA((LINE,)),
            pltpu.SemaphoreType.DMA((2,)),
            pltpu.SemaphoreType.DMA((LINE, groups)),
            pltpu.SemaphoreType.DMA((chunks,)),
            pltpu.SemaphoreType.DMA((chunks,)),
            pltpu.SemaphoreType.DMA((2,)),
            pltpu.SemaphoreType.DMA((2,)),
        ]
        + line_sems(chunks)
        + line_sems(chunks)
        + line_sems(chunks),
        input_output_aliases={0: 0},
        compiler_params=comm_params(1),
    )(x, weight, cot, entries, exits, *tables, leaf_parent, out_entry, finals, tokens, gain[None, :])


class Trees:
    def __init__(self, tree, ref, send, recv):
        self.tree, self.ref, self.sems = tree, ref, (send, recv)
        self.rounds = ref.shape[0].bit_length() - 1
        self.partners = [self.partner(number) for number in range(self.rounds)]

    def partner(self, number):
        size = 1 << number
        return self.tree + size - 2 * size * ((self.tree // size) % 2)

    def copy(self, number, owner):
        size = 1 << number
        here = pl.ds((owner // size) * size, size)
        return pltpu.make_async_remote_copy(
            src_ref=self.ref.at[here],
            dst_ref=self.ref.at[here],
            send_sem=self.sems[0].at[number],
            recv_sem=self.sems[1].at[number],
            device_id={"dp": self.partner(number)},
            device_id_type=MESH,
        )

    def send(self, number):
        self.copy(number, self.tree).start()

    def arrive(self, number):
        self.copy(number, self.partner(number)).wait_recv()

    def advance(self, number):
        if number < self.rounds:
            self.arrive(number - 1)
            self.send(number)

    def drain(self):
        for number in range(self.rounds):
            self.copy(number, self.tree).wait_send()


def back_body(
    chunks, seg,
    q_ref, w_ref, n_ref, mid_ref, middle_ref, res_ref, right_ref, left_ref, x_ref,
    o_ref, g_ref, lse_ref, p_ref, cos_ref, sin_ref, a_ref, e_ref, gain_ref, lone_ref, final_ref, exit_ref,
    out_ref, model_ref, head_ref, sum_ref,
    qv, dv, dq_t, dk_sum, dv_sum, part, held, acc, wv, midv, nv, terms, xv, outv, resv, model, head, low, block, extra,
    qsem, wsem, osem, e_send, e_recv, send, recv, x_send, x_recv, t_send, t_recv, h_send, h_recv,
):
    place = lax.axis_index("tensor")
    tree = lax.axis_index("dp")
    trees = Trees(tree, model_ref, t_send, t_recv)
    heads = Trees(tree, head_ref, h_send, h_recv)
    groups, total, width = q_ref.shape
    rank = a_ref.shape[1]
    (load_q,) = fetch([(q_ref, qv)], qsem)
    loads = fetch(
        [
            (w_ref.at[:, : groups * width], wv),
            (n_ref, nv),
            (mid_ref, midv),
            (middle_ref, acc),
            (res_ref.at[place], terms.at[0]),
            (x_ref, xv),
        ],
        wsem,
    )
    block[...] = jnp.zeros_like(block)
    for g in range(groups):
        block[g * rank : (g + 1) * rank, g * width : (g + 1) * width] = a_ref[g]
    greet(place, trees.partners)

    def exchange(side, target):
        index = 0 if side == 1 else 1
        return pltpu.make_async_remote_copy(
            src_ref=(right_ref, left_ref)[index],
            dst_ref=terms.at[index + 1],
            send_sem=e_send.at[index],
            recv_sem=e_recv.at[index],
            device_id={"tensor": target},
            device_id_type=MESH,
        )

    for side in SIDES:
        pl.when(far_of(place, side) < LINE - 1)(exchange(side, place + side).start)
    load_q.wait()
    pair = 2 * HEAD_DIM

    def one_pair(j, carry):
        lanes = pl.ds(pl.multiple_of(j * pair, pair), pair)
        attend_back_pair(
            seg, qv, lanes, o_ref, g_ref, lse_ref, j, p_ref[...], cos_ref, sin_ref, dv, dq_t, dk_sum, dv_sum
        )
        return carry

    lax.fori_loop(0, width // pair, one_pair, 0)
    loads[0].wait()
    rows = part.shape[1]
    summed = Sum(place, part, held, send, recv, chunks)
    gather = Gather(place, extra, x_send, x_recv, 1)
    entry = e_ref[:groups].reshape(groups * rank, -1)

    def rows_of(slot):
        shard = place ^ slot
        mine = pl.ds(pl.multiple_of(shard * rows, rows), rows)
        return shard, mine, jnp.concatenate([dv[g, mine] for g in range(groups)], axis=1)

    def lower(slot):
        _, mine, d = rows_of(slot)
        low[mine] = nt(d, block[...]).astype(bf16)

    def partial(slot):
        shard, mine, d = rows_of(slot)
        part[shard] = (nt(d, wv[...]) + nn(low[mine], entry)).astype(bf16)

    lower(3)
    partial(3)
    summed.begin(1, 0)
    summed.begin(1, 1)
    for slot in (2, 1, 0):
        lower(slot)
    for load in loads[1:]:
        load.wait()

    def turned(value):
        return value.astype(f32).T.astype(bf16)

    joined = nn(turned(low[...]), nv[...].reshape(total, -1))
    extra[place] = jnp.concatenate([joined, final_ref[...]], axis=0).astype(bf16)
    gather.send(1, 0)
    for chunk in range(2, chunks):
        summed.begin(1, chunk)
    for slot in (2, 1, 0):
        partial(slot)
    for step in (2, 3):
        for chunk in range(chunks):
            summed.begin(step, chunk)
    summed.relay(2, 0)
    summed.relay(2, 1)
    gather.arrive(1, 0)
    gather.send(2, 0)
    summed.relay(2, 2)
    low_one = turned(lone_ref[...])
    for g in range(groups):
        band = slice(g * rank, (g + 1) * rank)
        head[band] = nn(low_one[band], dv[g]).astype(bf16)
    head[groups * rank :] = exit_ref[...].astype(bf16)
    (store,) = fetch([(head, head_ref.at[tree])], osem)
    summed.relay(2, 3)
    store.wait()
    heads.send(0)
    gather.arrive(2, 0)
    gather.send(3, 0)
    heads.advance(1)
    summed.relay(3, 0)
    gather.arrive(3, 0)
    model[...] = functools.reduce(
        jnp.add, [extra[shard].astype(f32) for shard in range(LINE)]
    ).astype(bf16)
    (store,) = fetch([(model, model_ref.at[tree])], osem)
    for side in SIDES:
        pl.when(far_of(place, side) > 0)(exchange(side, place - side).wait_recv)
    value = acc[...] + terms[0].astype(f32)
    for index, side in enumerate(SIDES):
        value += jnp.where(far_of(place, side) > 0, terms[index + 1].astype(f32), 0.0)
    resv[...] = value.astype(bf16)
    store.wait()
    trees.send(0)
    (store,) = fetch([(resv, sum_ref)], osem)
    heads.advance(2)
    summed.relay(3, 1)
    trees.advance(1)
    summed.relay(3, 2)
    summed.relay(3, 3)
    trees.advance(2)
    store.wait()
    size = rows // chunks
    stores = []

    def finish(chunk):
        summed.total(chunk, acc)
        here = chunk_rows(chunk, size)
        values = xv[here].astype(f32)
        rms = lax.rsqrt(jnp.mean(values * values, axis=1, keepdims=True) + eps)
        scaled = acc[here] * gain_ref[...].astype(f32)
        mean = jnp.mean(scaled * values, axis=1, keepdims=True)
        outv[here] = (midv[here] + rms * (scaled - values * (rms * rms) * mean)).astype(bf16)
        copy = pltpu.make_async_copy(outv.at[here], out_ref.at[here], wsem.at[chunk])
        copy.start()
        stores.append(copy)

    finish(0)
    finish(1)
    for number in range(3, trees.rounds):
        trees.advance(number)
        heads.advance(number)
    finish(2)
    finish(3)
    for blocks in (trees, heads):
        blocks.arrive(blocks.rounds - 1)
        blocks.drain()
    for copy in stores:
        copy.wait()
    for side in SIDES:
        pl.when(far_of(place, side) < LINE - 1)(exchange(side, place + side).wait_send)
    summed.drain()
    gather.drain()


def back(
    qkv, weight, normed, grad_middle, middle, res_parts, right, left, x, attended, grad, lse, leaf_parent, tables, exits,
    entries, gain, low_one, final_grads, exit_grads, seg,
):
    chunks = LINE
    rows, features = x.shape
    groups, total, width = qkv.shape
    rank = exits.shape[1]
    deep = (groups + 1) * rank
    pair = 2 * HEAD_DIM
    trees = lax.axis_size("dp")
    sems = pltpu.SemaphoreType.DMA((trees.bit_length() - 1,))
    two = pltpu.SemaphoreType.DMA((2,))
    return pl.pallas_call(
        functools.partial(back_body, chunks, seg),
        in_specs=[IN_HBM] * 9 + [IN_VMEM] * 12,
        out_specs=[IN_HBM] * 4,
        out_shape=[
            jax.ShapeDtypeStruct((rows, features), bf16),
            jax.ShapeDtypeStruct((trees, deep, features), bf16),
            jax.ShapeDtypeStruct((trees, deep, width), bf16),
            jax.ShapeDtypeStruct((rows, features), bf16),
        ],
        scratch_shapes=[
            pltpu.VMEM((groups, total, width), bf16),
            pltpu.VMEM((groups, total, width), bf16),
            pltpu.VMEM((pair, total), f32),
            pltpu.VMEM((total, pair), f32),
            pltpu.VMEM((total, pair), f32),
            pltpu.VMEM((LINE, rows, features), bf16),
            pltpu.VMEM((2, LINE - 1, rows, features), bf16),
            pltpu.VMEM((rows, features), f32),
            pltpu.VMEM((features, groups * width), bf16),
            pltpu.VMEM((rows, features), f32),
            pltpu.VMEM((LINE, rows, features), bf16),
            pltpu.VMEM((3, rows, features), bf16),
            pltpu.VMEM((rows, features), bf16),
            pltpu.VMEM((rows, features), bf16),
            pltpu.VMEM((rows, features), bf16),
            pltpu.VMEM((deep, features), bf16),
            pltpu.VMEM((deep, width), bf16),
            pltpu.VMEM((total, groups * rank), bf16),
            pltpu.VMEM((groups * rank, groups * width), bf16),
            pltpu.VMEM((LINE, deep, features), bf16),
            pltpu.SemaphoreType.DMA((1,)),
            pltpu.SemaphoreType.DMA((6,)),
            pltpu.SemaphoreType.DMA((1,)),
            two,
            two,
        ]
        + line_sems(chunks)
        + line_sems(1)
        + [sems] * 4,
        compiler_params=comm_params(3),
    )(
        qkv, weight, normed, grad_middle, middle, res_parts, right, left, x, attended, grad[0], lse, leaf_parent, *tables,
        exits, entries, gain[None, :], low_one, final_grads, exit_grads,
    )


def tree_tiles(seg, rows, parent_row):
    trunk = TRUNK * seg
    leaves = trunk + BRANCHES * seg
    key = lax.broadcasted_iota(jnp.int32, (QT, QT), 0)
    query = lax.broadcasted_iota(jnp.int32, (QT, QT), 1)
    causal = key <= query
    own = causal & (key // seg == query // seg)
    tiles = []
    for start in range(0, trunk, QT):
        pieces = [(0, start, None)] if start else []
        tiles.append((start, pieces + [(start, QT, causal)]))
    tiles.append((trunk, [(0, trunk, None), (trunk, QT, own)]))
    branch = lax.broadcasted_iota(jnp.int32, (BRANCHES * seg, QT), 0) // seg
    for start in range(leaves, rows, QT):
        mine = branch == parent_row[:, start - leaves : start - leaves + QT]
        tiles.append(
            (start, [(0, trunk, None), (trunk, BRANCHES * seg, mine), (start, QT, own)])
        )
    return tiles


def attend_pair(seg, qkv_ref, lanes, parent_row, pair, o_ref, lse_ref):
    rows = qkv_ref.shape[1]
    value_t = qkv_ref[2, :, lanes].T
    lane = lax.broadcasted_iota(jnp.int32, (QT, 2 * HEAD_DIM), 1)
    for start, pieces in tree_tiles(seg, rows, parent_row):
        query = qkv_ref[0, start : start + QT, lanes] * bf16(HEAD_DIM**-0.5)
        outs = []
        for h in range(2):
            own_query = jnp.where(lane // HEAD_DIM == h, query, bf16(0))
            scores = []
            for k0, count, mask in pieces:
                s = nt(qkv_ref[1, k0 : k0 + count, lanes], own_query)
                scores.append(s if mask is None else jnp.where(mask, s, -1e30))
            top = functools.reduce(
                jnp.maximum, [jnp.max(s, axis=0, keepdims=True) for s in scores]
            )
            summed, out = 0.0, 0.0
            for (k0, count, _), s in zip(pieces, scores):
                weights = jnp.exp(s - top)
                summed += jnp.sum(weights, axis=0, keepdims=True)
                out += nn(
                    value_t[h * HEAD_DIM : (h + 1) * HEAD_DIM, k0 : k0 + count],
                    weights.astype(bf16),
                )
            outs.append(out / summed)
            lse_ref[pair, h : h + 1, start : start + QT] = top + jnp.log(summed)
        o_ref[start : start + QT, lanes] = jnp.concatenate(outs, axis=0).T.astype(bf16)


def attend_back_pair(
    seg, qkv_ref, lanes, o_ref, g_ref, lse_ref, pair, parent_row, cos_ref, sin_ref, d_ref, dq_t, dk, dv
):
    rows = qkv_ref.shape[1]
    scale = bf16(HEAD_DIM**-0.5)
    key_t = qkv_ref[1, :, lanes].T
    weighed_t = (g_ref[:, lanes].astype(f32) * o_ref[:, lanes].astype(f32)).T
    lane = lax.broadcasted_iota(jnp.int32, (QT, 2 * HEAD_DIM), 1)
    dk[...] = jnp.zeros_like(dk)
    dv[...] = jnp.zeros_like(dv)
    for start, pieces in tree_tiles(seg, rows, parent_row):
        query = qkv_ref[0, start : start + QT, lanes] * scale
        grad = g_ref[start : start + QT, lanes]
        for h in range(2):
            mine = lane // HEAD_DIM == h
            own_query = jnp.where(mine, query, bf16(0))
            own_grad = jnp.where(mine, grad, bf16(0))
            band = slice(h * HEAD_DIM, (h + 1) * HEAD_DIM)
            delta = jnp.sum(weighed_t[band, start : start + QT], axis=0, keepdims=True)
            lse = lse_ref[pair, h : h + 1, start : start + QT]
            grad_q = 0.0
            for k0, count, mask in pieces:
                probs = jnp.exp(nt(qkv_ref[1, k0 : k0 + count, lanes], own_query) - lse)
                if mask is not None:
                    probs = jnp.where(mask, probs, 0.0)
                grad_probs = nt(qkv_ref[2, k0 : k0 + count, lanes], own_grad)
                grad_scores = (probs * (grad_probs - delta)).astype(bf16)
                dk[k0 : k0 + count] += nn(grad_scores, own_query)
                dv[k0 : k0 + count] += nn(probs.astype(bf16), own_grad)
                grad_q += nn(key_t[band, k0 : k0 + count], grad_scores)
            dq_t[band, start : start + QT] = grad_q
    cosine, sine = cos_ref[...], -sin_ref[...]
    d_ref[0, :, lanes] = turn(dq_t[...].T * HEAD_DIM**-0.5, cosine, sine).astype(bf16)
    d_ref[1, :, lanes] = turn(dk[...], cosine, sine).astype(bf16)
    d_ref[2, :, lanes] = dv[...].astype(bf16)


def feed_body(
    rank, tile, chunks,
    n_ref, c_ref, far_ref, wg_ref, wu_ref, wd_ref, mid_ref, wo_ref,
    pick_ref, xu_in, xd_in, e_in, f_in, gain_ref, oe_ref, att_ref, lo_ref,
    grad_ref, res_ref, right_ref, left_ref, b_ref, held_ref, unit_out, model_out, y_ref, final_ref, exit_ref,
    unit_ref, model_ref, x_ref, e_ref, f_ref, midv, nbuf, cbuf, wbuf, low, low_t, acc_res, acc_back, acc_low,
    part, held, resv, own, extra, wo, nsem, csem, wsem, rsem, msem,
    send, recv, g_send, g_recv, x_send, x_recv, r_send, r_recv,
):
    place = lax.axis_index("tensor")
    units = unit_ref.shape[1]
    tiles = units // tile
    rows = part.shape[1]
    summed = Sum(place, part, held, send, recv, chunks)
    gather = Gather(place, b_ref, g_send, g_recv, chunks, own)
    joint = Gather(place, extra, x_send, x_recv, 1)

    def load_rows(order, act):
        into = order % 2
        shard = place ^ (LINE - 1 - order)
        act(pltpu.make_async_copy(n_ref.at[shard], nbuf.at[into], nsem.at[into]))

        def take(source):
            act(pltpu.make_async_copy(source, cbuf.at[into], csem.at[into]))

        pl.when(order == LINE - 1)(lambda: take(c_ref))
        pl.when(order < LINE - 1)(lambda: take(far_ref.at[shard]))

    def load_weights(index, into, act):
        columns = pl.ds(pl.multiple_of(index * tile, tile), tile)
        for k, w_ref in enumerate((wg_ref, wu_ref, wd_ref)):
            act(pltpu.make_async_copy(w_ref.at[:, columns], wbuf.at[into, k], wsem.at[into, k]))

    def start(copy):
        copy.start()

    def wait(copy):
        copy.wait()

    load_rows(jnp.int32(0), start)
    load_weights(0, 0, start)
    width = wo.shape[1]
    load_middle, load_out = fetch([(mid_ref, midv), (wo_ref.at[:, 3 * width :], wo)], msem)
    for padded in (x_ref, e_ref, f_ref):
        padded[...] = jnp.zeros_like(padded)
    x_ref[0, :rank] = xu_in[0]
    x_ref[1, rank : 2 * rank] = xu_in[1]
    x_ref[2, 2 * rank :] = xd_in[...]
    e_ref[: 2 * rank] = e_in[3:].reshape(2 * rank, -1)
    f_ref[2 * rank :] = f_in[1]
    unit_ref[...] = jnp.zeros_like(unit_ref)
    model_ref[...] = jnp.zeros_like(model_ref)
    greet(place)

    def one_shard(order, carry):
        into = order % 2
        shard = place ^ (LINE - 1 - order)
        load_rows(order, wait)

        @pl.when(order < LINE - 1)
        def _():
            load_rows(order + 1, start)

        first = nt(nbuf[into], e_ref[...]) + nt(cbuf[into], f_ref[...])
        low[...] = first.astype(bf16)
        low_t[...] = first.T.astype(bf16)
        acc_res[...] = jnp.zeros_like(acc_res)
        acc_back[...] = jnp.zeros_like(acc_back)
        acc_low[...] = jnp.zeros_like(acc_low)

        def one_tile(index, carry):
            stage = order * tiles + index
            at = stage % 2
            load_weights(index, at, wait)

            @pl.when(stage < LINE * tiles - 1)
            def _():
                load_weights((index + 1) % tiles, 1 - at, start)

            columns = pl.ds(pl.multiple_of(index * tile, tile), tile)
            x_gate, x_rise, x_fall = x_ref[0, :, columns], x_ref[1, :, columns], x_ref[2, :, columns]
            gate = nn(nbuf[into], wbuf[at, 0]) + nn(low[...], x_gate)
            rise = nn(nbuf[into], wbuf[at, 1]) + nn(low[...], x_rise)
            grad_hidden = nn(cbuf[into], wbuf[at, 2]) + nn(low[...], x_fall)
            sigmoid = jax.nn.sigmoid(gate)
            silu = gate * sigmoid
            hidden = (silu * rise).astype(bf16)
            grad_gate = (grad_hidden * rise * sigmoid * (1.0 + gate * (1.0 - sigmoid))).astype(bf16)
            grad_rise = (grad_hidden * silu).astype(bf16)
            acc_back[...] += nt(grad_gate, wbuf[at, 0]) + nt(grad_rise, wbuf[at, 1])
            acc_res[...] += nt(hidden, wbuf[at, 2])
            acc_low[...] += nt(grad_gate, x_gate) + nt(grad_rise, x_rise) + nt(hidden, x_fall)
            unit_ref[:rank, columns] += nn(low_t[:rank], grad_gate)
            unit_ref[rank : 2 * rank, columns] += nn(low_t[rank : 2 * rank], grad_rise)
            unit_ref[2 * rank :, columns] += nn(low_t[2 * rank : 3 * rank], hidden)
            return carry

        lax.fori_loop(0, tiles, one_tile, 0)
        joined = acc_low[...].astype(bf16)
        joined_t = acc_low[...].T.astype(bf16)
        part[shard] = (acc_back[...] + nn(joined, e_ref[...])).astype(bf16)
        for step in (1, 2, 3):

            @pl.when(order == step - 1)
            def _():
                for chunk in range(chunks):
                    summed.send(step, chunk)

        @pl.when(order > 0)
        def _():
            pltpu.make_async_copy(resv, res_ref.at[shard], rsem.at[0]).wait()

        resv[...] = (acc_res[...] + nn(joined, f_ref[...])).astype(bf16)
        pltpu.make_async_copy(resv, res_ref.at[shard], rsem.at[0]).start()
        model_ref[: 2 * rank] += nn(joined_t[: 2 * rank], nbuf[into])
        model_ref[2 * rank :] += nn(joined_t[2 * rank : 3 * rank], cbuf[into])
        return carry

    lax.fori_loop(0, LINE, one_shard, 0)
    extra[place] = model_ref[...].astype(bf16)
    joint.send(1, 0)
    size = rows // chunks
    last = (LINE - 1) % 2
    load_middle.wait()
    stores = []
    for chunk in range(chunks):
        summed.total(chunk, acc_back)
        here = chunk_rows(chunk, size)
        middle = midv[here]
        rms = lax.rsqrt(jnp.mean(middle * middle, axis=1, keepdims=True) + eps)
        scaled = acc_back[here] * gain_ref[...].astype(f32)
        mean = jnp.mean(scaled * middle, axis=1, keepdims=True)
        grad = cbuf[last, here].astype(f32) + rms * (scaled - middle * (rms * rms) * mean)
        own[here] = grad.astype(bf16)
        gather.send(1, chunk, least=1)
        midv[here] = grad
        store = pltpu.make_async_copy(midv.at[here], grad_ref.at[here], nsem.at[chunk % 2])
        if chunk >= 2:
            stores[chunk - 2].wait()
        store.start()
        stores.append(store)
    for chunk in range(chunks):
        gather.send(1, chunk, most=0)
    pltpu.make_async_copy(resv, res_ref.at[place], rsem.at[0]).wait()

    def pass_on(side, step, source, target):
        index = 0 if side == 1 else 1
        return pltpu.make_async_remote_copy(
            src_ref=source,
            dst_ref=held_ref.at[index, step - 1],
            send_sem=r_send.at[index, step - 1],
            recv_sem=r_recv.at[index, step - 1],
            device_id={"tensor": target},
            device_id_type=MESH,
        )

    def at_far(side, number, act):
        pl.when(far_of(place, side) == number)(act)

    def ready(side, step, shard):
        index = 0 if side == 1 else 1
        pass_on(side, step, resv, place - side).wait_recv()
        copies = [
            pltpu.make_async_copy(res_ref.at[shard], cbuf.at[0], csem.at[0]),
            pltpu.make_async_copy(held_ref.at[index, step - 1], cbuf.at[1], csem.at[1]),
        ]
        for copy in copies:
            copy.start()
        for copy in copies:
            copy.wait()
        cbuf[0] = (cbuf[0].astype(f32) + cbuf[1].astype(f32)).astype(bf16)

    for side in SIDES:
        for step in (1, 2):
            at_far(
                side,
                0,
                lambda: pass_on(side, step, res_ref.at[place + side * (LINE - step)], place + side).start(),
            )

    load_out.wait()
    for store in stores[-2:]:
        store.wait()

    def through(number, rows_ref, shard):
        mine = pl.ds(pl.multiple_of(shard * rows, rows), rows)
        value = rows_ref[...]
        reduced = nt(value, f_in[0])
        y_ref[0, mine] = (nn(value, wo[...]) + nn(reduced.astype(bf16), oe_ref[...])).astype(bf16)
        final = nn(lo_ref[mine].astype(f32).T.astype(bf16), value)
        leave = nn(reduced.T.astype(bf16), att_ref[mine])
        final_ref[...] = final if number == 0 else final_ref[...] + final
        exit_ref[...] = leave if number == 0 else exit_ref[...] + leave

    def take(number, shard):
        copy = pltpu.make_async_copy(b_ref.at[shard], nbuf.at[number % 2], nsem.at[number % 2])
        copy.start()
        copy.wait()
        through(number, nbuf.at[number % 2], shard)

    def edge_got(step):
        for side in SIDES:

            @pl.when(far_of(place, side) == LINE - 1)
            def _():
                for chunk in range(chunks):
                    gather.copy(side, step, chunk, place - side * step, place - side).wait_recv()

    inside = ((place + 1) // 2) % 2
    joint.relay(2, 0)
    through(0, own, place)
    unit_out[: 3 * rank] = unit_ref[...].astype(bf16)
    unit_out[3 * rank :] = jnp.full((rank, units), pick_ref[0, 0], f32).astype(bf16)
    for chunk in range(chunks):
        gather.relay(2, chunk)
    edge_got(1)
    joint.relay(3, 0)
    take(1, place ^ (1 + 2 * inside))
    for chunk in range(chunks):
        gather.relay(3, chunk)
    for side in SIDES:

        @pl.when(far_of(place, side) == 1)
        def _():
            ready(side, 1, place + side * 2)
            resv[...] = cbuf[0]
            pass_on(side, 2, resv, place + side).start()

    edge_got(2)
    take(2, place ^ (2 - inside))
    joint.close()
    model_out[...] = functools.reduce(
        jnp.add, [extra[shard].astype(f32) for shard in range(LINE)]
    ).astype(bf16)
    edge_got(3)
    take(3, place ^ (3 - inside))
    for index, side in enumerate(SIDES):
        target = (right_ref, left_ref)[index]

        @pl.when(far_of(place, side) == 0)
        def _():
            copy = pltpu.make_async_copy(res_ref.at[place + side], nbuf.at[index], nsem.at[index])
            copy.start()
            copy.wait()

        @pl.when((far_of(place, side) > 0) & (far_of(place, side) < LINE - 1))
        def _():
            ready(side, 2, place + side)
            nbuf[index] = cbuf[0]

        copy = pltpu.make_async_copy(nbuf.at[index], target, nsem.at[index])
        copy.start()
        copy.wait()
    for side in SIDES:
        for step in (1, 2):
            at_far(
                side,
                0,
                lambda: pass_on(side, step, res_ref.at[place + side * (LINE - step)], place + side).wait_send(),
            )
        at_far(side, 1, lambda: pass_on(side, 2, resv, place + side).wait_send())
    summed.drain()
    gather.drain()
    joint.drain()


def feed(
    normed, cots, weights, middle, w_heads, pick, units_exit, fall_entry, entries, finals, gain, out_entry,
    attended, low_out, tile=512, chunks=4,
):
    _, rows, features = normed.shape
    units = weights[0].shape[1]
    rank, width = out_entry.shape
    total = LINE * rows
    one = jax.ShapeDtypeStruct((rows, features), bf16)
    return pl.pallas_call(
        functools.partial(feed_body, rank, tile, chunks),
        in_specs=[IN_HBM] * 8 + [pl.BlockSpec(memory_space=pltpu.SMEM)] + [IN_VMEM] * 8,
        out_specs=[IN_HBM] * 6 + [IN_VMEM] * 5,
        out_shape=[
            jax.ShapeDtypeStruct((rows, features), f32),
            jax.ShapeDtypeStruct((LINE, rows, features), bf16),
            one,
            one,
            jax.ShapeDtypeStruct((LINE, rows, features), bf16),
            jax.ShapeDtypeStruct((2, LINE - 2, rows, features), bf16),
            jax.ShapeDtypeStruct((4 * rank, units), bf16),
            jax.ShapeDtypeStruct((3 * rank, features), bf16),
            jax.ShapeDtypeStruct((1, total, width), bf16),
            jax.ShapeDtypeStruct((rank, features), f32),
            jax.ShapeDtypeStruct((rank, width), f32),
        ],
        scratch_shapes=[
            pltpu.VMEM((3 * rank, units), f32),
            pltpu.VMEM((3 * rank, features), f32),
            pltpu.VMEM((3, 3 * rank, units), bf16),
            pltpu.VMEM((3 * rank, features), bf16),
            pltpu.VMEM((3 * rank, features), bf16),
            pltpu.VMEM((rows, features), f32),
            pltpu.VMEM((2, rows, features), bf16),
            pltpu.VMEM((2, rows, features), bf16),
            pltpu.VMEM((2, 3, features, tile), bf16),
            pltpu.VMEM((rows, 3 * rank), bf16),
            pltpu.VMEM((3 * rank, rows), bf16),
            pltpu.VMEM((rows, features), f32),
            pltpu.VMEM((rows, features), f32),
            pltpu.VMEM((rows, 3 * rank), f32),
            pltpu.VMEM((LINE, rows, features), bf16),
            pltpu.VMEM((2, LINE - 1, rows, features), bf16),
            pltpu.VMEM((rows, features), bf16),
            pltpu.VMEM((rows, features), bf16),
            pltpu.VMEM((LINE, 3 * rank, features), bf16),
            pltpu.VMEM((features, width), bf16),
            pltpu.SemaphoreType.DMA((2,)),
            pltpu.SemaphoreType.DMA((2,)),
            pltpu.SemaphoreType.DMA((2, 3)),
            pltpu.SemaphoreType.DMA((1,)),
            pltpu.SemaphoreType.DMA((2,)),
        ]
        + line_sems(chunks)
        + line_sems(chunks)
        + line_sems(1)
        + [pltpu.SemaphoreType.DMA((2, LINE - 2))] * 2,
        compiler_params=comm_params(5),
    )(
        normed, *cots, *weights, middle, w_heads, pick, units_exit, fall_entry, entries, finals, gain[None, :], out_entry,
        attended, low_out,
    )


def pick_body(pick_ref, *refs):
    count = len(refs) // 2
    for source, target in zip(refs[:count], refs[count:]):
        target[...] = source[...].reshape(target.shape)


def picked(pick, arrays):
    shapes = [a.shape[:1] + a.shape[2:] for a in arrays]
    return pl.pallas_call(
        pick_body,
        grid_spec=pltpu.PrefetchScalarGridSpec(
            num_scalar_prefetch=1,
            grid=(1,),
            in_specs=[
                pl.BlockSpec(a.shape[:1] + (1,) + a.shape[2:], lambda i, p: (0, p[0], 0, 0)) for a in arrays
            ],
            out_specs=[pl.BlockSpec(shape, lambda i, p: (0, 0, 0)) for shape in shapes],
        ),
        out_shape=[jax.ShapeDtypeStruct(shape, bf16) for shape in shapes],
    )(pick, *arrays)


def per_tree(block):
    return lax.all_gather(block, "dp", axis=0, tiled=False)


def combine_body(
    rank, pick_ref, early, model, late, head, one, two, entry_ref, final_ref, unit_ref, down_ref, exit_ref, out_ref,
    one_ref, two_ref,
):
    one_ref[...] = one[...]
    two_ref[...] = two[...]
    for ref in (entry_ref, final_ref, unit_ref, down_ref, exit_ref, out_ref):
        ref[...] = jnp.zeros_like(ref)

    def one_tree(tree, carry):
        pick = pick_ref[tree]

        def block(ref, index):
            return ref[tree, index * rank : (index + 1) * rank].astype(f32)

        for k in range(3):
            entry_ref[k, pick] += block(late, k)
            exit_ref[k, pick] += block(head, k)
        final_ref[0, pick] += block(late, 3)
        out_ref[pick] += block(head, 3)
        for k in range(2):
            entry_ref[3 + k, pick] += block(model, k)
            unit_ref[k, pick] += block(early, k)
        final_ref[1, pick] += block(model, 2)
        down_ref[pick] += block(early, 2)
        return carry

    lax.fori_loop(0, early.shape[0], one_tree, 0)


def combine(picks, early, model, late, head, one, two, adapters, steps=4):
    trees, _, features = early.shape
    rank = late.shape[1] // 4
    width = head.shape[2]
    wide, narrow = features // steps, width // steps

    def taken(array, tile):
        return pl.BlockSpec((trees, array.shape[1], tile), lambda i, p: (0, 0, i))

    def given(lead, tile):
        shape = lead + (adapters, rank, tile)
        return pl.BlockSpec(shape, lambda i, p: (0,) * (len(shape) - 1) + (i,))

    whole = pl.BlockSpec((one.shape[0] // steps, one.shape[1]), lambda i, p: (i, 0))

    def shape(lead, full):
        return jax.ShapeDtypeStruct(lead + (adapters, rank, full), f32)

    return pl.pallas_call(
        functools.partial(combine_body, rank),
        grid_spec=pltpu.PrefetchScalarGridSpec(
            num_scalar_prefetch=1,
            grid=(steps,),
            in_specs=[taken(early, wide), taken(model, wide), taken(late, wide), taken(head, narrow), whole, whole],
            out_specs=[
                given((5,), wide),
                given((2,), wide),
                given((2,), wide),
                given((), wide),
                given((3,), narrow),
                given((), narrow),
                whole,
                whole,
            ],
        ),
        out_shape=[
            shape((5,), features),
            shape((2,), features),
            shape((2,), features),
            shape((), features),
            shape((3,), width),
            shape((), width),
            jax.ShapeDtypeStruct(one.shape, bf16),
            jax.ShapeDtypeStruct(two.shape, bf16),
        ],
        compiler_params=pltpu.CompilerParams(vmem_limit_bytes=VMEM_LIMIT),
    )(picks, early, model, late, head, one, two)


def local(
    tokens,
    cotangent,
    attention_gain,
    feed_gain,
    query_weight,
    key_weight,
    value_weight,
    output_weight,
    gate_weight,
    up_weight,
    down_weight,
    entry_maps,
    head_exits,
    unit_exits,
    output_entry,
    down_entry,
    final_exits,
    parents,
    adapter_pick,
):
    adapters, rank = entry_maps.shape[1], entry_maps.shape[3]
    local_rows = tokens.shape[0]
    total = local_rows * lax.axis_size("tensor")
    blocks = parents.shape[1]
    seg = total // blocks
    tables = rope_tables(blocks, seg)
    leaf_parent = (jnp.repeat(parents[0, TRUNK + BRANCHES :], seg) - TRUNK)[None, :]
    gain_one, gain_two = attention_gain, feed_gain

    w_heads = lax.all_gather(
        jnp.concatenate([query_weight, key_weight, value_weight, output_weight], axis=1),
        "dp",
        axis=0,
        tiled=True,
    )

    w_units = [
        lax.all_gather(w, "dp", axis=0, tiled=True) for w in (gate_weight, up_weight, down_weight)
    ]
    entries, heads_exit, units_exit, out_entry, fall_entry, finals = picked(
        adapter_pick,
        (
            jnp.swapaxes(entry_maps, 2, 3),
            head_exits,
            unit_exits,
            jnp.swapaxes(output_entry, 1, 2)[None],
            jnp.swapaxes(down_entry, 1, 2)[None],
            final_exits,
        ),
    )
    out_entry, fall_entry = out_entry[0], fall_entry[0]

    most_one = gather_norm(tokens, gain_one)
    full_one, qkv, middle, full_two, full_cot, low_one, attended, lse, adapt_o = front(
        most_one, w_heads, cotangent, entries, heads_exit, tables, leaf_parent, out_entry, finals, tokens, gain_two, seg
    )

    (
        grad_middle, res_parts, res_right, res_left, _, _, early, model_sum, grad_attended, final_grads, exit_grads,
    ) = feed(
        full_two, (cotangent, full_cot), w_units, middle, w_heads, adapter_pick.astype(f32)[None, :],
        units_exit, fall_entry, entries, finals, gain_two, out_entry, attended, adapt_o,
    )
    early = per_tree(early)
    model_all = per_tree(model_sum)

    grad_tokens, late_model, late_head, result = back(
        qkv, w_heads, full_one, grad_middle, middle, res_parts, res_right, res_left, tokens, attended, grad_attended, lse,
        leaf_parent, tables, heads_exit, entries, gain_one, low_one, final_grads, exit_grads, seg,
    )

    picks = early[:, 3 * rank, 0].astype(jnp.int32)
    grad_entries, grad_finals, grad_units, grad_down, grad_heads, grad_output, result, grad_tokens = combine(
        picks, early, model_all, late_model, late_head, result, grad_tokens, adapters
    )
    grad_entries = grad_entries.swapaxes(2, 3)
    grad_output = grad_output.swapaxes(1, 2)
    grad_down = grad_down.swapaxes(1, 2)
    return (
        result,
        grad_tokens,
        grad_entries,
        grad_heads,
        grad_units,
        grad_output,
        grad_down,
        grad_finals,
    )


def solution(mesh):
    in_specs = (
        P(("dp", "tensor"), None),
        P(("dp", "tensor"), None),
        P(),
        P(),
        P("dp", "tensor"),
        P("dp", "tensor"),
        P("dp", "tensor"),
        P("dp", "tensor"),
        P("dp", "tensor"),
        P("dp", "tensor"),
        P("dp", "tensor"),
        P(),
        P(None, None, None, "tensor"),
        P(None, None, None, "tensor"),
        P(None, "tensor", None),
        P(None, "tensor", None),
        P(),
        P("dp", None),
        P("dp"),
    )
    out_specs = (
        P(("dp", "tensor"), None),
        P(("dp", "tensor"), None),
        P(),
        P(None, None, None, "tensor"),
        P(None, None, None, "tensor"),
        P(None, "tensor", None),
        P(None, "tensor", None),
        P(),
    )
    return jax.shard_map(local, mesh=mesh, in_specs=in_specs, out_specs=out_specs, check_vma=False)
```

```python
import functools

import jax
import jax.numpy as jnp
import numpy as np
from jax import lax
from jax.experimental import pallas as pl
from jax.experimental.pallas import tpu as pltpu
from jax.sharding import PartitionSpec as P

HEAD_DIM = 64
TRUNK, BRANCHES = 8, 4
QT = 256
VMEM_LIMIT = 60 * 1024 * 1024
LINE = 4
MESH = pl.DeviceIdType.MESH

eps = 1e-05
theta = 130000.0
bf16, f32 = jnp.bfloat16, jnp.float32


def nn(left, right):
    return jnp.dot(left, right, preferred_element_type=f32)


def nt(left, right):
    return lax.dot_general(left, right, (((1,), (1,)), ((), ())), preferred_element_type=f32)


def tn(left, right):
    return lax.dot_general(left, right, (((0,), (0,)), ((), ())), preferred_element_type=f32)


def rope_tables(blocks, seg):
    depth = np.minimum(np.arange(blocks), TRUNK)
    depth[TRUNK + BRANCHES :] = TRUNK + 1
    position = (np.repeat(depth, seg) * seg + np.arange(blocks * seg) % seg).astype(np.float32)
    half = HEAD_DIM // 2
    freq = (np.float32(theta) ** (-np.arange(half, dtype=np.float32) / half)).astype(np.float32)
    angle = (position[:, None] * freq[None, :]).astype(np.float32)
    cosine = np.tile(np.cos(angle), (1, 4)).astype(np.float32)
    sine = np.sin(angle).astype(np.float32)
    sine = np.concatenate([-sine, sine, -sine, sine], axis=1)
    return jnp.asarray(cosine), jnp.asarray(sine)


def turn(values, cosine, sine):
    width = values.shape[1]
    reps = width // cosine.shape[1]
    if reps > 1:
        cosine = jnp.concatenate([cosine] * reps, axis=1)
        sine = jnp.concatenate([sine] * reps, axis=1)
    lane = lax.broadcasted_iota(jnp.int32, values.shape, 1)
    half = HEAD_DIM // 2
    other = jnp.where(
        lane % HEAD_DIM < half, pltpu.roll(values, width - half, 1), pltpu.roll(values, half, 1)
    )
    return values * cosine + other * sine


SIDES = (1, -1)


def far_of(place, side):
    return place if side == 1 else LINE - 1 - place


def greet(place, partners=()):
    barrier = pltpu.get_barrier_semaphore()
    for partner in partners:
        pl.semaphore_signal(barrier, inc=1, device_id={"dp": partner}, device_id_type=MESH)
    for side in SIDES:

        @pl.when(far_of(place, side) < LINE - 1)
        def _():
            pl.semaphore_signal(
                barrier, inc=1, device_id={"tensor": place + side}, device_id_type=MESH
            )

    edge = (place == 0) | (place == LINE - 1)

    @pl.when(edge)
    def _():
        pl.semaphore_wait(barrier, 1 + len(partners))

    @pl.when(jnp.logical_not(edge))
    def _():
        pl.semaphore_wait(barrier, 2 + len(partners))


def chunk_rows(chunk, rows):
    return pl.ds(chunk * rows, rows)


class Gather:
    def __init__(self, place, buf, send, recv, chunks, own=None, second=None):
        self.place, self.buf, self.sems, self.chunks = place, buf, (send, recv), chunks
        self.rows = buf.shape[1] // chunks
        self.own, self.second = own, second

    def copy(self, side, step, chunk, shard, target):
        rows = chunk_rows(chunk, self.rows)
        where = self.buf.at[shard, rows]
        index = 0 if side == 1 else 1
        spot = (index, step - 1, chunk)
        source = where
        if step == 1 and self.own is not None:
            source = self.own.at[rows]
        if step == 2 and self.second is not None:
            source = self.second.at[shard, rows]
        return pltpu.make_async_remote_copy(
            src_ref=source,
            dst_ref=where,
            send_sem=self.sems[0].at[spot],
            recv_sem=self.sems[1].at[spot],
            device_id={"tensor": target},
            device_id_type=MESH,
        )

    def each_send(self, step, chunk, act, least=0, most=LINE):
        for side in SIDES:
            far = far_of(self.place, side)

            @pl.when((far < LINE - 1) & (far >= step - 1) & (far >= least) & (far <= most))
            def _():
                shard = self.place - side * (step - 1)
                act(self.copy(side, step, chunk, shard, self.place + side))

    def send(self, step, chunk, least=0, most=LINE):
        self.each_send(step, chunk, lambda copy: copy.start(), least, most)

    def arrive(self, step, chunk):
        for side in SIDES:

            @pl.when(far_of(self.place, side) >= step)
            def _():
                shard = self.place - side * step
                self.copy(side, step, chunk, shard, self.place - side).wait_recv()

    def relay(self, step, chunk, least=0, most=LINE):
        for side in SIDES:
            far = far_of(self.place, side)

            @pl.when((far < LINE - 1) & (far >= step - 1) & (far >= least) & (far <= most))
            def _():
                before = self.place - side * (step - 1)
                self.copy(side, step - 1, chunk, before, self.place - side).wait_recv()
                self.copy(side, step, chunk, before, self.place + side).start()

    def close(self):
        for side in SIDES:

            @pl.when(far_of(self.place, side) == LINE - 1)
            def _():
                for step in range(1, LINE):
                    for chunk in range(self.chunks):
                        shard = self.place - side * step
                        self.copy(side, step, chunk, shard, self.place - side).wait_recv()

    def end_got(self, step):
        for side in SIDES:

            @pl.when(far_of(self.place, side) == LINE - 1)
            def _():
                for chunk in range(self.chunks):
                    self.copy(side, step, chunk, self.place - side * step, self.place - side).wait_recv()

    def drain(self, stop=LINE, start=1):
        for step in range(start, stop):
            for chunk in range(self.chunks):
                self.each_send(step, chunk, lambda copy: copy.wait_send())


class Sum:
    def __init__(self, place, part, held, send, recv, chunks):
        self.place, self.part, self.held = place, part, held
        self.sems, self.chunks = (send, recv), chunks
        self.rows = part.shape[1] // chunks

    def copy(self, side, step, chunk, shard, target):
        rows = chunk_rows(chunk, self.rows)
        index = 0 if side == 1 else 1
        spot = (index, step - 1, chunk)
        return pltpu.make_async_remote_copy(
            src_ref=self.part.at[shard, rows],
            dst_ref=self.held.at[index, step - 1, rows],
            send_sem=self.sems[0].at[spot],
            recv_sem=self.sems[1].at[spot],
            device_id={"tensor": target},
            device_id_type=MESH,
        )

    def add(self, step, chunk):
        rows = chunk_rows(chunk, self.rows)
        for index, side in enumerate(SIDES):
            far = far_of(self.place, side)
            shard = self.place + side * (LINE - step)

            @pl.when((far >= 1) & (far <= step - 1))
            def _():
                self.copy(side, step - 1, chunk, self.place, self.place - side).wait_recv()
                self.part[shard, rows] = (
                    self.part[shard, rows].astype(f32)
                    + self.held[index, step - 2, rows].astype(f32)
                ).astype(bf16)

    def send(self, step, chunk, least=0, most=LINE):
        if step > 1 and most > 0:
            self.add(step, chunk)
        for side in SIDES:
            far = far_of(self.place, side)
            shard = self.place + side * (LINE - step)

            @pl.when((far <= step - 1) & (far >= least) & (far <= most))
            def _():
                self.copy(side, step, chunk, shard, self.place + side).start()

    def begin(self, step, chunk):
        self.send(step, chunk, most=0)

    def relay(self, step, chunk):
        self.send(step, chunk, least=1)

    def total(self, chunk, out):
        rows = chunk_rows(chunk, self.rows)
        out[rows] = self.part[self.place, rows].astype(f32)
        for index, side in enumerate(SIDES):

            @pl.when(far_of(self.place, side) >= 1)
            def _():
                self.copy(side, LINE - 1, chunk, self.place, self.place - side).wait_recv()
                out[rows] += self.held[index, LINE - 2, rows].astype(f32)

    def drain(self, stop=LINE):
        for step in range(1, stop):
            for chunk in range(self.chunks):
                for side in SIDES:
                    far = far_of(self.place, side)
                    shard = self.place + side * (LINE - step)

                    @pl.when(far <= step - 1)
                    def _():
                        self.copy(side, step, chunk, shard, self.place + side).wait_send()


class Near:
    def __init__(self, place, part, held, send, recv, chunks):
        self.place, self.part, self.held = place, part, held
        self.sems, self.chunks = (send, recv), chunks
        self.rows = part.shape[1] // chunks

    def copy(self, side, away, chunk, shard, target):
        rows = chunk_rows(chunk, self.rows)
        index = 0 if side == 1 else 1
        spot = (index, away - 1, chunk)
        return pltpu.make_async_remote_copy(
            src_ref=self.part.at[shard, rows],
            dst_ref=self.held.at[index, away - 1, rows],
            send_sem=self.sems[0].at[spot],
            recv_sem=self.sems[1].at[spot],
            device_id={"tensor": target},
            device_id_type=MESH,
        )

    def send(self, away, chunk, number):
        rows = chunk_rows(chunk, self.rows)
        for index, side in enumerate(SIDES):
            shard = self.place + side * away

            @pl.when(far_of(self.place, side) == number)
            def _():
                if number:
                    self.copy(side, away + 1, chunk, self.place, self.place - side).wait_recv()
                    self.part[shard, rows] = (
                        self.part[shard, rows].astype(f32) + self.held[index, away, rows].astype(f32)
                    ).astype(bf16)
                self.copy(side, away, chunk, shard, self.place + side).start()

    def total(self, chunk, out):
        rows = chunk_rows(chunk, self.rows)
        out[rows] = self.part[self.place, rows].astype(f32)
        for index, side in enumerate(SIDES):

            @pl.when(far_of(self.place, side) >= 1)
            def _():
                self.copy(side, 1, chunk, self.place, self.place - side).wait_recv()
                out[rows] += self.held[index, 0, rows].astype(f32)

    def drain(self):
        for number in range(LINE - 1):
            for away in range(1, LINE - number):
                for chunk in range(self.chunks):
                    for side in SIDES:

                        @pl.when(far_of(self.place, side) == number)
                        def _():
                            shard = self.place + side * away
                            self.copy(side, away, chunk, shard, self.place + side).wait_send()


def line_sems(chunks):
    return [pltpu.SemaphoreType.DMA((2, LINE - 1, chunks))] * 2


def fetch(pairs, sems):
    copies = [pltpu.make_async_copy(src, dst, sems.at[i]) for i, (src, dst) in enumerate(pairs)]
    for copy in copies:
        copy.start()
    return copies


IN_VMEM = pl.BlockSpec(memory_space=pltpu.VMEM)
IN_HBM = pl.BlockSpec(memory_space=pl.ANY)


def comm_params(number):
    return pltpu.CompilerParams(
        vmem_limit_bytes=VMEM_LIMIT, collective_id=number, has_side_effects=True
    )


def gather_norm_body(chunks, x_ref, gain_ref, buf, own, sem, send, recv):
    place = lax.axis_index("tensor")
    greet(place)
    rows = x_ref[...].astype(f32)
    rms = lax.rsqrt(jnp.mean(rows * rows, axis=1, keepdims=True) + eps)
    own[...] = (rows * rms * gain_ref[...].astype(f32)).astype(bf16)
    gather = Gather(place, buf, send, recv, chunks, own)
    for chunk in range(chunks):
        gather.send(1, chunk)
    (kept,) = fetch([(own, buf.at[place])], sem)
    for chunk in range(chunks):
        gather.arrive(1, chunk)
        gather.send(2, chunk)
    kept.wait()
    for chunk in range(chunks):
        gather.arrive(2, chunk)
    gather.drain(stop=LINE - 1)


def gather_norm(x, gain, chunks=2):
    rows, features = x.shape
    return pl.pallas_call(
        functools.partial(gather_norm_body, chunks),
        in_specs=[IN_VMEM, IN_VMEM],
        out_specs=IN_HBM,
        out_shape=jax.ShapeDtypeStruct((LINE, rows, features), bf16),
        scratch_shapes=[pltpu.VMEM((rows, features), bf16), pltpu.SemaphoreType.DMA((1,))]
        + line_sems(chunks),
        compiler_params=comm_params(0),
    )(x, gain[None, :])


def front_body(
    chunks, seg,
    x_ref, w_ref, c_ref, e_ref, a_ref, cos_ref, sin_ref, p_ref, oe_ref, f_ref, tok_ref, gain_ref,
    kept_ref, y_ref, mid_ref, n_ref, cot_ref, l_ref, att_ref, lse_ref, lo_ref,
    buf, yv, wv, wo, part, held, own, midv, xsem, wsem, ysem, nsem, msem, send, recv,
    s_send, s_recv, g_send, g_recv, c_send, c_recv,
):
    place = lax.axis_index("tensor")
    groups, total, width = y_ref.shape
    rows, rank = x_ref.shape[1], a_ref.shape[1]
    edge = (place == 0) | (place == LINE - 1)
    last = place ^ (LINE - 1)

    def passed(side):
        shard = place - side * (LINE - 2)
        index = 0 if side == 1 else 1
        return pltpu.make_async_remote_copy(
            src_ref=x_ref.at[shard],
            dst_ref=buf.at[shard],
            send_sem=send.at[index],
            recv_sem=recv.at[index],
            device_id={"tensor": place + side},
            device_id_type=MESH,
        )

    def came(side):
        index = 0 if side == 1 else 1
        return pltpu.make_async_remote_copy(
            src_ref=x_ref.at[last],
            dst_ref=buf.at[last],
            send_sem=send.at[index],
            recv_sem=recv.at[index],
            device_id={"tensor": place - side},
            device_id_type=MESH,
        )

    copies = []
    for slot in range(LINE):
        copy = pltpu.make_async_copy(x_ref.at[place ^ slot], buf.at[place ^ slot], xsem.at[slot])
        if slot < LINE - 1:
            copy.start()
        else:
            pl.when(jnp.logical_not(edge))(copy.start)
        copies.append(copy)
    load, load_out = fetch(
        [(w_ref.at[:, : groups * width], wv), (w_ref.at[:, groups * width :], wo)], wsem
    )
    greet(place)
    cots = Gather(place, cot_ref, c_send, c_recv, chunks, c_ref)
    summed = Sum(place, part, held, s_send, s_recv, chunks)
    gather = Gather(place, n_ref, g_send, g_recv, chunks, own)
    for side in SIDES:
        pl.when(far_of(place, side) == LINE - 2)(passed(side).start)
    for chunk in range(chunks):
        cots.send(1, chunk)

    for copy in copies[:-1]:
        copy.wait()
    load.wait()
    outs = []
    for slot in range(LINE):
        shard = place ^ slot
        if slot == LINE - 1:
            pl.when(jnp.logical_not(edge))(copies[slot].wait)
            for side in SIDES:
                pl.when(far_of(place, side) == LINE - 1)(came(side).wait_recv)
            kept = pltpu.make_async_copy(buf.at[last], kept_ref.at[last], xsem.at[slot])
            pl.when(edge)(kept.start)
        mine = pl.ds(pl.multiple_of(shard * rows, rows), rows)
        low = nt(buf[shard], e_ref[:groups].reshape(groups * rank, -1)).astype(bf16)
        l_ref[mine] = low
        for g in range(groups):
            band = slice(g * width, (g + 1) * width)
            value = nn(buf[shard], wv[:, band]) + nn(low[:, g * rank : (g + 1) * rank], a_ref[g])
            if g < groups - 1:
                value = turn(value, cos_ref[mine], sin_ref[mine])
            yv[g, mine] = value.astype(bf16)
            out = pltpu.make_async_copy(yv.at[g, mine], y_ref.at[g, mine], ysem.at[slot, g])
            out.start()
            outs.append(out)

    pair = 2 * HEAD_DIM

    def one_pair(j, carry):
        lanes = pl.ds(pl.multiple_of(j * pair, pair), pair)
        attend_pair(seg, yv, lanes, p_ref[...], j, att_ref, lse_ref)
        return carry

    lax.fori_loop(0, width // pair, one_pair, 0)

    load_out.wait()
    for slot in (3, 2, 1, 0):
        shard = place ^ slot
        mine = pl.ds(pl.multiple_of(shard * rows, rows), rows)
        d = att_ref[mine]
        low = nt(d, oe_ref[...]).astype(bf16)
        lo_ref[mine] = low
        part[shard] = (nt(d, wo[...]) + nn(low, f_ref[0])).astype(bf16)
        if slot == 3:
            summed.begin(1, 0)
    for chunk in range(chunks):
        for step in (1, 2, 3):
            if chunk or step > 1:
                summed.begin(step, chunk)
    size = rows // chunks
    stores = []
    for chunk in range(chunks):
        summed.relay(2, chunk)
        summed.relay(3, chunk)
        summed.total(chunk, midv)
        here = chunk_rows(chunk, size)
        value = midv[here] + tok_ref[here].astype(f32)
        midv[here] = value
        rms = lax.rsqrt(jnp.mean(value * value, axis=1, keepdims=True) + eps)
        own[here] = (value * rms * gain_ref[...].astype(f32)).astype(bf16)
        stores.append(pltpu.make_async_copy(own.at[here], n_ref.at[place, here], nsem.at[chunk]))
        stores.append(pltpu.make_async_copy(midv.at[here], mid_ref.at[here], msem.at[chunk]))
        gather.send(1, chunk, least=1)
        for store in stores[-2:]:
            store.start()
        if chunk:
            gather.relay(2, chunk - 1, least=2)
    for chunk in range(chunks):
        gather.send(1, chunk, most=0)
    gather.relay(2, chunks - 1, least=2)
    for chunk in range(chunks):
        gather.relay(2, chunk, most=1)
        if chunk:
            gather.relay(3, chunk - 1)
    gather.relay(3, chunks - 1)
    for chunk in range(chunks):
        cots.arrive(1, chunk)
    gather.close()
    pl.when(edge)(kept.wait)
    for out in outs + stores:
        out.wait()
    for side in SIDES:
        pl.when(far_of(place, side) == LINE - 2)(passed(side).wait_send)
    summed.drain()
    gather.drain()
    cots.drain(stop=2)


def front(x, weight, cot, entries, exits, tables, leaf_parent, out_entry, finals, tokens, gain, seg, chunks=4):
    _, rows, features = x.shape
    groups, rank, width = exits.shape
    total = LINE * rows
    shards = jax.ShapeDtypeStruct((LINE, rows, features), bf16)
    return pl.pallas_call(
        functools.partial(front_body, chunks, seg),
        in_specs=[IN_HBM] * 3 + [IN_VMEM] * 9,
        out_specs=[IN_HBM] * 5 + [IN_VMEM] * 4,
        out_shape=[
            shards,
            jax.ShapeDtypeStruct((groups, total, width), bf16),
            jax.ShapeDtypeStruct((rows, features), f32),
            shards,
            shards,
            jax.ShapeDtypeStruct((total, groups * rank), bf16),
            jax.ShapeDtypeStruct((total, width), bf16),
            jax.ShapeDtypeStruct((width // (2 * HEAD_DIM), 2, total), f32),
            jax.ShapeDtypeStruct((total, rank), bf16),
        ],
        scratch_shapes=[
            pltpu.VMEM((LINE, rows, features), bf16),
            pltpu.VMEM((groups, total, width), bf16),
            pltpu.VMEM((features, groups * width), bf16),
            pltpu.VMEM((features, width), bf16),
            pltpu.VMEM((LINE, rows, features), bf16),
            pltpu.VMEM((2, LINE - 1, rows, features), bf16),
            pltpu.VMEM((rows, features), bf16),
            pltpu.VMEM((rows, features), f32),
            pltpu.SemaphoreType.DMA((LINE,)),
            pltpu.SemaphoreType.DMA((2,)),
            pltpu.SemaphoreType.DMA((LINE, groups)),
            pltpu.SemaphoreType.DMA((chunks,)),
            pltpu.SemaphoreType.DMA((chunks,)),
            pltpu.SemaphoreType.DMA((2,)),
            pltpu.SemaphoreType.DMA((2,)),
        ]
        + line_sems(chunks)
        + line_sems(chunks)
        + line_sems(chunks),
        input_output_aliases={0: 0},
        compiler_params=comm_params(1),
    )(x, weight, cot, entries, exits, *tables, leaf_parent, out_entry, finals, tokens, gain[None, :])


class Trees:
    def __init__(self, tree, ref, send, recv):
        self.tree, self.ref, self.sems = tree, ref, (send, recv)
        self.rounds = ref.shape[0].bit_length() - 1
        self.partners = [self.partner(number) for number in range(self.rounds)]

    def partner(self, number):
        size = 1 << number
        return self.tree + size - 2 * size * ((self.tree // size) % 2)

    def copy(self, number, owner):
        size = 1 << number
        here = pl.ds((owner // size) * size, size)
        return pltpu.make_async_remote_copy(
            src_ref=self.ref.at[here],
            dst_ref=self.ref.at[here],
            send_sem=self.sems[0].at[number],
            recv_sem=self.sems[1].at[number],
            device_id={"dp": self.partner(number)},
            device_id_type=MESH,
        )

    def send(self, number):
        self.copy(number, self.tree).start()

    def arrive(self, number):
        self.copy(number, self.partner(number)).wait_recv()

    def advance(self, number):
        if number < self.rounds:
            self.arrive(number - 1)
            self.send(number)

    def drain(self):
        for number in range(self.rounds):
            self.copy(number, self.tree).wait_send()


def back_body(
    chunks, seg,
    q_ref, w_ref, n_ref, mid_ref, middle_ref, res_ref, right_ref, left_ref, x_ref,
    o_ref, g_ref, lse_ref, p_ref, cos_ref, sin_ref, a_ref, e_ref, gain_ref, lone_ref, final_ref, exit_ref,
    out_ref, model_ref, head_ref, sum_ref,
    qv, dv, dq_t, dk_sum, dv_sum, part, held, acc, wv, midv, nv, terms, xv, outv, resv, model, head, low, block, extra,
    qsem, wsem, osem, e_send, e_recv, send, recv, x_send, x_recv, t_send, t_recv, h_send, h_recv,
):
    place = lax.axis_index("tensor")
    tree = lax.axis_index("dp")
    trees = Trees(tree, model_ref, t_send, t_recv)
    heads = Trees(tree, head_ref, h_send, h_recv)
    groups, total, width = q_ref.shape
    rank = a_ref.shape[1]
    (load_q,) = fetch([(q_ref, qv)], qsem)
    loads = fetch(
        [
            (w_ref.at[:, : groups * width], wv),
            (n_ref, nv),
            (mid_ref, midv),
            (middle_ref, acc),
            (res_ref.at[place], terms.at[0]),
            (x_ref, xv),
        ],
        wsem,
    )
    block[...] = jnp.zeros_like(block)
    for g in range(groups):
        block[g * rank : (g + 1) * rank, g * width : (g + 1) * width] = a_ref[g]
    greet(place, trees.partners)

    def exchange(side, target):
        index = 0 if side == 1 else 1
        return pltpu.make_async_remote_copy(
            src_ref=(right_ref, left_ref)[index],
            dst_ref=terms.at[index + 1],
            send_sem=e_send.at[index],
            recv_sem=e_recv.at[index],
            device_id={"tensor": target},
            device_id_type=MESH,
        )

    for side in SIDES:
        pl.when(far_of(place, side) < LINE - 1)(exchange(side, place + side).start)
    load_q.wait()
    pair = 2 * HEAD_DIM

    def one_pair(j, carry):
        lanes = pl.ds(pl.multiple_of(j * pair, pair), pair)
        attend_back_pair(
            seg, qv, lanes, o_ref, g_ref, lse_ref, j, p_ref[...], cos_ref, sin_ref, dv, dq_t, dk_sum, dv_sum
        )
        return carry

    lax.fori_loop(0, width // pair, one_pair, 0)
    loads[0].wait()
    rows = part.shape[1]
    summed = Sum(place, part, held, send, recv, chunks)
    gather = Gather(place, extra, x_send, x_recv, 1)
    entry = e_ref[:groups].reshape(groups * rank, -1)

    def rows_of(slot):
        shard = place ^ slot
        mine = pl.ds(pl.multiple_of(shard * rows, rows), rows)
        return shard, mine, jnp.concatenate([dv[g, mine] for g in range(groups)], axis=1)

    def lower(slot):
        _, mine, d = rows_of(slot)
        low[mine] = nt(d, block[...]).astype(bf16)

    def partial(slot):
        shard, mine, d = rows_of(slot)
        part[shard] = (nt(d, wv[...]) + nn(low[mine], entry)).astype(bf16)

    lower(3)
    partial(3)
    summed.begin(1, 0)
    summed.begin(1, 1)
    for slot in (2, 1, 0):
        lower(slot)
    for load in loads[1:]:
        load.wait()

    def turned(value):
        return value.astype(f32).T.astype(bf16)

    joined = nn(turned(low[...]), nv[...].reshape(total, -1))
    extra[place] = jnp.concatenate([joined, final_ref[...]], axis=0).astype(bf16)
    gather.send(1, 0)
    for chunk in range(2, chunks):
        summed.begin(1, chunk)
    for slot in (2, 1, 0):
        partial(slot)
    for step in (2, 3):
        for chunk in range(chunks):
            summed.begin(step, chunk)
    summed.relay(2, 0)
    summed.relay(2, 1)
    gather.arrive(1, 0)
    gather.send(2, 0)
    summed.relay(2, 2)
    low_one = turned(lone_ref[...])
    for g in range(groups):
        band = slice(g * rank, (g + 1) * rank)
        head[band] = nn(low_one[band], dv[g]).astype(bf16)
    head[groups * rank :] = exit_ref[...].astype(bf16)
    (store,) = fetch([(head, head_ref.at[tree])], osem)
    summed.relay(2, 3)
    store.wait()
    heads.send(0)
    gather.arrive(2, 0)
    gather.send(3, 0)
    heads.advance(1)
    summed.relay(3, 0)
    gather.arrive(3, 0)
    model[...] = functools.reduce(
        jnp.add, [extra[shard].astype(f32) for shard in range(LINE)]
    ).astype(bf16)
    (store,) = fetch([(model, model_ref.at[tree])], osem)
    for side in SIDES:
        pl.when(far_of(place, side) > 0)(exchange(side, place - side).wait_recv)
    value = acc[...] + terms[0].astype(f32)
    for index, side in enumerate(SIDES):
        value += jnp.where(far_of(place, side) > 0, terms[index + 1].astype(f32), 0.0)
    resv[...] = value.astype(bf16)
    store.wait()
    trees.send(0)
    (store,) = fetch([(resv, sum_ref)], osem)
    heads.advance(2)
    summed.relay(3, 1)
    trees.advance(1)
    summed.relay(3, 2)
    summed.relay(3, 3)
    trees.advance(2)
    store.wait()
    size = rows // chunks
    stores = []

    def finish(chunk):
        summed.total(chunk, acc)
        here = chunk_rows(chunk, size)
        values = xv[here].astype(f32)
        rms = lax.rsqrt(jnp.mean(values * values, axis=1, keepdims=True) + eps)
        scaled = acc[here] * gain_ref[...].astype(f32)
        mean = jnp.mean(scaled * values, axis=1, keepdims=True)
        outv[here] = (midv[here] + rms * (scaled - values * (rms * rms) * mean)).astype(bf16)
        copy = pltpu.make_async_copy(outv.at[here], out_ref.at[here], wsem.at[chunk])
        copy.start()
        stores.append(copy)

    finish(0)
    finish(1)
    for number in range(3, trees.rounds):
        trees.advance(number)
        heads.advance(number)
    finish(2)
    finish(3)
    for blocks in (trees, heads):
        blocks.arrive(blocks.rounds - 1)
        blocks.drain()
    for copy in stores:
        copy.wait()
    for side in SIDES:
        pl.when(far_of(place, side) < LINE - 1)(exchange(side, place + side).wait_send)
    summed.drain()
    gather.drain()


def back(
    qkv, weight, normed, grad_middle, middle, res_parts, right, left, x, attended, grad, lse, leaf_parent, tables, exits,
    entries, gain, low_one, final_grads, exit_grads, seg,
):
    chunks = LINE
    rows, features = x.shape
    groups, total, width = qkv.shape
    rank = exits.shape[1]
    deep = (groups + 1) * rank
    pair = 2 * HEAD_DIM
    trees = lax.axis_size("dp")
    sems = pltpu.SemaphoreType.DMA((trees.bit_length() - 1,))
    two = pltpu.SemaphoreType.DMA((2,))
    return pl.pallas_call(
        functools.partial(back_body, chunks, seg),
        in_specs=[IN_HBM] * 9 + [IN_VMEM] * 12,
        out_specs=[IN_HBM] * 4,
        out_shape=[
            jax.ShapeDtypeStruct((rows, features), bf16),
            jax.ShapeDtypeStruct((trees, deep, features), bf16),
            jax.ShapeDtypeStruct((trees, deep, width), bf16),
            jax.ShapeDtypeStruct((rows, features), bf16),
        ],
        scratch_shapes=[
            pltpu.VMEM((groups, total, width), bf16),
            pltpu.VMEM((groups, total, width), bf16),
            pltpu.VMEM((pair, total), f32),
            pltpu.VMEM((total, pair), f32),
            pltpu.VMEM((total, pair), f32),
            pltpu.VMEM((LINE, rows, features), bf16),
            pltpu.VMEM((2, LINE - 1, rows, features), bf16),
            pltpu.VMEM((rows, features), f32),
            pltpu.VMEM((features, groups * width), bf16),
            pltpu.VMEM((rows, features), f32),
            pltpu.VMEM((LINE, rows, features), bf16),
            pltpu.VMEM((3, rows, features), bf16),
            pltpu.VMEM((rows, features), bf16),
            pltpu.VMEM((rows, features), bf16),
            pltpu.VMEM((rows, features), bf16),
            pltpu.VMEM((deep, features), bf16),
            pltpu.VMEM((deep, width), bf16),
            pltpu.VMEM((total, groups * rank), bf16),
            pltpu.VMEM((groups * rank, groups * width), bf16),
            pltpu.VMEM((LINE, deep, features), bf16),
            pltpu.SemaphoreType.DMA((1,)),
            pltpu.SemaphoreType.DMA((6,)),
            pltpu.SemaphoreType.DMA((1,)),
            two,
            two,
        ]
        + line_sems(chunks)
        + line_sems(1)
        + [sems] * 4,
        compiler_params=comm_params(3),
    )(
        qkv, weight, normed, grad_middle, middle, res_parts, right, left, x, attended, grad[0], lse, leaf_parent, *tables,
        exits, entries, gain[None, :], low_one, final_grads, exit_grads,
    )


def tree_tiles(seg, rows, parent_row):
    trunk = TRUNK * seg
    leaves = trunk + BRANCHES * seg
    key = lax.broadcasted_iota(jnp.int32, (QT, QT), 0)
    query = lax.broadcasted_iota(jnp.int32, (QT, QT), 1)
    causal = key <= query
    own = causal & (key // seg == query // seg)
    tiles = []
    for start in range(0, trunk, QT):
        pieces = [(0, start, None)] if start else []
        tiles.append((start, pieces + [(start, QT, causal)]))
    tiles.append((trunk, [(0, trunk, None), (trunk, QT, own)]))
    branch = lax.broadcasted_iota(jnp.int32, (BRANCHES * seg, QT), 0) // seg
    for start in range(leaves, rows, QT):
        mine = branch == parent_row[:, start - leaves : start - leaves + QT]
        tiles.append(
            (start, [(0, trunk, None), (trunk, BRANCHES * seg, mine), (start, QT, own)])
        )
    return tiles


def attend_pair(seg, qkv_ref, lanes, parent_row, pair, o_ref, lse_ref):
    rows = qkv_ref.shape[1]
    value_t = qkv_ref[2, :, lanes].T
    lane = lax.broadcasted_iota(jnp.int32, (QT, 2 * HEAD_DIM), 1)
    for start, pieces in tree_tiles(seg, rows, parent_row):
        query = qkv_ref[0, start : start + QT, lanes] * bf16(HEAD_DIM**-0.5)
        outs = []
        for h in range(2):
            own_query = jnp.where(lane // HEAD_DIM == h, query, bf16(0))
            scores = []
            for k0, count, mask in pieces:
                s = nt(qkv_ref[1, k0 : k0 + count, lanes], own_query)
                scores.append(s if mask is None else jnp.where(mask, s, -1e30))
            top = functools.reduce(
                jnp.maximum, [jnp.max(s, axis=0, keepdims=True) for s in scores]
            )
            summed, out = 0.0, 0.0
            for (k0, count, _), s in zip(pieces, scores):
                weights = jnp.exp(s - top)
                summed += jnp.sum(weights, axis=0, keepdims=True)
                out += nn(
                    value_t[h * HEAD_DIM : (h + 1) * HEAD_DIM, k0 : k0 + count],
                    weights.astype(bf16),
                )
            outs.append(out / summed)
            lse_ref[pair, h : h + 1, start : start + QT] = top + jnp.log(summed)
        o_ref[start : start + QT, lanes] = jnp.concatenate(outs, axis=0).T.astype(bf16)


def attend_back_pair(
    seg, qkv_ref, lanes, o_ref, g_ref, lse_ref, pair, parent_row, cos_ref, sin_ref, d_ref, dq_t, dk, dv
):
    rows = qkv_ref.shape[1]
    scale = bf16(HEAD_DIM**-0.5)
    key_t = qkv_ref[1, :, lanes].T
    weighed_t = (g_ref[:, lanes].astype(f32) * o_ref[:, lanes].astype(f32)).T
    lane = lax.broadcasted_iota(jnp.int32, (QT, 2 * HEAD_DIM), 1)
    dk[...] = jnp.zeros_like(dk)
    dv[...] = jnp.zeros_like(dv)
    for start, pieces in tree_tiles(seg, rows, parent_row):
        query = qkv_ref[0, start : start + QT, lanes] * scale
        grad = g_ref[start : start + QT, lanes]
        for h in range(2):
            mine = lane // HEAD_DIM == h
            own_query = jnp.where(mine, query, bf16(0))
            own_grad = jnp.where(mine, grad, bf16(0))
            band = slice(h * HEAD_DIM, (h + 1) * HEAD_DIM)
            delta = jnp.sum(weighed_t[band, start : start + QT], axis=0, keepdims=True)
            lse = lse_ref[pair, h : h + 1, start : start + QT]
            grad_q = 0.0
            for k0, count, mask in pieces:
                probs = jnp.exp(nt(qkv_ref[1, k0 : k0 + count, lanes], own_query) - lse)
                if mask is not None:
                    probs = jnp.where(mask, probs, 0.0)
                grad_probs = nt(qkv_ref[2, k0 : k0 + count, lanes], own_grad)
                grad_scores = (probs * (grad_probs - delta)).astype(bf16)
                dk[k0 : k0 + count] += nn(grad_scores, own_query)
                dv[k0 : k0 + count] += nn(probs.astype(bf16), own_grad)
                grad_q += nn(key_t[band, k0 : k0 + count], grad_scores)
            dq_t[band, start : start + QT] = grad_q
    cosine, sine = cos_ref[...], -sin_ref[...]
    d_ref[0, :, lanes] = turn(dq_t[...].T * HEAD_DIM**-0.5, cosine, sine).astype(bf16)
    d_ref[1, :, lanes] = turn(dk[...], cosine, sine).astype(bf16)
    d_ref[2, :, lanes] = dv[...].astype(bf16)


def feed_body(
    rank, tile, chunks,
    n_ref, c_ref, near_ref, wg_ref, wu_ref, wd_ref, mid_ref, wo_ref,
    pick_ref, xu_in, xd_in, e_in, f_in, gain_ref, oe_ref, att_ref, lo_ref,
    grad_ref, res_ref, right_ref, left_ref, b_ref, held_ref, far_ref, unit_out, model_out, y_ref, final_ref, exit_ref,
    unit_ref, model_ref, x_ref, e_ref, f_ref, midv, nbuf, cbuf, wbuf, low, low_t, acc_res, acc_back, acc_low,
    part, held, resv, own, extra, wo, nsem, csem, wsem, rsem, msem,
    send, recv, g_send, g_recv, x_send, x_recv, c_send, c_recv, r_send, r_recv,
):
    place = lax.axis_index("tensor")
    units = unit_ref.shape[1]
    tiles = units // tile
    rows = part.shape[1]
    summed = Near(place, part, held, send, recv, chunks)
    cots = Gather(place, far_ref, c_send, c_recv, 1, second=near_ref)
    inside = ((place + 1) // 2) % 2
    gather = Gather(place, b_ref, g_send, g_recv, chunks, own)
    joint = Gather(place, extra, x_send, x_recv, 1)

    def load_rows(order, act):
        into = order % 2
        shard = place ^ ((order + 1) % LINE)
        act(pltpu.make_async_copy(n_ref.at[shard], nbuf.at[into], nsem.at[into]))

        def take(source):
            act(pltpu.make_async_copy(source, cbuf.at[into], csem.at[into]))

        beside = (order == 0) | ((order == 2) & (inside == 1))
        pl.when(order == LINE - 1)(lambda: take(c_ref))
        pl.when(beside)(lambda: take(near_ref.at[shard]))
        pl.when(jnp.logical_not(beside) & (order < LINE - 1))(lambda: take(far_ref.at[shard]))

    def load_weights(index, into, act):
        columns = pl.ds(pl.multiple_of(index * tile, tile), tile)
        for k, w_ref in enumerate((wg_ref, wu_ref, wd_ref)):
            act(pltpu.make_async_copy(w_ref.at[:, columns], wbuf.at[into, k], wsem.at[into, k]))

    def start(copy):
        copy.start()

    def wait(copy):
        copy.wait()

    load_rows(jnp.int32(0), start)
    load_weights(0, 0, start)
    width = wo.shape[1]
    load_middle, load_out = fetch([(mid_ref, midv), (wo_ref.at[:, 3 * width :], wo)], msem)
    for padded in (x_ref, e_ref, f_ref):
        padded[...] = jnp.zeros_like(padded)
    x_ref[0, :rank] = xu_in[0]
    x_ref[1, rank : 2 * rank] = xu_in[1]
    x_ref[2, 2 * rank :] = xd_in[...]
    e_ref[: 2 * rank] = e_in[3:].reshape(2 * rank, -1)
    f_ref[2 * rank :] = f_in[1]
    unit_ref[...] = jnp.zeros_like(unit_ref)
    model_ref[...] = jnp.zeros_like(model_ref)
    greet(place)
    cots.send(2, 0)

    def one_shard(order, carry):
        into = order % 2
        shard = place ^ ((order + 1) % LINE)
        load_rows(order, wait)
        first = nt(nbuf[into], e_ref[...]) + nt(cbuf[into], f_ref[...])
        low[...] = first.astype(bf16)
        low_t[...] = first.T.astype(bf16)
        acc_res[...] = jnp.zeros_like(acc_res)
        acc_back[...] = jnp.zeros_like(acc_back)
        acc_low[...] = jnp.zeros_like(acc_low)

        def one_tile(index, carry):
            stage = order * tiles + index
            at = stage % 2
            load_weights(index, at, wait)

            @pl.when(stage < LINE * tiles - 1)
            def _():
                load_weights((index + 1) % tiles, 1 - at, start)

            columns = pl.ds(pl.multiple_of(index * tile, tile), tile)
            x_gate, x_rise, x_fall = x_ref[0, :, columns], x_ref[1, :, columns], x_ref[2, :, columns]
            gate = nn(nbuf[into], wbuf[at, 0]) + nn(low[...], x_gate)
            rise = nn(nbuf[into], wbuf[at, 1]) + nn(low[...], x_rise)
            grad_hidden = nn(cbuf[into], wbuf[at, 2]) + nn(low[...], x_fall)
            sigmoid = jax.nn.sigmoid(gate)
            silu = gate * sigmoid
            hidden = (silu * rise).astype(bf16)
            grad_gate = (grad_hidden * rise * sigmoid * (1.0 + gate * (1.0 - sigmoid))).astype(bf16)
            grad_rise = (grad_hidden * silu).astype(bf16)
            acc_back[...] += nt(grad_gate, wbuf[at, 0]) + nt(grad_rise, wbuf[at, 1])
            acc_res[...] += nt(hidden, wbuf[at, 2])
            acc_low[...] += nt(grad_gate, x_gate) + nt(grad_rise, x_rise) + nt(hidden, x_fall)
            unit_ref[:rank, columns] += nn(low_t[:rank], grad_gate)
            unit_ref[rank : 2 * rank, columns] += nn(low_t[rank : 2 * rank], grad_rise)
            unit_ref[2 * rank :, columns] += nn(low_t[2 * rank : 3 * rank], hidden)
            for number, (away, chunk) in enumerate(((1, 2), (1, 3), (2, 0), (2, 1))):

                @pl.when((order == LINE - 1) & (index == number))
                def _():
                    summed.send(away, chunk, 1)

            return carry

        lax.fori_loop(0, tiles, one_tile, 0)

        @pl.when(order == 0)
        def _():
            cots.relay(3, 0)
            cots.end_got(2)

        @pl.when(order == 1)
        def _():
            cots.end_got(3)

        @pl.when(order < LINE - 1)
        def _():
            load_rows(order + 1, start)

        joined = acc_low[...].astype(bf16)
        joined_t = acc_low[...].T.astype(bf16)
        part[shard] = (acc_back[...] + nn(joined, e_ref[...])).astype(bf16)
        for away in (1, 2, 3):

            @pl.when(order == away - 1)
            def _():
                for chunk in range(chunks):
                    summed.send(away, chunk, 0)
                if away == 3:
                    summed.send(1, 0, 1)
                    summed.send(1, 1, 1)

        @pl.when(order > 0)
        def _():
            pltpu.make_async_copy(resv, res_ref.at[shard], rsem.at[0]).wait()

        resv[...] = (acc_res[...] + nn(joined, f_ref[...])).astype(bf16)
        pltpu.make_async_copy(resv, res_ref.at[shard], rsem.at[0]).start()
        model_ref[: 2 * rank] += nn(joined_t[: 2 * rank], nbuf[into])
        model_ref[2 * rank :] += nn(joined_t[2 * rank : 3 * rank], cbuf[into])
        return carry

    lax.fori_loop(0, LINE, one_shard, 0)
    def pass_on(side, step, source, target):
        index = 0 if side == 1 else 1
        return pltpu.make_async_remote_copy(
            src_ref=source,
            dst_ref=held_ref.at[index, step - 1],
            send_sem=r_send.at[index, step - 1],
            recv_sem=r_recv.at[index, step - 1],
            device_id={"tensor": target},
            device_id_type=MESH,
        )

    def at_far(side, number, act):
        pl.when(far_of(place, side) == number)(act)

    def ready(side, step, shard):
        index = 0 if side == 1 else 1
        pass_on(side, step, resv, place - side).wait_recv()
        copies = [
            pltpu.make_async_copy(res_ref.at[shard], cbuf.at[0], csem.at[0]),
            pltpu.make_async_copy(held_ref.at[index, step - 1], cbuf.at[1], csem.at[1]),
        ]
        for copy in copies:
            copy.start()
        for copy in copies:
            copy.wait()
        cbuf[0] = (cbuf[0].astype(f32) + cbuf[1].astype(f32)).astype(bf16)

    def send_result(step):
        for side in SIDES:
            at_far(
                side,
                0,
                lambda: pass_on(side, step, res_ref.at[place + side * (LINE - step)], place + side).start(),
            )

    summed.send(2, 2, 1)
    summed.send(2, 3, 1)
    extra[place] = model_ref[...].astype(bf16)
    joint.send(1, 0)
    send_result(1)
    size = rows // chunks
    last = (LINE - 1) % 2
    load_middle.wait()
    stores = []
    for chunk in range(chunks):
        summed.send(1, chunk, 2)
        summed.total(chunk, acc_back)
        here = chunk_rows(chunk, size)
        middle = midv[here]
        rms = lax.rsqrt(jnp.mean(middle * middle, axis=1, keepdims=True) + eps)
        scaled = acc_back[here] * gain_ref[...].astype(f32)
        mean = jnp.mean(scaled * middle, axis=1, keepdims=True)
        grad = cbuf[last, here].astype(f32) + rms * (scaled - middle * (rms * rms) * mean)
        own[here] = grad.astype(bf16)
        gather.send(1, chunk)
        midv[here] = grad
        store = pltpu.make_async_copy(midv.at[here], grad_ref.at[here], nsem.at[chunk % 2])
        if chunk >= 2:
            stores[chunk - 2].wait()
        store.start()
        stores.append(store)
    send_result(2)
    pltpu.make_async_copy(resv, res_ref.at[place], rsem.at[0]).wait()

    load_out.wait()
    for store in stores[-2:]:
        store.wait()

    def through(number, rows_ref, shard):
        mine = pl.ds(pl.multiple_of(shard * rows, rows), rows)
        value = rows_ref[...]
        reduced = nt(value, f_in[0])
        y_ref[0, mine] = (nn(value, wo[...]) + nn(reduced.astype(bf16), oe_ref[...])).astype(bf16)
        final = nn(lo_ref[mine].astype(f32).T.astype(bf16), value)
        leave = nn(reduced.T.astype(bf16), att_ref[mine])
        final_ref[...] = final if number == 0 else final_ref[...] + final
        exit_ref[...] = leave if number == 0 else exit_ref[...] + leave

    def take(number, shard):
        copy = pltpu.make_async_copy(b_ref.at[shard], nbuf.at[number % 2], nsem.at[number % 2])
        copy.start()
        copy.wait()
        through(number, nbuf.at[number % 2], shard)

    joint.relay(2, 0)
    through(0, own, place)
    unit_out[: 3 * rank] = unit_ref[...].astype(bf16)
    unit_out[3 * rank :] = jnp.full((rank, units), pick_ref[0, 0], f32).astype(bf16)
    for chunk in range(chunks):
        gather.relay(2, chunk)
    gather.end_got(1)
    joint.relay(3, 0)
    take(1, place ^ (1 + 2 * inside))
    for chunk in range(chunks):
        gather.relay(3, chunk)
    for side in SIDES:

        @pl.when(far_of(place, side) == 1)
        def _():
            ready(side, 1, place + side * 2)
            resv[...] = cbuf[0]
            pass_on(side, 2, resv, place + side).start()

    gather.end_got(2)
    take(2, place ^ (2 - inside))
    joint.close()
    model_out[...] = functools.reduce(
        jnp.add, [extra[shard].astype(f32) for shard in range(LINE)]
    ).astype(bf16)
    gather.end_got(3)
    take(3, place ^ (3 - inside))
    for index, side in enumerate(SIDES):
        target = (right_ref, left_ref)[index]

        @pl.when(far_of(place, side) == 0)
        def _():
            copy = pltpu.make_async_copy(res_ref.at[place + side], nbuf.at[index], nsem.at[index])
            copy.start()
            copy.wait()

        @pl.when((far_of(place, side) > 0) & (far_of(place, side) < LINE - 1))
        def _():
            ready(side, 2, place + side)
            nbuf[index] = cbuf[0]

        copy = pltpu.make_async_copy(nbuf.at[index], target, nsem.at[index])
        copy.start()
        copy.wait()
    for side in SIDES:
        for step in (1, 2):
            at_far(
                side,
                0,
                lambda: pass_on(side, step, res_ref.at[place + side * (LINE - step)], place + side).wait_send(),
            )
        at_far(side, 1, lambda: pass_on(side, 2, resv, place + side).wait_send())
    summed.drain()
    gather.drain()
    joint.drain()
    cots.drain(start=2)


def feed(
    normed, cots, weights, middle, w_heads, pick, units_exit, fall_entry, entries, finals, gain, out_entry,
    attended, low_out, tile=512, chunks=4,
):
    _, rows, features = normed.shape
    units = weights[0].shape[1]
    rank, width = out_entry.shape
    total = LINE * rows
    one = jax.ShapeDtypeStruct((rows, features), bf16)
    return pl.pallas_call(
        functools.partial(feed_body, rank, tile, chunks),
        in_specs=[IN_HBM] * 8 + [pl.BlockSpec(memory_space=pltpu.SMEM)] + [IN_VMEM] * 8,
        out_specs=[IN_HBM] * 7 + [IN_VMEM] * 5,
        out_shape=[
            jax.ShapeDtypeStruct((rows, features), f32),
            jax.ShapeDtypeStruct((LINE, rows, features), bf16),
            one,
            one,
            jax.ShapeDtypeStruct((LINE, rows, features), bf16),
            jax.ShapeDtypeStruct((2, LINE - 2, rows, features), bf16),
            jax.ShapeDtypeStruct((LINE, rows, features), bf16),
            jax.ShapeDtypeStruct((4 * rank, units), bf16),
            jax.ShapeDtypeStruct((3 * rank, features), bf16),
            jax.ShapeDtypeStruct((1, total, width), bf16),
            jax.ShapeDtypeStruct((rank, features), f32),
            jax.ShapeDtypeStruct((rank, width), f32),
        ],
        scratch_shapes=[
            pltpu.VMEM((3 * rank, units), f32),
            pltpu.VMEM((3 * rank, features), f32),
            pltpu.VMEM((3, 3 * rank, units), bf16),
            pltpu.VMEM((3 * rank, features), bf16),
            pltpu.VMEM((3 * rank, features), bf16),
            pltpu.VMEM((rows, features), f32),
            pltpu.VMEM((2, rows, features), bf16),
            pltpu.VMEM((2, rows, features), bf16),
            pltpu.VMEM((2, 3, features, tile), bf16),
            pltpu.VMEM((rows, 3 * rank), bf16),
            pltpu.VMEM((3 * rank, rows), bf16),
            pltpu.VMEM((rows, features), f32),
            pltpu.VMEM((rows, features), f32),
            pltpu.VMEM((rows, 3 * rank), f32),
            pltpu.VMEM((LINE, rows, features), bf16),
            pltpu.VMEM((2, LINE - 1, rows, features), bf16),
            pltpu.VMEM((rows, features), bf16),
            pltpu.VMEM((rows, features), bf16),
            pltpu.VMEM((LINE, 3 * rank, features), bf16),
            pltpu.VMEM((features, width), bf16),
            pltpu.SemaphoreType.DMA((2,)),
            pltpu.SemaphoreType.DMA((2,)),
            pltpu.SemaphoreType.DMA((2, 3)),
            pltpu.SemaphoreType.DMA((1,)),
            pltpu.SemaphoreType.DMA((2,)),
        ]
        + line_sems(chunks)
        + line_sems(chunks)
        + line_sems(1)
        + line_sems(1)
        + [pltpu.SemaphoreType.DMA((2, LINE - 2))] * 2,
        compiler_params=comm_params(5),
    )(
        normed, *cots, *weights, middle, w_heads, pick, units_exit, fall_entry, entries, finals, gain[None, :], out_entry,
        attended, low_out,
    )


def pick_body(pick_ref, *refs):
    count = len(refs) // 2
    for source, target in zip(refs[:count], refs[count:]):
        target[...] = source[...].reshape(target.shape)


def picked(pick, arrays):
    shapes = [a.shape[:1] + a.shape[2:] for a in arrays]
    return pl.pallas_call(
        pick_body,
        grid_spec=pltpu.PrefetchScalarGridSpec(
            num_scalar_prefetch=1,
            grid=(1,),
            in_specs=[
                pl.BlockSpec(a.shape[:1] + (1,) + a.shape[2:], lambda i, p: (0, p[0], 0, 0)) for a in arrays
            ],
            out_specs=[pl.BlockSpec(shape, lambda i, p: (0, 0, 0)) for shape in shapes],
        ),
        out_shape=[jax.ShapeDtypeStruct(shape, bf16) for shape in shapes],
    )(pick, *arrays)


def per_tree(block):
    return lax.all_gather(block, "dp", axis=0, tiled=False)


def combine_body(
    rank, pick_ref, early, model, late, head, one, two, entry_ref, final_ref, unit_ref, down_ref, exit_ref, out_ref,
    one_ref, two_ref,
):
    one_ref[...] = one[...]
    two_ref[...] = two[...]
    for ref in (entry_ref, final_ref, unit_ref, down_ref, exit_ref, out_ref):
        ref[...] = jnp.zeros_like(ref)

    def one_tree(tree, carry):
        pick = pick_ref[tree]

        def block(ref, index):
            return ref[tree, index * rank : (index + 1) * rank].astype(f32)

        for k in range(3):
            entry_ref[k, pick] += block(late, k)
            exit_ref[k, pick] += block(head, k)
        final_ref[0, pick] += block(late, 3)
        out_ref[pick] += block(head, 3)
        for k in range(2):
            entry_ref[3 + k, pick] += block(model, k)
            unit_ref[k, pick] += block(early, k)
        final_ref[1, pick] += block(model, 2)
        down_ref[pick] += block(early, 2)
        return carry

    lax.fori_loop(0, early.shape[0], one_tree, 0)


def combine(picks, early, model, late, head, one, two, adapters, steps=4):
    trees, _, features = early.shape
    rank = late.shape[1] // 4
    width = head.shape[2]
    wide, narrow = features // steps, width // steps

    def taken(array, tile):
        return pl.BlockSpec((trees, array.shape[1], tile), lambda i, p: (0, 0, i))

    def given(lead, tile):
        shape = lead + (adapters, rank, tile)
        return pl.BlockSpec(shape, lambda i, p: (0,) * (len(shape) - 1) + (i,))

    whole = pl.BlockSpec((one.shape[0] // steps, one.shape[1]), lambda i, p: (i, 0))

    def shape(lead, full):
        return jax.ShapeDtypeStruct(lead + (adapters, rank, full), f32)

    return pl.pallas_call(
        functools.partial(combine_body, rank),
        grid_spec=pltpu.PrefetchScalarGridSpec(
            num_scalar_prefetch=1,
            grid=(steps,),
            in_specs=[taken(early, wide), taken(model, wide), taken(late, wide), taken(head, narrow), whole, whole],
            out_specs=[
                given((5,), wide),
                given((2,), wide),
                given((2,), wide),
                given((), wide),
                given((3,), narrow),
                given((), narrow),
                whole,
                whole,
            ],
        ),
        out_shape=[
            shape((5,), features),
            shape((2,), features),
            shape((2,), features),
            shape((), features),
            shape((3,), width),
            shape((), width),
            jax.ShapeDtypeStruct(one.shape, bf16),
            jax.ShapeDtypeStruct(two.shape, bf16),
        ],
        compiler_params=pltpu.CompilerParams(vmem_limit_bytes=VMEM_LIMIT),
    )(picks, early, model, late, head, one, two)


def local(
    tokens,
    cotangent,
    attention_gain,
    feed_gain,
    query_weight,
    key_weight,
    value_weight,
    output_weight,
    gate_weight,
    up_weight,
    down_weight,
    entry_maps,
    head_exits,
    unit_exits,
    output_entry,
    down_entry,
    final_exits,
    parents,
    adapter_pick,
):
    adapters, rank = entry_maps.shape[1], entry_maps.shape[3]
    local_rows = tokens.shape[0]
    total = local_rows * lax.axis_size("tensor")
    blocks = parents.shape[1]
    seg = total // blocks
    tables = rope_tables(blocks, seg)
    leaf_parent = (jnp.repeat(parents[0, TRUNK + BRANCHES :], seg) - TRUNK)[None, :]
    gain_one, gain_two = attention_gain, feed_gain

    w_heads = lax.all_gather(
        jnp.concatenate([query_weight, key_weight, value_weight, output_weight], axis=1),
        "dp",
        axis=0,
        tiled=True,
    )

    w_units = [
        lax.all_gather(w, "dp", axis=0, tiled=True) for w in (gate_weight, up_weight, down_weight)
    ]
    entries, heads_exit, units_exit, out_entry, fall_entry, finals = picked(
        adapter_pick,
        (
            jnp.swapaxes(entry_maps, 2, 3),
            head_exits,
            unit_exits,
            jnp.swapaxes(output_entry, 1, 2)[None],
            jnp.swapaxes(down_entry, 1, 2)[None],
            final_exits,
        ),
    )
    out_entry, fall_entry = out_entry[0], fall_entry[0]

    most_one = gather_norm(tokens, gain_one)
    full_one, qkv, middle, full_two, full_cot, low_one, attended, lse, adapt_o = front(
        most_one, w_heads, cotangent, entries, heads_exit, tables, leaf_parent, out_entry, finals, tokens, gain_two, seg
    )

    (
        grad_middle, res_parts, res_right, res_left, _, _, _, early, model_sum, grad_attended, final_grads, exit_grads,
    ) = feed(
        full_two, (cotangent, full_cot), w_units, middle, w_heads, adapter_pick.astype(f32)[None, :],
        units_exit, fall_entry, entries, finals, gain_two, out_entry, attended, adapt_o,
    )
    early = per_tree(early)
    model_all = per_tree(model_sum)

    grad_tokens, late_model, late_head, result = back(
        qkv, w_heads, full_one, grad_middle, middle, res_parts, res_right, res_left, tokens, attended, grad_attended, lse,
        leaf_parent, tables, heads_exit, entries, gain_one, low_one, final_grads, exit_grads, seg,
    )

    picks = early[:, 3 * rank, 0].astype(jnp.int32)
    grad_entries, grad_finals, grad_units, grad_down, grad_heads, grad_output, result, grad_tokens = combine(
        picks, early, model_all, late_model, late_head, result, grad_tokens, adapters
    )
    grad_entries = grad_entries.swapaxes(2, 3)
    grad_output = grad_output.swapaxes(1, 2)
    grad_down = grad_down.swapaxes(1, 2)
    return (
        result,
        grad_tokens,
        grad_entries,
        grad_heads,
        grad_units,
        grad_output,
        grad_down,
        grad_finals,
    )


def solution(mesh):
    in_specs = (
        P(("dp", "tensor"), None),
        P(("dp", "tensor"), None),
        P(),
        P(),
        P("dp", "tensor"),
        P("dp", "tensor"),
        P("dp", "tensor"),
        P("dp", "tensor"),
        P("dp", "tensor"),
        P("dp", "tensor"),
        P("dp", "tensor"),
        P(),
        P(None, None, None, "tensor"),
        P(None, None, None, "tensor"),
        P(None, "tensor", None),
        P(None, "tensor", None),
        P(),
        P("dp", None),
        P("dp"),
    )
    out_specs = (
        P(("dp", "tensor"), None),
        P(("dp", "tensor"), None),
        P(),
        P(None, None, None, "tensor"),
        P(None, None, None, "tensor"),
        P(None, "tensor", None),
        P(None, "tensor", None),
        P(),
    )
    return jax.shard_map(local, mesh=mesh, in_specs=in_specs, out_specs=out_specs, check_vma=False)
```

```python
import functools

import jax
import jax.numpy as jnp
import numpy as np
from jax import lax
from jax.experimental import pallas as pl
from jax.experimental.pallas import tpu as pltpu
from jax.sharding import PartitionSpec as P

HEAD_DIM = 64
TRUNK, BRANCHES = 8, 4
QT = 256
VMEM_LIMIT = 60 * 1024 * 1024
LINE = 4
MESH = pl.DeviceIdType.MESH

eps = 1e-05
theta = 130000.0
bf16, f32 = jnp.bfloat16, jnp.float32


def nn(left, right):
    return jnp.dot(left, right, preferred_element_type=f32)


def nt(left, right):
    return lax.dot_general(left, right, (((1,), (1,)), ((), ())), preferred_element_type=f32)


def tn(left, right):
    return lax.dot_general(left, right, (((0,), (0,)), ((), ())), preferred_element_type=f32)


def rope_tables(blocks, seg):
    depth = np.minimum(np.arange(blocks), TRUNK)
    depth[TRUNK + BRANCHES :] = TRUNK + 1
    position = (np.repeat(depth, seg) * seg + np.arange(blocks * seg) % seg).astype(np.float32)
    half = HEAD_DIM // 2
    freq = (np.float32(theta) ** (-np.arange(half, dtype=np.float32) / half)).astype(np.float32)
    angle = (position[:, None] * freq[None, :]).astype(np.float32)
    cosine = np.tile(np.cos(angle), (1, 4)).astype(np.float32)
    sine = np.sin(angle).astype(np.float32)
    sine = np.concatenate([-sine, sine, -sine, sine], axis=1)
    return jnp.asarray(cosine), jnp.asarray(sine)


def turn(values, cosine, sine):
    width = values.shape[1]
    reps = width // cosine.shape[1]
    if reps > 1:
        cosine = jnp.concatenate([cosine] * reps, axis=1)
        sine = jnp.concatenate([sine] * reps, axis=1)
    lane = lax.broadcasted_iota(jnp.int32, values.shape, 1)
    half = HEAD_DIM // 2
    other = jnp.where(
        lane % HEAD_DIM < half, pltpu.roll(values, width - half, 1), pltpu.roll(values, half, 1)
    )
    return values * cosine + other * sine


SIDES = (1, -1)


def far_of(place, side):
    return place if side == 1 else LINE - 1 - place


def greet(place, partners=()):
    barrier = pltpu.get_barrier_semaphore()
    for partner in partners:
        pl.semaphore_signal(barrier, inc=1, device_id={"dp": partner}, device_id_type=MESH)
    for side in SIDES:

        @pl.when(far_of(place, side) < LINE - 1)
        def _():
            pl.semaphore_signal(
                barrier, inc=1, device_id={"tensor": place + side}, device_id_type=MESH
            )

    edge = (place == 0) | (place == LINE - 1)

    @pl.when(edge)
    def _():
        pl.semaphore_wait(barrier, 1 + len(partners))

    @pl.when(jnp.logical_not(edge))
    def _():
        pl.semaphore_wait(barrier, 2 + len(partners))


def chunk_rows(chunk, rows):
    return pl.ds(chunk * rows, rows)


class Gather:
    def __init__(self, place, buf, send, recv, chunks, own=None, second=None):
        self.place, self.buf, self.sems, self.chunks = place, buf, (send, recv), chunks
        self.rows = buf.shape[1] // chunks
        self.own, self.second = own, second

    def copy(self, side, step, chunk, shard, target):
        rows = chunk_rows(chunk, self.rows)
        where = self.buf.at[shard, rows]
        index = 0 if side == 1 else 1
        spot = (index, step - 1, chunk)
        source = where
        if step == 1 and self.own is not None:
            source = self.own.at[rows]
        if step == 2 and self.second is not None:
            source = self.second.at[shard, rows]
        return pltpu.make_async_remote_copy(
            src_ref=source,
            dst_ref=where,
            send_sem=self.sems[0].at[spot],
            recv_sem=self.sems[1].at[spot],
            device_id={"tensor": target},
            device_id_type=MESH,
        )

    def each_send(self, step, chunk, act, least=0, most=LINE):
        for side in SIDES:
            far = far_of(self.place, side)

            @pl.when((far < LINE - 1) & (far >= step - 1) & (far >= least) & (far <= most))
            def _():
                shard = self.place - side * (step - 1)
                act(self.copy(side, step, chunk, shard, self.place + side))

    def send(self, step, chunk, least=0, most=LINE):
        self.each_send(step, chunk, lambda copy: copy.start(), least, most)

    def arrive(self, step, chunk):
        for side in SIDES:

            @pl.when(far_of(self.place, side) >= step)
            def _():
                shard = self.place - side * step
                self.copy(side, step, chunk, shard, self.place - side).wait_recv()

    def relay(self, step, chunk, least=0, most=LINE):
        for side in SIDES:
            far = far_of(self.place, side)

            @pl.when((far < LINE - 1) & (far >= step - 1) & (far >= least) & (far <= most))
            def _():
                before = self.place - side * (step - 1)
                self.copy(side, step - 1, chunk, before, self.place - side).wait_recv()
                self.copy(side, step, chunk, before, self.place + side).start()

    def close(self):
        for side in SIDES:

            @pl.when(far_of(self.place, side) == LINE - 1)
            def _():
                for step in range(1, LINE):
                    for chunk in range(self.chunks):
                        shard = self.place - side * step
                        self.copy(side, step, chunk, shard, self.place - side).wait_recv()

    def end_got(self, step):
        for side in SIDES:

            @pl.when(far_of(self.place, side) == LINE - 1)
            def _():
                for chunk in range(self.chunks):
                    self.copy(side, step, chunk, self.place - side * step, self.place - side).wait_recv()

    def drain(self, stop=LINE, start=1):
        for step in range(start, stop):
            for chunk in range(self.chunks):
                self.each_send(step, chunk, lambda copy: copy.wait_send())


class Sum:
    def __init__(self, place, part, held, send, recv, chunks):
        self.place, self.part, self.held = place, part, held
        self.sems, self.chunks = (send, recv), chunks
        self.rows = part.shape[1] // chunks

    def copy(self, side, step, chunk, shard, target):
        rows = chunk_rows(chunk, self.rows)
        index = 0 if side == 1 else 1
        spot = (index, step - 1, chunk)
        return pltpu.make_async_remote_copy(
            src_ref=self.part.at[shard, rows],
            dst_ref=self.held.at[index, step - 1, rows],
            send_sem=self.sems[0].at[spot],
            recv_sem=self.sems[1].at[spot],
            device_id={"tensor": target},
            device_id_type=MESH,
        )

    def add(self, step, chunk):
        rows = chunk_rows(chunk, self.rows)
        for index, side in enumerate(SIDES):
            far = far_of(self.place, side)
            shard = self.place + side * (LINE - step)

            @pl.when((far >= 1) & (far <= step - 1))
            def _():
                self.copy(side, step - 1, chunk, self.place, self.place - side).wait_recv()
                self.part[shard, rows] = (
                    self.part[shard, rows].astype(f32)
                    + self.held[index, step - 2, rows].astype(f32)
                ).astype(bf16)

    def send(self, step, chunk, least=0, most=LINE):
        if step > 1 and most > 0:
            self.add(step, chunk)
        for side in SIDES:
            far = far_of(self.place, side)
            shard = self.place + side * (LINE - step)

            @pl.when((far <= step - 1) & (far >= least) & (far <= most))
            def _():
                self.copy(side, step, chunk, shard, self.place + side).start()

    def begin(self, step, chunk):
        self.send(step, chunk, most=0)

    def relay(self, step, chunk):
        self.send(step, chunk, least=1)

    def total(self, chunk, out):
        rows = chunk_rows(chunk, self.rows)
        out[rows] = self.part[self.place, rows].astype(f32)
        for index, side in enumerate(SIDES):

            @pl.when(far_of(self.place, side) >= 1)
            def _():
                self.copy(side, LINE - 1, chunk, self.place, self.place - side).wait_recv()
                out[rows] += self.held[index, LINE - 2, rows].astype(f32)

    def drain(self, stop=LINE):
        for step in range(1, stop):
            for chunk in range(self.chunks):
                for side in SIDES:
                    far = far_of(self.place, side)
                    shard = self.place + side * (LINE - step)

                    @pl.when(far <= step - 1)
                    def _():
                        self.copy(side, step, chunk, shard, self.place + side).wait_send()


class Near:
    def __init__(self, place, part, held, send, recv, chunks):
        self.place, self.part, self.held = place, part, held
        self.sems, self.chunks = (send, recv), chunks
        self.rows = part.shape[1] // chunks

    def copy(self, side, away, chunk, shard, target):
        rows = chunk_rows(chunk, self.rows)
        index = 0 if side == 1 else 1
        spot = (index, away - 1, chunk)
        return pltpu.make_async_remote_copy(
            src_ref=self.part.at[shard, rows],
            dst_ref=self.held.at[index, away - 1, rows],
            send_sem=self.sems[0].at[spot],
            recv_sem=self.sems[1].at[spot],
            device_id={"tensor": target},
            device_id_type=MESH,
        )

    def send(self, away, chunk, number):
        rows = chunk_rows(chunk, self.rows)
        for index, side in enumerate(SIDES):
            shard = self.place + side * away

            @pl.when(far_of(self.place, side) == number)
            def _():
                if number:
                    self.copy(side, away + 1, chunk, self.place, self.place - side).wait_recv()
                    self.part[shard, rows] = (
                        self.part[shard, rows].astype(f32) + self.held[index, away, rows].astype(f32)
                    ).astype(bf16)
                self.copy(side, away, chunk, shard, self.place + side).start()

    def total(self, chunk, out):
        rows = chunk_rows(chunk, self.rows)
        out[rows] = self.part[self.place, rows].astype(f32)
        for index, side in enumerate(SIDES):

            @pl.when(far_of(self.place, side) >= 1)
            def _():
                self.copy(side, 1, chunk, self.place, self.place - side).wait_recv()
                out[rows] += self.held[index, 0, rows].astype(f32)

    def drain(self):
        for number in range(LINE - 1):
            for away in range(1, LINE - number):
                for chunk in range(self.chunks):
                    for side in SIDES:

                        @pl.when(far_of(self.place, side) == number)
                        def _():
                            shard = self.place + side * away
                            self.copy(side, away, chunk, shard, self.place + side).wait_send()


def line_sems(chunks):
    return [pltpu.SemaphoreType.DMA((2, LINE - 1, chunks))] * 2


def fetch(pairs, sems):
    copies = [pltpu.make_async_copy(src, dst, sems.at[i]) for i, (src, dst) in enumerate(pairs)]
    for copy in copies:
        copy.start()
    return copies


IN_VMEM = pl.BlockSpec(memory_space=pltpu.VMEM)
IN_HBM = pl.BlockSpec(memory_space=pl.ANY)


def comm_params(number):
    return pltpu.CompilerParams(
        vmem_limit_bytes=VMEM_LIMIT, collective_id=number, has_side_effects=True
    )


def gather_norm_body(chunks, x_ref, gain_ref, buf, own, sem, send, recv):
    place = lax.axis_index("tensor")
    greet(place)
    rows = x_ref[...].astype(f32)
    rms = lax.rsqrt(jnp.mean(rows * rows, axis=1, keepdims=True) + eps)
    own[...] = (rows * rms * gain_ref[...].astype(f32)).astype(bf16)
    gather = Gather(place, buf, send, recv, chunks, own)
    for chunk in range(chunks):
        gather.send(1, chunk)
    (kept,) = fetch([(own, buf.at[place])], sem)
    for chunk in range(chunks):
        gather.arrive(1, chunk)
        gather.send(2, chunk)
    kept.wait()
    for chunk in range(chunks):
        gather.arrive(2, chunk)
    gather.drain(stop=LINE - 1)


def gather_norm(x, gain, chunks=2):
    rows, features = x.shape
    return pl.pallas_call(
        functools.partial(gather_norm_body, chunks),
        in_specs=[IN_VMEM, IN_VMEM],
        out_specs=IN_HBM,
        out_shape=jax.ShapeDtypeStruct((LINE, rows, features), bf16),
        scratch_shapes=[pltpu.VMEM((rows, features), bf16), pltpu.SemaphoreType.DMA((1,))]
        + line_sems(chunks),
        compiler_params=comm_params(0),
    )(x, gain[None, :])


def front_body(
    chunks, seg,
    x_ref, w_ref, c_ref, e_ref, a_ref, cos_ref, sin_ref, p_ref, oe_ref, f_ref, tok_ref, gain_ref,
    kept_ref, y_ref, mid_ref, n_ref, cot_ref, l_ref, att_ref, lse_ref, lo_ref,
    buf, yv, wv, wo, part, held, own, midv, xsem, wsem, ysem, nsem, msem, send, recv,
    s_send, s_recv, g_send, g_recv, c_send, c_recv,
):
    place = lax.axis_index("tensor")
    groups, total, width = y_ref.shape
    rows, rank = x_ref.shape[1], a_ref.shape[1]
    edge = (place == 0) | (place == LINE - 1)
    last = place ^ (LINE - 1)

    def passed(side):
        shard = place - side * (LINE - 2)
        index = 0 if side == 1 else 1
        return pltpu.make_async_remote_copy(
            src_ref=x_ref.at[shard],
            dst_ref=buf.at[shard],
            send_sem=send.at[index],
            recv_sem=recv.at[index],
            device_id={"tensor": place + side},
            device_id_type=MESH,
        )

    def came(side):
        index = 0 if side == 1 else 1
        return pltpu.make_async_remote_copy(
            src_ref=x_ref.at[last],
            dst_ref=buf.at[last],
            send_sem=send.at[index],
            recv_sem=recv.at[index],
            device_id={"tensor": place - side},
            device_id_type=MESH,
        )

    copies = []
    for slot in range(LINE):
        copy = pltpu.make_async_copy(x_ref.at[place ^ slot], buf.at[place ^ slot], xsem.at[slot])
        if slot < LINE - 1:
            copy.start()
        else:
            pl.when(jnp.logical_not(edge))(copy.start)
        copies.append(copy)
    load, load_out = fetch(
        [(w_ref.at[:, : groups * width], wv), (w_ref.at[:, groups * width :], wo)], wsem
    )
    greet(place)
    cots = Gather(place, cot_ref, c_send, c_recv, chunks, c_ref)
    summed = Sum(place, part, held, s_send, s_recv, chunks)
    gather = Gather(place, n_ref, g_send, g_recv, chunks, own)
    for side in SIDES:
        pl.when(far_of(place, side) == LINE - 2)(passed(side).start)
    for chunk in range(chunks):
        cots.send(1, chunk)

    for copy in copies[:-1]:
        copy.wait()
    load.wait()
    outs = []
    for slot in range(LINE):
        shard = place ^ slot
        if slot == LINE - 1:
            pl.when(jnp.logical_not(edge))(copies[slot].wait)
            for side in SIDES:
                pl.when(far_of(place, side) == LINE - 1)(came(side).wait_recv)
            kept = pltpu.make_async_copy(buf.at[last], kept_ref.at[last], xsem.at[slot])
            pl.when(edge)(kept.start)
        mine = pl.ds(pl.multiple_of(shard * rows, rows), rows)
        low = nt(buf[shard], e_ref[:groups].reshape(groups * rank, -1)).astype(bf16)
        l_ref[mine] = low
        for g in range(groups):
            band = slice(g * width, (g + 1) * width)
            value = nn(buf[shard], wv[:, band]) + nn(low[:, g * rank : (g + 1) * rank], a_ref[g])
            if g < groups - 1:
                value = turn(value, cos_ref[mine], sin_ref[mine])
            yv[g, mine] = value.astype(bf16)
            out = pltpu.make_async_copy(yv.at[g, mine], y_ref.at[g, mine], ysem.at[slot, g])
            out.start()
            outs.append(out)

    pair = 2 * HEAD_DIM

    def one_pair(j, carry):
        lanes = pl.ds(pl.multiple_of(j * pair, pair), pair)
        attend_pair(seg, yv, lanes, p_ref[...], j, att_ref, lse_ref)
        return carry

    lax.fori_loop(0, width // pair, one_pair, 0)

    load_out.wait()
    for slot in (3, 2, 1, 0):
        shard = place ^ slot
        mine = pl.ds(pl.multiple_of(shard * rows, rows), rows)
        d = att_ref[mine]
        low = nt(d, oe_ref[...]).astype(bf16)
        lo_ref[mine] = low
        part[shard] = (nt(d, wo[...]) + nn(low, f_ref[0])).astype(bf16)
        if slot == 3:
            summed.begin(1, 0)
    for chunk in range(chunks):
        for step in (1, 2, 3):
            if chunk or step > 1:
                summed.begin(step, chunk)
    size = rows // chunks
    stores = []
    for chunk in range(chunks):
        summed.relay(2, chunk)
        summed.relay(3, chunk)
        summed.total(chunk, midv)
        here = chunk_rows(chunk, size)
        value = midv[here] + tok_ref[here].astype(f32)
        midv[here] = value
        rms = lax.rsqrt(jnp.mean(value * value, axis=1, keepdims=True) + eps)
        own[here] = (value * rms * gain_ref[...].astype(f32)).astype(bf16)
        stores.append(pltpu.make_async_copy(own.at[here], n_ref.at[place, here], nsem.at[chunk]))
        stores.append(pltpu.make_async_copy(midv.at[here], mid_ref.at[here], msem.at[chunk]))
        gather.send(1, chunk, least=1)
        for store in stores[-2:]:
            store.start()
        if chunk:
            gather.relay(2, chunk - 1, least=2)
    for chunk in range(chunks):
        gather.send(1, chunk, most=0)
    gather.relay(2, chunks - 1, least=2)
    for chunk in range(chunks):
        gather.relay(2, chunk, most=1)
        if chunk:
            gather.relay(3, chunk - 1)
    gather.relay(3, chunks - 1)
    for chunk in range(chunks):
        cots.arrive(1, chunk)
    gather.close()
    pl.when(edge)(kept.wait)
    for out in outs + stores:
        out.wait()
    for side in SIDES:
        pl.when(far_of(place, side) == LINE - 2)(passed(side).wait_send)
    summed.drain()
    gather.drain()
    cots.drain(stop=2)


def front(x, weight, cot, entries, exits, tables, leaf_parent, out_entry, finals, tokens, gain, seg, chunks=4):
    _, rows, features = x.shape
    groups, rank, width = exits.shape
    total = LINE * rows
    shards = jax.ShapeDtypeStruct((LINE, rows, features), bf16)
    return pl.pallas_call(
        functools.partial(front_body, chunks, seg),
        in_specs=[IN_HBM] * 3 + [IN_VMEM] * 9,
        out_specs=[IN_HBM] * 5 + [IN_VMEM] * 4,
        out_shape=[
            shards,
            jax.ShapeDtypeStruct((groups, total, width), bf16),
            jax.ShapeDtypeStruct((rows, features), f32),
            shards,
            shards,
            jax.ShapeDtypeStruct((total, groups * rank), bf16),
            jax.ShapeDtypeStruct((total, width), bf16),
            jax.ShapeDtypeStruct((width // (2 * HEAD_DIM), 2, total), f32),
            jax.ShapeDtypeStruct((total, rank), bf16),
        ],
        scratch_shapes=[
            pltpu.VMEM((LINE, rows, features), bf16),
            pltpu.VMEM((groups, total, width), bf16),
            pltpu.VMEM((features, groups * width), bf16),
            pltpu.VMEM((features, width), bf16),
            pltpu.VMEM((LINE, rows, features), bf16),
            pltpu.VMEM((2, LINE - 1, rows, features), bf16),
            pltpu.VMEM((rows, features), bf16),
            pltpu.VMEM((rows, features), f32),
            pltpu.SemaphoreType.DMA((LINE,)),
            pltpu.SemaphoreType.DMA((2,)),
            pltpu.SemaphoreType.DMA((LINE, groups)),
            pltpu.SemaphoreType.DMA((chunks,)),
            pltpu.SemaphoreType.DMA((chunks,)),
            pltpu.SemaphoreType.DMA((2,)),
            pltpu.SemaphoreType.DMA((2,)),
        ]
        + line_sems(chunks)
        + line_sems(chunks)
        + line_sems(chunks),
        input_output_aliases={0: 0},
        compiler_params=comm_params(1),
    )(x, weight, cot, entries, exits, *tables, leaf_parent, out_entry, finals, tokens, gain[None, :])


class Trees:
    def __init__(self, tree, ref, send, recv):
        self.tree, self.ref, self.sems = tree, ref, (send, recv)
        self.rounds = ref.shape[0].bit_length() - 1
        self.partners = [self.partner(number) for number in range(self.rounds)]

    def partner(self, number):
        size = 1 << number
        return self.tree + size - 2 * size * ((self.tree // size) % 2)

    def copy(self, number, owner):
        size = 1 << number
        here = pl.ds((owner // size) * size, size)
        return pltpu.make_async_remote_copy(
            src_ref=self.ref.at[here],
            dst_ref=self.ref.at[here],
            send_sem=self.sems[0].at[number],
            recv_sem=self.sems[1].at[number],
            device_id={"dp": self.partner(number)},
            device_id_type=MESH,
        )

    def send(self, number):
        self.copy(number, self.tree).start()

    def arrive(self, number):
        self.copy(number, self.partner(number)).wait_recv()

    def advance(self, number):
        if number < self.rounds:
            self.arrive(number - 1)
            self.send(number)

    def drain(self):
        for number in range(self.rounds):
            self.copy(number, self.tree).wait_send()


def back_body(
    chunks, seg,
    q_ref, w_ref, n_ref, mid_ref, middle_ref, res_ref, right_ref, left_ref, x_ref,
    o_ref, g_ref, lse_ref, p_ref, cos_ref, sin_ref, a_ref, e_ref, gain_ref, lone_ref, final_ref, exit_ref,
    out_ref, model_ref, head_ref, sum_ref,
    qv, dv, dq_t, dk_sum, dv_sum, part, held, acc, wv, midv, nv, terms, xv, outv, resv, model, head, low, block, extra,
    qsem, wsem, osem, e_send, e_recv, send, recv, x_send, x_recv, t_send, t_recv, h_send, h_recv,
):
    place = lax.axis_index("tensor")
    tree = lax.axis_index("dp")
    trees = Trees(tree, model_ref, t_send, t_recv)
    heads = Trees(tree, head_ref, h_send, h_recv)
    groups, total, width = q_ref.shape
    rank = a_ref.shape[1]
    (load_q,) = fetch([(q_ref, qv)], qsem)
    loads = fetch(
        [
            (w_ref.at[:, : groups * width], wv),
            (n_ref, nv),
            (mid_ref, midv),
            (middle_ref, acc),
            (res_ref.at[place], terms.at[0]),
            (x_ref, xv),
        ],
        wsem,
    )
    block[...] = jnp.zeros_like(block)
    for g in range(groups):
        block[g * rank : (g + 1) * rank, g * width : (g + 1) * width] = a_ref[g]
    greet(place, trees.partners)

    def exchange(side, target):
        index = 0 if side == 1 else 1
        return pltpu.make_async_remote_copy(
            src_ref=(right_ref, left_ref)[index],
            dst_ref=terms.at[index + 1],
            send_sem=e_send.at[index],
            recv_sem=e_recv.at[index],
            device_id={"tensor": target},
            device_id_type=MESH,
        )

    for side in SIDES:
        pl.when(far_of(place, side) < LINE - 1)(exchange(side, place + side).start)
    load_q.wait()
    pair = 2 * HEAD_DIM

    def one_pair(j, carry):
        lanes = pl.ds(pl.multiple_of(j * pair, pair), pair)
        attend_back_pair(
            seg, qv, lanes, o_ref, g_ref, lse_ref, j, p_ref[...], cos_ref, sin_ref, dv, dq_t, dk_sum, dv_sum
        )
        return carry

    lax.fori_loop(0, width // pair, one_pair, 0)
    loads[0].wait()
    rows = part.shape[1]
    summed = Sum(place, part, held, send, recv, chunks)
    gather = Gather(place, extra, x_send, x_recv, 1)
    entry = e_ref[:groups].reshape(groups * rank, -1)

    def rows_of(slot):
        shard = place ^ slot
        mine = pl.ds(pl.multiple_of(shard * rows, rows), rows)
        return shard, mine, jnp.concatenate([dv[g, mine] for g in range(groups)], axis=1)

    def lower(slot):
        _, mine, d = rows_of(slot)
        low[mine] = nt(d, block[...]).astype(bf16)

    def partial(slot):
        shard, mine, d = rows_of(slot)
        part[shard] = (nt(d, wv[...]) + nn(low[mine], entry)).astype(bf16)

    lower(3)
    partial(3)
    summed.begin(1, 0)
    summed.begin(1, 1)
    for slot in (2, 1, 0):
        lower(slot)
    for load in loads[1:]:
        load.wait()

    def turned(value):
        return value.astype(f32).T.astype(bf16)

    joined = nn(turned(low[...]), nv[...].reshape(total, -1))
    extra[place] = jnp.concatenate([joined, final_ref[...]], axis=0).astype(bf16)
    gather.send(1, 0)
    for chunk in range(2, chunks):
        summed.begin(1, chunk)
    for slot in (2, 1, 0):
        partial(slot)
    for step in (2, 3):
        for chunk in range(chunks):
            summed.begin(step, chunk)
    summed.relay(2, 0)
    summed.relay(2, 1)
    gather.arrive(1, 0)
    gather.send(2, 0)
    summed.relay(2, 2)
    low_one = turned(lone_ref[...])
    for g in range(groups):
        band = slice(g * rank, (g + 1) * rank)
        head[band] = nn(low_one[band], dv[g]).astype(bf16)
    head[groups * rank :] = exit_ref[...].astype(bf16)
    (store,) = fetch([(head, head_ref.at[tree])], osem)
    summed.relay(2, 3)
    store.wait()
    heads.send(0)
    gather.arrive(2, 0)
    gather.send(3, 0)
    heads.advance(1)
    summed.relay(3, 0)
    gather.arrive(3, 0)
    model[...] = functools.reduce(
        jnp.add, [extra[shard].astype(f32) for shard in range(LINE)]
    ).astype(bf16)
    (store,) = fetch([(model, model_ref.at[tree])], osem)
    for side in SIDES:
        pl.when(far_of(place, side) > 0)(exchange(side, place - side).wait_recv)
    value = acc[...] + terms[0].astype(f32)
    for index, side in enumerate(SIDES):
        value += jnp.where(far_of(place, side) > 0, terms[index + 1].astype(f32), 0.0)
    resv[...] = value.astype(bf16)
    store.wait()
    trees.send(0)
    (store,) = fetch([(resv, sum_ref)], osem)
    heads.advance(2)
    summed.relay(3, 1)
    trees.advance(1)
    summed.relay(3, 2)
    summed.relay(3, 3)
    trees.advance(2)
    store.wait()
    size = rows // chunks
    stores = []

    def finish(chunk):
        summed.total(chunk, acc)
        here = chunk_rows(chunk, size)
        values = xv[here].astype(f32)
        rms = lax.rsqrt(jnp.mean(values * values, axis=1, keepdims=True) + eps)
        scaled = acc[here] * gain_ref[...].astype(f32)
        mean = jnp.mean(scaled * values, axis=1, keepdims=True)
        outv[here] = (midv[here] + rms * (scaled - values * (rms * rms) * mean)).astype(bf16)
        copy = pltpu.make_async_copy(outv.at[here], out_ref.at[here], wsem.at[chunk])
        copy.start()
        stores.append(copy)

    finish(0)
    finish(1)
    for number in range(3, trees.rounds):
        trees.advance(number)
        heads.advance(number)
    finish(2)
    finish(3)
    for blocks in (trees, heads):
        blocks.arrive(blocks.rounds - 1)
        blocks.drain()
    for copy in stores:
        copy.wait()
    for side in SIDES:
        pl.when(far_of(place, side) < LINE - 1)(exchange(side, place + side).wait_send)
    summed.drain()
    gather.drain()


def back(
    qkv, weight, normed, grad_middle, middle, res_parts, right, left, x, attended, grad, lse, leaf_parent, tables, exits,
    entries, gain, low_one, final_grads, exit_grads, seg,
):
    chunks = LINE
    rows, features = x.shape
    groups, total, width = qkv.shape
    rank = exits.shape[1]
    deep = (groups + 1) * rank
    pair = 2 * HEAD_DIM
    trees = lax.axis_size("dp")
    sems = pltpu.SemaphoreType.DMA((trees.bit_length() - 1,))
    two = pltpu.SemaphoreType.DMA((2,))
    return pl.pallas_call(
        functools.partial(back_body, chunks, seg),
        in_specs=[IN_HBM] * 9 + [IN_VMEM] * 12,
        out_specs=[IN_HBM] * 4,
        out_shape=[
            jax.ShapeDtypeStruct((rows, features), bf16),
            jax.ShapeDtypeStruct((trees, deep, features), bf16),
            jax.ShapeDtypeStruct((trees, deep, width), bf16),
            jax.ShapeDtypeStruct((rows, features), bf16),
        ],
        scratch_shapes=[
            pltpu.VMEM((groups, total, width), bf16),
            pltpu.VMEM((groups, total, width), bf16),
            pltpu.VMEM((pair, total), f32),
            pltpu.VMEM((total, pair), f32),
            pltpu.VMEM((total, pair), f32),
            pltpu.VMEM((LINE, rows, features), bf16),
            pltpu.VMEM((2, LINE - 1, rows, features), bf16),
            pltpu.VMEM((rows, features), f32),
            pltpu.VMEM((features, groups * width), bf16),
            pltpu.VMEM((rows, features), f32),
            pltpu.VMEM((LINE, rows, features), bf16),
            pltpu.VMEM((3, rows, features), bf16),
            pltpu.VMEM((rows, features), bf16),
            pltpu.VMEM((rows, features), bf16),
            pltpu.VMEM((rows, features), bf16),
            pltpu.VMEM((deep, features), bf16),
            pltpu.VMEM((deep, width), bf16),
            pltpu.VMEM((total, groups * rank), bf16),
            pltpu.VMEM((groups * rank, groups * width), bf16),
            pltpu.VMEM((LINE, deep, features), bf16),
            pltpu.SemaphoreType.DMA((1,)),
            pltpu.SemaphoreType.DMA((6,)),
            pltpu.SemaphoreType.DMA((1,)),
            two,
            two,
        ]
        + line_sems(chunks)
        + line_sems(1)
        + [sems] * 4,
        compiler_params=comm_params(3),
    )(
        qkv, weight, normed, grad_middle, middle, res_parts, right, left, x, attended, grad[0], lse, leaf_parent, *tables,
        exits, entries, gain[None, :], low_one, final_grads, exit_grads,
    )


def tree_tiles(seg, rows, parent_row):
    trunk = TRUNK * seg
    leaves = trunk + BRANCHES * seg
    key = lax.broadcasted_iota(jnp.int32, (QT, QT), 0)
    query = lax.broadcasted_iota(jnp.int32, (QT, QT), 1)
    causal = key <= query
    own = causal & (key // seg == query // seg)
    tiles = []
    for start in range(0, trunk, QT):
        pieces = [(0, start, None)] if start else []
        tiles.append((start, pieces + [(start, QT, causal)]))
    tiles.append((trunk, [(0, trunk, None), (trunk, QT, own)]))
    branch = lax.broadcasted_iota(jnp.int32, (BRANCHES * seg, QT), 0) // seg
    for start in range(leaves, rows, QT):
        mine = branch == parent_row[:, start - leaves : start - leaves + QT]
        tiles.append(
            (start, [(0, trunk, None), (trunk, BRANCHES * seg, mine), (start, QT, own)])
        )
    return tiles


def attend_pair(seg, qkv_ref, lanes, parent_row, pair, o_ref, lse_ref):
    rows = qkv_ref.shape[1]
    value_t = qkv_ref[2, :, lanes].T
    lane = lax.broadcasted_iota(jnp.int32, (QT, 2 * HEAD_DIM), 1)
    for start, pieces in tree_tiles(seg, rows, parent_row):
        query = qkv_ref[0, start : start + QT, lanes] * bf16(HEAD_DIM**-0.5)
        outs = []
        for h in range(2):
            own_query = jnp.where(lane // HEAD_DIM == h, query, bf16(0))
            scores = []
            for k0, count, mask in pieces:
                s = nt(qkv_ref[1, k0 : k0 + count, lanes], own_query)
                scores.append(s if mask is None else jnp.where(mask, s, -1e30))
            top = functools.reduce(
                jnp.maximum, [jnp.max(s, axis=0, keepdims=True) for s in scores]
            )
            summed, out = 0.0, 0.0
            for (k0, count, _), s in zip(pieces, scores):
                weights = jnp.exp(s - top)
                summed += jnp.sum(weights, axis=0, keepdims=True)
                out += nn(
                    value_t[h * HEAD_DIM : (h + 1) * HEAD_DIM, k0 : k0 + count],
                    weights.astype(bf16),
                )
            outs.append(out / summed)
            lse_ref[pair, h : h + 1, start : start + QT] = top + jnp.log(summed)
        o_ref[start : start + QT, lanes] = jnp.concatenate(outs, axis=0).T.astype(bf16)


def attend_back_pair(
    seg, qkv_ref, lanes, o_ref, g_ref, lse_ref, pair, parent_row, cos_ref, sin_ref, d_ref, dq_t, dk, dv
):
    rows = qkv_ref.shape[1]
    scale = bf16(HEAD_DIM**-0.5)
    key_t = qkv_ref[1, :, lanes].T
    weighed_t = (g_ref[:, lanes].astype(f32) * o_ref[:, lanes].astype(f32)).T
    lane = lax.broadcasted_iota(jnp.int32, (QT, 2 * HEAD_DIM), 1)
    dk[...] = jnp.zeros_like(dk)
    dv[...] = jnp.zeros_like(dv)
    for start, pieces in tree_tiles(seg, rows, parent_row):
        query = qkv_ref[0, start : start + QT, lanes] * scale
        grad = g_ref[start : start + QT, lanes]
        for h in range(2):
            mine = lane // HEAD_DIM == h
            own_query = jnp.where(mine, query, bf16(0))
            own_grad = jnp.where(mine, grad, bf16(0))
            band = slice(h * HEAD_DIM, (h + 1) * HEAD_DIM)
            delta = jnp.sum(weighed_t[band, start : start + QT], axis=0, keepdims=True)
            lse = lse_ref[pair, h : h + 1, start : start + QT]
            grad_q = 0.0
            for k0, count, mask in pieces:
                probs = jnp.exp(nt(qkv_ref[1, k0 : k0 + count, lanes], own_query) - lse)
                if mask is not None:
                    probs = jnp.where(mask, probs, 0.0)
                grad_probs = nt(qkv_ref[2, k0 : k0 + count, lanes], own_grad)
                grad_scores = (probs * (grad_probs - delta)).astype(bf16)
                dk[k0 : k0 + count] += nn(grad_scores, own_query)
                dv[k0 : k0 + count] += nn(probs.astype(bf16), own_grad)
                grad_q += nn(key_t[band, k0 : k0 + count], grad_scores)
            dq_t[band, start : start + QT] = grad_q
    cosine, sine = cos_ref[...], -sin_ref[...]
    d_ref[0, :, lanes] = turn(dq_t[...].T * HEAD_DIM**-0.5, cosine, sine).astype(bf16)
    d_ref[1, :, lanes] = turn(dk[...], cosine, sine).astype(bf16)
    d_ref[2, :, lanes] = dv[...].astype(bf16)


def feed_body(
    rank, tile, chunks,
    n_ref, c_ref, near_ref, wg_ref, wu_ref, wd_ref, mid_ref, wo_ref,
    pick_ref, xu_in, xd_in, e_in, f_in, gain_ref, oe_ref, att_ref, lo_ref,
    grad_ref, res_ref, right_ref, left_ref, b_ref, held_ref, far_ref, unit_out, model_out, y_ref, final_ref, exit_ref,
    unit_ref, model_ref, x_ref, e_ref, f_ref, midv, nbuf, cbuf, wbuf, low, low_t, acc_res, acc_back, acc_low,
    part, held, resv, own, extra, wo, nsem, csem, wsem, rsem, msem,
    send, recv, g_send, g_recv, x_send, x_recv, c_send, c_recv, r_send, r_recv,
):
    place = lax.axis_index("tensor")
    units = unit_ref.shape[1]
    tiles = units // tile
    rows = part.shape[1]
    summed = Near(place, part, held, send, recv, chunks)
    cots = Gather(place, far_ref, c_send, c_recv, 1, second=near_ref)
    inside = ((place + 1) // 2) % 2
    gather = Gather(place, b_ref, g_send, g_recv, chunks, own)
    joint = Gather(place, extra, x_send, x_recv, 1)

    def load_rows(order, act):
        into = order % 2
        shard = place ^ ((order + 1) % LINE)
        act(pltpu.make_async_copy(n_ref.at[shard], nbuf.at[into], nsem.at[into]))

        def take(source):
            act(pltpu.make_async_copy(source, cbuf.at[into], csem.at[into]))

        beside = (order == 0) | ((order == 2) & (inside == 1))
        pl.when(order == LINE - 1)(lambda: take(c_ref))
        pl.when(beside)(lambda: take(near_ref.at[shard]))
        pl.when(jnp.logical_not(beside) & (order < LINE - 1))(lambda: take(far_ref.at[shard]))

    def load_weights(index, into, act):
        columns = pl.ds(pl.multiple_of(index * tile, tile), tile)
        for k, w_ref in enumerate((wg_ref, wu_ref, wd_ref)):
            act(pltpu.make_async_copy(w_ref.at[:, columns], wbuf.at[into, k], wsem.at[into, k]))

    def start(copy):
        copy.start()

    def wait(copy):
        copy.wait()

    load_rows(jnp.int32(0), start)
    load_weights(0, 0, start)
    width = wo.shape[1]
    load_middle, load_out = fetch([(mid_ref, midv), (wo_ref.at[:, 3 * width :], wo)], msem)
    for padded in (x_ref, e_ref, f_ref):
        padded[...] = jnp.zeros_like(padded)
    x_ref[0, :rank] = xu_in[0]
    x_ref[1, rank : 2 * rank] = xu_in[1]
    x_ref[2, 2 * rank :] = xd_in[...]
    e_ref[: 2 * rank] = e_in[3:].reshape(2 * rank, -1)
    f_ref[2 * rank :] = f_in[1]
    unit_ref[...] = jnp.zeros_like(unit_ref)
    model_ref[...] = jnp.zeros_like(model_ref)
    greet(place)
    cots.send(2, 0)

    def one_shard(order, carry):
        into = order % 2
        shard = place ^ ((order + 1) % LINE)
        load_rows(order, wait)
        first = nt(nbuf[into], e_ref[...]) + nt(cbuf[into], f_ref[...])
        low[...] = first.astype(bf16)
        low_t[...] = first.T.astype(bf16)
        acc_res[...] = jnp.zeros_like(acc_res)
        acc_back[...] = jnp.zeros_like(acc_back)
        acc_low[...] = jnp.zeros_like(acc_low)

        def one_tile(index, carry):
            stage = order * tiles + index
            at = stage % 2
            load_weights(index, at, wait)

            @pl.when(stage < LINE * tiles - 1)
            def _():
                load_weights((index + 1) % tiles, 1 - at, start)

            columns = pl.ds(pl.multiple_of(index * tile, tile), tile)
            x_gate, x_rise, x_fall = x_ref[0, :, columns], x_ref[1, :, columns], x_ref[2, :, columns]
            gate = nn(nbuf[into], wbuf[at, 0]) + nn(low[...], x_gate)
            rise = nn(nbuf[into], wbuf[at, 1]) + nn(low[...], x_rise)
            grad_hidden = nn(cbuf[into], wbuf[at, 2]) + nn(low[...], x_fall)
            sigmoid = jax.nn.sigmoid(gate)
            silu = gate * sigmoid
            hidden = (silu * rise).astype(bf16)
            grad_gate = (grad_hidden * rise * sigmoid * (1.0 + gate * (1.0 - sigmoid))).astype(bf16)
            grad_rise = (grad_hidden * silu).astype(bf16)
            acc_back[...] += nt(grad_gate, wbuf[at, 0]) + nt(grad_rise, wbuf[at, 1])
            acc_res[...] += nt(hidden, wbuf[at, 2])
            acc_low[...] += nt(grad_gate, x_gate) + nt(grad_rise, x_rise) + nt(hidden, x_fall)
            unit_ref[:rank, columns] += nn(low_t[:rank], grad_gate)
            unit_ref[rank : 2 * rank, columns] += nn(low_t[rank : 2 * rank], grad_rise)
            unit_ref[2 * rank :, columns] += nn(low_t[2 * rank : 3 * rank], hidden)
            for number, (away, chunk) in enumerate(((1, 2), (1, 3), (2, 0), (2, 1))):

                @pl.when((order == LINE - 1) & (index == number))
                def _():
                    summed.send(away, chunk, 1)

            return carry

        lax.fori_loop(0, tiles, one_tile, 0)

        @pl.when(order == 0)
        def _():
            cots.relay(3, 0)
            cots.end_got(2)

        @pl.when(order == 1)
        def _():
            cots.end_got(3)

        @pl.when(order < LINE - 1)
        def _():
            load_rows(order + 1, start)

        joined = acc_low[...].astype(bf16)
        joined_t = acc_low[...].T.astype(bf16)
        part[shard] = (acc_back[...] + nn(joined, e_ref[...])).astype(bf16)
        for away in (1, 2, 3):

            @pl.when(order == away - 1)
            def _():
                for chunk in range(chunks):
                    summed.send(away, chunk, 0)
                if away == 3:
                    summed.send(1, 0, 1)
                    summed.send(1, 1, 1)

        @pl.when(order > 0)
        def _():
            pltpu.make_async_copy(resv, res_ref.at[shard], rsem.at[0]).wait()

        resv[...] = (acc_res[...] + nn(joined, f_ref[...])).astype(bf16)
        pltpu.make_async_copy(resv, res_ref.at[shard], rsem.at[0]).start()
        model_ref[: 2 * rank] += nn(joined_t[: 2 * rank], nbuf[into])
        model_ref[2 * rank :] += nn(joined_t[2 * rank : 3 * rank], cbuf[into])
        return carry

    lax.fori_loop(0, LINE, one_shard, 0)
    def pass_on(side, step, source, target):
        index = 0 if side == 1 else 1
        return pltpu.make_async_remote_copy(
            src_ref=source,
            dst_ref=held_ref.at[index, step - 1],
            send_sem=r_send.at[index, step - 1],
            recv_sem=r_recv.at[index, step - 1],
            device_id={"tensor": target},
            device_id_type=MESH,
        )

    def at_far(side, number, act):
        pl.when(far_of(place, side) == number)(act)

    def ready(side, step, shard):
        index = 0 if side == 1 else 1
        pass_on(side, step, resv, place - side).wait_recv()
        copies = [
            pltpu.make_async_copy(res_ref.at[shard], cbuf.at[0], csem.at[0]),
            pltpu.make_async_copy(held_ref.at[index, step - 1], cbuf.at[1], csem.at[1]),
        ]
        for copy in copies:
            copy.start()
        for copy in copies:
            copy.wait()
        cbuf[0] = (cbuf[0].astype(f32) + cbuf[1].astype(f32)).astype(bf16)

    def send_result(step):
        for side in SIDES:
            at_far(
                side,
                0,
                lambda: pass_on(side, step, res_ref.at[place + side * (LINE - step)], place + side).start(),
            )

    extra[place] = model_ref[...].astype(bf16)
    size = rows // chunks
    last = (LINE - 1) % 2
    load_middle.wait()
    send_result(1)

    def finish(chunk):
        summed.total(chunk, acc_back)
        here = chunk_rows(chunk, size)
        middle = midv[here]
        rms = lax.rsqrt(jnp.mean(middle * middle, axis=1, keepdims=True) + eps)
        scaled = acc_back[here] * gain_ref[...].astype(f32)
        mean = jnp.mean(scaled * middle, axis=1, keepdims=True)
        grad = cbuf[last, here].astype(f32) + rms * (scaled - middle * (rms * rms) * mean)
        own[here] = grad.astype(bf16)
        midv[here] = grad

    @pl.when(inside == 1)
    def _():
        for chunk in range(chunks):
            finish(chunk)
            gather.send(1, chunk, least=2)

    joint.send(1, 0)
    summed.send(2, 2, 1)
    summed.send(2, 3, 1)
    for chunk in range(chunks):
        summed.send(1, chunk, 2)
    for chunk in range(chunks):
        gather.send(1, chunk, least=1, most=1)

    @pl.when(inside == 0)
    def _():
        for chunk in range(chunks):
            finish(chunk)
            gather.send(1, chunk)

    send_result(2)
    (store,) = fetch([(midv, grad_ref)], msem)
    pltpu.make_async_copy(resv, res_ref.at[place], rsem.at[0]).wait()

    load_out.wait()

    def through(number, rows_ref, shard):
        mine = pl.ds(pl.multiple_of(shard * rows, rows), rows)
        value = rows_ref[...]
        reduced = nt(value, f_in[0])
        y_ref[0, mine] = (nn(value, wo[...]) + nn(reduced.astype(bf16), oe_ref[...])).astype(bf16)
        final = nn(lo_ref[mine].astype(f32).T.astype(bf16), value)
        leave = nn(reduced.T.astype(bf16), att_ref[mine])
        final_ref[...] = final if number == 0 else final_ref[...] + final
        exit_ref[...] = leave if number == 0 else exit_ref[...] + leave

    def take(number, shard):
        copy = pltpu.make_async_copy(b_ref.at[shard], nbuf.at[number % 2], nsem.at[number % 2])
        copy.start()
        copy.wait()
        through(number, nbuf.at[number % 2], shard)

    joint.relay(2, 0)
    through(0, own, place)
    unit_out[: 3 * rank] = unit_ref[...].astype(bf16)
    unit_out[3 * rank :] = jnp.full((rank, units), pick_ref[0, 0], f32).astype(bf16)
    for chunk in range(chunks):
        gather.relay(2, chunk, least=2)
    gather.end_got(1)
    joint.relay(3, 0)
    take(1, place ^ (1 + 2 * inside))
    for chunk in range(chunks):
        gather.relay(2, chunk, most=1)
        if chunk:
            gather.relay(3, chunk - 1)
    gather.relay(3, chunks - 1)
    for side in SIDES:

        @pl.when(far_of(place, side) == 1)
        def _():
            ready(side, 1, place + side * 2)
            resv[...] = cbuf[0]
            pass_on(side, 2, resv, place + side).start()

    gather.end_got(2)
    take(2, place ^ (2 - inside))
    joint.close()
    model_out[...] = functools.reduce(
        jnp.add, [extra[shard].astype(f32) for shard in range(LINE)]
    ).astype(bf16)
    gather.end_got(3)
    take(3, place ^ (3 - inside))
    for index, side in enumerate(SIDES):
        target = (right_ref, left_ref)[index]

        @pl.when(far_of(place, side) == 0)
        def _():
            copy = pltpu.make_async_copy(res_ref.at[place + side], nbuf.at[index], nsem.at[index])
            copy.start()
            copy.wait()

        @pl.when((far_of(place, side) > 0) & (far_of(place, side) < LINE - 1))
        def _():
            ready(side, 2, place + side)
            nbuf[index] = cbuf[0]

        copy = pltpu.make_async_copy(nbuf.at[index], target, nsem.at[index])
        copy.start()
        copy.wait()
    for side in SIDES:
        for step in (1, 2):
            at_far(
                side,
                0,
                lambda: pass_on(side, step, res_ref.at[place + side * (LINE - step)], place + side).wait_send(),
            )
        at_far(side, 1, lambda: pass_on(side, 2, resv, place + side).wait_send())
    summed.drain()
    gather.drain()
    joint.drain()
    cots.drain(start=2)
    store.wait()


def feed(
    normed, cots, weights, middle, w_heads, pick, units_exit, fall_entry, entries, finals, gain, out_entry,
    attended, low_out, tile=512, chunks=4,
):
    _, rows, features = normed.shape
    units = weights[0].shape[1]
    rank, width = out_entry.shape
    total = LINE * rows
    one = jax.ShapeDtypeStruct((rows, features), bf16)
    return pl.pallas_call(
        functools.partial(feed_body, rank, tile, chunks),
        in_specs=[IN_HBM] * 8 + [pl.BlockSpec(memory_space=pltpu.SMEM)] + [IN_VMEM] * 8,
        out_specs=[IN_HBM] * 7 + [IN_VMEM] * 5,
        out_shape=[
            jax.ShapeDtypeStruct((rows, features), f32),
            jax.ShapeDtypeStruct((LINE, rows, features), bf16),
            one,
            one,
            jax.ShapeDtypeStruct((LINE, rows, features), bf16),
            jax.ShapeDtypeStruct((2, LINE - 2, rows, features), bf16),
            jax.ShapeDtypeStruct((LINE, rows, features), bf16),
            jax.ShapeDtypeStruct((4 * rank, units), bf16),
            jax.ShapeDtypeStruct((3 * rank, features), bf16),
            jax.ShapeDtypeStruct((1, total, width), bf16),
            jax.ShapeDtypeStruct((rank, features), f32),
            jax.ShapeDtypeStruct((rank, width), f32),
        ],
        scratch_shapes=[
            pltpu.VMEM((3 * rank, units), f32),
            pltpu.VMEM((3 * rank, features), f32),
            pltpu.VMEM((3, 3 * rank, units), bf16),
            pltpu.VMEM((3 * rank, features), bf16),
            pltpu.VMEM((3 * rank, features), bf16),
            pltpu.VMEM((rows, features), f32),
            pltpu.VMEM((2, rows, features), bf16),
            pltpu.VMEM((2, rows, features), bf16),
            pltpu.VMEM((2, 3, features, tile), bf16),
            pltpu.VMEM((rows, 3 * rank), bf16),
            pltpu.VMEM((3 * rank, rows), bf16),
            pltpu.VMEM((rows, features), f32),
            pltpu.VMEM((rows, features), f32),
            pltpu.VMEM((rows, 3 * rank), f32),
            pltpu.VMEM((LINE, rows, features), bf16),
            pltpu.VMEM((2, LINE - 1, rows, features), bf16),
            pltpu.VMEM((rows, features), bf16),
            pltpu.VMEM((rows, features), bf16),
            pltpu.VMEM((LINE, 3 * rank, features), bf16),
            pltpu.VMEM((features, width), bf16),
            pltpu.SemaphoreType.DMA((2,)),
            pltpu.SemaphoreType.DMA((2,)),
            pltpu.SemaphoreType.DMA((2, 3)),
            pltpu.SemaphoreType.DMA((1,)),
            pltpu.SemaphoreType.DMA((2,)),
        ]
        + line_sems(chunks)
        + line_sems(chunks)
        + line_sems(1)
        + line_sems(1)
        + [pltpu.SemaphoreType.DMA((2, LINE - 2))] * 2,
        compiler_params=comm_params(5),
    )(
        normed, *cots, *weights, middle, w_heads, pick, units_exit, fall_entry, entries, finals, gain[None, :], out_entry,
        attended, low_out,
    )


def pick_body(pick_ref, *refs):
    count = len(refs) // 2
    for source, target in zip(refs[:count], refs[count:]):
        target[...] = source[...].reshape(target.shape)


def picked(pick, arrays):
    shapes = [a.shape[:1] + a.shape[2:] for a in arrays]
    return pl.pallas_call(
        pick_body,
        grid_spec=pltpu.PrefetchScalarGridSpec(
            num_scalar_prefetch=1,
            grid=(1,),
            in_specs=[
                pl.BlockSpec(a.shape[:1] + (1,) + a.shape[2:], lambda i, p: (0, p[0], 0, 0)) for a in arrays
            ],
            out_specs=[pl.BlockSpec(shape, lambda i, p: (0, 0, 0)) for shape in shapes],
        ),
        out_shape=[jax.ShapeDtypeStruct(shape, bf16) for shape in shapes],
    )(pick, *arrays)


def per_tree(block):
    return lax.all_gather(block, "dp", axis=0, tiled=False)


def combine_body(
    rank, pick_ref, early, model, late, head, one, two, entry_ref, final_ref, unit_ref, down_ref, exit_ref, out_ref,
    one_ref, two_ref,
):
    one_ref[...] = one[...]
    two_ref[...] = two[...]
    for ref in (entry_ref, final_ref, unit_ref, down_ref, exit_ref, out_ref):
        ref[...] = jnp.zeros_like(ref)

    def one_tree(tree, carry):
        pick = pick_ref[tree]

        def block(ref, index):
            return ref[tree, index * rank : (index + 1) * rank].astype(f32)

        for k in range(3):
            entry_ref[k, pick] += block(late, k)
            exit_ref[k, pick] += block(head, k)
        final_ref[0, pick] += block(late, 3)
        out_ref[pick] += block(head, 3)
        for k in range(2):
            entry_ref[3 + k, pick] += block(model, k)
            unit_ref[k, pick] += block(early, k)
        final_ref[1, pick] += block(model, 2)
        down_ref[pick] += block(early, 2)
        return carry

    lax.fori_loop(0, early.shape[0], one_tree, 0)


def combine(picks, early, model, late, head, one, two, adapters, steps=4):
    trees, _, features = early.shape
    rank = late.shape[1] // 4
    width = head.shape[2]
    wide, narrow = features // steps, width // steps

    def taken(array, tile):
        return pl.BlockSpec((trees, array.shape[1], tile), lambda i, p: (0, 0, i))

    def given(lead, tile):
        shape = lead + (adapters, rank, tile)
        return pl.BlockSpec(shape, lambda i, p: (0,) * (len(shape) - 1) + (i,))

    whole = pl.BlockSpec((one.shape[0] // steps, one.shape[1]), lambda i, p: (i, 0))

    def shape(lead, full):
        return jax.ShapeDtypeStruct(lead + (adapters, rank, full), f32)

    return pl.pallas_call(
        functools.partial(combine_body, rank),
        grid_spec=pltpu.PrefetchScalarGridSpec(
            num_scalar_prefetch=1,
            grid=(steps,),
            in_specs=[taken(early, wide), taken(model, wide), taken(late, wide), taken(head, narrow), whole, whole],
            out_specs=[
                given((5,), wide),
                given((2,), wide),
                given((2,), wide),
                given((), wide),
                given((3,), narrow),
                given((), narrow),
                whole,
                whole,
            ],
        ),
        out_shape=[
            shape((5,), features),
            shape((2,), features),
            shape((2,), features),
            shape((), features),
            shape((3,), width),
            shape((), width),
            jax.ShapeDtypeStruct(one.shape, bf16),
            jax.ShapeDtypeStruct(two.shape, bf16),
        ],
        compiler_params=pltpu.CompilerParams(vmem_limit_bytes=VMEM_LIMIT),
    )(picks, early, model, late, head, one, two)


def local(
    tokens,
    cotangent,
    attention_gain,
    feed_gain,
    query_weight,
    key_weight,
    value_weight,
    output_weight,
    gate_weight,
    up_weight,
    down_weight,
    entry_maps,
    head_exits,
    unit_exits,
    output_entry,
    down_entry,
    final_exits,
    parents,
    adapter_pick,
):
    adapters, rank = entry_maps.shape[1], entry_maps.shape[3]
    local_rows = tokens.shape[0]
    total = local_rows * lax.axis_size("tensor")
    blocks = parents.shape[1]
    seg = total // blocks
    tables = rope_tables(blocks, seg)
    leaf_parent = (jnp.repeat(parents[0, TRUNK + BRANCHES :], seg) - TRUNK)[None, :]
    gain_one, gain_two = attention_gain, feed_gain

    w_heads = lax.all_gather(
        jnp.concatenate([query_weight, key_weight, value_weight, output_weight], axis=1),
        "dp",
        axis=0,
        tiled=True,
    )

    w_units = [
        lax.all_gather(w, "dp", axis=0, tiled=True) for w in (gate_weight, up_weight, down_weight)
    ]
    entries, heads_exit, units_exit, out_entry, fall_entry, finals = picked(
        adapter_pick,
        (
            jnp.swapaxes(entry_maps, 2, 3),
            head_exits,
            unit_exits,
            jnp.swapaxes(output_entry, 1, 2)[None],
            jnp.swapaxes(down_entry, 1, 2)[None],
            final_exits,
        ),
    )
    out_entry, fall_entry = out_entry[0], fall_entry[0]

    most_one = gather_norm(tokens, gain_one)
    full_one, qkv, middle, full_two, full_cot, low_one, attended, lse, adapt_o = front(
        most_one, w_heads, cotangent, entries, heads_exit, tables, leaf_parent, out_entry, finals, tokens, gain_two, seg
    )

    (
        grad_middle, res_parts, res_right, res_left, _, _, _, early, model_sum, grad_attended, final_grads, exit_grads,
    ) = feed(
        full_two, (cotangent, full_cot), w_units, middle, w_heads, adapter_pick.astype(f32)[None, :],
        units_exit, fall_entry, entries, finals, gain_two, out_entry, attended, adapt_o,
    )
    early = per_tree(early)
    model_all = per_tree(model_sum)

    grad_tokens, late_model, late_head, result = back(
        qkv, w_heads, full_one, grad_middle, middle, res_parts, res_right, res_left, tokens, attended, grad_attended, lse,
        leaf_parent, tables, heads_exit, entries, gain_one, low_one, final_grads, exit_grads, seg,
    )

    picks = early[:, 3 * rank, 0].astype(jnp.int32)
    grad_entries, grad_finals, grad_units, grad_down, grad_heads, grad_output, result, grad_tokens = combine(
        picks, early, model_all, late_model, late_head, result, grad_tokens, adapters
    )
    grad_entries = grad_entries.swapaxes(2, 3)
    grad_output = grad_output.swapaxes(1, 2)
    grad_down = grad_down.swapaxes(1, 2)
    return (
        result,
        grad_tokens,
        grad_entries,
        grad_heads,
        grad_units,
        grad_output,
        grad_down,
        grad_finals,
    )


def solution(mesh):
    in_specs = (
        P(("dp", "tensor"), None),
        P(("dp", "tensor"), None),
        P(),
        P(),
        P("dp", "tensor"),
        P("dp", "tensor"),
        P("dp", "tensor"),
        P("dp", "tensor"),
        P("dp", "tensor"),
        P("dp", "tensor"),
        P("dp", "tensor"),
        P(),
        P(None, None, None, "tensor"),
        P(None, None, None, "tensor"),
        P(None, "tensor", None),
        P(None, "tensor", None),
        P(),
        P("dp", None),
        P("dp"),
    )
    out_specs = (
        P(("dp", "tensor"), None),
        P(("dp", "tensor"), None),
        P(),
        P(None, None, None, "tensor"),
        P(None, None, None, "tensor"),
        P(None, "tensor", None),
        P(None, "tensor", None),
        P(),
    )
    return jax.shard_map(local, mesh=mesh, in_specs=in_specs, out_specs=out_specs, check_vma=False)
```

```python
import functools

import jax
import jax.numpy as jnp
import numpy as np
from jax import lax
from jax.experimental import pallas as pl
from jax.experimental.pallas import tpu as pltpu
from jax.sharding import PartitionSpec as P

HEAD_DIM = 64
TRUNK, BRANCHES = 8, 4
QT = 256
VMEM_LIMIT = 60 * 1024 * 1024
LINE = 4
MESH = pl.DeviceIdType.MESH

eps = 1e-05
theta = 130000.0
bf16, f32 = jnp.bfloat16, jnp.float32


def nn(left, right):
    return jnp.dot(left, right, preferred_element_type=f32)


def nt(left, right):
    return lax.dot_general(left, right, (((1,), (1,)), ((), ())), preferred_element_type=f32)


def tn(left, right):
    return lax.dot_general(left, right, (((0,), (0,)), ((), ())), preferred_element_type=f32)


def rope_tables(blocks, seg):
    depth = np.minimum(np.arange(blocks), TRUNK)
    depth[TRUNK + BRANCHES :] = TRUNK + 1
    position = (np.repeat(depth, seg) * seg + np.arange(blocks * seg) % seg).astype(np.float32)
    half = HEAD_DIM // 2
    freq = (np.float32(theta) ** (-np.arange(half, dtype=np.float32) / half)).astype(np.float32)
    angle = (position[:, None] * freq[None, :]).astype(np.float32)
    cosine = np.tile(np.cos(angle), (1, 4)).astype(np.float32)
    sine = np.sin(angle).astype(np.float32)
    sine = np.concatenate([-sine, sine, -sine, sine], axis=1)
    return jnp.asarray(cosine), jnp.asarray(sine)


def turn(values, cosine, sine):
    width = values.shape[1]
    reps = width // cosine.shape[1]
    if reps > 1:
        cosine = jnp.concatenate([cosine] * reps, axis=1)
        sine = jnp.concatenate([sine] * reps, axis=1)
    lane = lax.broadcasted_iota(jnp.int32, values.shape, 1)
    half = HEAD_DIM // 2
    other = jnp.where(
        lane % HEAD_DIM < half, pltpu.roll(values, width - half, 1), pltpu.roll(values, half, 1)
    )
    return values * cosine + other * sine


SIDES = (1, -1)


def far_of(place, side):
    return place if side == 1 else LINE - 1 - place


def greet(place, partners=()):
    barrier = pltpu.get_barrier_semaphore()
    for partner in partners:
        pl.semaphore_signal(barrier, inc=1, device_id={"dp": partner}, device_id_type=MESH)
    for side in SIDES:

        @pl.when(far_of(place, side) < LINE - 1)
        def _():
            pl.semaphore_signal(
                barrier, inc=1, device_id={"tensor": place + side}, device_id_type=MESH
            )

    edge = (place == 0) | (place == LINE - 1)

    @pl.when(edge)
    def _():
        pl.semaphore_wait(barrier, 1 + len(partners))

    @pl.when(jnp.logical_not(edge))
    def _():
        pl.semaphore_wait(barrier, 2 + len(partners))


def chunk_rows(chunk, rows):
    return pl.ds(chunk * rows, rows)


class Gather:
    def __init__(self, place, buf, send, recv, chunks, own=None, second=None):
        self.place, self.buf, self.sems, self.chunks = place, buf, (send, recv), chunks
        self.rows = buf.shape[1] // chunks
        self.own, self.second = own, second

    def copy(self, side, step, chunk, shard, target):
        rows = chunk_rows(chunk, self.rows)
        where = self.buf.at[shard, rows]
        index = 0 if side == 1 else 1
        spot = (index, step - 1, chunk)
        source = where
        if step == 1 and self.own is not None:
            source = self.own.at[rows]
        if step == 2 and self.second is not None:
            source = self.second.at[shard, rows]
        return pltpu.make_async_remote_copy(
            src_ref=source,
            dst_ref=where,
            send_sem=self.sems[0].at[spot],
            recv_sem=self.sems[1].at[spot],
            device_id={"tensor": target},
            device_id_type=MESH,
        )

    def each_send(self, step, chunk, act, least=0, most=LINE):
        for side in SIDES:
            far = far_of(self.place, side)

            @pl.when((far < LINE - 1) & (far >= step - 1) & (far >= least) & (far <= most))
            def _():
                shard = self.place - side * (step - 1)
                act(self.copy(side, step, chunk, shard, self.place + side))

    def send(self, step, chunk, least=0, most=LINE):
        self.each_send(step, chunk, lambda copy: copy.start(), least, most)

    def arrive(self, step, chunk):
        for side in SIDES:

            @pl.when(far_of(self.place, side) >= step)
            def _():
                shard = self.place - side * step
                self.copy(side, step, chunk, shard, self.place - side).wait_recv()

    def relay(self, step, chunk, least=0, most=LINE):
        for side in SIDES:
            far = far_of(self.place, side)

            @pl.when((far < LINE - 1) & (far >= step - 1) & (far >= least) & (far <= most))
            def _():
                before = self.place - side * (step - 1)
                self.copy(side, step - 1, chunk, before, self.place - side).wait_recv()
                self.copy(side, step, chunk, before, self.place + side).start()

    def close(self):
        for side in SIDES:

            @pl.when(far_of(self.place, side) == LINE - 1)
            def _():
                for step in range(1, LINE):
                    for chunk in range(self.chunks):
                        shard = self.place - side * step
                        self.copy(side, step, chunk, shard, self.place - side).wait_recv()

    def end_got(self, step):
        for side in SIDES:

            @pl.when(far_of(self.place, side) == LINE - 1)
            def _():
                for chunk in range(self.chunks):
                    self.copy(side, step, chunk, self.place - side * step, self.place - side).wait_recv()

    def drain(self, stop=LINE, start=1):
        for step in range(start, stop):
            for chunk in range(self.chunks):
                self.each_send(step, chunk, lambda copy: copy.wait_send())


class Sum:
    def __init__(self, place, part, held, send, recv, chunks):
        self.place, self.part, self.held = place, part, held
        self.sems, self.chunks = (send, recv), chunks
        self.rows = part.shape[1] // chunks

    def copy(self, side, step, chunk, shard, target):
        rows = chunk_rows(chunk, self.rows)
        index = 0 if side == 1 else 1
        spot = (index, step - 1, chunk)
        return pltpu.make_async_remote_copy(
            src_ref=self.part.at[shard, rows],
            dst_ref=self.held.at[index, step - 1, rows],
            send_sem=self.sems[0].at[spot],
            recv_sem=self.sems[1].at[spot],
            device_id={"tensor": target},
            device_id_type=MESH,
        )

    def add(self, step, chunk):
        rows = chunk_rows(chunk, self.rows)
        for index, side in enumerate(SIDES):
            far = far_of(self.place, side)
            shard = self.place + side * (LINE - step)

            @pl.when((far >= 1) & (far <= step - 1))
            def _():
                self.copy(side, step - 1, chunk, self.place, self.place - side).wait_recv()
                self.part[shard, rows] = (
                    self.part[shard, rows].astype(f32)
                    + self.held[index, step - 2, rows].astype(f32)
                ).astype(bf16)

    def send(self, step, chunk, least=0, most=LINE):
        if step > 1 and most > 0:
            self.add(step, chunk)
        for side in SIDES:
            far = far_of(self.place, side)
            shard = self.place + side * (LINE - step)

            @pl.when((far <= step - 1) & (far >= least) & (far <= most))
            def _():
                self.copy(side, step, chunk, shard, self.place + side).start()

    def begin(self, step, chunk):
        self.send(step, chunk, most=0)

    def relay(self, step, chunk):
        self.send(step, chunk, least=1)

    def total(self, chunk, out):
        rows = chunk_rows(chunk, self.rows)
        out[rows] = self.part[self.place, rows].astype(f32)
        for index, side in enumerate(SIDES):

            @pl.when(far_of(self.place, side) >= 1)
            def _():
                self.copy(side, LINE - 1, chunk, self.place, self.place - side).wait_recv()
                out[rows] += self.held[index, LINE - 2, rows].astype(f32)

    def drain(self, stop=LINE):
        for step in range(1, stop):
            for chunk in range(self.chunks):
                for side in SIDES:
                    far = far_of(self.place, side)
                    shard = self.place + side * (LINE - step)

                    @pl.when(far <= step - 1)
                    def _():
                        self.copy(side, step, chunk, shard, self.place + side).wait_send()


class Near:
    def __init__(self, place, part, held, send, recv, chunks):
        self.place, self.part, self.held = place, part, held
        self.sems, self.chunks = (send, recv), chunks
        self.rows = part.shape[1] // chunks

    def copy(self, side, away, chunk, shard, target):
        rows = chunk_rows(chunk, self.rows)
        index = 0 if side == 1 else 1
        spot = (index, away - 1, chunk)
        return pltpu.make_async_remote_copy(
            src_ref=self.part.at[shard, rows],
            dst_ref=self.held.at[index, away - 1, rows],
            send_sem=self.sems[0].at[spot],
            recv_sem=self.sems[1].at[spot],
            device_id={"tensor": target},
            device_id_type=MESH,
        )

    def send(self, away, chunk, number):
        rows = chunk_rows(chunk, self.rows)
        for index, side in enumerate(SIDES):
            shard = self.place + side * away

            @pl.when(far_of(self.place, side) == number)
            def _():
                if number:
                    self.copy(side, away + 1, chunk, self.place, self.place - side).wait_recv()
                    self.part[shard, rows] = (
                        self.part[shard, rows].astype(f32) + self.held[index, away, rows].astype(f32)
                    ).astype(bf16)
                self.copy(side, away, chunk, shard, self.place + side).start()

    def total(self, chunk, out):
        rows = chunk_rows(chunk, self.rows)
        out[rows] = self.part[self.place, rows].astype(f32)
        for index, side in enumerate(SIDES):

            @pl.when(far_of(self.place, side) >= 1)
            def _():
                self.copy(side, 1, chunk, self.place, self.place - side).wait_recv()
                out[rows] += self.held[index, 0, rows].astype(f32)

    def drain(self):
        for number in range(LINE - 1):
            for away in range(1, LINE - number):
                for chunk in range(self.chunks):
                    for side in SIDES:

                        @pl.when(far_of(self.place, side) == number)
                        def _():
                            shard = self.place + side * away
                            self.copy(side, away, chunk, shard, self.place + side).wait_send()


def line_sems(chunks):
    return [pltpu.SemaphoreType.DMA((2, LINE - 1, chunks))] * 2


def fetch(pairs, sems):
    copies = [pltpu.make_async_copy(src, dst, sems.at[i]) for i, (src, dst) in enumerate(pairs)]
    for copy in copies:
        copy.start()
    return copies


IN_VMEM = pl.BlockSpec(memory_space=pltpu.VMEM)
IN_HBM = pl.BlockSpec(memory_space=pl.ANY)


def comm_params(number):
    return pltpu.CompilerParams(
        vmem_limit_bytes=VMEM_LIMIT, collective_id=number, has_side_effects=True
    )


def gather_norm_body(chunks, x_ref, gain_ref, buf, own, sem, send, recv):
    place = lax.axis_index("tensor")
    greet(place)
    rows = x_ref[...].astype(f32)
    rms = lax.rsqrt(jnp.mean(rows * rows, axis=1, keepdims=True) + eps)
    own[...] = (rows * rms * gain_ref[...].astype(f32)).astype(bf16)
    gather = Gather(place, buf, send, recv, chunks, own)
    for chunk in range(chunks):
        gather.send(1, chunk)
    (kept,) = fetch([(own, buf.at[place])], sem)
    for chunk in range(chunks):
        gather.arrive(1, chunk)
        gather.send(2, chunk)
    kept.wait()
    for chunk in range(chunks):
        gather.arrive(2, chunk)
    gather.drain(stop=LINE - 1)


def gather_norm(x, gain, chunks=2):
    rows, features = x.shape
    return pl.pallas_call(
        functools.partial(gather_norm_body, chunks),
        in_specs=[IN_VMEM, IN_VMEM],
        out_specs=IN_HBM,
        out_shape=jax.ShapeDtypeStruct((LINE, rows, features), bf16),
        scratch_shapes=[pltpu.VMEM((rows, features), bf16), pltpu.SemaphoreType.DMA((1,))]
        + line_sems(chunks),
        compiler_params=comm_params(0),
    )(x, gain[None, :])


def front_body(
    chunks, seg,
    x_ref, w_ref, c_ref, e_ref, a_ref, cos_ref, sin_ref, p_ref, oe_ref, f_ref, tok_ref, gain_ref,
    kept_ref, y_ref, mid_ref, n_ref, cot_ref, l_ref, att_ref, lse_ref, lo_ref,
    buf, yv, wv, wo, part, held, own, midv, xsem, wsem, ysem, nsem, msem, send, recv,
    s_send, s_recv, g_send, g_recv, c_send, c_recv,
):
    place = lax.axis_index("tensor")
    groups, total, width = y_ref.shape
    rows, rank = x_ref.shape[1], a_ref.shape[1]
    edge = (place == 0) | (place == LINE - 1)
    last = place ^ (LINE - 1)

    def passed(side):
        shard = place - side * (LINE - 2)
        index = 0 if side == 1 else 1
        return pltpu.make_async_remote_copy(
            src_ref=x_ref.at[shard],
            dst_ref=buf.at[shard],
            send_sem=send.at[index],
            recv_sem=recv.at[index],
            device_id={"tensor": place + side},
            device_id_type=MESH,
        )

    def came(side):
        index = 0 if side == 1 else 1
        return pltpu.make_async_remote_copy(
            src_ref=x_ref.at[last],
            dst_ref=buf.at[last],
            send_sem=send.at[index],
            recv_sem=recv.at[index],
            device_id={"tensor": place - side},
            device_id_type=MESH,
        )

    copies = []
    for slot in range(LINE):
        copy = pltpu.make_async_copy(x_ref.at[place ^ slot], buf.at[place ^ slot], xsem.at[slot])
        if slot < LINE - 1:
            copy.start()
        else:
            pl.when(jnp.logical_not(edge))(copy.start)
        copies.append(copy)
    load, load_out = fetch(
        [(w_ref.at[:, : groups * width], wv), (w_ref.at[:, groups * width :], wo)], wsem
    )
    greet(place)
    cots = Gather(place, cot_ref, c_send, c_recv, chunks, c_ref)
    summed = Sum(place, part, held, s_send, s_recv, chunks)
    gather = Gather(place, n_ref, g_send, g_recv, chunks, own)
    for side in SIDES:
        pl.when(far_of(place, side) == LINE - 2)(passed(side).start)
    for chunk in range(chunks):
        cots.send(1, chunk)

    for copy in copies[:-1]:
        copy.wait()
    load.wait()
    outs = []
    for slot in range(LINE):
        shard = place ^ slot
        if slot == LINE - 1:
            pl.when(jnp.logical_not(edge))(copies[slot].wait)
            for side in SIDES:
                pl.when(far_of(place, side) == LINE - 1)(came(side).wait_recv)
            kept = pltpu.make_async_copy(buf.at[last], kept_ref.at[last], xsem.at[slot])
            pl.when(edge)(kept.start)
        mine = pl.ds(pl.multiple_of(shard * rows, rows), rows)
        low = nt(buf[shard], e_ref[:groups].reshape(groups * rank, -1)).astype(bf16)
        l_ref[mine] = low
        for g in range(groups):
            band = slice(g * width, (g + 1) * width)
            value = nn(buf[shard], wv[:, band]) + nn(low[:, g * rank : (g + 1) * rank], a_ref[g])
            if g < groups - 1:
                value = turn(value, cos_ref[mine], sin_ref[mine])
            yv[g, mine] = value.astype(bf16)
            out = pltpu.make_async_copy(yv.at[g, mine], y_ref.at[g, mine], ysem.at[slot, g])
            out.start()
            outs.append(out)

    pair = 2 * HEAD_DIM

    def one_pair(j, carry):
        lanes = pl.ds(pl.multiple_of(j * pair, pair), pair)
        attend_pair(seg, yv, lanes, p_ref[...], j, att_ref, lse_ref)
        return carry

    lax.fori_loop(0, width // pair, one_pair, 0)

    load_out.wait()
    for slot in (3, 2, 1, 0):
        shard = place ^ slot
        mine = pl.ds(pl.multiple_of(shard * rows, rows), rows)
        d = att_ref[mine]
        low = nt(d, oe_ref[...]).astype(bf16)
        lo_ref[mine] = low
        part[shard] = (nt(d, wo[...]) + nn(low, f_ref[0])).astype(bf16)
        if slot == 3:
            summed.begin(1, 0)
    for chunk in range(chunks):
        for step in (1, 2, 3):
            if chunk or step > 1:
                summed.begin(step, chunk)
    size = rows // chunks
    stores = []
    for chunk in range(chunks):
        summed.relay(2, chunk)
        summed.relay(3, chunk)
        summed.total(chunk, midv)
        here = chunk_rows(chunk, size)
        value = midv[here] + tok_ref[here].astype(f32)
        midv[here] = value
        rms = lax.rsqrt(jnp.mean(value * value, axis=1, keepdims=True) + eps)
        own[here] = (value * rms * gain_ref[...].astype(f32)).astype(bf16)
        stores.append(pltpu.make_async_copy(own.at[here], n_ref.at[place, here], nsem.at[chunk]))
        stores.append(pltpu.make_async_copy(midv.at[here], mid_ref.at[here], msem.at[chunk]))
        gather.send(1, chunk, least=1)
        for store in stores[-2:]:
            store.start()
        if chunk:
            gather.relay(2, chunk - 1, least=2)
    for chunk in range(chunks):
        gather.send(1, chunk, most=0)
    gather.relay(2, chunks - 1, least=2)
    for chunk in range(chunks):
        gather.relay(2, chunk, most=1)
        if chunk:
            gather.relay(3, chunk - 1)
    gather.relay(3, chunks - 1)
    for chunk in range(chunks):
        cots.arrive(1, chunk)
    gather.close()
    pl.when(edge)(kept.wait)
    for out in outs + stores:
        out.wait()
    for side in SIDES:
        pl.when(far_of(place, side) == LINE - 2)(passed(side).wait_send)
    summed.drain()
    gather.drain()
    cots.drain(stop=2)


def front(x, weight, cot, entries, exits, tables, leaf_parent, out_entry, finals, tokens, gain, seg, chunks=5):
    _, rows, features = x.shape
    groups, rank, width = exits.shape
    total = LINE * rows
    shards = jax.ShapeDtypeStruct((LINE, rows, features), bf16)
    return pl.pallas_call(
        functools.partial(front_body, chunks, seg),
        in_specs=[IN_HBM] * 3 + [IN_VMEM] * 9,
        out_specs=[IN_HBM] * 5 + [IN_VMEM] * 4,
        out_shape=[
            shards,
            jax.ShapeDtypeStruct((groups, total, width), bf16),
            jax.ShapeDtypeStruct((rows, features), f32),
            shards,
            shards,
            jax.ShapeDtypeStruct((total, groups * rank), bf16),
            jax.ShapeDtypeStruct((total, width), bf16),
            jax.ShapeDtypeStruct((width // (2 * HEAD_DIM), 2, total), f32),
            jax.ShapeDtypeStruct((total, rank), bf16),
        ],
        scratch_shapes=[
            pltpu.VMEM((LINE, rows, features), bf16),
            pltpu.VMEM((groups, total, width), bf16),
            pltpu.VMEM((features, groups * width), bf16),
            pltpu.VMEM((features, width), bf16),
            pltpu.VMEM((LINE, rows, features), bf16),
            pltpu.VMEM((2, LINE - 1, rows, features), bf16),
            pltpu.VMEM((rows, features), bf16),
            pltpu.VMEM((rows, features), f32),
            pltpu.SemaphoreType.DMA((LINE,)),
            pltpu.SemaphoreType.DMA((2,)),
            pltpu.SemaphoreType.DMA((LINE, groups)),
            pltpu.SemaphoreType.DMA((chunks,)),
            pltpu.SemaphoreType.DMA((chunks,)),
            pltpu.SemaphoreType.DMA((2,)),
            pltpu.SemaphoreType.DMA((2,)),
        ]
        + line_sems(chunks)
        + line_sems(chunks)
        + line_sems(chunks),
        input_output_aliases={0: 0},
        compiler_params=comm_params(1),
    )(x, weight, cot, entries, exits, *tables, leaf_parent, out_entry, finals, tokens, gain[None, :])


class Trees:
    def __init__(self, tree, ref, send, recv):
        self.tree, self.ref, self.sems = tree, ref, (send, recv)
        self.rounds = ref.shape[0].bit_length() - 1
        self.partners = [self.partner(number) for number in range(self.rounds)]

    def partner(self, number):
        size = 1 << number
        return self.tree + size - 2 * size * ((self.tree // size) % 2)

    def copy(self, number, owner):
        size = 1 << number
        here = pl.ds((owner // size) * size, size)
        return pltpu.make_async_remote_copy(
            src_ref=self.ref.at[here],
            dst_ref=self.ref.at[here],
            send_sem=self.sems[0].at[number],
            recv_sem=self.sems[1].at[number],
            device_id={"dp": self.partner(number)},
            device_id_type=MESH,
        )

    def send(self, number):
        self.copy(number, self.tree).start()

    def arrive(self, number):
        self.copy(number, self.partner(number)).wait_recv()

    def advance(self, number):
        if number < self.rounds:
            self.arrive(number - 1)
            self.send(number)

    def drain(self):
        for number in range(self.rounds):
            self.copy(number, self.tree).wait_send()


def back_body(
    chunks, seg,
    q_ref, w_ref, n_ref, mid_ref, middle_ref, res_ref, right_ref, left_ref, x_ref,
    o_ref, g_ref, lse_ref, p_ref, cos_ref, sin_ref, a_ref, e_ref, gain_ref, lone_ref, final_ref, exit_ref,
    out_ref, model_ref, head_ref, sum_ref,
    qv, dv, dq_t, dk_sum, dv_sum, part, held, acc, wv, midv, nv, terms, xv, outv, resv, model, head, low, block, extra,
    qsem, wsem, osem, e_send, e_recv, send, recv, x_send, x_recv, t_send, t_recv, h_send, h_recv,
):
    place = lax.axis_index("tensor")
    tree = lax.axis_index("dp")
    trees = Trees(tree, model_ref, t_send, t_recv)
    heads = Trees(tree, head_ref, h_send, h_recv)
    groups, total, width = q_ref.shape
    rank = a_ref.shape[1]
    (load_q,) = fetch([(q_ref, qv)], qsem)
    loads = fetch(
        [
            (w_ref.at[:, : groups * width], wv),
            (n_ref, nv),
            (mid_ref, midv),
            (middle_ref, acc),
            (res_ref.at[place], terms.at[0]),
            (x_ref, xv),
        ],
        wsem,
    )
    block[...] = jnp.zeros_like(block)
    for g in range(groups):
        block[g * rank : (g + 1) * rank, g * width : (g + 1) * width] = a_ref[g]
    greet(place, trees.partners)

    def exchange(side, target):
        index = 0 if side == 1 else 1
        return pltpu.make_async_remote_copy(
            src_ref=(right_ref, left_ref)[index],
            dst_ref=terms.at[index + 1],
            send_sem=e_send.at[index],
            recv_sem=e_recv.at[index],
            device_id={"tensor": target},
            device_id_type=MESH,
        )

    for side in SIDES:
        pl.when(far_of(place, side) < LINE - 1)(exchange(side, place + side).start)
    load_q.wait()
    pair = 2 * HEAD_DIM

    def one_pair(j, carry):
        lanes = pl.ds(pl.multiple_of(j * pair, pair), pair)
        attend_back_pair(
            seg, qv, lanes, o_ref, g_ref, lse_ref, j, p_ref[...], cos_ref, sin_ref, dv, dq_t, dk_sum, dv_sum
        )
        return carry

    lax.fori_loop(0, width // pair, one_pair, 0)
    loads[0].wait()
    rows = part.shape[1]
    summed = Sum(place, part, held, send, recv, chunks)
    gather = Gather(place, extra, x_send, x_recv, 1)
    entry = e_ref[:groups].reshape(groups * rank, -1)

    def rows_of(slot):
        shard = place ^ slot
        mine = pl.ds(pl.multiple_of(shard * rows, rows), rows)
        return shard, mine, jnp.concatenate([dv[g, mine] for g in range(groups)], axis=1)

    def lower(slot):
        _, mine, d = rows_of(slot)
        low[mine] = nt(d, block[...]).astype(bf16)

    def partial(slot):
        shard, mine, d = rows_of(slot)
        part[shard] = (nt(d, wv[...]) + nn(low[mine], entry)).astype(bf16)

    lower(3)
    partial(3)
    summed.begin(1, 0)
    summed.begin(1, 1)
    for slot in (2, 1, 0):
        lower(slot)
    for load in loads[1:]:
        load.wait()

    def turned(value):
        return value.astype(f32).T.astype(bf16)

    joined = nn(turned(low[...]), nv[...].reshape(total, -1))
    extra[place] = jnp.concatenate([joined, final_ref[...]], axis=0).astype(bf16)
    gather.send(1, 0)
    for chunk in range(2, chunks):
        summed.begin(1, chunk)
    for slot in (2, 1, 0):
        partial(slot)
    for step in (2, 3):
        for chunk in range(chunks):
            summed.begin(step, chunk)
    summed.relay(2, 0)
    summed.relay(2, 1)
    gather.arrive(1, 0)
    gather.send(2, 0)
    summed.relay(2, 2)
    low_one = turned(lone_ref[...])
    for g in range(groups):
        band = slice(g * rank, (g + 1) * rank)
        head[band] = nn(low_one[band], dv[g]).astype(bf16)
    head[groups * rank :] = exit_ref[...].astype(bf16)
    (store,) = fetch([(head, head_ref.at[tree])], osem)
    summed.relay(2, 3)
    store.wait()
    heads.send(0)
    gather.arrive(2, 0)
    gather.send(3, 0)
    heads.advance(1)
    summed.relay(3, 0)
    gather.arrive(3, 0)
    model[...] = functools.reduce(
        jnp.add, [extra[shard].astype(f32) for shard in range(LINE)]
    ).astype(bf16)
    (store,) = fetch([(model, model_ref.at[tree])], osem)
    for side in SIDES:
        pl.when(far_of(place, side) > 0)(exchange(side, place - side).wait_recv)
    value = acc[...] + terms[0].astype(f32)
    for index, side in enumerate(SIDES):
        value += jnp.where(far_of(place, side) > 0, terms[index + 1].astype(f32), 0.0)
    resv[...] = value.astype(bf16)
    store.wait()
    trees.send(0)
    (store,) = fetch([(resv, sum_ref)], osem)
    heads.advance(2)
    summed.relay(3, 1)
    trees.advance(1)
    summed.relay(3, 2)
    summed.relay(3, 3)
    trees.advance(2)
    store.wait()
    size = rows // chunks
    stores = []

    def finish(chunk):
        summed.total(chunk, acc)
        here = chunk_rows(chunk, size)
        values = xv[here].astype(f32)
        rms = lax.rsqrt(jnp.mean(values * values, axis=1, keepdims=True) + eps)
        scaled = acc[here] * gain_ref[...].astype(f32)
        mean = jnp.mean(scaled * values, axis=1, keepdims=True)
        outv[here] = (midv[here] + rms * (scaled - values * (rms * rms) * mean)).astype(bf16)
        copy = pltpu.make_async_copy(outv.at[here], out_ref.at[here], wsem.at[chunk])
        copy.start()
        stores.append(copy)

    finish(0)
    finish(1)
    for number in range(3, trees.rounds):
        trees.advance(number)
        heads.advance(number)
    finish(2)
    finish(3)
    for blocks in (trees, heads):
        blocks.arrive(blocks.rounds - 1)
        blocks.drain()
    for copy in stores:
        copy.wait()
    for side in SIDES:
        pl.when(far_of(place, side) < LINE - 1)(exchange(side, place + side).wait_send)
    summed.drain()
    gather.drain()


def back(
    qkv, weight, normed, grad_middle, middle, res_parts, right, left, x, attended, grad, lse, leaf_parent, tables, exits,
    entries, gain, low_one, final_grads, exit_grads, seg,
):
    chunks = LINE
    rows, features = x.shape
    groups, total, width = qkv.shape
    rank = exits.shape[1]
    deep = (groups + 1) * rank
    pair = 2 * HEAD_DIM
    trees = lax.axis_size("dp")
    sems = pltpu.SemaphoreType.DMA((trees.bit_length() - 1,))
    two = pltpu.SemaphoreType.DMA((2,))
    return pl.pallas_call(
        functools.partial(back_body, chunks, seg),
        in_specs=[IN_HBM] * 9 + [IN_VMEM] * 12,
        out_specs=[IN_HBM] * 4,
        out_shape=[
            jax.ShapeDtypeStruct((rows, features), bf16),
            jax.ShapeDtypeStruct((trees, deep, features), bf16),
            jax.ShapeDtypeStruct((trees, deep, width), bf16),
            jax.ShapeDtypeStruct((rows, features), bf16),
        ],
        scratch_shapes=[
            pltpu.VMEM((groups, total, width), bf16),
            pltpu.VMEM((groups, total, width), bf16),
            pltpu.VMEM((pair, total), f32),
            pltpu.VMEM((total, pair), f32),
            pltpu.VMEM((total, pair), f32),
            pltpu.VMEM((LINE, rows, features), bf16),
            pltpu.VMEM((2, LINE - 1, rows, features), bf16),
            pltpu.VMEM((rows, features), f32),
            pltpu.VMEM((features, groups * width), bf16),
            pltpu.VMEM((rows, features), f32),
            pltpu.VMEM((LINE, rows, features), bf16),
            pltpu.VMEM((3, rows, features), bf16),
            pltpu.VMEM((rows, features), bf16),
            pltpu.VMEM((rows, features), bf16),
            pltpu.VMEM((rows, features), bf16),
            pltpu.VMEM((deep, features), bf16),
            pltpu.VMEM((deep, width), bf16),
            pltpu.VMEM((total, groups * rank), bf16),
            pltpu.VMEM((groups * rank, groups * width), bf16),
            pltpu.VMEM((LINE, deep, features), bf16),
            pltpu.SemaphoreType.DMA((1,)),
            pltpu.SemaphoreType.DMA((6,)),
            pltpu.SemaphoreType.DMA((1,)),
            two,
            two,
        ]
        + line_sems(chunks)
        + line_sems(1)
        + [sems] * 4,
        compiler_params=comm_params(3),
    )(
        qkv, weight, normed, grad_middle, middle, res_parts, right, left, x, attended, grad[0], lse, leaf_parent, *tables,
        exits, entries, gain[None, :], low_one, final_grads, exit_grads,
    )


def tree_tiles(seg, rows, parent_row):
    trunk = TRUNK * seg
    leaves = trunk + BRANCHES * seg
    key = lax.broadcasted_iota(jnp.int32, (QT, QT), 0)
    query = lax.broadcasted_iota(jnp.int32, (QT, QT), 1)
    causal = key <= query
    own = causal & (key // seg == query // seg)
    tiles = []
    for start in range(0, trunk, QT):
        pieces = [(0, start, None)] if start else []
        tiles.append((start, pieces + [(start, QT, causal)]))
    tiles.append((trunk, [(0, trunk, None), (trunk, QT, own)]))
    branch = lax.broadcasted_iota(jnp.int32, (BRANCHES * seg, QT), 0) // seg
    for start in range(leaves, rows, QT):
        mine = branch == parent_row[:, start - leaves : start - leaves + QT]
        tiles.append(
            (start, [(0, trunk, None), (trunk, BRANCHES * seg, mine), (start, QT, own)])
        )
    return tiles


def attend_pair(seg, qkv_ref, lanes, parent_row, pair, o_ref, lse_ref):
    rows = qkv_ref.shape[1]
    value_t = qkv_ref[2, :, lanes].T
    lane = lax.broadcasted_iota(jnp.int32, (QT, 2 * HEAD_DIM), 1)
    for start, pieces in tree_tiles(seg, rows, parent_row):
        query = qkv_ref[0, start : start + QT, lanes] * bf16(HEAD_DIM**-0.5)
        outs = []
        for h in range(2):
            own_query = jnp.where(lane // HEAD_DIM == h, query, bf16(0))
            scores = []
            for k0, count, mask in pieces:
                s = nt(qkv_ref[1, k0 : k0 + count, lanes], own_query)
                scores.append(s if mask is None else jnp.where(mask, s, -1e30))
            top = functools.reduce(
                jnp.maximum, [jnp.max(s, axis=0, keepdims=True) for s in scores]
            )
            summed, out = 0.0, 0.0
            for (k0, count, _), s in zip(pieces, scores):
                weights = jnp.exp(s - top)
                summed += jnp.sum(weights, axis=0, keepdims=True)
                out += nn(
                    value_t[h * HEAD_DIM : (h + 1) * HEAD_DIM, k0 : k0 + count],
                    weights.astype(bf16),
                )
            outs.append(out / summed)
            lse_ref[pair, h : h + 1, start : start + QT] = top + jnp.log(summed)
        o_ref[start : start + QT, lanes] = jnp.concatenate(outs, axis=0).T.astype(bf16)


def attend_back_pair(
    seg, qkv_ref, lanes, o_ref, g_ref, lse_ref, pair, parent_row, cos_ref, sin_ref, d_ref, dq_t, dk, dv
):
    rows = qkv_ref.shape[1]
    scale = bf16(HEAD_DIM**-0.5)
    key_t = qkv_ref[1, :, lanes].T
    weighed_t = (g_ref[:, lanes].astype(f32) * o_ref[:, lanes].astype(f32)).T
    lane = lax.broadcasted_iota(jnp.int32, (QT, 2 * HEAD_DIM), 1)
    dk[...] = jnp.zeros_like(dk)
    dv[...] = jnp.zeros_like(dv)
    for start, pieces in tree_tiles(seg, rows, parent_row):
        query = qkv_ref[0, start : start + QT, lanes] * scale
        grad = g_ref[start : start + QT, lanes]
        for h in range(2):
            mine = lane // HEAD_DIM == h
            own_query = jnp.where(mine, query, bf16(0))
            own_grad = jnp.where(mine, grad, bf16(0))
            band = slice(h * HEAD_DIM, (h + 1) * HEAD_DIM)
            delta = jnp.sum(weighed_t[band, start : start + QT], axis=0, keepdims=True)
            lse = lse_ref[pair, h : h + 1, start : start + QT]
            grad_q = 0.0
            for k0, count, mask in pieces:
                probs = jnp.exp(nt(qkv_ref[1, k0 : k0 + count, lanes], own_query) - lse)
                if mask is not None:
                    probs = jnp.where(mask, probs, 0.0)
                grad_probs = nt(qkv_ref[2, k0 : k0 + count, lanes], own_grad)
                grad_scores = (probs * (grad_probs - delta)).astype(bf16)
                dk[k0 : k0 + count] += nn(grad_scores, own_query)
                dv[k0 : k0 + count] += nn(probs.astype(bf16), own_grad)
                grad_q += nn(key_t[band, k0 : k0 + count], grad_scores)
            dq_t[band, start : start + QT] = grad_q
    cosine, sine = cos_ref[...], -sin_ref[...]
    d_ref[0, :, lanes] = turn(dq_t[...].T * HEAD_DIM**-0.5, cosine, sine).astype(bf16)
    d_ref[1, :, lanes] = turn(dk[...], cosine, sine).astype(bf16)
    d_ref[2, :, lanes] = dv[...].astype(bf16)


def feed_body(
    rank, tile, chunks,
    n_ref, c_ref, near_ref, wg_ref, wu_ref, wd_ref, mid_ref, wo_ref,
    pick_ref, xu_in, xd_in, e_in, f_in, gain_ref, oe_ref, att_ref, lo_ref,
    grad_ref, res_ref, right_ref, left_ref, b_ref, held_ref, far_ref, unit_out, model_out, y_ref, final_ref, exit_ref,
    unit_ref, model_ref, x_ref, e_ref, f_ref, midv, nbuf, cbuf, wbuf, low, low_t, acc_res, acc_back, acc_low,
    part, held, resv, own, extra, wo, nsem, csem, wsem, rsem, msem,
    send, recv, g_send, g_recv, x_send, x_recv, c_send, c_recv, r_send, r_recv,
):
    place = lax.axis_index("tensor")
    units = unit_ref.shape[1]
    tiles = units // tile
    rows = part.shape[1]
    summed = Near(place, part, held, send, recv, chunks)
    cots = Gather(place, far_ref, c_send, c_recv, 1, second=near_ref)
    inside = ((place + 1) // 2) % 2
    gather = Gather(place, b_ref, g_send, g_recv, chunks, own)
    joint = Gather(place, extra, x_send, x_recv, 1)

    def load_rows(order, act):
        into = order % 2
        shard = place ^ ((order + 1) % LINE)
        act(pltpu.make_async_copy(n_ref.at[shard], nbuf.at[into], nsem.at[into]))

        def take(source):
            act(pltpu.make_async_copy(source, cbuf.at[into], csem.at[into]))

        beside = (order == 0) | ((order == 2) & (inside == 1))
        pl.when(order == LINE - 1)(lambda: take(c_ref))
        pl.when(beside)(lambda: take(near_ref.at[shard]))
        pl.when(jnp.logical_not(beside) & (order < LINE - 1))(lambda: take(far_ref.at[shard]))

    def load_weights(index, into, act):
        columns = pl.ds(pl.multiple_of(index * tile, tile), tile)
        for k, w_ref in enumerate((wg_ref, wu_ref, wd_ref)):
            act(pltpu.make_async_copy(w_ref.at[:, columns], wbuf.at[into, k], wsem.at[into, k]))

    def start(copy):
        copy.start()

    def wait(copy):
        copy.wait()

    during = ((1, (2,)), (1, range(3, chunks)), (2, (0,)), (2, (1,)))
    load_rows(jnp.int32(0), start)
    load_weights(0, 0, start)
    width = wo.shape[1]
    load_middle, load_out = fetch([(mid_ref, midv), (wo_ref.at[:, 3 * width :], wo)], msem)
    for padded in (x_ref, e_ref, f_ref):
        padded[...] = jnp.zeros_like(padded)
    x_ref[0, :rank] = xu_in[0]
    x_ref[1, rank : 2 * rank] = xu_in[1]
    x_ref[2, 2 * rank :] = xd_in[...]
    e_ref[: 2 * rank] = e_in[3:].reshape(2 * rank, -1)
    f_ref[2 * rank :] = f_in[1]
    unit_ref[...] = jnp.zeros_like(unit_ref)
    model_ref[...] = jnp.zeros_like(model_ref)
    greet(place)
    cots.send(2, 0)

    def one_shard(order, carry):
        into = order % 2
        shard = place ^ ((order + 1) % LINE)
        load_rows(order, wait)
        first = nt(nbuf[into], e_ref[...]) + nt(cbuf[into], f_ref[...])
        low[...] = first.astype(bf16)
        low_t[...] = first.T.astype(bf16)
        acc_res[...] = jnp.zeros_like(acc_res)
        acc_back[...] = jnp.zeros_like(acc_back)
        acc_low[...] = jnp.zeros_like(acc_low)

        def one_tile(index, carry):
            stage = order * tiles + index
            at = stage % 2
            load_weights(index, at, wait)

            @pl.when(stage < LINE * tiles - 1)
            def _():
                load_weights((index + 1) % tiles, 1 - at, start)

            columns = pl.ds(pl.multiple_of(index * tile, tile), tile)
            x_gate, x_rise, x_fall = x_ref[0, :, columns], x_ref[1, :, columns], x_ref[2, :, columns]
            gate = nn(nbuf[into], wbuf[at, 0]) + nn(low[...], x_gate)
            rise = nn(nbuf[into], wbuf[at, 1]) + nn(low[...], x_rise)
            grad_hidden = nn(cbuf[into], wbuf[at, 2]) + nn(low[...], x_fall)
            sigmoid = jax.nn.sigmoid(gate)
            silu = gate * sigmoid
            hidden = (silu * rise).astype(bf16)
            grad_gate = (grad_hidden * rise * sigmoid * (1.0 + gate * (1.0 - sigmoid))).astype(bf16)
            grad_rise = (grad_hidden * silu).astype(bf16)
            acc_back[...] += nt(grad_gate, wbuf[at, 0]) + nt(grad_rise, wbuf[at, 1])
            acc_res[...] += nt(hidden, wbuf[at, 2])
            acc_low[...] += nt(grad_gate, x_gate) + nt(grad_rise, x_rise) + nt(hidden, x_fall)
            unit_ref[:rank, columns] += nn(low_t[:rank], grad_gate)
            unit_ref[rank : 2 * rank, columns] += nn(low_t[rank : 2 * rank], grad_rise)
            unit_ref[2 * rank :, columns] += nn(low_t[2 * rank : 3 * rank], hidden)
            for number, (away, part_chunks) in enumerate(during):

                @pl.when((order == LINE - 1) & (index == number))
                def _():
                    for chunk in part_chunks:
                        summed.send(away, chunk, 1)

            return carry

        lax.fori_loop(0, tiles, one_tile, 0)

        @pl.when(order == 0)
        def _():
            cots.relay(3, 0)
            cots.end_got(2)

        @pl.when(order == 1)
        def _():
            cots.end_got(3)

        @pl.when(order < LINE - 1)
        def _():
            load_rows(order + 1, start)

        joined = acc_low[...].astype(bf16)
        joined_t = acc_low[...].T.astype(bf16)
        part[shard] = (acc_back[...] + nn(joined, e_ref[...])).astype(bf16)
        for away in (1, 2, 3):

            @pl.when(order == away - 1)
            def _():
                for chunk in range(chunks):
                    summed.send(away, chunk, 0)
                if away == 3:
                    summed.send(1, 0, 1)
                    summed.send(1, 1, 1)

        @pl.when(order > 0)
        def _():
            pltpu.make_async_copy(resv, res_ref.at[shard], rsem.at[0]).wait()

        resv[...] = (acc_res[...] + nn(joined, f_ref[...])).astype(bf16)
        pltpu.make_async_copy(resv, res_ref.at[shard], rsem.at[0]).start()
        model_ref[: 2 * rank] += nn(joined_t[: 2 * rank], nbuf[into])
        model_ref[2 * rank :] += nn(joined_t[2 * rank : 3 * rank], cbuf[into])
        return carry

    lax.fori_loop(0, LINE, one_shard, 0)
    def pass_on(side, step, source, target):
        index = 0 if side == 1 else 1
        return pltpu.make_async_remote_copy(
            src_ref=source,
            dst_ref=held_ref.at[index, step - 1],
            send_sem=r_send.at[index, step - 1],
            recv_sem=r_recv.at[index, step - 1],
            device_id={"tensor": target},
            device_id_type=MESH,
        )

    def at_far(side, number, act):
        pl.when(far_of(place, side) == number)(act)

    def ready(side, step, shard):
        index = 0 if side == 1 else 1
        pass_on(side, step, resv, place - side).wait_recv()
        copies = [
            pltpu.make_async_copy(res_ref.at[shard], cbuf.at[0], csem.at[0]),
            pltpu.make_async_copy(held_ref.at[index, step - 1], cbuf.at[1], csem.at[1]),
        ]
        for copy in copies:
            copy.start()
        for copy in copies:
            copy.wait()
        cbuf[0] = (cbuf[0].astype(f32) + cbuf[1].astype(f32)).astype(bf16)

    def send_result(step):
        for side in SIDES:
            at_far(
                side,
                0,
                lambda: pass_on(side, step, res_ref.at[place + side * (LINE - step)], place + side).start(),
            )

    extra[place] = model_ref[...].astype(bf16)
    size = rows // chunks
    last = (LINE - 1) % 2
    load_middle.wait()
    send_result(1)

    def finish(chunk):
        summed.total(chunk, acc_back)
        here = chunk_rows(chunk, size)
        middle = midv[here]
        rms = lax.rsqrt(jnp.mean(middle * middle, axis=1, keepdims=True) + eps)
        scaled = acc_back[here] * gain_ref[...].astype(f32)
        mean = jnp.mean(scaled * middle, axis=1, keepdims=True)
        grad = cbuf[last, here].astype(f32) + rms * (scaled - middle * (rms * rms) * mean)
        own[here] = grad.astype(bf16)
        midv[here] = grad

    @pl.when(inside == 1)
    def _():
        for chunk in range(chunks):
            finish(chunk)
            gather.send(1, chunk, least=2)

    joint.send(1, 0)
    for chunk in range(2, chunks):
        summed.send(2, chunk, 1)
    for chunk in range(chunks):
        summed.send(1, chunk, 2)
    for chunk in range(chunks):
        gather.send(1, chunk, least=1, most=1)

    @pl.when(inside == 0)
    def _():
        for chunk in range(chunks):
            finish(chunk)
            gather.send(1, chunk)

    send_result(2)
    (store,) = fetch([(midv, grad_ref)], msem)
    pltpu.make_async_copy(resv, res_ref.at[place], rsem.at[0]).wait()

    load_out.wait()

    def through(number, rows_ref, shard):
        mine = pl.ds(pl.multiple_of(shard * rows, rows), rows)
        value = rows_ref[...]
        reduced = nt(value, f_in[0])
        y_ref[0, mine] = (nn(value, wo[...]) + nn(reduced.astype(bf16), oe_ref[...])).astype(bf16)
        final = nn(lo_ref[mine].astype(f32).T.astype(bf16), value)
        leave = nn(reduced.T.astype(bf16), att_ref[mine])
        final_ref[...] = final if number == 0 else final_ref[...] + final
        exit_ref[...] = leave if number == 0 else exit_ref[...] + leave

    def take(number, shard):
        copy = pltpu.make_async_copy(b_ref.at[shard], nbuf.at[number % 2], nsem.at[number % 2])
        copy.start()
        copy.wait()
        through(number, nbuf.at[number % 2], shard)

    joint.relay(2, 0)
    through(0, own, place)
    unit_out[: 3 * rank] = unit_ref[...].astype(bf16)
    unit_out[3 * rank :] = jnp.full((rank, units), pick_ref[0, 0], f32).astype(bf16)
    for chunk in range(chunks):
        gather.relay(2, chunk, least=2)
    gather.end_got(1)
    joint.relay(3, 0)
    take(1, place ^ (1 + 2 * inside))
    for chunk in range(chunks):
        gather.relay(2, chunk, most=1)
        if chunk:
            gather.relay(3, chunk - 1)
    gather.relay(3, chunks - 1)
    for side in SIDES:

        @pl.when(far_of(place, side) == 1)
        def _():
            ready(side, 1, place + side * 2)
            resv[...] = cbuf[0]
            pass_on(side, 2, resv, place + side).start()

    gather.end_got(2)
    take(2, place ^ (2 - inside))
    joint.close()
    model_out[...] = functools.reduce(
        jnp.add, [extra[shard].astype(f32) for shard in range(LINE)]
    ).astype(bf16)
    gather.end_got(3)
    take(3, place ^ (3 - inside))
    for index, side in enumerate(SIDES):
        target = (right_ref, left_ref)[index]

        @pl.when(far_of(place, side) == 0)
        def _():
            copy = pltpu.make_async_copy(res_ref.at[place + side], nbuf.at[index], nsem.at[index])
            copy.start()
            copy.wait()

        @pl.when((far_of(place, side) > 0) & (far_of(place, side) < LINE - 1))
        def _():
            ready(side, 2, place + side)
            nbuf[index] = cbuf[0]

        copy = pltpu.make_async_copy(nbuf.at[index], target, nsem.at[index])
        copy.start()
        copy.wait()
    for side in SIDES:
        for step in (1, 2):
            at_far(
                side,
                0,
                lambda: pass_on(side, step, res_ref.at[place + side * (LINE - step)], place + side).wait_send(),
            )
        at_far(side, 1, lambda: pass_on(side, 2, resv, place + side).wait_send())
    summed.drain()
    gather.drain()
    joint.drain()
    cots.drain(start=2)
    store.wait()


def feed(
    normed, cots, weights, middle, w_heads, pick, units_exit, fall_entry, entries, finals, gain, out_entry,
    attended, low_out, tile=512, chunks=5,
):
    _, rows, features = normed.shape
    units = weights[0].shape[1]
    rank, width = out_entry.shape
    total = LINE * rows
    one = jax.ShapeDtypeStruct((rows, features), bf16)
    return pl.pallas_call(
        functools.partial(feed_body, rank, tile, chunks),
        in_specs=[IN_HBM] * 8 + [pl.BlockSpec(memory_space=pltpu.SMEM)] + [IN_VMEM] * 8,
        out_specs=[IN_HBM] * 7 + [IN_VMEM] * 5,
        out_shape=[
            jax.ShapeDtypeStruct((rows, features), f32),
            jax.ShapeDtypeStruct((LINE, rows, features), bf16),
            one,
            one,
            jax.ShapeDtypeStruct((LINE, rows, features), bf16),
            jax.ShapeDtypeStruct((2, LINE - 2, rows, features), bf16),
            jax.ShapeDtypeStruct((LINE, rows, features), bf16),
            jax.ShapeDtypeStruct((4 * rank, units), bf16),
            jax.ShapeDtypeStruct((3 * rank, features), bf16),
            jax.ShapeDtypeStruct((1, total, width), bf16),
            jax.ShapeDtypeStruct((rank, features), f32),
            jax.ShapeDtypeStruct((rank, width), f32),
        ],
        scratch_shapes=[
            pltpu.VMEM((3 * rank, units), f32),
            pltpu.VMEM((3 * rank, features), f32),
            pltpu.VMEM((3, 3 * rank, units), bf16),
            pltpu.VMEM((3 * rank, features), bf16),
            pltpu.VMEM((3 * rank, features), bf16),
            pltpu.VMEM((rows, features), f32),
            pltpu.VMEM((2, rows, features), bf16),
            pltpu.VMEM((2, rows, features), bf16),
            pltpu.VMEM((2, 3, features, tile), bf16),
            pltpu.VMEM((rows, 3 * rank), bf16),
            pltpu.VMEM((3 * rank, rows), bf16),
            pltpu.VMEM((rows, features), f32),
            pltpu.VMEM((rows, features), f32),
            pltpu.VMEM((rows, 3 * rank), f32),
            pltpu.VMEM((LINE, rows, features), bf16),
            pltpu.VMEM((2, LINE - 1, rows, features), bf16),
            pltpu.VMEM((rows, features), bf16),
            pltpu.VMEM((rows, features), bf16),
            pltpu.VMEM((LINE, 3 * rank, features), bf16),
            pltpu.VMEM((features, width), bf16),
            pltpu.SemaphoreType.DMA((2,)),
            pltpu.SemaphoreType.DMA((2,)),
            pltpu.SemaphoreType.DMA((2, 3)),
            pltpu.SemaphoreType.DMA((1,)),
            pltpu.SemaphoreType.DMA((2,)),
        ]
        + line_sems(chunks)
        + line_sems(chunks)
        + line_sems(1)
        + line_sems(1)
        + [pltpu.SemaphoreType.DMA((2, LINE - 2))] * 2,
        compiler_params=comm_params(5),
    )(
        normed, *cots, *weights, middle, w_heads, pick, units_exit, fall_entry, entries, finals, gain[None, :], out_entry,
        attended, low_out,
    )


def pick_body(pick_ref, *refs):
    count = len(refs) // 2
    for source, target in zip(refs[:count], refs[count:]):
        target[...] = source[...].reshape(target.shape)


def picked(pick, arrays):
    shapes = [a.shape[:1] + a.shape[2:] for a in arrays]
    return pl.pallas_call(
        pick_body,
        grid_spec=pltpu.PrefetchScalarGridSpec(
            num_scalar_prefetch=1,
            grid=(1,),
            in_specs=[
                pl.BlockSpec(a.shape[:1] + (1,) + a.shape[2:], lambda i, p: (0, p[0], 0, 0)) for a in arrays
            ],
            out_specs=[pl.BlockSpec(shape, lambda i, p: (0, 0, 0)) for shape in shapes],
        ),
        out_shape=[jax.ShapeDtypeStruct(shape, bf16) for shape in shapes],
    )(pick, *arrays)


def per_tree(block):
    return lax.all_gather(block, "dp", axis=0, tiled=False)


def combine_body(
    rank, pick_ref, early, model, late, head, one, two, entry_ref, final_ref, unit_ref, down_ref, exit_ref, out_ref,
    one_ref, two_ref,
):
    one_ref[...] = one[...]
    two_ref[...] = two[...]
    for ref in (entry_ref, final_ref, unit_ref, down_ref, exit_ref, out_ref):
        ref[...] = jnp.zeros_like(ref)

    def one_tree(tree, carry):
        pick = pick_ref[tree]

        def block(ref, index):
            return ref[tree, index * rank : (index + 1) * rank].astype(f32)

        for k in range(3):
            entry_ref[k, pick] += block(late, k)
            exit_ref[k, pick] += block(head, k)
        final_ref[0, pick] += block(late, 3)
        out_ref[pick] += block(head, 3)
        for k in range(2):
            entry_ref[3 + k, pick] += block(model, k)
            unit_ref[k, pick] += block(early, k)
        final_ref[1, pick] += block(model, 2)
        down_ref[pick] += block(early, 2)
        return carry

    lax.fori_loop(0, early.shape[0], one_tree, 0)


def combine(picks, early, model, late, head, one, two, adapters, steps=4):
    trees, _, features = early.shape
    rank = late.shape[1] // 4
    width = head.shape[2]
    wide, narrow = features // steps, width // steps

    def taken(array, tile):
        return pl.BlockSpec((trees, array.shape[1], tile), lambda i, p: (0, 0, i))

    def given(lead, tile):
        shape = lead + (adapters, rank, tile)
        return pl.BlockSpec(shape, lambda i, p: (0,) * (len(shape) - 1) + (i,))

    whole = pl.BlockSpec((one.shape[0] // steps, one.shape[1]), lambda i, p: (i, 0))

    def shape(lead, full):
        return jax.ShapeDtypeStruct(lead + (adapters, rank, full), f32)

    return pl.pallas_call(
        functools.partial(combine_body, rank),
        grid_spec=pltpu.PrefetchScalarGridSpec(
            num_scalar_prefetch=1,
            grid=(steps,),
            in_specs=[taken(early, wide), taken(model, wide), taken(late, wide), taken(head, narrow), whole, whole],
            out_specs=[
                given((5,), wide),
                given((2,), wide),
                given((2,), wide),
                given((), wide),
                given((3,), narrow),
                given((), narrow),
                whole,
                whole,
            ],
        ),
        out_shape=[
            shape((5,), features),
            shape((2,), features),
            shape((2,), features),
            shape((), features),
            shape((3,), width),
            shape((), width),
            jax.ShapeDtypeStruct(one.shape, bf16),
            jax.ShapeDtypeStruct(two.shape, bf16),
        ],
        compiler_params=pltpu.CompilerParams(vmem_limit_bytes=VMEM_LIMIT),
    )(picks, early, model, late, head, one, two)


def local(
    tokens,
    cotangent,
    attention_gain,
    feed_gain,
    query_weight,
    key_weight,
    value_weight,
    output_weight,
    gate_weight,
    up_weight,
    down_weight,
    entry_maps,
    head_exits,
    unit_exits,
    output_entry,
    down_entry,
    final_exits,
    parents,
    adapter_pick,
):
    adapters, rank = entry_maps.shape[1], entry_maps.shape[3]
    local_rows = tokens.shape[0]
    total = local_rows * lax.axis_size("tensor")
    blocks = parents.shape[1]
    seg = total // blocks
    tables = rope_tables(blocks, seg)
    leaf_parent = (jnp.repeat(parents[0, TRUNK + BRANCHES :], seg) - TRUNK)[None, :]
    gain_one, gain_two = attention_gain, feed_gain

    w_heads = lax.all_gather(
        jnp.concatenate([query_weight, key_weight, value_weight, output_weight], axis=1),
        "dp",
        axis=0,
        tiled=True,
    )

    w_units = [
        lax.all_gather(w, "dp", axis=0, tiled=True) for w in (gate_weight, up_weight, down_weight)
    ]
    entries, heads_exit, units_exit, out_entry, fall_entry, finals = picked(
        adapter_pick,
        (
            jnp.swapaxes(entry_maps, 2, 3),
            head_exits,
            unit_exits,
            jnp.swapaxes(output_entry, 1, 2)[None],
            jnp.swapaxes(down_entry, 1, 2)[None],
            final_exits,
        ),
    )
    out_entry, fall_entry = out_entry[0], fall_entry[0]

    most_one = gather_norm(tokens, gain_one)
    full_one, qkv, middle, full_two, full_cot, low_one, attended, lse, adapt_o = front(
        most_one, w_heads, cotangent, entries, heads_exit, tables, leaf_parent, out_entry, finals, tokens, gain_two, seg
    )

    (
        grad_middle, res_parts, res_right, res_left, _, _, _, early, model_sum, grad_attended, final_grads, exit_grads,
    ) = feed(
        full_two, (cotangent, full_cot), w_units, middle, w_heads, adapter_pick.astype(f32)[None, :],
        units_exit, fall_entry, entries, finals, gain_two, out_entry, attended, adapt_o,
    )
    early = per_tree(early)
    model_all = per_tree(model_sum)

    grad_tokens, late_model, late_head, result = back(
        qkv, w_heads, full_one, grad_middle, middle, res_parts, res_right, res_left, tokens, attended, grad_attended, lse,
        leaf_parent, tables, heads_exit, entries, gain_one, low_one, final_grads, exit_grads, seg,
    )

    picks = early[:, 3 * rank, 0].astype(jnp.int32)
    grad_entries, grad_finals, grad_units, grad_down, grad_heads, grad_output, result, grad_tokens = combine(
        picks, early, model_all, late_model, late_head, result, grad_tokens, adapters
    )
    grad_entries = grad_entries.swapaxes(2, 3)
    grad_output = grad_output.swapaxes(1, 2)
    grad_down = grad_down.swapaxes(1, 2)
    return (
        result,
        grad_tokens,
        grad_entries,
        grad_heads,
        grad_units,
        grad_output,
        grad_down,
        grad_finals,
    )


def solution(mesh):
    in_specs = (
        P(("dp", "tensor"), None),
        P(("dp", "tensor"), None),
        P(),
        P(),
        P("dp", "tensor"),
        P("dp", "tensor"),
        P("dp", "tensor"),
        P("dp", "tensor"),
        P("dp", "tensor"),
        P("dp", "tensor"),
        P("dp", "tensor"),
        P(),
        P(None, None, None, "tensor"),
        P(None, None, None, "tensor"),
        P(None, "tensor", None),
        P(None, "tensor", None),
        P(),
        P("dp", None),
        P("dp"),
    )
    out_specs = (
        P(("dp", "tensor"), None),
        P(("dp", "tensor"), None),
        P(),
        P(None, None, None, "tensor"),
        P(None, None, None, "tensor"),
        P(None, "tensor", None),
        P(None, "tensor", None),
        P(),
    )
    return jax.shard_map(local, mesh=mesh, in_specs=in_specs, out_specs=out_specs, check_vma=False)
```

```python
import functools

import jax
import jax.numpy as jnp
import numpy as np
from jax import lax
from jax.experimental import pallas as pl
from jax.experimental.pallas import tpu as pltpu
from jax.sharding import PartitionSpec as P

HEAD_DIM = 64
TRUNK, BRANCHES = 8, 4
QT = 256
VMEM_LIMIT = 60 * 1024 * 1024
LINE = 4
MESH = pl.DeviceIdType.MESH

eps = 1e-05
theta = 130000.0
bf16, f32 = jnp.bfloat16, jnp.float32


def nn(left, right):
    return jnp.dot(left, right, preferred_element_type=f32)


def nt(left, right):
    return lax.dot_general(left, right, (((1,), (1,)), ((), ())), preferred_element_type=f32)


def tn(left, right):
    return lax.dot_general(left, right, (((0,), (0,)), ((), ())), preferred_element_type=f32)


def rope_tables(blocks, seg):
    depth = np.minimum(np.arange(blocks), TRUNK)
    depth[TRUNK + BRANCHES :] = TRUNK + 1
    position = (np.repeat(depth, seg) * seg + np.arange(blocks * seg) % seg).astype(np.float32)
    half = HEAD_DIM // 2
    freq = (np.float32(theta) ** (-np.arange(half, dtype=np.float32) / half)).astype(np.float32)
    angle = (position[:, None] * freq[None, :]).astype(np.float32)
    cosine = np.tile(np.cos(angle), (1, 4)).astype(np.float32)
    sine = np.sin(angle).astype(np.float32)
    sine = np.concatenate([-sine, sine, -sine, sine], axis=1)
    return jnp.asarray(cosine), jnp.asarray(sine)


def turn(values, cosine, sine):
    width = values.shape[1]
    reps = width // cosine.shape[1]
    if reps > 1:
        cosine = jnp.concatenate([cosine] * reps, axis=1)
        sine = jnp.concatenate([sine] * reps, axis=1)
    lane = lax.broadcasted_iota(jnp.int32, values.shape, 1)
    half = HEAD_DIM // 2
    other = jnp.where(
        lane % HEAD_DIM < half, pltpu.roll(values, width - half, 1), pltpu.roll(values, half, 1)
    )
    return values * cosine + other * sine


SIDES = (1, -1)


def far_of(place, side):
    return place if side == 1 else LINE - 1 - place


def greet(place, partners=()):
    barrier = pltpu.get_barrier_semaphore()
    for partner in partners:
        pl.semaphore_signal(barrier, inc=1, device_id={"dp": partner}, device_id_type=MESH)
    for side in SIDES:

        @pl.when(far_of(place, side) < LINE - 1)
        def _():
            pl.semaphore_signal(
                barrier, inc=1, device_id={"tensor": place + side}, device_id_type=MESH
            )

    edge = (place == 0) | (place == LINE - 1)

    @pl.when(edge)
    def _():
        pl.semaphore_wait(barrier, 1 + len(partners))

    @pl.when(jnp.logical_not(edge))
    def _():
        pl.semaphore_wait(barrier, 2 + len(partners))


def chunk_rows(chunk, rows):
    return pl.ds(chunk * rows, rows)


class Gather:
    def __init__(self, place, buf, send, recv, chunks, own=None, second=None):
        self.place, self.buf, self.sems, self.chunks = place, buf, (send, recv), chunks
        self.rows = buf.shape[1] // chunks
        self.own, self.second = own, second

    def copy(self, side, step, chunk, shard, target):
        rows = chunk_rows(chunk, self.rows)
        where = self.buf.at[shard, rows]
        index = 0 if side == 1 else 1
        spot = (index, step - 1, chunk)
        source = where
        if step == 1 and self.own is not None:
            source = self.own.at[rows]
        if step == 2 and self.second is not None:
            source = self.second.at[shard, rows]
        return pltpu.make_async_remote_copy(
            src_ref=source,
            dst_ref=where,
            send_sem=self.sems[0].at[spot],
            recv_sem=self.sems[1].at[spot],
            device_id={"tensor": target},
            device_id_type=MESH,
        )

    def each_send(self, step, chunk, act, least=0, most=LINE):
        for side in SIDES:
            far = far_of(self.place, side)

            @pl.when((far < LINE - 1) & (far >= step - 1) & (far >= least) & (far <= most))
            def _():
                shard = self.place - side * (step - 1)
                act(self.copy(side, step, chunk, shard, self.place + side))

    def send(self, step, chunk, least=0, most=LINE):
        self.each_send(step, chunk, lambda copy: copy.start(), least, most)

    def arrive(self, step, chunk):
        for side in SIDES:

            @pl.when(far_of(self.place, side) >= step)
            def _():
                shard = self.place - side * step
                self.copy(side, step, chunk, shard, self.place - side).wait_recv()

    def relay(self, step, chunk, least=0, most=LINE):
        for side in SIDES:
            far = far_of(self.place, side)

            @pl.when((far < LINE - 1) & (far >= step - 1) & (far >= least) & (far <= most))
            def _():
                before = self.place - side * (step - 1)
                self.copy(side, step - 1, chunk, before, self.place - side).wait_recv()
                self.copy(side, step, chunk, before, self.place + side).start()

    def close(self):
        for side in SIDES:

            @pl.when(far_of(self.place, side) == LINE - 1)
            def _():
                for step in range(1, LINE):
                    for chunk in range(self.chunks):
                        shard = self.place - side * step
                        self.copy(side, step, chunk, shard, self.place - side).wait_recv()

    def end_got(self, step):
        for side in SIDES:

            @pl.when(far_of(self.place, side) == LINE - 1)
            def _():
                for chunk in range(self.chunks):
                    self.copy(side, step, chunk, self.place - side * step, self.place - side).wait_recv()

    def drain(self, stop=LINE, start=1):
        for step in range(start, stop):
            for chunk in range(self.chunks):
                self.each_send(step, chunk, lambda copy: copy.wait_send())


class Sum:
    def __init__(self, place, part, held, send, recv, chunks):
        self.place, self.part, self.held = place, part, held
        self.sems, self.chunks = (send, recv), chunks
        self.rows = part.shape[1] // chunks

    def copy(self, side, step, chunk, shard, target):
        rows = chunk_rows(chunk, self.rows)
        index = 0 if side == 1 else 1
        spot = (index, step - 1, chunk)
        return pltpu.make_async_remote_copy(
            src_ref=self.part.at[shard, rows],
            dst_ref=self.held.at[index, step - 1, rows],
            send_sem=self.sems[0].at[spot],
            recv_sem=self.sems[1].at[spot],
            device_id={"tensor": target},
            device_id_type=MESH,
        )

    def add(self, step, chunk):
        rows = chunk_rows(chunk, self.rows)
        for index, side in enumerate(SIDES):
            far = far_of(self.place, side)
            shard = self.place + side * (LINE - step)

            @pl.when((far >= 1) & (far <= step - 1))
            def _():
                self.copy(side, step - 1, chunk, self.place, self.place - side).wait_recv()
                self.part[shard, rows] = (
                    self.part[shard, rows].astype(f32)
                    + self.held[index, step - 2, rows].astype(f32)
                ).astype(bf16)

    def send(self, step, chunk, least=0, most=LINE):
        if step > 1 and most > 0:
            self.add(step, chunk)
        for side in SIDES:
            far = far_of(self.place, side)
            shard = self.place + side * (LINE - step)

            @pl.when((far <= step - 1) & (far >= least) & (far <= most))
            def _():
                self.copy(side, step, chunk, shard, self.place + side).start()

    def begin(self, step, chunk):
        self.send(step, chunk, most=0)

    def relay(self, step, chunk):
        self.send(step, chunk, least=1)

    def total(self, chunk, out):
        rows = chunk_rows(chunk, self.rows)
        out[rows] = self.part[self.place, rows].astype(f32)
        for index, side in enumerate(SIDES):

            @pl.when(far_of(self.place, side) >= 1)
            def _():
                self.copy(side, LINE - 1, chunk, self.place, self.place - side).wait_recv()
                out[rows] += self.held[index, LINE - 2, rows].astype(f32)

    def drain(self, stop=LINE):
        for step in range(1, stop):
            for chunk in range(self.chunks):
                for side in SIDES:
                    far = far_of(self.place, side)
                    shard = self.place + side * (LINE - step)

                    @pl.when(far <= step - 1)
                    def _():
                        self.copy(side, step, chunk, shard, self.place + side).wait_send()


class Near:
    def __init__(self, place, part, held, send, recv, chunks):
        self.place, self.part, self.held = place, part, held
        self.sems, self.chunks = (send, recv), chunks
        self.rows = part.shape[1] // chunks

    def copy(self, side, away, chunk, shard, target):
        rows = chunk_rows(chunk, self.rows)
        index = 0 if side == 1 else 1
        spot = (index, away - 1, chunk)
        return pltpu.make_async_remote_copy(
            src_ref=self.part.at[shard, rows],
            dst_ref=self.held.at[index, away - 1, rows],
            send_sem=self.sems[0].at[spot],
            recv_sem=self.sems[1].at[spot],
            device_id={"tensor": target},
            device_id_type=MESH,
        )

    def send(self, away, chunk, number):
        rows = chunk_rows(chunk, self.rows)
        for index, side in enumerate(SIDES):
            shard = self.place + side * away

            @pl.when(far_of(self.place, side) == number)
            def _():
                if number:
                    self.copy(side, away + 1, chunk, self.place, self.place - side).wait_recv()
                    self.part[shard, rows] = (
                        self.part[shard, rows].astype(f32) + self.held[index, away, rows].astype(f32)
                    ).astype(bf16)
                self.copy(side, away, chunk, shard, self.place + side).start()

    def total(self, chunk, out):
        rows = chunk_rows(chunk, self.rows)
        out[rows] = self.part[self.place, rows].astype(f32)
        for index, side in enumerate(SIDES):

            @pl.when(far_of(self.place, side) >= 1)
            def _():
                self.copy(side, 1, chunk, self.place, self.place - side).wait_recv()
                out[rows] += self.held[index, 0, rows].astype(f32)

    def drain(self):
        for number in range(LINE - 1):
            for away in range(1, LINE - number):
                for chunk in range(self.chunks):
                    for side in SIDES:

                        @pl.when(far_of(self.place, side) == number)
                        def _():
                            shard = self.place + side * away
                            self.copy(side, away, chunk, shard, self.place + side).wait_send()


def line_sems(chunks):
    return [pltpu.SemaphoreType.DMA((2, LINE - 1, chunks))] * 2


def fetch(pairs, sems):
    copies = [pltpu.make_async_copy(src, dst, sems.at[i]) for i, (src, dst) in enumerate(pairs)]
    for copy in copies:
        copy.start()
    return copies


IN_VMEM = pl.BlockSpec(memory_space=pltpu.VMEM)
IN_HBM = pl.BlockSpec(memory_space=pl.ANY)


def comm_params(number):
    return pltpu.CompilerParams(
        vmem_limit_bytes=VMEM_LIMIT, collective_id=number, has_side_effects=True
    )


def gather_norm_body(chunks, x_ref, gain_ref, buf, own, sem, send, recv):
    place = lax.axis_index("tensor")
    greet(place)
    rows = x_ref[...].astype(f32)
    rms = lax.rsqrt(jnp.mean(rows * rows, axis=1, keepdims=True) + eps)
    own[...] = (rows * rms * gain_ref[...].astype(f32)).astype(bf16)
    gather = Gather(place, buf, send, recv, chunks, own)
    for chunk in range(chunks):
        gather.send(1, chunk)
    (kept,) = fetch([(own, buf.at[place])], sem)
    for chunk in range(chunks):
        gather.arrive(1, chunk)
        gather.send(2, chunk)
    kept.wait()
    for chunk in range(chunks):
        gather.arrive(2, chunk)
    gather.drain(stop=LINE - 1)


def gather_norm(x, gain, chunks=5):
    rows, features = x.shape
    return pl.pallas_call(
        functools.partial(gather_norm_body, chunks),
        in_specs=[IN_VMEM, IN_VMEM],
        out_specs=IN_HBM,
        out_shape=jax.ShapeDtypeStruct((LINE, rows, features), bf16),
        scratch_shapes=[pltpu.VMEM((rows, features), bf16), pltpu.SemaphoreType.DMA((1,))]
        + line_sems(chunks),
        compiler_params=comm_params(0),
    )(x, gain[None, :])


def front_body(
    chunks, seg,
    x_ref, w_ref, c_ref, e_ref, a_ref, cos_ref, sin_ref, p_ref, oe_ref, f_ref, tok_ref, gain_ref,
    kept_ref, y_ref, mid_ref, n_ref, cot_ref, l_ref, att_ref, lse_ref, lo_ref,
    buf, yv, wv, wo, part, held, own, midv, xsem, wsem, ysem, nsem, msem, send, recv,
    s_send, s_recv, g_send, g_recv, c_send, c_recv,
):
    place = lax.axis_index("tensor")
    groups, total, width = y_ref.shape
    rows, rank = x_ref.shape[1], a_ref.shape[1]
    edge = (place == 0) | (place == LINE - 1)
    last = place ^ (LINE - 1)

    def passed(side):
        shard = place - side * (LINE - 2)
        index = 0 if side == 1 else 1
        return pltpu.make_async_remote_copy(
            src_ref=x_ref.at[shard],
            dst_ref=buf.at[shard],
            send_sem=send.at[index],
            recv_sem=recv.at[index],
            device_id={"tensor": place + side},
            device_id_type=MESH,
        )

    def came(side):
        index = 0 if side == 1 else 1
        return pltpu.make_async_remote_copy(
            src_ref=x_ref.at[last],
            dst_ref=buf.at[last],
            send_sem=send.at[index],
            recv_sem=recv.at[index],
            device_id={"tensor": place - side},
            device_id_type=MESH,
        )

    copies = []
    for slot in range(LINE):
        copy = pltpu.make_async_copy(x_ref.at[place ^ slot], buf.at[place ^ slot], xsem.at[slot])
        if slot < LINE - 1:
            copy.start()
        else:
            pl.when(jnp.logical_not(edge))(copy.start)
        copies.append(copy)
    load, load_out = fetch(
        [(w_ref.at[:, : groups * width], wv), (w_ref.at[:, groups * width :], wo)], wsem
    )
    greet(place)
    cots = Gather(place, cot_ref, c_send, c_recv, chunks, c_ref)
    summed = Sum(place, part, held, s_send, s_recv, chunks)
    gather = Gather(place, n_ref, g_send, g_recv, chunks, own)
    for side in SIDES:
        pl.when(far_of(place, side) == LINE - 2)(passed(side).start)
    for chunk in range(chunks):
        cots.send(1, chunk)

    for copy in copies[:-1]:
        copy.wait()
    load.wait()
    outs = []
    for slot in range(LINE):
        shard = place ^ slot
        if slot == LINE - 1:
            pl.when(jnp.logical_not(edge))(copies[slot].wait)
            for side in SIDES:
                pl.when(far_of(place, side) == LINE - 1)(came(side).wait_recv)
            kept = pltpu.make_async_copy(buf.at[last], kept_ref.at[last], xsem.at[slot])
            pl.when(edge)(kept.start)
        mine = pl.ds(pl.multiple_of(shard * rows, rows), rows)
        low = nt(buf[shard], e_ref[:groups].reshape(groups * rank, -1)).astype(bf16)
        l_ref[mine] = low
        for g in range(groups):
            band = slice(g * width, (g + 1) * width)
            value = nn(buf[shard], wv[:, band]) + nn(low[:, g * rank : (g + 1) * rank], a_ref[g])
            if g < groups - 1:
                value = turn(value, cos_ref[mine], sin_ref[mine])
            yv[g, mine] = value.astype(bf16)
            out = pltpu.make_async_copy(yv.at[g, mine], y_ref.at[g, mine], ysem.at[slot, g])
            out.start()
            outs.append(out)

    pair = 2 * HEAD_DIM

    def one_pair(j, carry):
        lanes = pl.ds(pl.multiple_of(j * pair, pair), pair)
        attend_pair(seg, yv, lanes, p_ref[...], j, att_ref, lse_ref)
        return carry

    lax.fori_loop(0, width // pair, one_pair, 0)

    load_out.wait()
    for slot in (3, 2, 1, 0):
        shard = place ^ slot
        mine = pl.ds(pl.multiple_of(shard * rows, rows), rows)
        d = att_ref[mine]
        low = nt(d, oe_ref[...]).astype(bf16)
        lo_ref[mine] = low
        part[shard] = (nt(d, wo[...]) + nn(low, f_ref[0])).astype(bf16)
        if slot == 3:
            summed.begin(1, 0)
    for chunk in range(chunks):
        for step in (1, 2, 3):
            if chunk or step > 1:
                summed.begin(step, chunk)
    size = rows // chunks
    stores = []
    for chunk in range(chunks):
        summed.relay(2, chunk)
        summed.relay(3, chunk)
        summed.total(chunk, midv)
        here = chunk_rows(chunk, size)
        value = midv[here] + tok_ref[here].astype(f32)
        midv[here] = value
        rms = lax.rsqrt(jnp.mean(value * value, axis=1, keepdims=True) + eps)
        own[here] = (value * rms * gain_ref[...].astype(f32)).astype(bf16)
        stores.append(pltpu.make_async_copy(own.at[here], n_ref.at[place, here], nsem.at[chunk]))
        stores.append(pltpu.make_async_copy(midv.at[here], mid_ref.at[here], msem.at[chunk]))
        gather.send(1, chunk, least=1)
        for store in stores[-2:]:
            store.start()
        if chunk:
            gather.relay(2, chunk - 1, least=2)
    for chunk in range(chunks):
        gather.send(1, chunk, most=0)
    gather.relay(2, chunks - 1, least=2)
    for chunk in range(chunks):
        gather.relay(2, chunk, most=1)
        if chunk:
            gather.relay(3, chunk - 1)
    gather.relay(3, chunks - 1)
    for chunk in range(chunks):
        cots.arrive(1, chunk)
    gather.close()
    pl.when(edge)(kept.wait)
    for out in outs + stores:
        out.wait()
    for side in SIDES:
        pl.when(far_of(place, side) == LINE - 2)(passed(side).wait_send)
    summed.drain()
    gather.drain()
    cots.drain(stop=2)


def front(x, weight, cot, entries, exits, tables, leaf_parent, out_entry, finals, tokens, gain, seg, chunks=5):
    _, rows, features = x.shape
    groups, rank, width = exits.shape
    total = LINE * rows
    shards = jax.ShapeDtypeStruct((LINE, rows, features), bf16)
    return pl.pallas_call(
        functools.partial(front_body, chunks, seg),
        in_specs=[IN_HBM] * 3 + [IN_VMEM] * 9,
        out_specs=[IN_HBM] * 5 + [IN_VMEM] * 4,
        out_shape=[
            shards,
            jax.ShapeDtypeStruct((groups, total, width), bf16),
            jax.ShapeDtypeStruct((rows, features), f32),
            shards,
            shards,
            jax.ShapeDtypeStruct((total, groups * rank), bf16),
            jax.ShapeDtypeStruct((total, width), bf16),
            jax.ShapeDtypeStruct((width // (2 * HEAD_DIM), 2, total), f32),
            jax.ShapeDtypeStruct((total, rank), bf16),
        ],
        scratch_shapes=[
            pltpu.VMEM((LINE, rows, features), bf16),
            pltpu.VMEM((groups, total, width), bf16),
            pltpu.VMEM((features, groups * width), bf16),
            pltpu.VMEM((features, width), bf16),
            pltpu.VMEM((LINE, rows, features), bf16),
            pltpu.VMEM((2, LINE - 1, rows, features), bf16),
            pltpu.VMEM((rows, features), bf16),
            pltpu.VMEM((rows, features), f32),
            pltpu.SemaphoreType.DMA((LINE,)),
            pltpu.SemaphoreType.DMA((2,)),
            pltpu.SemaphoreType.DMA((LINE, groups)),
            pltpu.SemaphoreType.DMA((chunks,)),
            pltpu.SemaphoreType.DMA((chunks,)),
            pltpu.SemaphoreType.DMA((2,)),
            pltpu.SemaphoreType.DMA((2,)),
        ]
        + line_sems(chunks)
        + line_sems(chunks)
        + line_sems(chunks),
        input_output_aliases={0: 0},
        compiler_params=comm_params(1),
    )(x, weight, cot, entries, exits, *tables, leaf_parent, out_entry, finals, tokens, gain[None, :])


class Trees:
    def __init__(self, tree, ref, send, recv):
        self.tree, self.ref, self.sems = tree, ref, (send, recv)
        self.rounds = ref.shape[0].bit_length() - 1
        self.partners = [self.partner(number) for number in range(self.rounds)]

    def partner(self, number):
        size = 1 << number
        return self.tree + size - 2 * size * ((self.tree // size) % 2)

    def copy(self, number, owner):
        size = 1 << number
        here = pl.ds((owner // size) * size, size)
        return pltpu.make_async_remote_copy(
            src_ref=self.ref.at[here],
            dst_ref=self.ref.at[here],
            send_sem=self.sems[0].at[number],
            recv_sem=self.sems[1].at[number],
            device_id={"dp": self.partner(number)},
            device_id_type=MESH,
        )

    def send(self, number):
        self.copy(number, self.tree).start()

    def arrive(self, number):
        self.copy(number, self.partner(number)).wait_recv()

    def advance(self, number):
        if number < self.rounds:
            self.arrive(number - 1)
            self.send(number)

    def drain(self):
        for number in range(self.rounds):
            self.copy(number, self.tree).wait_send()


def back_body(
    chunks, seg,
    q_ref, w_ref, n_ref, mid_ref, middle_ref, res_ref, right_ref, left_ref, x_ref,
    o_ref, g_ref, lse_ref, p_ref, cos_ref, sin_ref, a_ref, e_ref, gain_ref, lone_ref, final_ref, exit_ref,
    out_ref, model_ref, head_ref, sum_ref,
    qv, dv, dq_t, dk_sum, dv_sum, part, held, acc, wv, midv, nv, terms, xv, outv, resv, model, head, low, block, extra,
    qsem, wsem, osem, e_send, e_recv, send, recv, x_send, x_recv, t_send, t_recv, h_send, h_recv,
):
    place = lax.axis_index("tensor")
    tree = lax.axis_index("dp")
    trees = Trees(tree, model_ref, t_send, t_recv)
    heads = Trees(tree, head_ref, h_send, h_recv)
    groups, total, width = q_ref.shape
    rank = a_ref.shape[1]
    (load_q,) = fetch([(q_ref, qv)], qsem)
    loads = fetch(
        [
            (w_ref.at[:, : groups * width], wv),
            (n_ref, nv),
            (mid_ref, midv),
            (middle_ref, acc),
            (res_ref.at[place], terms.at[0]),
            (x_ref, xv),
        ],
        wsem,
    )
    block[...] = jnp.zeros_like(block)
    for g in range(groups):
        block[g * rank : (g + 1) * rank, g * width : (g + 1) * width] = a_ref[g]
    greet(place, trees.partners)

    def exchange(side, target):
        index = 0 if side == 1 else 1
        return pltpu.make_async_remote_copy(
            src_ref=(right_ref, left_ref)[index],
            dst_ref=terms.at[index + 1],
            send_sem=e_send.at[index],
            recv_sem=e_recv.at[index],
            device_id={"tensor": target},
            device_id_type=MESH,
        )

    for side in SIDES:
        pl.when(far_of(place, side) < LINE - 1)(exchange(side, place + side).start)
    load_q.wait()
    pair = 2 * HEAD_DIM

    def one_pair(j, carry):
        lanes = pl.ds(pl.multiple_of(j * pair, pair), pair)
        attend_back_pair(
            seg, qv, lanes, o_ref, g_ref, lse_ref, j, p_ref[...], cos_ref, sin_ref, dv, dq_t, dk_sum, dv_sum
        )
        return carry

    lax.fori_loop(0, width // pair, one_pair, 0)
    loads[0].wait()
    rows = part.shape[1]
    summed = Sum(place, part, held, send, recv, chunks)
    gather = Gather(place, extra, x_send, x_recv, 1)
    entry = e_ref[:groups].reshape(groups * rank, -1)

    def rows_of(slot):
        shard = place ^ slot
        mine = pl.ds(pl.multiple_of(shard * rows, rows), rows)
        return shard, mine, jnp.concatenate([dv[g, mine] for g in range(groups)], axis=1)

    def lower(slot):
        _, mine, d = rows_of(slot)
        low[mine] = nt(d, block[...]).astype(bf16)

    def partial(slot):
        shard, mine, d = rows_of(slot)
        part[shard] = (nt(d, wv[...]) + nn(low[mine], entry)).astype(bf16)

    lower(3)
    partial(3)
    summed.begin(1, 0)
    summed.begin(1, 1)
    for slot in (2, 1, 0):
        lower(slot)
    for load in loads[1:]:
        load.wait()

    def turned(value):
        return value.astype(f32).T.astype(bf16)

    joined = nn(turned(low[...]), nv[...].reshape(total, -1))
    extra[place] = jnp.concatenate([joined, final_ref[...]], axis=0).astype(bf16)
    gather.send(1, 0)
    for chunk in range(2, chunks):
        summed.begin(1, chunk)
    for slot in (2, 1, 0):
        partial(slot)
    for step in (2, 3):
        for chunk in range(chunks):
            summed.begin(step, chunk)
    summed.relay(2, 0)
    summed.relay(2, 1)
    gather.arrive(1, 0)
    gather.send(2, 0)
    summed.relay(2, 2)
    low_one = turned(lone_ref[...])
    for g in range(groups):
        band = slice(g * rank, (g + 1) * rank)
        head[band] = nn(low_one[band], dv[g]).astype(bf16)
    head[groups * rank :] = exit_ref[...].astype(bf16)
    (store,) = fetch([(head, head_ref.at[tree])], osem)
    summed.relay(2, 3)
    store.wait()
    heads.send(0)
    gather.arrive(2, 0)
    gather.send(3, 0)
    heads.advance(1)
    summed.relay(3, 0)
    gather.arrive(3, 0)
    model[...] = functools.reduce(
        jnp.add, [extra[shard].astype(f32) for shard in range(LINE)]
    ).astype(bf16)
    (store,) = fetch([(model, model_ref.at[tree])], osem)
    for side in SIDES:
        pl.when(far_of(place, side) > 0)(exchange(side, place - side).wait_recv)
    value = acc[...] + terms[0].astype(f32)
    for index, side in enumerate(SIDES):
        value += jnp.where(far_of(place, side) > 0, terms[index + 1].astype(f32), 0.0)
    resv[...] = value.astype(bf16)
    store.wait()
    trees.send(0)
    (store,) = fetch([(resv, sum_ref)], osem)
    heads.advance(2)
    summed.relay(3, 1)
    trees.advance(1)
    summed.relay(3, 2)
    summed.relay(3, 3)
    trees.advance(2)
    store.wait()
    size = rows // chunks
    stores = []

    def finish(chunk):
        summed.total(chunk, acc)
        here = chunk_rows(chunk, size)
        values = xv[here].astype(f32)
        rms = lax.rsqrt(jnp.mean(values * values, axis=1, keepdims=True) + eps)
        scaled = acc[here] * gain_ref[...].astype(f32)
        mean = jnp.mean(scaled * values, axis=1, keepdims=True)
        outv[here] = (midv[here] + rms * (scaled - values * (rms * rms) * mean)).astype(bf16)
        copy = pltpu.make_async_copy(outv.at[here], out_ref.at[here], wsem.at[chunk])
        copy.start()
        stores.append(copy)

    finish(0)
    finish(1)
    for number in range(3, trees.rounds):
        trees.advance(number)
        heads.advance(number)
    finish(2)
    finish(3)
    for blocks in (trees, heads):
        blocks.arrive(blocks.rounds - 1)
        blocks.drain()
    for copy in stores:
        copy.wait()
    for side in SIDES:
        pl.when(far_of(place, side) < LINE - 1)(exchange(side, place + side).wait_send)
    summed.drain()
    gather.drain()


def back(
    qkv, weight, normed, grad_middle, middle, res_parts, right, left, x, attended, grad, lse, leaf_parent, tables, exits,
    entries, gain, low_one, final_grads, exit_grads, seg,
):
    chunks = LINE
    rows, features = x.shape
    groups, total, width = qkv.shape
    rank = exits.shape[1]
    deep = (groups + 1) * rank
    pair = 2 * HEAD_DIM
    trees = lax.axis_size("dp")
    sems = pltpu.SemaphoreType.DMA((trees.bit_length() - 1,))
    two = pltpu.SemaphoreType.DMA((2,))
    return pl.pallas_call(
        functools.partial(back_body, chunks, seg),
        in_specs=[IN_HBM] * 9 + [IN_VMEM] * 12,
        out_specs=[IN_HBM] * 4,
        out_shape=[
            jax.ShapeDtypeStruct((rows, features), bf16),
            jax.ShapeDtypeStruct((trees, deep, features), bf16),
            jax.ShapeDtypeStruct((trees, deep, width), bf16),
            jax.ShapeDtypeStruct((rows, features), bf16),
        ],
        scratch_shapes=[
            pltpu.VMEM((groups, total, width), bf16),
            pltpu.VMEM((groups, total, width), bf16),
            pltpu.VMEM((pair, total), f32),
            pltpu.VMEM((total, pair), f32),
            pltpu.VMEM((total, pair), f32),
            pltpu.VMEM((LINE, rows, features), bf16),
            pltpu.VMEM((2, LINE - 1, rows, features), bf16),
            pltpu.VMEM((rows, features), f32),
            pltpu.VMEM((features, groups * width), bf16),
            pltpu.VMEM((rows, features), f32),
            pltpu.VMEM((LINE, rows, features), bf16),
            pltpu.VMEM((3, rows, features), bf16),
            pltpu.VMEM((rows, features), bf16),
            pltpu.VMEM((rows, features), bf16),
            pltpu.VMEM((rows, features), bf16),
            pltpu.VMEM((deep, features), bf16),
            pltpu.VMEM((deep, width), bf16),
            pltpu.VMEM((total, groups * rank), bf16),
            pltpu.VMEM((groups * rank, groups * width), bf16),
            pltpu.VMEM((LINE, deep, features), bf16),
            pltpu.SemaphoreType.DMA((1,)),
            pltpu.SemaphoreType.DMA((6,)),
            pltpu.SemaphoreType.DMA((1,)),
            two,
            two,
        ]
        + line_sems(chunks)
        + line_sems(1)
        + [sems] * 4,
        compiler_params=comm_params(3),
    )(
        qkv, weight, normed, grad_middle, middle, res_parts, right, left, x, attended, grad[0], lse, leaf_parent, *tables,
        exits, entries, gain[None, :], low_one, final_grads, exit_grads,
    )


def tree_tiles(seg, rows, parent_row):
    trunk = TRUNK * seg
    leaves = trunk + BRANCHES * seg
    key = lax.broadcasted_iota(jnp.int32, (QT, QT), 0)
    query = lax.broadcasted_iota(jnp.int32, (QT, QT), 1)
    causal = key <= query
    own = causal & (key // seg == query // seg)
    tiles = []
    for start in range(0, trunk, QT):
        pieces = [(0, start, None)] if start else []
        tiles.append((start, pieces + [(start, QT, causal)]))
    tiles.append((trunk, [(0, trunk, None), (trunk, QT, own)]))
    branch = lax.broadcasted_iota(jnp.int32, (BRANCHES * seg, QT), 0) // seg
    for start in range(leaves, rows, QT):
        mine = branch == parent_row[:, start - leaves : start - leaves + QT]
        tiles.append(
            (start, [(0, trunk, None), (trunk, BRANCHES * seg, mine), (start, QT, own)])
        )
    return tiles


def attend_pair(seg, qkv_ref, lanes, parent_row, pair, o_ref, lse_ref):
    rows = qkv_ref.shape[1]
    value_t = qkv_ref[2, :, lanes].T
    lane = lax.broadcasted_iota(jnp.int32, (QT, 2 * HEAD_DIM), 1)
    for start, pieces in tree_tiles(seg, rows, parent_row):
        query = qkv_ref[0, start : start + QT, lanes] * bf16(HEAD_DIM**-0.5)
        outs = []
        for h in range(2):
            own_query = jnp.where(lane // HEAD_DIM == h, query, bf16(0))
            scores = []
            for k0, count, mask in pieces:
                s = nt(qkv_ref[1, k0 : k0 + count, lanes], own_query)
                scores.append(s if mask is None else jnp.where(mask, s, -1e30))
            top = functools.reduce(
                jnp.maximum, [jnp.max(s, axis=0, keepdims=True) for s in scores]
            )
            summed, out = 0.0, 0.0
            for (k0, count, _), s in zip(pieces, scores):
                weights = jnp.exp(s - top)
                summed += jnp.sum(weights, axis=0, keepdims=True)
                out += nn(
                    value_t[h * HEAD_DIM : (h + 1) * HEAD_DIM, k0 : k0 + count],
                    weights.astype(bf16),
                )
            outs.append(out / summed)
            lse_ref[pair, h : h + 1, start : start + QT] = top + jnp.log(summed)
        o_ref[start : start + QT, lanes] = jnp.concatenate(outs, axis=0).T.astype(bf16)


def attend_back_pair(
    seg, qkv_ref, lanes, o_ref, g_ref, lse_ref, pair, parent_row, cos_ref, sin_ref, d_ref, dq_t, dk, dv
):
    rows = qkv_ref.shape[1]
    scale = bf16(HEAD_DIM**-0.5)
    key_t = qkv_ref[1, :, lanes].T
    weighed_t = (g_ref[:, lanes].astype(f32) * o_ref[:, lanes].astype(f32)).T
    lane = lax.broadcasted_iota(jnp.int32, (QT, 2 * HEAD_DIM), 1)
    dk[...] = jnp.zeros_like(dk)
    dv[...] = jnp.zeros_like(dv)
    for start, pieces in tree_tiles(seg, rows, parent_row):
        query = qkv_ref[0, start : start + QT, lanes] * scale
        grad = g_ref[start : start + QT, lanes]
        for h in range(2):
            mine = lane // HEAD_DIM == h
            own_query = jnp.where(mine, query, bf16(0))
            own_grad = jnp.where(mine, grad, bf16(0))
            band = slice(h * HEAD_DIM, (h + 1) * HEAD_DIM)
            delta = jnp.sum(weighed_t[band, start : start + QT], axis=0, keepdims=True)
            lse = lse_ref[pair, h : h + 1, start : start + QT]
            grad_q = 0.0
            for k0, count, mask in pieces:
                probs = jnp.exp(nt(qkv_ref[1, k0 : k0 + count, lanes], own_query) - lse)
                if mask is not None:
                    probs = jnp.where(mask, probs, 0.0)
                grad_probs = nt(qkv_ref[2, k0 : k0 + count, lanes], own_grad)
                grad_scores = (probs * (grad_probs - delta)).astype(bf16)
                dk[k0 : k0 + count] += nn(grad_scores, own_query)
                dv[k0 : k0 + count] += nn(probs.astype(bf16), own_grad)
                grad_q += nn(key_t[band, k0 : k0 + count], grad_scores)
            dq_t[band, start : start + QT] = grad_q
    cosine, sine = cos_ref[...], -sin_ref[...]
    d_ref[0, :, lanes] = turn(dq_t[...].T * HEAD_DIM**-0.5, cosine, sine).astype(bf16)
    d_ref[1, :, lanes] = turn(dk[...], cosine, sine).astype(bf16)
    d_ref[2, :, lanes] = dv[...].astype(bf16)


def feed_body(
    rank, tile, chunks,
    n_ref, c_ref, near_ref, wg_ref, wu_ref, wd_ref, mid_ref, wo_ref,
    pick_ref, xu_in, xd_in, e_in, f_in, gain_ref, oe_ref, att_ref, lo_ref,
    grad_ref, res_ref, right_ref, left_ref, b_ref, held_ref, far_ref, unit_out, model_out, y_ref, final_ref, exit_ref,
    unit_ref, model_ref, x_ref, e_ref, f_ref, midv, nbuf, cbuf, wbuf, low, low_t, acc_res, acc_back, acc_low,
    part, held, resv, own, extra, wo, nsem, csem, wsem, rsem, msem,
    send, recv, g_send, g_recv, x_send, x_recv, c_send, c_recv, r_send, r_recv,
):
    place = lax.axis_index("tensor")
    units = unit_ref.shape[1]
    tiles = units // tile
    rows = part.shape[1]
    summed = Near(place, part, held, send, recv, chunks)
    cots = Gather(place, far_ref, c_send, c_recv, 1, second=near_ref)
    inside = ((place + 1) // 2) % 2
    gather = Gather(place, b_ref, g_send, g_recv, chunks, own)
    joint = Gather(place, extra, x_send, x_recv, 1)

    def load_rows(order, act):
        into = order % 2
        shard = place ^ ((order + 1) % LINE)
        act(pltpu.make_async_copy(n_ref.at[shard], nbuf.at[into], nsem.at[into]))

        def take(source):
            act(pltpu.make_async_copy(source, cbuf.at[into], csem.at[into]))

        beside = (order == 0) | ((order == 2) & (inside == 1))
        pl.when(order == LINE - 1)(lambda: take(c_ref))
        pl.when(beside)(lambda: take(near_ref.at[shard]))
        pl.when(jnp.logical_not(beside) & (order < LINE - 1))(lambda: take(far_ref.at[shard]))

    def load_weights(index, into, act):
        columns = pl.ds(pl.multiple_of(index * tile, tile), tile)
        for k, w_ref in enumerate((wg_ref, wu_ref, wd_ref)):
            act(pltpu.make_async_copy(w_ref.at[:, columns], wbuf.at[into, k], wsem.at[into, k]))

    def start(copy):
        copy.start()

    def wait(copy):
        copy.wait()

    during = ((1, (2,)), (1, range(3, chunks)), (2, (0,)), (2, (1,)))
    load_rows(jnp.int32(0), start)
    load_weights(0, 0, start)
    width = wo.shape[1]
    load_middle, load_out = fetch([(mid_ref, midv), (wo_ref.at[:, 3 * width :], wo)], msem)
    for padded in (x_ref, e_ref, f_ref):
        padded[...] = jnp.zeros_like(padded)
    x_ref[0, :rank] = xu_in[0]
    x_ref[1, rank : 2 * rank] = xu_in[1]
    x_ref[2, 2 * rank :] = xd_in[...]
    e_ref[: 2 * rank] = e_in[3:].reshape(2 * rank, -1)
    f_ref[2 * rank :] = f_in[1]
    unit_ref[...] = jnp.zeros_like(unit_ref)
    model_ref[...] = jnp.zeros_like(model_ref)
    greet(place)
    cots.send(2, 0)

    def one_shard(order, carry):
        into = order % 2
        shard = place ^ ((order + 1) % LINE)
        load_rows(order, wait)
        first = nt(nbuf[into], e_ref[...]) + nt(cbuf[into], f_ref[...])
        low[...] = first.astype(bf16)
        low_t[...] = first.T.astype(bf16)
        acc_res[...] = jnp.zeros_like(acc_res)
        acc_back[...] = jnp.zeros_like(acc_back)
        acc_low[...] = jnp.zeros_like(acc_low)

        def one_tile(index, carry):
            stage = order * tiles + index
            at = stage % 2
            load_weights(index, at, wait)

            @pl.when(stage < LINE * tiles - 1)
            def _():
                load_weights((index + 1) % tiles, 1 - at, start)

            columns = pl.ds(pl.multiple_of(index * tile, tile), tile)
            x_gate, x_rise, x_fall = x_ref[0, :, columns], x_ref[1, :, columns], x_ref[2, :, columns]
            gate = nn(nbuf[into], wbuf[at, 0]) + nn(low[...], x_gate)
            rise = nn(nbuf[into], wbuf[at, 1]) + nn(low[...], x_rise)
            grad_hidden = nn(cbuf[into], wbuf[at, 2]) + nn(low[...], x_fall)
            sigmoid = jax.nn.sigmoid(gate)
            silu = gate * sigmoid
            hidden = (silu * rise).astype(bf16)
            grad_gate = (grad_hidden * rise * sigmoid * (1.0 + gate * (1.0 - sigmoid))).astype(bf16)
            grad_rise = (grad_hidden * silu).astype(bf16)
            acc_back[...] += nt(grad_gate, wbuf[at, 0]) + nt(grad_rise, wbuf[at, 1])
            acc_res[...] += nt(hidden, wbuf[at, 2])
            acc_low[...] += nt(grad_gate, x_gate) + nt(grad_rise, x_rise) + nt(hidden, x_fall)
            unit_ref[:rank, columns] += nn(low_t[:rank], grad_gate)
            unit_ref[rank : 2 * rank, columns] += nn(low_t[rank : 2 * rank], grad_rise)
            unit_ref[2 * rank :, columns] += nn(low_t[2 * rank : 3 * rank], hidden)
            for number, (away, part_chunks) in enumerate(during):

                @pl.when((order == LINE - 1) & (index == number))
                def _():
                    for chunk in part_chunks:
                        summed.send(away, chunk, 1)

            return carry

        lax.fori_loop(0, tiles, one_tile, 0)

        @pl.when(order == 0)
        def _():
            cots.relay(3, 0)
            cots.end_got(2)

        @pl.when(order == 1)
        def _():
            cots.end_got(3)

        @pl.when(order < LINE - 1)
        def _():
            load_rows(order + 1, start)

        joined = acc_low[...].astype(bf16)
        joined_t = acc_low[...].T.astype(bf16)
        part[shard] = (acc_back[...] + nn(joined, e_ref[...])).astype(bf16)
        for away in (1, 2, 3):

            @pl.when(order == away - 1)
            def _():
                for chunk in range(chunks):
                    summed.send(away, chunk, 0)
                if away == 3:
                    summed.send(1, 0, 1)
                    summed.send(1, 1, 1)

        @pl.when(order > 0)
        def _():
            pltpu.make_async_copy(resv, res_ref.at[shard], rsem.at[0]).wait()

        resv[...] = (acc_res[...] + nn(joined, f_ref[...])).astype(bf16)
        pltpu.make_async_copy(resv, res_ref.at[shard], rsem.at[0]).start()
        model_ref[: 2 * rank] += nn(joined_t[: 2 * rank], nbuf[into])
        model_ref[2 * rank :] += nn(joined_t[2 * rank : 3 * rank], cbuf[into])
        return carry

    lax.fori_loop(0, LINE, one_shard, 0)
    def pass_on(side, step, source, target):
        index = 0 if side == 1 else 1
        return pltpu.make_async_remote_copy(
            src_ref=source,
            dst_ref=held_ref.at[index, step - 1],
            send_sem=r_send.at[index, step - 1],
            recv_sem=r_recv.at[index, step - 1],
            device_id={"tensor": target},
            device_id_type=MESH,
        )

    def at_far(side, number, act):
        pl.when(far_of(place, side) == number)(act)

    def ready(side, step, shard):
        index = 0 if side == 1 else 1
        pass_on(side, step, resv, place - side).wait_recv()
        copies = [
            pltpu.make_async_copy(res_ref.at[shard], cbuf.at[0], csem.at[0]),
            pltpu.make_async_copy(held_ref.at[index, step - 1], cbuf.at[1], csem.at[1]),
        ]
        for copy in copies:
            copy.start()
        for copy in copies:
            copy.wait()
        cbuf[0] = (cbuf[0].astype(f32) + cbuf[1].astype(f32)).astype(bf16)

    def send_result(step):
        for side in SIDES:
            at_far(
                side,
                0,
                lambda: pass_on(side, step, res_ref.at[place + side * (LINE - step)], place + side).start(),
            )

    extra[place] = model_ref[...].astype(bf16)
    size = rows // chunks
    last = (LINE - 1) % 2
    load_middle.wait()
    send_result(1)

    def finish(chunk):
        summed.total(chunk, acc_back)
        here = chunk_rows(chunk, size)
        middle = midv[here]
        rms = lax.rsqrt(jnp.mean(middle * middle, axis=1, keepdims=True) + eps)
        scaled = acc_back[here] * gain_ref[...].astype(f32)
        mean = jnp.mean(scaled * middle, axis=1, keepdims=True)
        grad = cbuf[last, here].astype(f32) + rms * (scaled - middle * (rms * rms) * mean)
        own[here] = grad.astype(bf16)
        midv[here] = grad

    @pl.when(inside == 1)
    def _():
        for chunk in range(chunks):
            finish(chunk)
            gather.send(1, chunk, least=2)

    joint.send(1, 0)
    for chunk in range(2, chunks):
        summed.send(2, chunk, 1)
    for chunk in range(chunks):
        summed.send(1, chunk, 2)
    for chunk in range(chunks):
        gather.send(1, chunk, least=1, most=1)

    @pl.when(inside == 0)
    def _():
        for chunk in range(chunks):
            finish(chunk)
            gather.send(1, chunk)

    send_result(2)
    (store,) = fetch([(midv, grad_ref)], msem)
    pltpu.make_async_copy(resv, res_ref.at[place], rsem.at[0]).wait()

    load_out.wait()

    def through(number, rows_ref, shard):
        mine = pl.ds(pl.multiple_of(shard * rows, rows), rows)
        value = rows_ref[...]
        reduced = nt(value, f_in[0])
        y_ref[0, mine] = (nn(value, wo[...]) + nn(reduced.astype(bf16), oe_ref[...])).astype(bf16)
        final = nn(lo_ref[mine].astype(f32).T.astype(bf16), value)
        leave = nn(reduced.T.astype(bf16), att_ref[mine])
        final_ref[...] = final if number == 0 else final_ref[...] + final
        exit_ref[...] = leave if number == 0 else exit_ref[...] + leave

    def take(number, shard):
        copy = pltpu.make_async_copy(b_ref.at[shard], nbuf.at[number % 2], nsem.at[number % 2])
        copy.start()
        copy.wait()
        through(number, nbuf.at[number % 2], shard)

    joint.relay(2, 0)
    through(0, own, place)
    unit_out[: 3 * rank] = unit_ref[...].astype(bf16)
    unit_out[3 * rank :] = jnp.full((rank, units), pick_ref[0, 0], f32).astype(bf16)
    for chunk in range(chunks):
        gather.relay(2, chunk, least=2)
    gather.end_got(1)
    joint.relay(3, 0)
    take(1, place ^ (1 + 2 * inside))
    for chunk in range(chunks):
        gather.relay(2, chunk, most=1)
        if chunk:
            gather.relay(3, chunk - 1)
    gather.relay(3, chunks - 1)
    for side in SIDES:

        @pl.when(far_of(place, side) == 1)
        def _():
            ready(side, 1, place + side * 2)
            resv[...] = cbuf[0]
            pass_on(side, 2, resv, place + side).start()

    gather.end_got(2)
    take(2, place ^ (2 - inside))
    joint.close()
    model_out[...] = functools.reduce(
        jnp.add, [extra[shard].astype(f32) for shard in range(LINE)]
    ).astype(bf16)
    gather.end_got(3)
    take(3, place ^ (3 - inside))
    for index, side in enumerate(SIDES):
        target = (right_ref, left_ref)[index]

        @pl.when(far_of(place, side) == 0)
        def _():
            copy = pltpu.make_async_copy(res_ref.at[place + side], nbuf.at[index], nsem.at[index])
            copy.start()
            copy.wait()

        @pl.when((far_of(place, side) > 0) & (far_of(place, side) < LINE - 1))
        def _():
            ready(side, 2, place + side)
            nbuf[index] = cbuf[0]

        copy = pltpu.make_async_copy(nbuf.at[index], target, nsem.at[index])
        copy.start()
        copy.wait()
    for side in SIDES:
        for step in (1, 2):
            at_far(
                side,
                0,
                lambda: pass_on(side, step, res_ref.at[place + side * (LINE - step)], place + side).wait_send(),
            )
        at_far(side, 1, lambda: pass_on(side, 2, resv, place + side).wait_send())
    summed.drain()
    gather.drain()
    joint.drain()
    cots.drain(start=2)
    store.wait()


def feed(
    normed, cots, weights, middle, w_heads, pick, units_exit, fall_entry, entries, finals, gain, out_entry,
    attended, low_out, tile=512, chunks=5,
):
    _, rows, features = normed.shape
    units = weights[0].shape[1]
    rank, width = out_entry.shape
    total = LINE * rows
    one = jax.ShapeDtypeStruct((rows, features), bf16)
    return pl.pallas_call(
        functools.partial(feed_body, rank, tile, chunks),
        in_specs=[IN_HBM] * 8 + [pl.BlockSpec(memory_space=pltpu.SMEM)] + [IN_VMEM] * 8,
        out_specs=[IN_HBM] * 7 + [IN_VMEM] * 5,
        out_shape=[
            jax.ShapeDtypeStruct((rows, features), f32),
            jax.ShapeDtypeStruct((LINE, rows, features), bf16),
            one,
            one,
            jax.ShapeDtypeStruct((LINE, rows, features), bf16),
            jax.ShapeDtypeStruct((2, LINE - 2, rows, features), bf16),
            jax.ShapeDtypeStruct((LINE, rows, features), bf16),
            jax.ShapeDtypeStruct((4 * rank, units), bf16),
            jax.ShapeDtypeStruct((3 * rank, features), bf16),
            jax.ShapeDtypeStruct((1, total, width), bf16),
            jax.ShapeDtypeStruct((rank, features), f32),
            jax.ShapeDtypeStruct((rank, width), f32),
        ],
        scratch_shapes=[
            pltpu.VMEM((3 * rank, units), f32),
            pltpu.VMEM((3 * rank, features), f32),
            pltpu.VMEM((3, 3 * rank, units), bf16),
            pltpu.VMEM((3 * rank, features), bf16),
            pltpu.VMEM((3 * rank, features), bf16),
            pltpu.VMEM((rows, features), f32),
            pltpu.VMEM((2, rows, features), bf16),
            pltpu.VMEM((2, rows, features), bf16),
            pltpu.VMEM((2, 3, features, tile), bf16),
            pltpu.VMEM((rows, 3 * rank), bf16),
            pltpu.VMEM((3 * rank, rows), bf16),
            pltpu.VMEM((rows, features), f32),
            pltpu.VMEM((rows, features), f32),
            pltpu.VMEM((rows, 3 * rank), f32),
            pltpu.VMEM((LINE, rows, features), bf16),
            pltpu.VMEM((2, LINE - 1, rows, features), bf16),
            pltpu.VMEM((rows, features), bf16),
            pltpu.VMEM((rows, features), bf16),
            pltpu.VMEM((LINE, 3 * rank, features), bf16),
            pltpu.VMEM((features, width), bf16),
            pltpu.SemaphoreType.DMA((2,)),
            pltpu.SemaphoreType.DMA((2,)),
            pltpu.SemaphoreType.DMA((2, 3)),
            pltpu.SemaphoreType.DMA((1,)),
            pltpu.SemaphoreType.DMA((2,)),
        ]
        + line_sems(chunks)
        + line_sems(chunks)
        + line_sems(1)
        + line_sems(1)
        + [pltpu.SemaphoreType.DMA((2, LINE - 2))] * 2,
        compiler_params=comm_params(5),
    )(
        normed, *cots, *weights, middle, w_heads, pick, units_exit, fall_entry, entries, finals, gain[None, :], out_entry,
        attended, low_out,
    )


def pick_body(pick_ref, *refs):
    count = len(refs) // 2
    for source, target in zip(refs[:count], refs[count:]):
        target[...] = source[...].reshape(target.shape)


def picked(pick, arrays):
    shapes = [a.shape[:1] + a.shape[2:] for a in arrays]
    return pl.pallas_call(
        pick_body,
        grid_spec=pltpu.PrefetchScalarGridSpec(
            num_scalar_prefetch=1,
            grid=(1,),
            in_specs=[
                pl.BlockSpec(a.shape[:1] + (1,) + a.shape[2:], lambda i, p: (0, p[0], 0, 0)) for a in arrays
            ],
            out_specs=[pl.BlockSpec(shape, lambda i, p: (0, 0, 0)) for shape in shapes],
        ),
        out_shape=[jax.ShapeDtypeStruct(shape, bf16) for shape in shapes],
    )(pick, *arrays)


def per_tree(block):
    return lax.all_gather(block, "dp", axis=0, tiled=False)


def combine_body(
    rank, pick_ref, early, model, late, head, one, two, entry_ref, final_ref, unit_ref, down_ref, exit_ref, out_ref,
    one_ref, two_ref,
):
    one_ref[...] = one[...]
    two_ref[...] = two[...]
    for ref in (entry_ref, final_ref, unit_ref, down_ref, exit_ref, out_ref):
        ref[...] = jnp.zeros_like(ref)

    def one_tree(tree, carry):
        pick = pick_ref[tree]

        def block(ref, index):
            return ref[tree, index * rank : (index + 1) * rank].astype(f32)

        for k in range(3):
            entry_ref[k, pick] += block(late, k)
            exit_ref[k, pick] += block(head, k)
        final_ref[0, pick] += block(late, 3)
        out_ref[pick] += block(head, 3)
        for k in range(2):
            entry_ref[3 + k, pick] += block(model, k)
            unit_ref[k, pick] += block(early, k)
        final_ref[1, pick] += block(model, 2)
        down_ref[pick] += block(early, 2)
        return carry

    lax.fori_loop(0, early.shape[0], one_tree, 0)


def combine(picks, early, model, late, head, one, two, adapters, steps=4):
    trees, _, features = early.shape
    rank = late.shape[1] // 4
    width = head.shape[2]
    wide, narrow = features // steps, width // steps

    def taken(array, tile):
        return pl.BlockSpec((trees, array.shape[1], tile), lambda i, p: (0, 0, i))

    def given(lead, tile):
        shape = lead + (adapters, rank, tile)
        return pl.BlockSpec(shape, lambda i, p: (0,) * (len(shape) - 1) + (i,))

    whole = pl.BlockSpec((one.shape[0] // steps, one.shape[1]), lambda i, p: (i, 0))

    def shape(lead, full):
        return jax.ShapeDtypeStruct(lead + (adapters, rank, full), f32)

    return pl.pallas_call(
        functools.partial(combine_body, rank),
        grid_spec=pltpu.PrefetchScalarGridSpec(
            num_scalar_prefetch=1,
            grid=(steps,),
            in_specs=[taken(early, wide), taken(model, wide), taken(late, wide), taken(head, narrow), whole, whole],
            out_specs=[
                given((5,), wide),
                given((2,), wide),
                given((2,), wide),
                given((), wide),
                given((3,), narrow),
                given((), narrow),
                whole,
                whole,
            ],
        ),
        out_shape=[
            shape((5,), features),
            shape((2,), features),
            shape((2,), features),
            shape((), features),
            shape((3,), width),
            shape((), width),
            jax.ShapeDtypeStruct(one.shape, bf16),
            jax.ShapeDtypeStruct(two.shape, bf16),
        ],
        compiler_params=pltpu.CompilerParams(vmem_limit_bytes=VMEM_LIMIT),
    )(picks, early, model, late, head, one, two)


def local(
    tokens,
    cotangent,
    attention_gain,
    feed_gain,
    query_weight,
    key_weight,
    value_weight,
    output_weight,
    gate_weight,
    up_weight,
    down_weight,
    entry_maps,
    head_exits,
    unit_exits,
    output_entry,
    down_entry,
    final_exits,
    parents,
    adapter_pick,
):
    adapters, rank = entry_maps.shape[1], entry_maps.shape[3]
    local_rows = tokens.shape[0]
    total = local_rows * lax.axis_size("tensor")
    blocks = parents.shape[1]
    seg = total // blocks
    tables = rope_tables(blocks, seg)
    leaf_parent = (jnp.repeat(parents[0, TRUNK + BRANCHES :], seg) - TRUNK)[None, :]
    gain_one, gain_two = attention_gain, feed_gain

    w_heads = lax.all_gather(
        jnp.concatenate([query_weight, key_weight, value_weight, output_weight], axis=1),
        "dp",
        axis=0,
        tiled=True,
    )

    w_units = [
        lax.all_gather(w, "dp", axis=0, tiled=True) for w in (gate_weight, up_weight, down_weight)
    ]
    entries, heads_exit, units_exit, out_entry, fall_entry, finals = picked(
        adapter_pick,
        (
            jnp.swapaxes(entry_maps, 2, 3),
            head_exits,
            unit_exits,
            jnp.swapaxes(output_entry, 1, 2)[None],
            jnp.swapaxes(down_entry, 1, 2)[None],
            final_exits,
        ),
    )
    out_entry, fall_entry = out_entry[0], fall_entry[0]

    most_one = gather_norm(tokens, gain_one)
    full_one, qkv, middle, full_two, full_cot, low_one, attended, lse, adapt_o = front(
        most_one, w_heads, cotangent, entries, heads_exit, tables, leaf_parent, out_entry, finals, tokens, gain_two, seg
    )

    (
        grad_middle, res_parts, res_right, res_left, _, _, _, early, model_sum, grad_attended, final_grads, exit_grads,
    ) = feed(
        full_two, (cotangent, full_cot), w_units, middle, w_heads, adapter_pick.astype(f32)[None, :],
        units_exit, fall_entry, entries, finals, gain_two, out_entry, attended, adapt_o,
    )
    early = per_tree(early)
    model_all = per_tree(model_sum)

    grad_tokens, late_model, late_head, result = back(
        qkv, w_heads, full_one, grad_middle, middle, res_parts, res_right, res_left, tokens, attended, grad_attended, lse,
        leaf_parent, tables, heads_exit, entries, gain_one, low_one, final_grads, exit_grads, seg,
    )

    picks = early[:, 3 * rank, 0].astype(jnp.int32)
    grad_entries, grad_finals, grad_units, grad_down, grad_heads, grad_output, result, grad_tokens = combine(
        picks, early, model_all, late_model, late_head, result, grad_tokens, adapters
    )
    grad_entries = grad_entries.swapaxes(2, 3)
    grad_output = grad_output.swapaxes(1, 2)
    grad_down = grad_down.swapaxes(1, 2)
    return (
        result,
        grad_tokens,
        grad_entries,
        grad_heads,
        grad_units,
        grad_output,
        grad_down,
        grad_finals,
    )


def solution(mesh):
    in_specs = (
        P(("dp", "tensor"), None),
        P(("dp", "tensor"), None),
        P(),
        P(),
        P("dp", "tensor"),
        P("dp", "tensor"),
        P("dp", "tensor"),
        P("dp", "tensor"),
        P("dp", "tensor"),
        P("dp", "tensor"),
        P("dp", "tensor"),
        P(),
        P(None, None, None, "tensor"),
        P(None, None, None, "tensor"),
        P(None, "tensor", None),
        P(None, "tensor", None),
        P(),
        P("dp", None),
        P("dp"),
    )
    out_specs = (
        P(("dp", "tensor"), None),
        P(("dp", "tensor"), None),
        P(),
        P(None, None, None, "tensor"),
        P(None, None, None, "tensor"),
        P(None, "tensor", None),
        P(None, "tensor", None),
        P(),
    )
    return jax.shard_map(local, mesh=mesh, in_specs=in_specs, out_specs=out_specs, check_vma=False)
```
